32 devices in a mesh: dp: 16 (over z, y, x), seq: 2 (over core).
Axes of the slice: x: 2, y: 2, z: 4, core: 2. Of those that a mesh axis runs over, the one named last changes fastest.
Arguments:
- tokens: bfloat16 [16384, 1024], P(('dp', 'seq')), may hold values from -6 to 6
- seq_lengths: int32 [16, 3], P('dp'), may hold values from 1 to 1022, as said below
- w_query: bfloat16 [1024, 1024], P('dp', 'seq'), may hold values from -0.1875 to 0.1875
- w_key: bfloat16 [1024, 1024], P('dp', 'seq'), may hold values from -0.1875 to 0.1875
- w_value: bfloat16 [1024, 1024], P('dp', 'seq'), may hold values from -0.1875 to 0.1875
- w_out: bfloat16 [1024, 1024], P('dp', 'seq'), may hold values from -1.5 to 1.5
- w_gate: bfloat16 [1024, 2752], P('dp', 'seq'), may hold values from -0.1875 to 0.1875
- w_up: bfloat16 [1024, 2752], P('dp', 'seq'), may hold values from -0.1875 to 0.1875
- w_down: bfloat16 [2752, 1024], P('dp', 'seq'), may hold values from -0.109375 to 0.109375
- gain_attn: bfloat16 [1024], P('dp'), may hold values from 0.099609375 to 1.8984375
- gain_mlp: bfloat16 [1024], P('dp'), may hold values from 0.099609375 to 1.8984375
- cotangent: bfloat16 [16384, 1024], P(('dp', 'seq')), may hold values from -6 to 6
Outputs:
- mixed: bfloat16 [16384, 1024], P(('dp', 'seq'))
- grad_tokens: float32 [16384, 1024], P(('dp', 'seq'))
- grad_query: float32 [1024, 1024], P('dp', 'seq')
- grad_key: float32 [1024, 1024], P('dp', 'seq')
- grad_value: float32 [1024, 1024], P('dp', 'seq')
- grad_out: float32 [1024, 1024], P('dp', 'seq')
- grad_gate: float32 [1024, 2752], P('dp', 'seq')
- grad_up: float32 [1024, 2752], P('dp', 'seq')
- grad_down: float32 [2752, 1024], P('dp', 'seq')
- grad_gain_attn: float32 [1024], P('dp')
- grad_gain_mlp: float32 [1024], P('dp')
The draws below stay inside these ranges and needn't reach their ends.
Inputs may be any that keep to these rules, and one draw needn't show every extreme that they name: `seq_lengths`: each group's row holds three lengths in order: a first sequence of 1 to 256 tokens, a middle one that reaches from the group's first device to its last, and a last one of 1 to 256 tokens; the three sum to 1024; in some group the first and last sequences have one token each.
All inputs are finite; a program needn't handle non-finite values.
Results may differ from the reference program's by a relative error of at most 0.02.
Values may be sent and summed in bfloat16 or wider, within the bound.
A program may use at most 192 MiB of HBM per device.

```python
import jax
import jax.numpy as jnp
from jax import lax

D = 1024
HEADS = 16
HEAD_DIM = 64
FF = 2752
WINDOW = 64
TOK_DEV = 512
TOKENS = 16384
N_DP = 16
N_SEQ = 2


def draw_seq_lengths(key, part):
    key = jax.random.fold_in(key, 11)
    head_key, tail_key, pick_key = jax.random.split(key, 3)
    head_len = jax.random.randint(head_key, (N_DP, 1), 1, TOK_DEV // 2 + 1, dtype=jnp.int32)
    tail_len = jax.random.randint(tail_key, (N_DP, 1), 1, TOK_DEV // 2 + 1, dtype=jnp.int32)
    chosen = jax.random.randint(pick_key, (), 0, N_DP, dtype=jnp.int32)
    is_chosen = (jnp.arange(N_DP, dtype=jnp.int32) == chosen)[:, None]
    head_len = jnp.where(is_chosen, jnp.int32(1), head_len)
    tail_len = jnp.where(is_chosen, jnp.int32(1), tail_len)
    middle_len = N_SEQ * TOK_DEV - head_len - tail_len
    return jnp.concatenate([head_len, middle_len, tail_len], axis=1)


def strengthened(array, own_key, source, target, parts, factor):
    owner, partner = [(jnp.arange(array.shape[dim]) // (array.shape[dim] // parts)).reshape([-1 if axis == dim else 1 for axis in range(array.ndim)]) for dim in (source, target)]
    chosen = jax.random.permutation(own_key, parts)[partner]
    strong = (owner == chosen) | (owner == (partner + parts // 2) % parts)
    return jnp.where(strong, factor * array, array)


def steps_of(own_key, extent, cuts, smallest, top_value):
    def one(position, parts):
        draws = jax.random.uniform(jax.random.fold_in(jax.random.fold_in(own_key, 6), position), (parts,), jnp.float32, smallest / len(cuts), top_value / len(cuts))
        return jnp.repeat(jnp.exp(draws), extent[position] // parts).reshape((-1,) + (1,) * (len(extent) - position - 1))

    level = one(*cuts[0])
    for cut in cuts[1:]:
        level = level * one(*cut)
    return level


def normal_values(key, extent, width, reach, cuts=(), held_as=jnp.bfloat16):
    loudness = steps_of(key, extent, cuts, -0.22, 0.18) if cuts else 1.0
    entries = jax.random.normal(key, extent, jnp.float32) * width * loudness
    return jnp.minimum(jnp.maximum(entries, -reach), reach).astype(held_as)


def heavy_noise(stream_key, shape, spread, most, cuts, heavy, kind=jnp.bfloat16):
    values = spread * jax.random.normal(stream_key, shape, jnp.float32)
    if cuts:
        values = values * steps_of(stream_key, shape, cuts, -0.22, 0.18)
    return jnp.clip(strengthened(values, jax.random.fold_in(stream_key, 3), *heavy), -most, most).astype(kind)


def setup_inputs(seed: int = 0) -> dict:
    splits = jax.random.split(jax.random.key(seed), 13)
    return {
        "tokens": heavy_noise(splits[0], (TOKENS, D), 1.0, 6.0, ((0, 32),), (0, 1, 32, 2.75)),
        "seq_lengths": draw_seq_lengths(jax.random.fold_in(splits[12], 71), 0),
        "w_query": normal_values(splits[2], (D, D), D ** -0.5, 0.1875, ((0, 16), (1, 2))),
        "w_key": normal_values(splits[3], (D, D), D ** -0.5, 0.1875, ((0, 16), (1, 2))),
        "w_value": normal_values(splits[4], (D, D), D ** -0.5, 0.1875, ((0, 16), (1, 2))),
        "w_out": normal_values(splits[5], (D, D), (D // 64) ** -0.5, 1.5, ((0, 16), (1, 2))),
        "w_gate": normal_values(splits[6], (D, FF), D ** -0.5, 0.1875, ((0, 16), (1, 2))),
        "w_up": normal_values(splits[7], (D, FF), D ** -0.5, 0.1875, ((0, 16), (1, 2))),
        "w_down": normal_values(splits[8], (FF, D), FF ** -0.5, 0.109375, ((0, 16), (1, 2))),
        "gain_attn": jnp.clip(1.0 + 0.18 * jax.random.normal(splits[9], (D,), jnp.float32), 0.099609375, 1.8984375).astype(jnp.bfloat16),
        "gain_mlp": jnp.clip(1.0 + 0.18 * jax.random.normal(splits[10], (D,), jnp.float32), 0.099609375, 1.8984375).astype(jnp.bfloat16),
        "cotangent": heavy_noise(splits[11], (TOKENS, D), 1.0, 6.0, ((0, 32),), (0, 1, 32, 2.75)),
    }


@jax.custom_vjp
def low(v):
    return lax.optimization_barrier(v.astype(jnp.bfloat16)).astype(jnp.float32)

@jax.custom_vjp
def low_back(v):
    return v

def low_keep(v):
    return (low(v), None)

def low_pass(kept, grad):
    return (grad,)

def back_keep(v):
    return (v, None)

def back_low(kept, grad):
    return (low(grad),)
low.defvjp(low_keep, low_pass)
low_back.defvjp(back_keep, back_low)

def highest(left, right):
    return jnp.dot(left, right, precision=lax.Precision.HIGHEST)

def normalize(values, gain):
    inverse = lax.rsqrt(lax.optimization_barrier(jnp.mean(values * values, axis=-1, keepdims=True)) + 1e-05)
    return values * inverse * gain

def doc_numbers(lengths_row, positions):
    first_end = lengths_row[0]
    second_end = lengths_row[0] + lengths_row[1]
    return (positions >= first_end).astype(jnp.int32) + (positions >= second_end).astype(jnp.int32)

def window_mask(query_pos, query_doc, key_pos, key_doc, window):
    after = key_pos[None, :] >= query_pos[:, None] - window
    before = key_pos[None, :] <= query_pos[:, None]
    inside = (key_pos[None, :] >= 0) & (key_doc[None, :] == query_doc[:, None])
    return after & before & inside

def attend_group(query, keys, values, doc_ids):
    length = query.shape[0]
    block_rows = min(512, TOK_DEV)
    zeros_rim = jnp.zeros((WINDOW, HEADS, HEAD_DIM), jnp.float32)
    keys_ext = jnp.concatenate([zeros_rim, keys], axis=0)
    values_ext = jnp.concatenate([zeros_rim, values], axis=0)
    key_docs = jnp.concatenate([jnp.zeros((WINDOW,), jnp.int32), doc_ids], axis=0)

    def one_block(block_index):
        row_start = (block_index * block_rows).astype(jnp.int32)
        query_pos = row_start + jnp.arange(block_rows, dtype=jnp.int32)
        key_pos = row_start - WINDOW + jnp.arange(block_rows + WINDOW, dtype=jnp.int32)
        query_tile = lax.dynamic_slice_in_dim(query, row_start, block_rows, 0)
        key_tile = lax.dynamic_slice_in_dim(keys_ext, row_start, block_rows + WINDOW, 0)
        value_tile = lax.dynamic_slice_in_dim(values_ext, row_start, block_rows + WINDOW, 0)
        visible = window_mask(query_pos, lax.dynamic_slice_in_dim(doc_ids, row_start, block_rows, 0), key_pos, lax.dynamic_slice_in_dim(key_docs, row_start, block_rows + WINDOW, 0), WINDOW)
        scores_raw = jnp.einsum('qhd,khd->hqk', query_tile, key_tile, precision=lax.Precision.HIGHEST)
        scores = low_back(scores_raw * HEAD_DIM ** (-0.5))
        probs = jax.nn.softmax(jnp.where(visible[None], scores, -1e+30), axis=-1)
        return jnp.einsum('hqk,khd->qhd', low(probs), value_tile, precision=lax.Precision.HIGHEST)
    block_outs = lax.map(jax.checkpoint(one_block), jnp.arange(length // block_rows, dtype=jnp.int32))
    return block_outs.reshape(length, HEADS * HEAD_DIM)

def group_forward(inputs, lengths_row, weights):
    query_w, key_w, value_w, out_w, gate_w, up_w, down_w, gain_one, gain_two = weights
    length = inputs.shape[0]
    normed_one = low(normalize(inputs, gain_one))
    query = low(low_back(highest(normed_one, query_w)))
    keys = low(low_back(highest(normed_one, key_w)))
    values = low(low_back(highest(normed_one, value_w)))
    doc_ids = doc_numbers(lengths_row, jnp.arange(length, dtype=jnp.int32))
    attended = attend_group(query.reshape(length, HEADS, HEAD_DIM), keys.reshape(length, HEADS, HEAD_DIM), values.reshape(length, HEADS, HEAD_DIM), doc_ids)
    attended = low(low_back(attended))
    middle = inputs + low_back(highest(attended, out_w))
    normed_two = low(normalize(middle, gain_two))
    gate_pre = low_back(highest(normed_two, gate_w))
    up_pre = low_back(highest(normed_two, up_w))
    hidden = low(jax.nn.silu(gate_pre) * up_pre)
    return middle + low_back(highest(hidden, down_w))

def reference(tokens, seq_lengths, w_query, w_key, w_value, w_out, w_gate, w_up, w_down, gain_attn, gain_mlp, cotangent):
    group_rows = N_SEQ * TOK_DEV
    weights = (w_query.astype(jnp.float32), w_key.astype(jnp.float32), w_value.astype(jnp.float32), w_out.astype(jnp.float32), w_gate.astype(jnp.float32), w_up.astype(jnp.float32), w_down.astype(jnp.float32), gain_attn.astype(jnp.float32), gain_mlp.astype(jnp.float32))
    inputs = tokens.astype(jnp.float32)

    def forward(inputs_all, weight_set):
        groups = inputs_all.reshape(N_DP, group_rows, D)
        group_step = jax.checkpoint(lambda group_pair: group_forward(group_pair[0], group_pair[1], weight_set))
        return lax.map(group_step, (groups, seq_lengths)).reshape(N_DP * group_rows, D)
    result, pullback = jax.vjp(forward, inputs, weights)
    grad_inputs, grad_weights = pullback(cotangent.astype(jnp.float32))
    return (result.astype(jnp.bfloat16), grad_inputs, grad_weights[0], grad_weights[1], grad_weights[2], grad_weights[3], grad_weights[4], grad_weights[5], grad_weights[6], grad_weights[7], grad_weights[8])
```

```python
import functools

import jax
import jax.numpy as jnp
from jax import lax
from jax.experimental import pallas as pl
from jax.experimental.pallas import tpu as pltpu
from jax.sharding import PartitionSpec as P

HEADS = 16
HEAD_DIM = 64
WINDOW = 64


eps_norm = 1e-05


def from_behind(block, axis, distance):
    devices = range(lax.axis_size(axis))
    route = [(i - distance, i) for i in devices if i - distance in devices]
    return lax.ppermute(block, axis, route)


def inverse_rms(values):
    return lax.rsqrt(jnp.mean(values * values, axis=-1, keepdims=True) + eps_norm)


def doc_numbers(lengths_row, positions):
    first_end = lengths_row[0]
    second_end = lengths_row[0] + lengths_row[1]
    return (positions >= first_end).astype(jnp.int32) + (positions >= second_end).astype(jnp.int32)


def window_mask(query_pos, query_doc, key_pos, key_doc, window):
    after = key_pos[None, :] >= query_pos[:, None] - window
    before = key_pos[None, :] <= query_pos[:, None]
    inside = (key_pos[None, :] >= 0) & (key_doc[None, :] == query_doc[:, None])
    return after & before & inside


def norm_back(values, inverse, gain, grad_norm):
    scaled = grad_norm * gain
    mean_term = jnp.mean(values * scaled, axis=-1, keepdims=True)
    grad_values = inverse * scaled - values * (inverse * inverse * inverse) * mean_term
    grad_gain = jnp.sum(values * inverse * grad_norm, axis=0)
    return (grad_values, grad_gain)


def project(left, right):
    return jnp.dot(left, right, preferred_element_type=jnp.float32)


def project_back(grad_rows, weight):
    return jnp.einsum("tf,df->td", grad_rows, weight, preferred_element_type=jnp.float32)


def weight_grad(inputs, grad_rows):
    return jnp.einsum("td,tf->df", inputs, grad_rows, preferred_element_type=jnp.float32)


def plain_block(
    tokens,
    seq_lengths,
    w_query,
    w_key,
    w_value,
    w_out,
    w_gate,
    w_up,
    w_down,
    gain_attn,
    gain_mlp,
    cotangent,
):
    row_count = tokens.shape[0]
    block_rows = min(512, row_count)
    head_group = HEADS // 2
    score_scale = HEAD_DIM ** (-0.5)
    row_parts = (
        lax.all_gather(w_query, "dp", axis=0, tiled=True),
        lax.all_gather(w_key, "dp", axis=0, tiled=True),
        lax.all_gather(w_value, "dp", axis=0, tiled=True),
        lax.all_gather(w_out, "dp", axis=0, tiled=True),
        lax.all_gather(w_gate, "dp", axis=0, tiled=True),
        lax.all_gather(w_up, "dp", axis=0, tiled=True),
        lax.all_gather(w_down, "dp", axis=0, tiled=True),
        lax.all_gather(gain_attn, "dp", axis=0, tiled=True),
        lax.all_gather(gain_mlp, "dp", axis=0, tiled=True),
    )
    full_mats = (
        lax.all_gather(row_parts[0], "seq", axis=1, tiled=True),
        lax.all_gather(row_parts[1], "seq", axis=1, tiled=True),
        lax.all_gather(row_parts[2], "seq", axis=1, tiled=True),
        lax.all_gather(row_parts[3], "seq", axis=1, tiled=True),
        lax.all_gather(row_parts[4], "seq", axis=1, tiled=True),
        lax.all_gather(row_parts[5], "seq", axis=1, tiled=True),
        lax.all_gather(row_parts[6], "seq", axis=1, tiled=True),
    )
    query_w, key_w, value_w, out_w, gate_w, up_w, down_full = full_mats
    gain_one = row_parts[7].astype(jnp.float32)
    gain_two = row_parts[8].astype(jnp.float32)
    inputs = tokens.astype(jnp.float32)
    inv_one = inverse_rms(inputs)
    normed_one = (inputs * inv_one * gain_one).astype(jnp.bfloat16)
    query_low = project(normed_one, query_w).astype(jnp.bfloat16)
    key_low = project(normed_one, key_w).astype(jnp.bfloat16)
    value_low = project(normed_one, value_w).astype(jnp.bfloat16)
    rim_pairs = from_behind(
        (key_low[row_count - WINDOW :], value_low[row_count - WINDOW :]), "seq", 1
    )
    keys_ext = jnp.concatenate([rim_pairs[0], key_low], axis=0).reshape(
        row_count + WINDOW, HEADS, HEAD_DIM
    )
    values_ext = jnp.concatenate([rim_pairs[1], value_low], axis=0).reshape(
        row_count + WINDOW, HEADS, HEAD_DIM
    )
    query_heads = query_low.reshape(row_count, HEADS, HEAD_DIM)
    span_start = lax.axis_index("seq") * row_count
    query_pos = span_start + jnp.arange(row_count, dtype=jnp.int32)
    key_pos = span_start - WINDOW + jnp.arange(row_count + WINDOW, dtype=jnp.int32)
    query_doc = doc_numbers(seq_lengths[0], query_pos)
    key_doc = doc_numbers(seq_lengths[0], key_pos)

    def tile_scores(row_start, head_start):
        visible = window_mask(query_pos, query_doc, key_pos, key_doc, WINDOW)
        scores_raw = (
            jnp.einsum(
                "qhd,khd->hqk",
                query_heads[
                    row_start : row_start + block_rows, head_start : head_start + head_group
                ],
                keys_ext[
                    row_start : row_start + block_rows + WINDOW,
                    head_start : head_start + head_group,
                ],
                preferred_element_type=jnp.float32,
            )
            * score_scale
        )
        return jnp.where(visible[None], scores_raw, -1e30)

    log_totals = {}
    row_start = 0
    head_parts = []
    for head_start in range(0, HEADS, head_group):
        masked_scores = tile_scores(row_start, head_start)
        top_score = jnp.max(masked_scores, axis=-1, keepdims=True)
        log_total = top_score + jnp.log(
            jnp.sum(jnp.exp(masked_scores - top_score), axis=-1, keepdims=True)
        )
        prob_low = jnp.exp(masked_scores - log_total).astype(jnp.bfloat16)
        value_tile = values_ext[
            row_start : row_start + block_rows + WINDOW, head_start : head_start + head_group
        ]
        head_parts.append(
            jnp.einsum("hqk,khd->qhd", prob_low, value_tile, preferred_element_type=jnp.float32)
        )
        log_totals[row_start, head_start] = log_total
    attn_blocks = jnp.concatenate(head_parts, axis=1)
    attended = attn_blocks.reshape(row_count, HEADS * HEAD_DIM).astype(jnp.bfloat16)
    middle = inputs + project(attended, out_w)
    inv_two = inverse_rms(middle)
    normed_two = (middle * inv_two * gain_two).astype(jnp.bfloat16)
    gate_pre = project(normed_two, gate_w)
    up_pre = project(normed_two, up_w)
    gate_act = jax.nn.silu(gate_pre)
    hidden = (gate_act * up_pre).astype(jnp.bfloat16)
    block_out = (middle + project(hidden, down_full)).astype(jnp.bfloat16)
    rows_again = (
        lax.all_gather(w_query, "dp", axis=0, tiled=True),
        lax.all_gather(w_key, "dp", axis=0, tiled=True),
        lax.all_gather(w_value, "dp", axis=0, tiled=True),
        lax.all_gather(w_out, "dp", axis=0, tiled=True),
        lax.all_gather(w_gate, "dp", axis=0, tiled=True),
        lax.all_gather(w_up, "dp", axis=0, tiled=True),
        lax.all_gather(w_down, "dp", axis=0, tiled=True),
        lax.all_gather(gain_attn, "dp", axis=0, tiled=True),
        lax.all_gather(gain_mlp, "dp", axis=0, tiled=True),
    )
    mats_again = (
        lax.all_gather(rows_again[0], "seq", axis=1, tiled=True),
        lax.all_gather(rows_again[1], "seq", axis=1, tiled=True),
        lax.all_gather(rows_again[2], "seq", axis=1, tiled=True),
        lax.all_gather(rows_again[3], "seq", axis=1, tiled=True),
        lax.all_gather(rows_again[4], "seq", axis=1, tiled=True),
        lax.all_gather(rows_again[5], "seq", axis=1, tiled=True),
        lax.all_gather(rows_again[6], "seq", axis=1, tiled=True),
    )
    back_query, back_key, back_value, back_out, back_gate, back_up, back_down = mats_again
    back_gain_one = rows_again[7].astype(jnp.float32)
    back_gain_two = rows_again[8].astype(jnp.float32)
    grad_final = cotangent.astype(jnp.float32)
    d_down = weight_grad(hidden, cotangent)
    grad_hidden = project_back(cotangent, back_down)
    sigmoid_gate = jax.nn.sigmoid(gate_pre)
    grad_gate_low = (
        grad_hidden * up_pre * sigmoid_gate * (1.0 + gate_pre * (1.0 - sigmoid_gate))
    ).astype(jnp.bfloat16)
    grad_up_low = (grad_hidden * gate_act).astype(jnp.bfloat16)
    d_gate = weight_grad(normed_two, grad_gate_low)
    d_up = weight_grad(normed_two, grad_up_low)
    grad_normed_two = project_back(grad_gate_low, back_gate) + project_back(grad_up_low, back_up)
    grad_mid_norm, d_gain_two = norm_back(middle, inv_two, back_gain_two, grad_normed_two)
    grad_middle = grad_final + grad_mid_norm
    grad_proj = grad_middle.astype(jnp.bfloat16)
    d_out = weight_grad(attended, grad_proj)
    grad_attended = (
        project_back(grad_proj, back_out).astype(jnp.bfloat16).reshape(row_count, HEADS, HEAD_DIM)
    )
    grad_keys_ext = jnp.zeros((row_count + WINDOW, HEADS, HEAD_DIM), jnp.float32)
    grad_values_ext = jnp.zeros((row_count + WINDOW, HEADS, HEAD_DIM), jnp.float32)
    row_start = 0
    head_parts = []
    for head_start in range(0, HEADS, head_group):
        head_end = head_start + head_group
        masked_scores = tile_scores(row_start, head_start)
        prob_full = jnp.exp(masked_scores - log_totals[row_start, head_start])
        grad_tile = grad_attended[row_start : row_start + block_rows, head_start:head_end]
        key_tile = keys_ext[row_start : row_start + block_rows + WINDOW, head_start:head_end]
        value_tile = values_ext[row_start : row_start + block_rows + WINDOW, head_start:head_end]
        query_tile = query_heads[row_start : row_start + block_rows, head_start:head_end]
        grad_prob = jnp.einsum(
            "qhd,khd->hqk", grad_tile, value_tile, preferred_element_type=jnp.float32
        )
        inner = jnp.sum(prob_full * grad_prob, axis=-1, keepdims=True)
        grad_score = (prob_full * (grad_prob - inner)).astype(jnp.bfloat16)
        head_parts.append(
            jnp.einsum("hqk,khd->qhd", grad_score, key_tile, preferred_element_type=jnp.float32)
            * score_scale
        )
        key_term = (
            jnp.einsum("hqk,qhd->khd", grad_score, query_tile, preferred_element_type=jnp.float32)
            * score_scale
        )
        value_term = jnp.einsum(
            "hqk,qhd->khd",
            prob_full.astype(jnp.bfloat16),
            grad_tile,
            preferred_element_type=jnp.float32,
        )
        grad_keys_ext = grad_keys_ext.at[
            row_start : row_start + block_rows + WINDOW, head_start:head_end
        ].add(key_term)
        grad_values_ext = grad_values_ext.at[
            row_start : row_start + block_rows + WINDOW, head_start:head_end
        ].add(value_term)
    grad_query_blocks = jnp.concatenate(head_parts, axis=1)
    rim_back = (
        from_behind(
            grad_keys_ext[:WINDOW].reshape(WINDOW, HEADS * HEAD_DIM).astype(jnp.bfloat16), "seq", -1
        ).astype(jnp.float32),
        from_behind(
            grad_values_ext[:WINDOW].reshape(WINDOW, HEADS * HEAD_DIM).astype(jnp.bfloat16),
            "seq",
            -1,
        ).astype(jnp.float32),
    )
    grad_keys = (
        grad_keys_ext[WINDOW:]
        .reshape(row_count, HEADS * HEAD_DIM)
        .at[row_count - WINDOW :]
        .add(rim_back[0])
    )
    grad_values = (
        grad_values_ext[WINDOW:]
        .reshape(row_count, HEADS * HEAD_DIM)
        .at[row_count - WINDOW :]
        .add(rim_back[1])
    )
    grad_query_low = grad_query_blocks.reshape(row_count, HEADS * HEAD_DIM).astype(jnp.bfloat16)
    grad_key_low = grad_keys.astype(jnp.bfloat16)
    grad_value_low = grad_values.astype(jnp.bfloat16)
    d_query = weight_grad(normed_one, grad_query_low)
    d_key = weight_grad(normed_one, grad_key_low)
    d_value = weight_grad(normed_one, grad_value_low)
    grad_normed_one = (
        project_back(grad_query_low, back_query)
        + project_back(grad_key_low, back_key)
        + project_back(grad_value_low, back_value)
    )
    grad_in_norm, d_gain_one = norm_back(inputs, inv_one, back_gain_one, grad_normed_one)
    grad_inputs = grad_middle + grad_in_norm
    row_sums = (
        lax.psum_scatter(
            d_query.astype(jnp.bfloat16), "dp", scatter_dimension=0, tiled=True
        ).astype(jnp.float32),
        lax.psum_scatter(d_key.astype(jnp.bfloat16), "dp", scatter_dimension=0, tiled=True).astype(
            jnp.float32
        ),
        lax.psum_scatter(
            d_value.astype(jnp.bfloat16), "dp", scatter_dimension=0, tiled=True
        ).astype(jnp.float32),
        lax.psum_scatter(d_out.astype(jnp.bfloat16), "dp", scatter_dimension=0, tiled=True).astype(
            jnp.float32
        ),
        lax.psum_scatter(d_gate.astype(jnp.bfloat16), "dp", scatter_dimension=0, tiled=True).astype(
            jnp.float32
        ),
        lax.psum_scatter(d_up.astype(jnp.bfloat16), "dp", scatter_dimension=0, tiled=True).astype(
            jnp.float32
        ),
        lax.psum_scatter(d_down.astype(jnp.bfloat16), "dp", scatter_dimension=0, tiled=True).astype(
            jnp.float32
        ),
        lax.psum_scatter(
            d_gain_one.astype(jnp.bfloat16), "dp", scatter_dimension=0, tiled=True
        ).astype(jnp.float32),
        lax.psum_scatter(
            d_gain_two.astype(jnp.bfloat16), "dp", scatter_dimension=0, tiled=True
        ).astype(jnp.float32),
    )
    owned_mats = (
        lax.psum_scatter(
            row_sums[0].astype(jnp.bfloat16), "seq", scatter_dimension=1, tiled=True
        ).astype(jnp.float32),
        lax.psum_scatter(
            row_sums[1].astype(jnp.bfloat16), "seq", scatter_dimension=1, tiled=True
        ).astype(jnp.float32),
        lax.psum_scatter(
            row_sums[2].astype(jnp.bfloat16), "seq", scatter_dimension=1, tiled=True
        ).astype(jnp.float32),
        lax.psum_scatter(
            row_sums[3].astype(jnp.bfloat16), "seq", scatter_dimension=1, tiled=True
        ).astype(jnp.float32),
        lax.psum_scatter(
            row_sums[4].astype(jnp.bfloat16), "seq", scatter_dimension=1, tiled=True
        ).astype(jnp.float32),
        lax.psum_scatter(
            row_sums[5].astype(jnp.bfloat16), "seq", scatter_dimension=1, tiled=True
        ).astype(jnp.float32),
        lax.psum_scatter(
            row_sums[6].astype(jnp.bfloat16), "seq", scatter_dimension=1, tiled=True
        ).astype(jnp.float32),
    )
    owned_gains = lax.psum((row_sums[7], row_sums[8]), "seq")
    return (
        block_out,
        grad_inputs,
        owned_mats[0],
        owned_mats[1],
        owned_mats[2],
        owned_mats[3],
        owned_mats[4],
        owned_mats[5],
        owned_mats[6],
        owned_gains[0],
        owned_gains[1],
    )


MESH = pl.DeviceIdType.MESH
NZ, NY, NX = 4, 2, 2
SEQUENCE = {"zfx": "zxy", "zfy": "zyx", "zmx": "xzy", "zmy": "yzx"}
ALL_Z, ALL_Y, ALL_X = pl.ds(0, NZ), pl.ds(0, NY), pl.ds(0, NX)


class Plan:
    def __init__(self, tensors):
        self.tensors = tensors
        self.items, self.of_tensor = [], []
        for t, (rows, _, kind, splits, _) in enumerate(tensors):
            begin, mine = 0, []
            for half, count in enumerate(splits):
                mine.append(len(self.items))
                self.items.append((t, SEQUENCE[kind + "xy"[half]], begin, count))
                begin += count
            self.of_tensor.append(mine)


class Place:
    def __init__(self):
        self.c, self.s = lax.axis_index("dp"), lax.axis_index("seq")
        self.z, self.y, self.x = self.c // 4, (self.c // 2) % 2, self.c % 2

    def at(self, z, y, x):
        return (z * 4 + y * 2 + x, self.s)

    def to_x(self):
        return self.at(self.z, self.y, 1 - self.x)

    def to_y(self):
        return self.at(self.z, 1 - self.y, self.x)

    def to_z(self, step):
        return self.at((self.z + step) % NZ, self.y, self.x)

    def to_core(self):
        return (self.c, 1 - self.s)

    def greet(self):
        barrier = pltpu.get_barrier_semaphore()
        peers = [self.to_x(), self.to_y(), self.to_core()] + [self.to_z(k) for k in (1, 2, 3)]
        for peer in peers:
            pl.semaphore_signal(barrier, inc=1, device_id=peer, device_id_type=MESH)
        pl.semaphore_wait(barrier, len(peers))


def remote(src, dst, send, recv, device):
    return pltpu.make_async_remote_copy(
        src_ref=src, dst_ref=dst, send_sem=send, recv_sem=recv, device_id=device, device_id_type=MESH
    )


class Gather:
    def __init__(self, plan, place, shards, bufs, send, recv, local):
        self.plan, self.me, self.shards, self.bufs = plan, place, shards, bufs
        self.send, self.recv, self.local = send, recv, local

    def own_copy(self, t):
        me = self.me
        return pltpu.make_async_copy(
            self.shards[t], self.bufs[t].at[me.s, me.z, me.y, me.x], self.local.at[t]
        )

    def moves(self, i, phase):
        t, seq, begin, count = self.plan.items[i]
        me, buf = self.me, self.bufs[t]
        rows = pl.ds(begin, count)

        def view(z, y, x, half=me.s):
            return buf.at[half, z, y, x, rows, :]

        if phase == 3:
            whole = view(ALL_Z, ALL_Y, ALL_X)
            return [(whole, whole, me.to_core(), view(ALL_Z, ALL_Y, ALL_X, 1 - me.s), 0)]
        done, axis = seq[:phase], seq[phase]
        z = ALL_Z if "z" in done else me.z
        y = ALL_Y if "y" in done else me.y
        x = ALL_X if "x" in done else me.x
        there = view(z, y, x)
        here = self.shards[t].at[rows, :] if phase == 0 else there
        if axis == "x":
            return [(here, there, me.to_x(), view(z, y, 1 - me.x), 0)]
        if axis == "y":
            return [(here, there, me.to_y(), view(z, 1 - me.y, x), 0)]
        return [
            (here, there, me.to_z(k), view((me.z + NZ - k) % NZ, y, x), k - 1) for k in (1, 2, 3)
        ]

    def copy(self, i, phase, src, dst, device, k):
        return remote(src, dst, self.send.at[i, phase, k], self.recv.at[i, phase, k], device)

    def start(self, i, phase):
        for here, there, device, _, k in self.moves(i, phase):
            self.copy(i, phase, here, there, device, k).start()

    def wait(self, i, phase):
        for _, _, device, arrived, k in self.moves(i, phase):
            self.copy(i, phase, arrived, arrived, device, k).wait_recv()

    def finish(self, i):
        for phase in range(4):
            for here, there, device, _, k in self.moves(i, phase):
                self.copy(i, phase, here, there, device, k).wait_send()


def staged_order(tensors, lags):
    order = []
    for step in range(tensors + max(lags)):
        for phase, lag in enumerate(lags):
            if 0 <= step - lag < tensors:
                order.append((step - lag, phase))
    return order


def got_shapes(plan):
    shapes = []
    for rows, columns, kind, _, dtype in plan.tensors:
        second, third = ((1, NZ), (3,)) if kind == "zf" else ((3, 2), (1,))
        shapes.append([(d + (rows, columns), dtype) for d in ((NZ, 2), second, third)])
    return shapes


class Scatter:
    def __init__(self, plan, place, total, got, out, send, recv):
        self.plan, self.me, self.total, self.got, self.out = plan, place, total, got, out
        self.send, self.recv = send, recv

    def moves(self, i, phase):
        t, seq, begin, count = self.plan.items[i]
        me, total, got = self.me, self.total[t], self.got[t][phase]
        rows = pl.ds(begin, count)
        axis, done = seq[2 - phase], seq[3 - phase :]
        z = me.z if "z" in done else ALL_Z
        y = me.y if "y" in done else ALL_Y
        x = me.x if "x" in done else ALL_X
        if phase == 0:
            lands = [got.at[ALL_Z, pl.ds(0, 2), rows, :]]
        elif phase == 1:
            lands = [got.at[k, pl.ds(0, got.shape[1]), rows, :] for k in range(got.shape[0])]
        else:
            lands = [got.at[k, rows, :] for k in range(got.shape[0])]
        if axis == "x":
            return [(total.at[z, y, 1 - me.x, rows, :], lands[0], me.to_x(), 0)]
        if axis == "y":
            return [(total.at[z, 1 - me.y, x, rows, :], lands[0], me.to_y(), 0)]
        return [
            (total.at[(me.z + k) % NZ, y, x, rows, :], lands[k - 1], me.to_z(k), k - 1)
            for k in (1, 2, 3)
        ]

    def copy(self, i, phase, src, dst, device, k):
        return remote(src, dst, self.send.at[i, phase, k], self.recv.at[i, phase, k], device)

    def start(self, i, phase):
        for here, there, device, k in self.moves(i, phase):
            self.copy(i, phase, here, there, device, k).start()

    def wait(self, i, phase):
        for here, there, device, k in self.moves(i, phase):
            self.copy(i, phase, there, there, device, k).wait_recv()

    def add(self, i, phase):
        t, seq, begin, count = self.plan.items[i]
        me, total, got = self.me, self.total[t], self.got[t][phase]
        rows = pl.ds(begin, count)
        if phase == 0:
            for z in range(NZ):
                for o in range(2):
                    at = (z, me.y, o) if seq[2] == "y" else (z, o, me.x)
                    total[at + (rows,)] += got[z, o, rows]
        elif phase == 1 and seq[1] != "z":
            for z in range(NZ):
                total[z, me.y, me.x, rows] += got[0, z, rows]
        elif phase == 1:
            for o in range(2):
                at = (me.z, me.y, o) if seq[2] == "y" else (me.z, o, me.x)
                part = total[at + (rows,)].astype(jnp.float32)
                for k in range(3):
                    part += got[k, o, rows].astype(jnp.float32)
                total[at + (rows,)] = part.astype(total.dtype)
        else:
            part = total[me.z, me.y, me.x, rows].astype(jnp.float32)
            for k in range(got.shape[0]):
                part += got[k, rows].astype(jnp.float32)
            self.out[t][rows] = part

    def finish(self, i):
        for phase in range(3):
            for here, there, device, k in self.moves(i, phase):
                self.copy(i, phase, here, there, device, k).wait_send()


def gather_kernel(plan, *refs):
    n = len(plan.tensors)
    shards, bufs = refs[:n], refs[n : 2 * n]
    send, recv, local = refs[2 * n :]
    me = Place()
    me.greet()
    gather = Gather(plan, me, shards, bufs, send, recv, local)
    for t in range(n):
        gather.own_copy(t).start()
    for i in range(len(plan.items)):
        gather.start(i, 0)
    for t in range(n):
        gather.own_copy(t).wait()
    for t, phase in staged_order(n, (0, 2, 4)):
        for i in plan.of_tensor[t]:
            gather.wait(i, phase)
            gather.start(i, phase + 1)
    for i in range(len(plan.items)):
        gather.wait(i, 3)
    for i in range(len(plan.items)):
        gather.finish(i)


def gather_all(plan, shards):
    n, k = len(plan.tensors), len(plan.items)
    anywhere = pl.BlockSpec(memory_space=pl.ANY)
    return pl.pallas_call(
        functools.partial(gather_kernel, plan),
        out_shape=[
            jax.ShapeDtypeStruct((2, NZ, NY, NX) + t[:2], jnp.bfloat16) for t in plan.tensors
        ],
        in_specs=[anywhere] * n,
        out_specs=[anywhere] * n,
        scratch_shapes=[
            pltpu.SemaphoreType.DMA((k, 4, 3)),
            pltpu.SemaphoreType.DMA((k, 4, 3)),
            pltpu.SemaphoreType.DMA((n,)),
        ],
        compiler_params=pltpu.CompilerParams(collective_id=0, has_side_effects=True),
        name="gather_all",
    )(*shards)


def scatter_kernel(plan, *refs):
    n = len(plan.tensors)
    parts, outs, refs = refs[:n], refs[n : 2 * n], refs[2 * n :]
    total, other, refs = refs[:n], refs[n : 2 * n], refs[2 * n :]
    got, refs = [refs[3 * t : 3 * t + 3] for t in range(n)], refs[3 * n :]
    send, recv, core_send, core_recv, local = refs
    me = Place()
    me.greet()
    scatter = Scatter(plan, me, total, got, outs, send, recv)
    own, across = [], []
    for t in range(n):
        across.append(
            remote(parts[t].at[1 - me.s], other[t], core_send.at[t], core_recv.at[t], me.to_core())
        )
        across[t].start()
        own.append(pltpu.make_async_copy(parts[t].at[me.s], total[t], local.at[t]))
        own[t].start()
    for t, step in staged_order(n, (0, 2, 4, 6)):
        if step == 0:
            own[t].wait()
            across[t].wait_recv()

            def add(j, _):
                at = (j // (NY * NX), (j // NX) % NY, j % NX)
                total[t][at] += other[t][at]
                return 0

            lax.fori_loop(0, NZ * NY * NX, add, 0)
        for i in plan.of_tensor[t]:
            if step:
                scatter.wait(i, step - 1)
                scatter.add(i, step - 1)
            if step < 3:
                scatter.start(i, step)
    for i in range(len(plan.items)):
        scatter.finish(i)
    for t in range(n):
        across[t].wait_send()


def scatter_all(plan, parts):
    n, k = len(plan.tensors), len(plan.items)
    anywhere = pl.BlockSpec(memory_space=pl.ANY)
    inside = pl.BlockSpec(memory_space=pltpu.VMEM)
    halves = [pltpu.VMEM((NZ, NY, NX) + t[:2], t[4]) for t in plan.tensors]
    got = [pltpu.VMEM(*shape) for shapes in got_shapes(plan) for shape in shapes]
    return pl.pallas_call(
        functools.partial(scatter_kernel, plan),
        out_shape=[jax.ShapeDtypeStruct(t[:2], jnp.float32) for t in plan.tensors],
        in_specs=[anywhere] * n,
        out_specs=[inside] * n,
        scratch_shapes=halves
        + halves
        + got
        + [
            pltpu.SemaphoreType.DMA((k, 3, 3)),
            pltpu.SemaphoreType.DMA((k, 3, 3)),
            pltpu.SemaphoreType.DMA((n,)),
            pltpu.SemaphoreType.DMA((n,)),
            pltpu.SemaphoreType.DMA((n,)),
        ],
        compiler_params=pltpu.CompilerParams(
            collective_id=1, has_side_effects=True, vmem_limit_bytes=60 * 2**20
        ),
        name="scatter_all",
    )(*parts)


def swift_block(
    tokens,
    seq_lengths,
    w_query,
    w_key,
    w_value,
    w_out,
    w_gate,
    w_up,
    w_down,
    gain_attn,
    gain_mlp,
    cotangent,
):
    row_count, width = tokens.shape
    chips = NZ * NY * NX
    rows, columns = w_query.shape
    ff_part = w_down.shape[0]
    ff_tile = -(-ff_part // 16) * 16
    wide = w_gate.shape[1] // ff_part * ff_tile
    low = jnp.bfloat16
    square = (rows, columns, "zf", (rows // 2, rows // 2), low)
    square_m = (rows, columns, "zm", (rows // 2, rows // 2), low)
    broad = (rows, wide, "zf", (rows // 2, rows // 2), low)
    first = ff_tile // 32 * 16 + 16 * (ff_tile // 16 % 2)
    tall = (ff_tile, columns, "zm", (first, ff_tile - first), low)
    place = lax.axis_index("dp")

    def pad_columns(w):
        return jnp.pad(w.reshape(rows, -1, ff_part), ((0, 0), (0, 0), (0, ff_tile - ff_part))).reshape(rows, wide)

    def unpad_columns(w):
        return w.reshape(rows, -1, ff_tile)[:, :, :ff_part].reshape(rows, -1)

    pair = jnp.zeros((2, 16, 2 * rows), low).at[0, 0:2, :rows].set(jnp.stack([gain_attn, gain_mlp]))
    pair = pair.at[1, 0:2, rows:].set(jnp.stack([gain_attn, gain_mlp]))[place % 2]
    plan = Plan([(16, 2 * rows, "zf", (16,), low), square, square, square_m, square, broad, broad, tall])
    bufs = gather_all(
        plan,
        [pair, w_query, w_key, w_value, w_out, pad_columns(w_gate), pad_columns(w_up), jnp.pad(w_down, ((0, ff_tile - ff_part), (0, 0)))],
    )
    gains = bufs[0][0, ..., 0:2, :].reshape(chips // 2, 2, 2, 2 * rows).sum(1).transpose(1, 0, 2).reshape(2, width)
    gain_one, gain_two = gains[0].astype(jnp.float32), gains[1].astype(jnp.float32)
    query_w, key_w, value_w, out_w, gate_w, up_w, down_full = [
        b.reshape(2, -1, b.shape[-1]).transpose(1, 0, 2).reshape(b.shape[-2] * chips, -1) for b in bufs[1:]
    ]
    outs = compute_block(
        tokens, seq_lengths, query_w, key_w, value_w, out_w, gate_w, up_w, down_full, gain_one, gain_two, cotangent
    )
    block_out, grad_inputs, d_query, d_key, d_value, d_out, d_gate, d_up, d_down, d_gain_one, d_gain_two = outs

    def halves(d):
        d = d.astype(low)
        return d.reshape(d.shape[0], 2, -1).transpose(1, 0, 2).reshape(2, NZ, NY, NX, d.shape[0] // chips, -1)

    d_gains = jnp.stack([d_gain_one, d_gain_two]).reshape(2, chips // 2, 1, 2 * rows)
    d_gains = jnp.broadcast_to(d_gains, (2, chips // 2, 2, 2 * rows)).reshape(2, chips, 2 * rows).transpose(1, 0, 2)
    d_gains = jnp.pad(d_gains, ((0, 0), (0, 6), (0, 0))).reshape(1, NZ, NY, NX, 8, 2 * rows)
    d_gains = jnp.concatenate([d_gains, d_gains], axis=0)
    plan_back = Plan([tall, broad, broad, square, square, square, square_m, (8, 2 * rows, "zf", (8,), jnp.float32)])
    sums = scatter_all(
        plan_back, [halves(d) for d in (d_down, d_up, d_gate, d_out, d_query, d_key, d_value)] + [d_gains]
    )
    own = lax.dynamic_slice_in_dim(sums[7], (place % 2) * rows, rows, 1)
    return (
        block_out,
        grad_inputs,
        sums[4],
        sums[5],
        sums[6],
        sums[3],
        unpad_columns(sums[2]),
        unpad_columns(sums[1]),
        sums[0][:ff_part],
        own[0],
        own[1],
    )


def compute_block(
    tokens,
    seq_lengths,
    query_w,
    key_w,
    value_w,
    out_w,
    gate_w,
    up_w,
    down_full,
    gain_one,
    gain_two,
    cotangent,
):
    row_count = tokens.shape[0]
    block_rows = min(512, row_count)
    head_group = HEADS // 2
    score_scale = HEAD_DIM ** (-0.5)
    inputs = tokens.astype(jnp.float32)
    inv_one = inverse_rms(inputs)
    normed_one = (inputs * inv_one * gain_one).astype(jnp.bfloat16)
    query_low = project(normed_one, query_w).astype(jnp.bfloat16)
    key_low = project(normed_one, key_w).astype(jnp.bfloat16)
    value_low = project(normed_one, value_w).astype(jnp.bfloat16)
    rim_pairs = from_behind(
        (key_low[row_count - WINDOW :], value_low[row_count - WINDOW :]), "seq", 1
    )
    keys_ext = jnp.concatenate([rim_pairs[0], key_low], axis=0).reshape(
        row_count + WINDOW, HEADS, HEAD_DIM
    )
    values_ext = jnp.concatenate([rim_pairs[1], value_low], axis=0).reshape(
        row_count + WINDOW, HEADS, HEAD_DIM
    )
    query_heads = query_low.reshape(row_count, HEADS, HEAD_DIM)
    span_start = lax.axis_index("seq") * row_count
    query_pos = span_start + jnp.arange(row_count, dtype=jnp.int32)
    key_pos = span_start - WINDOW + jnp.arange(row_count + WINDOW, dtype=jnp.int32)
    query_doc = doc_numbers(seq_lengths[0], query_pos)
    key_doc = doc_numbers(seq_lengths[0], key_pos)

    def tile_scores(row_start, head_start):
        visible = window_mask(query_pos, query_doc, key_pos, key_doc, WINDOW)
        scores_raw = (
            jnp.einsum(
                "qhd,khd->hqk",
                query_heads[
                    row_start : row_start + block_rows, head_start : head_start + head_group
                ],
                keys_ext[
                    row_start : row_start + block_rows + WINDOW,
                    head_start : head_start + head_group,
                ],
                preferred_element_type=jnp.float32,
            )
            * score_scale
        )
        return jnp.where(visible[None], scores_raw, -1e30)

    log_totals = {}
    row_start = 0
    head_parts = []
    for head_start in range(0, HEADS, head_group):
        masked_scores = tile_scores(row_start, head_start)
        top_score = jnp.max(masked_scores, axis=-1, keepdims=True)
        log_total = top_score + jnp.log(
            jnp.sum(jnp.exp(masked_scores - top_score), axis=-1, keepdims=True)
        )
        prob_low = jnp.exp(masked_scores - log_total).astype(jnp.bfloat16)
        value_tile = values_ext[
            row_start : row_start + block_rows + WINDOW, head_start : head_start + head_group
        ]
        head_parts.append(
            jnp.einsum("hqk,khd->qhd", prob_low, value_tile, preferred_element_type=jnp.float32)
        )
        log_totals[row_start, head_start] = log_total
    attn_blocks = jnp.concatenate(head_parts, axis=1)
    attended = attn_blocks.reshape(row_count, HEADS * HEAD_DIM).astype(jnp.bfloat16)
    middle = inputs + project(attended, out_w)
    inv_two = inverse_rms(middle)
    normed_two = (middle * inv_two * gain_two).astype(jnp.bfloat16)
    gate_pre = project(normed_two, gate_w)
    up_pre = project(normed_two, up_w)
    gate_act = jax.nn.silu(gate_pre)
    hidden = (gate_act * up_pre).astype(jnp.bfloat16)
    block_out = (middle + project(hidden, down_full)).astype(jnp.bfloat16)
    grad_final = cotangent.astype(jnp.float32)
    d_down = weight_grad(hidden, cotangent)
    grad_hidden = project_back(cotangent, down_full)
    sigmoid_gate = jax.nn.sigmoid(gate_pre)
    grad_gate_low = (
        grad_hidden * up_pre * sigmoid_gate * (1.0 + gate_pre * (1.0 - sigmoid_gate))
    ).astype(jnp.bfloat16)
    grad_up_low = (grad_hidden * gate_act).astype(jnp.bfloat16)
    d_gate = weight_grad(normed_two, grad_gate_low)
    d_up = weight_grad(normed_two, grad_up_low)
    grad_normed_two = project_back(grad_gate_low, gate_w) + project_back(grad_up_low, up_w)
    grad_mid_norm, d_gain_two = norm_back(middle, inv_two, gain_two, grad_normed_two)
    grad_middle = grad_final + grad_mid_norm
    grad_proj = grad_middle.astype(jnp.bfloat16)
    d_out = weight_grad(attended, grad_proj)
    grad_attended = (
        project_back(grad_proj, out_w).astype(jnp.bfloat16).reshape(row_count, HEADS, HEAD_DIM)
    )
    grad_keys_ext = jnp.zeros((row_count + WINDOW, HEADS, HEAD_DIM), jnp.float32)
    grad_values_ext = jnp.zeros((row_count + WINDOW, HEADS, HEAD_DIM), jnp.float32)
    row_start = 0
    head_parts = []
    for head_start in range(0, HEADS, head_group):
        head_end = head_start + head_group
        masked_scores = tile_scores(row_start, head_start)
        prob_full = jnp.exp(masked_scores - log_totals[row_start, head_start])
        grad_tile = grad_attended[row_start : row_start + block_rows, head_start:head_end]
        key_tile = keys_ext[row_start : row_start + block_rows + WINDOW, head_start:head_end]
        value_tile = values_ext[row_start : row_start + block_rows + WINDOW, head_start:head_end]
        query_tile = query_heads[row_start : row_start + block_rows, head_start:head_end]
        grad_prob = jnp.einsum(
            "qhd,khd->hqk", grad_tile, value_tile, preferred_element_type=jnp.float32
        )
        inner = jnp.sum(prob_full * grad_prob, axis=-1, keepdims=True)
        grad_score = (prob_full * (grad_prob - inner)).astype(jnp.bfloat16)
        head_parts.append(
            jnp.einsum("hqk,khd->qhd", grad_score, key_tile, preferred_element_type=jnp.float32)
            * score_scale
        )
        key_term = (
            jnp.einsum("hqk,qhd->khd", grad_score, query_tile, preferred_element_type=jnp.float32)
            * score_scale
        )
        value_term = jnp.einsum(
            "hqk,qhd->khd",
            prob_full.astype(jnp.bfloat16),
            grad_tile,
            preferred_element_type=jnp.float32,
        )
        grad_keys_ext = grad_keys_ext.at[
            row_start : row_start + block_rows + WINDOW, head_start:head_end
        ].add(key_term)
        grad_values_ext = grad_values_ext.at[
            row_start : row_start + block_rows + WINDOW, head_start:head_end
        ].add(value_term)
    grad_query_blocks = jnp.concatenate(head_parts, axis=1)
    rim_back = (
        from_behind(
            grad_keys_ext[:WINDOW].reshape(WINDOW, HEADS * HEAD_DIM).astype(jnp.bfloat16), "seq", -1
        ).astype(jnp.float32),
        from_behind(
            grad_values_ext[:WINDOW].reshape(WINDOW, HEADS * HEAD_DIM).astype(jnp.bfloat16),
            "seq",
            -1,
        ).astype(jnp.float32),
    )
    grad_keys = (
        grad_keys_ext[WINDOW:]
        .reshape(row_count, HEADS * HEAD_DIM)
        .at[row_count - WINDOW :]
        .add(rim_back[0])
    )
    grad_values = (
        grad_values_ext[WINDOW:]
        .reshape(row_count, HEADS * HEAD_DIM)
        .at[row_count - WINDOW :]
        .add(rim_back[1])
    )
    grad_query_low = grad_query_blocks.reshape(row_count, HEADS * HEAD_DIM).astype(jnp.bfloat16)
    grad_key_low = grad_keys.astype(jnp.bfloat16)
    grad_value_low = grad_values.astype(jnp.bfloat16)
    d_query = weight_grad(normed_one, grad_query_low)
    d_key = weight_grad(normed_one, grad_key_low)
    d_value = weight_grad(normed_one, grad_value_low)
    grad_normed_one = (
        project_back(grad_query_low, query_w)
        + project_back(grad_key_low, key_w)
        + project_back(grad_value_low, value_w)
    )
    grad_in_norm, d_gain_one = norm_back(inputs, inv_one, gain_one, grad_normed_one)
    grad_inputs = grad_middle + grad_in_norm
    return (block_out, grad_inputs, d_query, d_key, d_value, d_out, d_gate, d_up, d_down, d_gain_one, d_gain_two)


def solution(mesh):
    fast = (mesh.shape["dp"], mesh.shape["seq"]) == (NZ * NY * NX, 2)
    shards = swift_block if fast else plain_block
    in_specs = (
        P(("dp", "seq"), None),
        P("dp", None),
        P("dp", "seq"),
        P("dp", "seq"),
        P("dp", "seq"),
        P("dp", "seq"),
        P("dp", "seq"),
        P("dp", "seq"),
        P("dp", "seq"),
        P("dp"),
        P("dp"),
        P(("dp", "seq"), None),
    )
    out_specs = (
        P(("dp", "seq"), None),
        P(("dp", "seq"), None),
        P("dp", "seq"),
        P("dp", "seq"),
        P("dp", "seq"),
        P("dp", "seq"),
        P("dp", "seq"),
        P("dp", "seq"),
        P("dp", "seq"),
        P("dp"),
        P("dp"),
    )
    return jax.shard_map(shards, mesh=mesh, in_specs=in_specs, out_specs=out_specs, check_vma=False)
```

```python
import functools

import jax
import jax.numpy as jnp
from jax import lax
from jax.experimental import pallas as pl
from jax.experimental.pallas import tpu as pltpu
from jax.sharding import PartitionSpec as P

HEADS = 16
HEAD_DIM = 64
WINDOW = 64


eps_norm = 1e-05


def from_behind(block, axis, distance):
    devices = range(lax.axis_size(axis))
    route = [(i - distance, i) for i in devices if i - distance in devices]
    return lax.ppermute(block, axis, route)


def inverse_rms(values):
    return lax.rsqrt(jnp.mean(values * values, axis=-1, keepdims=True) + eps_norm)


def doc_numbers(lengths_row, positions):
    first_end = lengths_row[0]
    second_end = lengths_row[0] + lengths_row[1]
    return (positions >= first_end).astype(jnp.int32) + (positions >= second_end).astype(jnp.int32)


def window_mask(query_pos, query_doc, key_pos, key_doc, window):
    after = key_pos[None, :] >= query_pos[:, None] - window
    before = key_pos[None, :] <= query_pos[:, None]
    inside = (key_pos[None, :] >= 0) & (key_doc[None, :] == query_doc[:, None])
    return after & before & inside


def norm_back(values, inverse, gain, grad_norm):
    scaled = grad_norm * gain
    mean_term = jnp.mean(values * scaled, axis=-1, keepdims=True)
    grad_values = inverse * scaled - values * (inverse * inverse * inverse) * mean_term
    grad_gain = jnp.sum(values * inverse * grad_norm, axis=0)
    return (grad_values, grad_gain)


def project(left, right):
    return jnp.dot(left, right, preferred_element_type=jnp.float32)


def project_back(grad_rows, weight):
    return jnp.einsum("tf,df->td", grad_rows, weight, preferred_element_type=jnp.float32)


def weight_grad(inputs, grad_rows):
    return jnp.einsum("td,tf->df", inputs, grad_rows, preferred_element_type=jnp.float32)


def plain_block(
    tokens,
    seq_lengths,
    w_query,
    w_key,
    w_value,
    w_out,
    w_gate,
    w_up,
    w_down,
    gain_attn,
    gain_mlp,
    cotangent,
):
    row_count = tokens.shape[0]
    block_rows = min(512, row_count)
    head_group = HEADS // 2
    score_scale = HEAD_DIM ** (-0.5)
    row_parts = (
        lax.all_gather(w_query, "dp", axis=0, tiled=True),
        lax.all_gather(w_key, "dp", axis=0, tiled=True),
        lax.all_gather(w_value, "dp", axis=0, tiled=True),
        lax.all_gather(w_out, "dp", axis=0, tiled=True),
        lax.all_gather(w_gate, "dp", axis=0, tiled=True),
        lax.all_gather(w_up, "dp", axis=0, tiled=True),
        lax.all_gather(w_down, "dp", axis=0, tiled=True),
        lax.all_gather(gain_attn, "dp", axis=0, tiled=True),
        lax.all_gather(gain_mlp, "dp", axis=0, tiled=True),
    )
    full_mats = (
        lax.all_gather(row_parts[0], "seq", axis=1, tiled=True),
        lax.all_gather(row_parts[1], "seq", axis=1, tiled=True),
        lax.all_gather(row_parts[2], "seq", axis=1, tiled=True),
        lax.all_gather(row_parts[3], "seq", axis=1, tiled=True),
        lax.all_gather(row_parts[4], "seq", axis=1, tiled=True),
        lax.all_gather(row_parts[5], "seq", axis=1, tiled=True),
        lax.all_gather(row_parts[6], "seq", axis=1, tiled=True),
    )
    query_w, key_w, value_w, out_w, gate_w, up_w, down_full = full_mats
    gain_one = row_parts[7].astype(jnp.float32)
    gain_two = row_parts[8].astype(jnp.float32)
    inputs = tokens.astype(jnp.float32)
    inv_one = inverse_rms(inputs)
    normed_one = (inputs * inv_one * gain_one).astype(jnp.bfloat16)
    query_low = project(normed_one, query_w).astype(jnp.bfloat16)
    key_low = project(normed_one, key_w).astype(jnp.bfloat16)
    value_low = project(normed_one, value_w).astype(jnp.bfloat16)
    rim_pairs = from_behind(
        (key_low[row_count - WINDOW :], value_low[row_count - WINDOW :]), "seq", 1
    )
    keys_ext = jnp.concatenate([rim_pairs[0], key_low], axis=0).reshape(
        row_count + WINDOW, HEADS, HEAD_DIM
    )
    values_ext = jnp.concatenate([rim_pairs[1], value_low], axis=0).reshape(
        row_count + WINDOW, HEADS, HEAD_DIM
    )
    query_heads = query_low.reshape(row_count, HEADS, HEAD_DIM)
    span_start = lax.axis_index("seq") * row_count
    query_pos = span_start + jnp.arange(row_count, dtype=jnp.int32)
    key_pos = span_start - WINDOW + jnp.arange(row_count + WINDOW, dtype=jnp.int32)
    query_doc = doc_numbers(seq_lengths[0], query_pos)
    key_doc = doc_numbers(seq_lengths[0], key_pos)

    def tile_scores(row_start, head_start):
        visible = window_mask(query_pos, query_doc, key_pos, key_doc, WINDOW)
        scores_raw = (
            jnp.einsum(
                "qhd,khd->hqk",
                query_heads[
                    row_start : row_start + block_rows, head_start : head_start + head_group
                ],
                keys_ext[
                    row_start : row_start + block_rows + WINDOW,
                    head_start : head_start + head_group,
                ],
                preferred_element_type=jnp.float32,
            )
            * score_scale
        )
        return jnp.where(visible[None], scores_raw, -1e30)

    log_totals = {}
    row_start = 0
    head_parts = []
    for head_start in range(0, HEADS, head_group):
        masked_scores = tile_scores(row_start, head_start)
        top_score = jnp.max(masked_scores, axis=-1, keepdims=True)
        log_total = top_score + jnp.log(
            jnp.sum(jnp.exp(masked_scores - top_score), axis=-1, keepdims=True)
        )
        prob_low = jnp.exp(masked_scores - log_total).astype(jnp.bfloat16)
        value_tile = values_ext[
            row_start : row_start + block_rows + WINDOW, head_start : head_start + head_group
        ]
        head_parts.append(
            jnp.einsum("hqk,khd->qhd", prob_low, value_tile, preferred_element_type=jnp.float32)
        )
        log_totals[row_start, head_start] = log_total
    attn_blocks = jnp.concatenate(head_parts, axis=1)
    attended = attn_blocks.reshape(row_count, HEADS * HEAD_DIM).astype(jnp.bfloat16)
    middle = inputs + project(attended, out_w)
    inv_two = inverse_rms(middle)
    normed_two = (middle * inv_two * gain_two).astype(jnp.bfloat16)
    gate_pre = project(normed_two, gate_w)
    up_pre = project(normed_two, up_w)
    gate_act = jax.nn.silu(gate_pre)
    hidden = (gate_act * up_pre).astype(jnp.bfloat16)
    block_out = (middle + project(hidden, down_full)).astype(jnp.bfloat16)
    rows_again = (
        lax.all_gather(w_query, "dp", axis=0, tiled=True),
        lax.all_gather(w_key, "dp", axis=0, tiled=True),
        lax.all_gather(w_value, "dp", axis=0, tiled=True),
        lax.all_gather(w_out, "dp", axis=0, tiled=True),
        lax.all_gather(w_gate, "dp", axis=0, tiled=True),
        lax.all_gather(w_up, "dp", axis=0, tiled=True),
        lax.all_gather(w_down, "dp", axis=0, tiled=True),
        lax.all_gather(gain_attn, "dp", axis=0, tiled=True),
        lax.all_gather(gain_mlp, "dp", axis=0, tiled=True),
    )
    mats_again = (
        lax.all_gather(rows_again[0], "seq", axis=1, tiled=True),
        lax.all_gather(rows_again[1], "seq", axis=1, tiled=True),
        lax.all_gather(rows_again[2], "seq", axis=1, tiled=True),
        lax.all_gather(rows_again[3], "seq", axis=1, tiled=True),
        lax.all_gather(rows_again[4], "seq", axis=1, tiled=True),
        lax.all_gather(rows_again[5], "seq", axis=1, tiled=True),
        lax.all_gather(rows_again[6], "seq", axis=1, tiled=True),
    )
    back_query, back_key, back_value, back_out, back_gate, back_up, back_down = mats_again
    back_gain_one = rows_again[7].astype(jnp.float32)
    back_gain_two = rows_again[8].astype(jnp.float32)
    grad_final = cotangent.astype(jnp.float32)
    d_down = weight_grad(hidden, cotangent)
    grad_hidden = project_back(cotangent, back_down)
    sigmoid_gate = jax.nn.sigmoid(gate_pre)
    grad_gate_low = (
        grad_hidden * up_pre * sigmoid_gate * (1.0 + gate_pre * (1.0 - sigmoid_gate))
    ).astype(jnp.bfloat16)
    grad_up_low = (grad_hidden * gate_act).astype(jnp.bfloat16)
    d_gate = weight_grad(normed_two, grad_gate_low)
    d_up = weight_grad(normed_two, grad_up_low)
    grad_normed_two = project_back(grad_gate_low, back_gate) + project_back(grad_up_low, back_up)
    grad_mid_norm, d_gain_two = norm_back(middle, inv_two, back_gain_two, grad_normed_two)
    grad_middle = grad_final + grad_mid_norm
    grad_proj = grad_middle.astype(jnp.bfloat16)
    d_out = weight_grad(attended, grad_proj)
    grad_attended = (
        project_back(grad_proj, back_out).astype(jnp.bfloat16).reshape(row_count, HEADS, HEAD_DIM)
    )
    grad_keys_ext = jnp.zeros((row_count + WINDOW, HEADS, HEAD_DIM), jnp.float32)
    grad_values_ext = jnp.zeros((row_count + WINDOW, HEADS, HEAD_DIM), jnp.float32)
    row_start = 0
    head_parts = []
    for head_start in range(0, HEADS, head_group):
        head_end = head_start + head_group
        masked_scores = tile_scores(row_start, head_start)
        prob_full = jnp.exp(masked_scores - log_totals[row_start, head_start])
        grad_tile = grad_attended[row_start : row_start + block_rows, head_start:head_end]
        key_tile = keys_ext[row_start : row_start + block_rows + WINDOW, head_start:head_end]
        value_tile = values_ext[row_start : row_start + block_rows + WINDOW, head_start:head_end]
        query_tile = query_heads[row_start : row_start + block_rows, head_start:head_end]
        grad_prob = jnp.einsum(
            "qhd,khd->hqk", grad_tile, value_tile, preferred_element_type=jnp.float32
        )
        inner = jnp.sum(prob_full * grad_prob, axis=-1, keepdims=True)
        grad_score = (prob_full * (grad_prob - inner)).astype(jnp.bfloat16)
        head_parts.append(
            jnp.einsum("hqk,khd->qhd", grad_score, key_tile, preferred_element_type=jnp.float32)
            * score_scale
        )
        key_term = (
            jnp.einsum("hqk,qhd->khd", grad_score, query_tile, preferred_element_type=jnp.float32)
            * score_scale
        )
        value_term = jnp.einsum(
            "hqk,qhd->khd",
            prob_full.astype(jnp.bfloat16),
            grad_tile,
            preferred_element_type=jnp.float32,
        )
        grad_keys_ext = grad_keys_ext.at[
            row_start : row_start + block_rows + WINDOW, head_start:head_end
        ].add(key_term)
        grad_values_ext = grad_values_ext.at[
            row_start : row_start + block_rows + WINDOW, head_start:head_end
        ].add(value_term)
    grad_query_blocks = jnp.concatenate(head_parts, axis=1)
    rim_back = (
        from_behind(
            grad_keys_ext[:WINDOW].reshape(WINDOW, HEADS * HEAD_DIM).astype(jnp.bfloat16), "seq", -1
        ).astype(jnp.float32),
        from_behind(
            grad_values_ext[:WINDOW].reshape(WINDOW, HEADS * HEAD_DIM).astype(jnp.bfloat16),
            "seq",
            -1,
        ).astype(jnp.float32),
    )
    grad_keys = (
        grad_keys_ext[WINDOW:]
        .reshape(row_count, HEADS * HEAD_DIM)
        .at[row_count - WINDOW :]
        .add(rim_back[0])
    )
    grad_values = (
        grad_values_ext[WINDOW:]
        .reshape(row_count, HEADS * HEAD_DIM)
        .at[row_count - WINDOW :]
        .add(rim_back[1])
    )
    grad_query_low = grad_query_blocks.reshape(row_count, HEADS * HEAD_DIM).astype(jnp.bfloat16)
    grad_key_low = grad_keys.astype(jnp.bfloat16)
    grad_value_low = grad_values.astype(jnp.bfloat16)
    d_query = weight_grad(normed_one, grad_query_low)
    d_key = weight_grad(normed_one, grad_key_low)
    d_value = weight_grad(normed_one, grad_value_low)
    grad_normed_one = (
        project_back(grad_query_low, back_query)
        + project_back(grad_key_low, back_key)
        + project_back(grad_value_low, back_value)
    )
    grad_in_norm, d_gain_one = norm_back(inputs, inv_one, back_gain_one, grad_normed_one)
    grad_inputs = grad_middle + grad_in_norm
    row_sums = (
        lax.psum_scatter(
            d_query.astype(jnp.bfloat16), "dp", scatter_dimension=0, tiled=True
        ).astype(jnp.float32),
        lax.psum_scatter(d_key.astype(jnp.bfloat16), "dp", scatter_dimension=0, tiled=True).astype(
            jnp.float32
        ),
        lax.psum_scatter(
            d_value.astype(jnp.bfloat16), "dp", scatter_dimension=0, tiled=True
        ).astype(jnp.float32),
        lax.psum_scatter(d_out.astype(jnp.bfloat16), "dp", scatter_dimension=0, tiled=True).astype(
            jnp.float32
        ),
        lax.psum_scatter(d_gate.astype(jnp.bfloat16), "dp", scatter_dimension=0, tiled=True).astype(
            jnp.float32
        ),
        lax.psum_scatter(d_up.astype(jnp.bfloat16), "dp", scatter_dimension=0, tiled=True).astype(
            jnp.float32
        ),
        lax.psum_scatter(d_down.astype(jnp.bfloat16), "dp", scatter_dimension=0, tiled=True).astype(
            jnp.float32
        ),
        lax.psum_scatter(
            d_gain_one.astype(jnp.bfloat16), "dp", scatter_dimension=0, tiled=True
        ).astype(jnp.float32),
        lax.psum_scatter(
            d_gain_two.astype(jnp.bfloat16), "dp", scatter_dimension=0, tiled=True
        ).astype(jnp.float32),
    )
    owned_mats = (
        lax.psum_scatter(
            row_sums[0].astype(jnp.bfloat16), "seq", scatter_dimension=1, tiled=True
        ).astype(jnp.float32),
        lax.psum_scatter(
            row_sums[1].astype(jnp.bfloat16), "seq", scatter_dimension=1, tiled=True
        ).astype(jnp.float32),
        lax.psum_scatter(
            row_sums[2].astype(jnp.bfloat16), "seq", scatter_dimension=1, tiled=True
        ).astype(jnp.float32),
        lax.psum_scatter(
            row_sums[3].astype(jnp.bfloat16), "seq", scatter_dimension=1, tiled=True
        ).astype(jnp.float32),
        lax.psum_scatter(
            row_sums[4].astype(jnp.bfloat16), "seq", scatter_dimension=1, tiled=True
        ).astype(jnp.float32),
        lax.psum_scatter(
            row_sums[5].astype(jnp.bfloat16), "seq", scatter_dimension=1, tiled=True
        ).astype(jnp.float32),
        lax.psum_scatter(
            row_sums[6].astype(jnp.bfloat16), "seq", scatter_dimension=1, tiled=True
        ).astype(jnp.float32),
    )
    owned_gains = lax.psum((row_sums[7], row_sums[8]), "seq")
    return (
        block_out,
        grad_inputs,
        owned_mats[0],
        owned_mats[1],
        owned_mats[2],
        owned_mats[3],
        owned_mats[4],
        owned_mats[5],
        owned_mats[6],
        owned_gains[0],
        owned_gains[1],
    )


MESH = pl.DeviceIdType.MESH
NZ, NY, NX = 4, 2, 2
SEQUENCE = {"zfx": "zxy", "zfy": "zyx", "zmx": "xzy", "zmy": "yzx"}
ALL_Z, ALL_Y, ALL_X = pl.ds(0, NZ), pl.ds(0, NY), pl.ds(0, NX)


class Plan:
    def __init__(self, tensors):
        self.tensors = tensors
        self.items, self.of_tensor = [], []
        for t, (rows, _, kind, splits, _) in enumerate(tensors):
            begin, mine = 0, []
            for half, count in enumerate(splits):
                mine.append(len(self.items))
                self.items.append((t, SEQUENCE[kind + "xy"[half]], begin, count))
                begin += count
            self.of_tensor.append(mine)


class Place:
    def __init__(self):
        self.c, self.s = lax.axis_index("dp"), lax.axis_index("seq")
        self.z, self.y, self.x = self.c // 4, (self.c // 2) % 2, self.c % 2

    def at(self, z, y, x):
        return (z * 4 + y * 2 + x, self.s)

    def to_x(self):
        return self.at(self.z, self.y, 1 - self.x)

    def to_y(self):
        return self.at(self.z, 1 - self.y, self.x)

    def to_z(self, step):
        return self.at((self.z + step) % NZ, self.y, self.x)

    def to_core(self):
        return (self.c, 1 - self.s)

    def greet(self):
        barrier = pltpu.get_barrier_semaphore()
        peers = [self.to_x(), self.to_y(), self.to_core()] + [self.to_z(k) for k in (1, 2, 3)]
        for peer in peers:
            pl.semaphore_signal(barrier, inc=1, device_id=peer, device_id_type=MESH)
        pl.semaphore_wait(barrier, len(peers))


def remote(src, dst, send, recv, device):
    return pltpu.make_async_remote_copy(
        src_ref=src, dst_ref=dst, send_sem=send, recv_sem=recv, device_id=device, device_id_type=MESH
    )


class Gather:
    def __init__(self, plan, place, shards, bufs, send, recv, local):
        self.plan, self.me, self.shards, self.bufs = plan, place, shards, bufs
        self.send, self.recv, self.local = send, recv, local

    def own_copy(self, t):
        me = self.me
        return pltpu.make_async_copy(
            self.shards[t], self.bufs[t].at[me.s, me.z, me.y, me.x], self.local.at[t]
        )

    def moves(self, i, phase):
        t, seq, begin, count = self.plan.items[i]
        me, buf = self.me, self.bufs[t]
        rows = pl.ds(begin, count)

        def view(z, y, x, half=me.s):
            return buf.at[half, z, y, x, rows, :]

        if phase == 3:
            whole = view(ALL_Z, ALL_Y, ALL_X)
            return [(whole, whole, me.to_core(), view(ALL_Z, ALL_Y, ALL_X, 1 - me.s), 0)]
        done, axis = seq[:phase], seq[phase]
        z = ALL_Z if "z" in done else me.z
        y = ALL_Y if "y" in done else me.y
        x = ALL_X if "x" in done else me.x
        there = view(z, y, x)
        here = self.shards[t].at[rows, :] if phase == 0 else there
        if axis == "x":
            return [(here, there, me.to_x(), view(z, y, 1 - me.x), 0)]
        if axis == "y":
            return [(here, there, me.to_y(), view(z, 1 - me.y, x), 0)]
        return [
            (here, there, me.to_z(k), view((me.z + NZ - k) % NZ, y, x), k - 1) for k in (1, 2, 3)
        ]

    def copy(self, i, phase, src, dst, device, k):
        return remote(src, dst, self.send.at[i, phase, k], self.recv.at[i, phase, k], device)

    def start(self, i, phase):
        for here, there, device, _, k in self.moves(i, phase):
            self.copy(i, phase, here, there, device, k).start()

    def wait(self, i, phase):
        for _, _, device, arrived, k in self.moves(i, phase):
            self.copy(i, phase, arrived, arrived, device, k).wait_recv()

    def finish(self, i):
        for phase in range(4):
            for here, there, device, _, k in self.moves(i, phase):
                self.copy(i, phase, here, there, device, k).wait_send()


def staged_order(tensors, lags):
    order = []
    for step in range(tensors + max(lags)):
        for phase, lag in enumerate(lags):
            if 0 <= step - lag < tensors:
                order.append((step - lag, phase))
    return order


def got_shapes(plan):
    shapes = []
    for rows, columns, kind, _, dtype in plan.tensors:
        second, third = ((1, NZ), (3,)) if kind == "zf" else ((3, 2), (1,))
        shapes.append([(d + (rows, columns), dtype) for d in ((NZ, 2), second, third)])
    return shapes


class Scatter:
    def __init__(self, plan, place, total, got, out, send, recv):
        self.plan, self.me, self.total, self.got, self.out = plan, place, total, got, out
        self.send, self.recv = send, recv

    def moves(self, i, phase):
        t, seq, begin, count = self.plan.items[i]
        me, total, got = self.me, self.total[t], self.got[t][phase]
        rows = pl.ds(begin, count)
        axis, done = seq[2 - phase], seq[3 - phase :]
        z = me.z if "z" in done else ALL_Z
        y = me.y if "y" in done else ALL_Y
        x = me.x if "x" in done else ALL_X
        if phase == 0:
            lands = [got.at[ALL_Z, pl.ds(0, 2), rows, :]]
        elif phase == 1:
            lands = [got.at[k, pl.ds(0, got.shape[1]), rows, :] for k in range(got.shape[0])]
        else:
            lands = [got.at[k, rows, :] for k in range(got.shape[0])]
        if axis == "x":
            return [(total.at[z, y, 1 - me.x, rows, :], lands[0], me.to_x(), 0)]
        if axis == "y":
            return [(total.at[z, 1 - me.y, x, rows, :], lands[0], me.to_y(), 0)]
        return [
            (total.at[(me.z + k) % NZ, y, x, rows, :], lands[k - 1], me.to_z(k), k - 1)
            for k in (1, 2, 3)
        ]

    def copy(self, i, phase, src, dst, device, k):
        return remote(src, dst, self.send.at[i, phase, k], self.recv.at[i, phase, k], device)

    def start(self, i, phase):
        for here, there, device, k in self.moves(i, phase):
            self.copy(i, phase, here, there, device, k).start()

    def wait(self, i, phase):
        for here, there, device, k in self.moves(i, phase):
            self.copy(i, phase, there, there, device, k).wait_recv()

    def add(self, i, phase):
        t, seq, begin, count = self.plan.items[i]
        me, total, got = self.me, self.total[t], self.got[t][phase]
        rows = pl.ds(begin, count)
        if phase == 0:
            for z in range(NZ):
                for o in range(2):
                    at = (z, me.y, o) if seq[2] == "y" else (z, o, me.x)
                    total[at + (rows,)] += got[z, o, rows]
        elif phase == 1 and seq[1] != "z":
            for z in range(NZ):
                total[z, me.y, me.x, rows] += got[0, z, rows]
        elif phase == 1:
            for o in range(2):
                at = (me.z, me.y, o) if seq[2] == "y" else (me.z, o, me.x)
                part = total[at + (rows,)].astype(jnp.float32)
                for k in range(3):
                    part += got[k, o, rows].astype(jnp.float32)
                total[at + (rows,)] = part.astype(total.dtype)
        else:
            part = total[me.z, me.y, me.x, rows].astype(jnp.float32)
            for k in range(got.shape[0]):
                part += got[k, rows].astype(jnp.float32)
            self.out[t][rows] = part

    def finish(self, i):
        for phase in range(3):
            for here, there, device, k in self.moves(i, phase):
                self.copy(i, phase, here, there, device, k).wait_send()


EPS = 1e-05
PAIR = 2 * HEAD_DIM
SPAN = 2 * WINDOW
LOW = jnp.bfloat16
F32 = jnp.float32


def mm(left, right):
    return jnp.dot(left, right, preferred_element_type=F32)


def mm_nt(left, right):
    return lax.dot_general(left, right, (((1,), (1,)), ((), ())), preferred_element_type=F32)


def mm_tn(left, right):
    return lax.dot_general(left, right, (((0,), (0,)), ((), ())), preferred_element_type=F32)


def column_tiles(columns, size):
    full = columns // size
    tiles = [(0, size, full)]
    if columns % size:
        tiles.append((full * size, columns % size, 1))
    return tiles


def each_tile(columns, size, body):
    for begin, width, count in column_tiles(columns, size):
        if count == 1:
            body(begin, width)
        else:

            def step(j, _, begin=begin, width=width):
                body(pl.multiple_of(begin + j * width, 128), width)
                return 0

            lax.fori_loop(0, count, step, 0)


def each_rows(rows, size, body):
    def step(j, _):
        body(pl.ds(pl.multiple_of(j * size, size), size))
        return 0

    lax.fori_loop(0, rows // size, step, 0)


def both_heads(block):
    first = lax.broadcasted_iota(jnp.int32, block.shape, 1) < HEAD_DIM
    zero = jnp.zeros_like(block)
    return jnp.concatenate([jnp.where(first, block, zero), jnp.where(first, zero, block)], axis=0)


def merge_heads(stacked):
    rows = stacked.shape[0] // 2
    first = lax.broadcasted_iota(jnp.int32, (rows, PAIR), 1) < HEAD_DIM
    return jnp.where(first, stacked[:rows], stacked[rows:])


class Copies:
    def __init__(self, sems):
        self.sems, self.made = sems, []

    def start(self, src, dst):
        copy = pltpu.make_async_copy(src, dst, self.sems.at[len(self.made)])
        copy.start()
        self.made.append(copy)
        return copy

    def wait_all(self):
        for copy in self.made:
            copy.wait()


FORWARD_ORDER = staged_order(8, (0, 2, 4))


def forward_kernel(plan, *refs):
    n = len(plan.tensors)
    lens, x_in, dy_in, refs = refs[0], refs[1], refs[2], refs[3:]
    shards, refs = refs[:n], refs[n:]
    w_out, refs = refs[: n - 1], refs[n - 1 :]
    (mixed_o, q_o, k_o, v_o, p_o, x1_o, ha_o, ho_o, hm_o, hid_o, dact_o, act_o, dyh_o, gain_o), refs = refs[:14], refs[14:]
    bufs, refs = refs[:n], refs[n:]
    (gains, h1, q, kx, vx, probs, o, x1, h2, hid, act, dact, ha, ho, hm, hidt, mixed), refs = refs[:17], refs[17:]
    send, recv, own_sem, out_sem, rim_send, rim_recv, half_send, half_recv = refs
    rows, width = x_in.shape
    chips = NZ * NY * NX
    me = Place()
    me.greet()
    gather = Gather(plan, me, shards, bufs, send, recv, own_sem)
    copies = Copies(out_sem)
    sends = []

    def to_partner(k, src, dst):
        copy = remote(src, dst, half_send.at[k], half_recv.at[k], me.to_core())
        copy.start()
        sends.append(copy)

    def lanes(ref):
        return ref.at[:, pl.ds(pl.multiple_of(me.s * rows, 128), rows)]

    def share(k, mine, whole):
        copies.start(mine, lanes(whole))
        to_partner(k, mine, lanes(whole))

    for t in range(n):
        gather.own_copy(t).start()
    for i in range(len(plan.items)):
        gather.start(i, 0)
    for t in range(n):
        gather.own_copy(t).wait()
    half = dyh_o.shape[1]
    mine = pl.ds(pl.multiple_of(me.s * rows, 16), rows)
    copies.start(dy_in.at[:, pl.ds(pl.multiple_of(me.s * half, 128), half)], dyh_o.at[mine, :])
    to_partner(0, dy_in.at[:, pl.ds(pl.multiple_of((1 - me.s) * half, 128), half)], dyh_o.at[mine, :])

    def weight(t, side, cols):
        w = bufs[t][side, :, :, :, :, cols]
        return w.reshape(chips * w.shape[3], w.shape[4])

    def norm(values, gain):
        inverse = lax.rsqrt(jnp.mean(values * values, axis=-1, keepdims=True) + EPS)
        return (values * inverse * gain).astype(LOW)

    def first_norm():
        parts = []
        for z in range(NZ):
            for y in range(NY):
                pair = [bufs[0][me.s, z, y, x].astype(F32) for x in range(NX)]
                parts.append(pair[0] + pair[1])
        gains[...] = jnp.concatenate(parts, axis=1)[0:8]
        copies.start(gains, gain_o)

        def body(at):
            h1[at, :] = norm(x_in[at, :].astype(F32), gains[0:1, :])

        each_rows(rows, 64, body)
        turn(h1, ha)
        share(1, ha, ha_o)

    def turn(src, dst):
        def body(j, _):
            at = pl.ds(pl.multiple_of(j * 128, 128), 128)
            dst[at, :] = src[:, at].T
            return 0

        lax.fori_loop(0, src.shape[1] // 128, body, 0)

    def project_to(t, src, dst, skip):
        columns = plan.tensors[t][1]
        for side in range(2):

            def body(begin, size, side=side):
                part = mm(src[...], weight(t, side, pl.ds(begin, size)))
                dst[pl.ds(skip, rows), pl.ds(side * columns + begin, size)] = part.astype(LOW)

            each_tile(columns, 256, body)

    def rim(k, ref):
        return remote(ref.at[pl.ds(rows, WINDOW), :], ref.at[pl.ds(0, WINDOW), :], rim_send.at[k], rim_recv.at[k], me.to_core())

    def do_query():
        project_to(1, h1, q, 0)
        copies.start(q, q_o)

    def do_key():
        project_to(2, h1, kx, WINDOW)
        rim(0, kx).start()

    def do_value():
        project_to(3, h1, vx, WINDOW)
        rim(1, vx).start()

    def rims():
        for k, ref in ((0, kx), (1, vx)):
            rim(k, ref).wait_recv()
        copies.start(kx, k_o)
        copies.start(vx, v_o)

    first_end = lens[0, 0]
    second_end = first_end + lens[0, 1]

    def attend(b):
        base = me.s * rows + b * WINDOW
        at = pl.ds(pl.multiple_of(b * WINDOW, WINDOW), WINDOW)
        over = pl.ds(pl.multiple_of(b * WINDOW, WINDOW), SPAN)
        row = lax.broadcasted_iota(jnp.int32, (WINDOW, SPAN), 0)
        col = lax.broadcasted_iota(jnp.int32, (WINDOW, SPAN), 1)
        q_pos, k_pos = base + row, base - WINDOW + col

        def doc(pos):
            return (pos >= first_end).astype(jnp.int32) + (pos >= second_end).astype(jnp.int32)

        visible = (col >= row) & (col <= row + WINDOW) & (k_pos >= 0) & (doc(q_pos) == doc(k_pos))
        bias = jnp.where(visible, 0.0, -1e30)
        bias = jnp.concatenate([bias, bias], axis=0)
        for p in range(HEADS // 2):
            cols = slice(p * PAIR, (p + 1) * PAIR)
            q2 = both_heads(q[at, cols])
            s = mm_nt(q2, kx[over, cols]) * HEAD_DIM ** (-0.5) + bias
            e = jnp.exp(s - jnp.max(s, axis=-1, keepdims=True))
            prob = (e / jnp.sum(e, axis=-1, keepdims=True)).astype(LOW)
            probs[at, 2 * p * SPAN : (2 * p + 1) * SPAN] = prob[:WINDOW]
            probs[at, (2 * p + 1) * SPAN : (2 * p + 2) * SPAN] = prob[WINDOW:]
            o[at, cols] = merge_heads(mm(prob, vx[over, cols])).astype(LOW)

    def attend_some(begin, count):
        def step(b, _):
            attend(b)
            return 0

        lax.fori_loop(begin, begin + count, step, 0)

    def after_attention():
        copies.start(probs, p_o)
        turn(o, ho)
        share(2, ho, ho_o)

    def add_out():
        columns = plan.tensors[4][1]
        for side in range(2):

            def body(begin, size, side=side):
                cols = pl.ds(side * columns + begin, size)
                x1[:, cols] = x_in[:, cols].astype(F32) + mm(o[...], weight(4, side, pl.ds(begin, size)))

            each_tile(columns, 256, body)
        copies.start(x1, x1_o)

        def body(at):
            h2[at, :] = norm(x1[at, :], gains[1:2, :])

        each_rows(rows, 64, body)
        turn(h2, hm)
        share(3, hm, hm_o)

    wide = plan.tensors[5][1]

    def mlp(side, begin, size):
        cols = pl.ds(begin, size)
        a = mm(h2[...], weight(5, side, cols))
        b = mm(h2[...], weight(6, side, cols))
        sig = 1.0 / (1.0 + jnp.exp(-a))
        silu = a * sig
        to = pl.ds(side * wide + begin, size)
        act[:, to] = silu.astype(LOW)
        dact[:, to] = (b * sig * (1.0 + a * (1.0 - sig))).astype(LOW)
        hidden = (silu * b).astype(LOW)
        hid[:, to] = hidden
        hidt[to, :] = hidden.T

    def mlp_some(side, begin, size, count):
        def step(j, _):
            mlp(side, pl.multiple_of(begin + j * size, 128), size)
            return 0

        lax.fori_loop(0, count, step, 0)

    def after_mlp():
        copies.start(act, act_o)
        copies.start(dact, dact_o)
        share(4, hidt, hid_o)

    def add_down():
        columns = plan.tensors[7][1]
        for side in range(2):

            def body(begin, size, side=side):
                cols = pl.ds(side * columns + begin, size)
                part = mm(hid[...], weight(7, side, pl.ds(begin, size)))
                mixed[:, cols] = (x1[:, cols] + part).astype(LOW)

            each_tile(columns, 256, body)
        copies.start(mixed, mixed_o)

    blocks = rows // WINDOW
    whole = wide // 256
    rest = wide - whole * 256
    work = [(0, first_norm), (1, do_query), (2, do_key), (3, do_value), (3, rims)]
    work += [(3, functools.partial(attend_some, b, 2)) for b in range(0, blocks, 2)]
    work += [(3, after_attention), (4, add_out)]
    for side in range(2):
        work += [(6, functools.partial(mlp_some, side, 0, 256, whole))]
        work += [(6, functools.partial(mlp, side, whole * 256, rest))] if rest else []
    work += [(6, after_mlp), (7, add_down)]
    passed, done = set(), set()

    def arrive(t):
        if t in passed:
            return
        passed.add(t)
        for i in plan.of_tensor[t]:
            gather.wait(i, 3)
        if t:
            copies.start(bufs[t], w_out[t - 1])

    for t, phase in FORWARD_ORDER:
        for i in plan.of_tensor[t]:
            gather.wait(i, phase)
            gather.start(i, phase + 1)
        if phase == 2:
            done.add(t)
        for _ in range(2):
            if work and all(k in done for k in range(work[0][0] + 1)) and not (phase == 2 and t == work[0][0]):
                need, piece = work.pop(0)
                for k in range(need + 1):
                    arrive(k)
                piece()
    for need, piece in work:
        for k in range(need + 1):
            arrive(k)
        piece()
    for i in range(len(plan.items)):
        gather.finish(i)
    for k, ref in ((0, kx), (1, vx)):
        rim(k, ref).wait_send()
    for copy in sends:
        copy.wait()
    copies.wait_all()


def forward_all(plan, lens, tokens, cotangent, shards):
    n, k = len(plan.tensors), len(plan.items)
    rows, width = tokens.shape
    wide = 2 * plan.tensors[5][1]
    anywhere = pl.BlockSpec(memory_space=pl.ANY)
    inside = pl.BlockSpec(memory_space=pltpu.VMEM)
    shape = jax.ShapeDtypeStruct
    bufs = [(2, NZ, NY, NX) + t[:2] for t in plan.tensors]
    over = WINDOW + rows
    kept = [
        ((rows, width), LOW),
        ((rows, width), LOW),
        ((over, width), LOW),
        ((over, width), LOW),
        ((rows, HEADS * SPAN), LOW),
        ((rows, width), F32),
        ((width, 2 * rows), LOW),
        ((width, 2 * rows), LOW),
        ((width, 2 * rows), LOW),
        ((wide, 2 * rows), LOW),
        ((rows, wide), LOW),
        ((rows, wide), LOW),
        ((2 * rows, width // 2), LOW),
        ((8, width), F32),
    ]
    scratch = [
        ((8, width), F32),
        ((rows, width), LOW),
        ((rows, width), LOW),
        ((over, width), LOW),
        ((over, width), LOW),
        ((rows, HEADS * SPAN), LOW),
        ((rows, width), LOW),
        ((rows, width), F32),
        ((rows, width), LOW),
        ((rows, wide), LOW),
        ((rows, wide), LOW),
        ((rows, wide), LOW),
        ((width, rows), LOW),
        ((width, rows), LOW),
        ((width, rows), LOW),
        ((wide, rows), LOW),
        ((rows, width), LOW),
    ]
    dma = pltpu.SemaphoreType.DMA
    outs = pl.pallas_call(
        functools.partial(forward_kernel, plan),
        out_shape=[shape(b, LOW) for b in bufs[1:]] + [shape(*s) for s in kept],
        in_specs=[pl.BlockSpec(memory_space=pltpu.SMEM), inside, anywhere] + [anywhere] * n,
        out_specs=[anywhere] * (n - 1 + len(kept)),
        scratch_shapes=[pltpu.VMEM(b, LOW) for b in bufs]
        + [pltpu.VMEM(*s) for s in scratch]
        + [dma((k, 4, 3)), dma((k, 4, 3)), dma((n,)), dma((24,)), dma((2,)), dma((2,)), dma((5,)), dma((5,))],
        compiler_params=pltpu.CompilerParams(
            collective_id=0, has_side_effects=True, vmem_limit_bytes=62 * 2**20
        ),
        name="forward_all",
    )(lens, tokens, cotangent, *shards)
    return outs[: n - 1], outs[n - 1 :]


class Stream:
    def __init__(self, count, sems, fetch):
        self.count, self.sems, self.fetch = count, sems, fetch

    def copies(self, j, slot):
        return [
            pltpu.make_async_copy(src, dst, self.sems.at[slot, k])
            for k, (src, dst) in enumerate(self.fetch(j, slot))
        ]

    def prime(self):
        for copy in self.copies(0, 0):
            copy.start()

    def run(self, body):
        def step(j, _):
            slot = j % 2

            @pl.when(j + 1 < self.count)
            def _():
                for copy in self.copies(j + 1, 1 - slot):
                    copy.start()

            for copy in self.copies(j, slot):
                copy.wait()
            body(j, slot)
            return 0

        lax.fori_loop(0, self.count, step, 0)


BACKWARD_EVENTS = {
    "hidden": [],
    "up": [(0, 0)],
    "gate": [],
    "dh2": [(0, 1), (1, 0)],
    "norm2": [],
    "out": [(0, 2), (2, 0)],
    "attend": [(1, 1), (2, 1), (1, 2), (3, 0)],
    "qkv": [(2, 2), (3, 1)],
    "dh1": [(3, 2), (4, 0)],
    "end": [(5, 0), (4, 1), (6, 0), (5, 1), (7, 0), (4, 2), (6, 1), (7, 1), (5, 2), (6, 2), (7, 2)],
}


def backward_kernel(plan, *refs):
    n = len(plan.tensors)
    ws, refs = refs[:7], refs[7:]
    (x_h, dy_h, q_h, k_h, v_h, p_h, x1_h, ha_h, ho_h, hm_h, hid_h, dact_h, act_h, dyh_h, gains), refs = refs[:15], refs[15:]
    (gtok_o,), outs, refs = refs[:1], refs[1 : 1 + n], refs[1 + n :]
    total, refs = refs[:n], refs[n:]
    got, refs = [refs[3 * t : 3 * t + 3] for t in range(n)], refs[3 * n :]
    (da, db, kx, vx, dar, dbr, dxr_r, qr, kr, vr, dyh, turned, small, broad, dy, x1, dh, dxr, do), refs = refs[:19], refs[19:]
    (kc, vc, rim_k, rim_v, gain_sum, gain_other), refs = refs[:6], refs[6:]
    send, recv, load_sem, small_sem, broad_sem, turn_sem, half_send, half_recv, out_sem = refs
    wq, wk, wv, wo, wg, wu, wd = ws
    rows, width = dy.shape
    wide = wg.shape[2]
    columns = wq.shape[2]
    me = Place()
    me.greet()
    scatter = Scatter(plan, me, total, got, outs, send, recv)
    halves = []

    def to_partner(k, src, dst):
        copy = remote(src, dst, half_send.at[k], half_recv.at[k], me.to_core())
        copy.start()
        halves.append(copy)
        return copy

    loads = [0]

    def load(src, dst):
        copy = pltpu.make_async_copy(src, dst, load_sem.at[loads[0]])
        loads[0] += 1
        copy.start()
        return copy

    def own(size, side=0):
        return pl.ds(pl.multiple_of((me.s if side == 0 else 1 - me.s) * size, 128), size)

    tall = plan.tensors[0][0] * NY * NX
    hid_tiles = Stream(
        NZ, turn_sem, lambda j, slot: [(hid_h.at[pl.ds(pl.multiple_of(j * tall, 16), tall), :], turned.at[slot, pl.ds(0, tall), :])]
    )
    tile = 256

    def weight_tiles(w, k=0, slots=small):
        return lambda j, slot: (w.at[:, pl.ds(pl.multiple_of(j * tile, tile), tile), :], slots.at[slot, k])

    def stream_of(fetchers, count, sems):
        return Stream(count, sems, lambda j, slot: [f(j, slot) for f in fetchers])

    down_tiles = stream_of([weight_tiles(wd)], wd.shape[1] // tile, small_sem)
    mlp_tiles = stream_of([weight_tiles(wg, 0, broad), weight_tiles(wu, 1, broad)], width // tile, broad_sem)
    out_tiles = stream_of([weight_tiles(wo)], width // tile, small_sem)
    qkv_tiles = stream_of([weight_tiles(w, k) for k, w in enumerate((wq, wk, wv))], width // tile, small_sem)

    get_dyh = load(dyh_h, dyh)
    hid_tiles.prime()
    get_dy = load(dy_h, dy)
    down_tiles.prime()
    get_dact = load(dact_h, da)
    get_act = load(act_h, db)
    mlp_tiles.prime()
    get_x1 = load(x1_h, x1)
    get_k, get_v = load(k_h, kx), load(v_h, vx)

    def events(name):
        for t, phase in BACKWARD_EVENTS[name]:
            for i in plan.of_tensor[t]:
                scatter.wait(i, phase)
                scatter.add(i, phase)
                if phase < 2:
                    scatter.start(i, phase + 1)

    def begin(t):
        for i in plan.of_tensor[t]:
            scatter.start(i, 0)

    def put(t, z, part):
        row_count, column_count = plan.tensors[t][:2]
        total[t][z] = part.reshape(NY, NX, row_count, column_count).astype(total[t].dtype)

    get_dyh.wait()

    def down_body(z, slot):
        put(0, z, mm(turned[slot, :tall], dyh[...]))

    hid_tiles.run(down_body)
    begin(0)
    get_hm = load(hm_h, turned.at[0])
    get_ho = load(ho_h, turned.at[1])
    events("hidden")

    for copy in (get_dy, get_dact, get_act):
        copy.wait()

    def hidden_body(j, slot):
        part = mm_nt(dy[:, :columns], small[slot, 0, 0]) + mm_nt(dy[:, columns:], small[slot, 0, 1])
        at = pl.ds(pl.multiple_of(j * tile, tile), tile)
        da[:, at] = (part * da[:, at].astype(F32)).astype(LOW)
        db[:, at] = (part * db[:, at].astype(F32)).astype(LOW)

    down_tiles.run(hidden_body)
    out_tiles.prime()
    got_db = to_partner(0, db.at[:, own(wide, 1)], dbr)
    got_da = to_partner(1, da.at[:, own(wide, 1)], dar)
    events("up")

    def weight_grad_to(t, slot, mine, theirs):
        row_count = plan.tensors[t][0] * NY * NX

        def step(z, _):
            at = pl.ds(pl.multiple_of(z * row_count, 16), row_count)
            put(t, z, mm(turned[slot, at, own(rows)], mine()) + mm(turned[slot, at, own(rows, 1)], theirs[...]))
            return 0

        lax.fori_loop(0, NZ, step, 0)
        begin(t)

    get_hm.wait()
    got_db.wait_recv()
    weight_grad_to(1, 0, lambda: db[:, own(wide)], dbr)
    events("gate")
    got_da.wait_recv()
    weight_grad_to(2, 0, lambda: da[:, own(wide)], dar)
    get_ha = load(ha_h, turned.at[0])
    events("dh2")

    def dh2_body(j, slot):
        part = None
        for k, grad in ((0, da), (1, db)):
            for side in range(2):
                term = mm_nt(grad[:, side * wide : (side + 1) * wide], broad[slot, k, side])
                part = term if part is None else part + term
        dh[:, pl.ds(pl.multiple_of(j * tile, tile), tile)] = part

    mlp_tiles.run(dh2_body)
    for copy in halves[:2]:
        copy.wait_send()
    get_q = load(q_h, da.at[:, pl.ds(0, width)])
    get_p = load(p_h, db.at[:, pl.ds(0, HEADS * SPAN)])
    get_x = load(x_h, da.at[:, pl.ds(width, width)])
    events("norm2")

    def norm_grad(values, grad_norm, gain):
        inverse = lax.rsqrt(jnp.mean(values * values, axis=-1, keepdims=True) + EPS)
        scaled = grad_norm * gain
        mean_term = jnp.mean(values * scaled, axis=-1, keepdims=True)
        back = inverse * scaled - values * (inverse * inverse * inverse) * mean_term
        return back, jnp.sum(values * inverse * grad_norm, axis=0, keepdims=True)

    gain_sum[...] = jnp.zeros_like(gain_sum)
    get_x1.wait()

    def norm2_body(at):
        back, gain_part = norm_grad(x1[at, :], dh[at, :], gains[1:2, :])
        gain_sum[1:2, :] += gain_part
        grad = dy[at, :].astype(F32) + back
        x1[at, :] = grad
        dxr[at, :] = grad.astype(LOW)

    each_rows(rows, 64, norm2_body)
    got_dxr = to_partner(2, dxr.at[:, own(columns, 1)], dxr_r)
    events("out")

    def out_body(j, slot):
        part = mm_nt(dxr[:, :columns], small[slot, 0, 0]) + mm_nt(dxr[:, columns:], small[slot, 0, 1])
        do[:, pl.ds(pl.multiple_of(j * tile, tile), tile)] = part.astype(LOW)

    out_tiles.run(out_body)
    qkv_tiles.prime()
    get_ho.wait()
    got_dxr.wait_recv()
    weight_grad_to(3, 1, lambda: dxr[:, own(columns)], dxr_r)
    events("attend")

    kc[...] = jnp.zeros_like(kc)
    vc[...] = jnp.zeros_like(vc)
    for copy in (get_q, get_p, get_k, get_v):
        copy.wait()
    scale = HEAD_DIM ** (-0.5)

    def attend(b, _):
        at = pl.ds(pl.multiple_of(b * WINDOW, WINDOW), WINDOW)
        over = pl.ds(pl.multiple_of(b * WINDOW, WINDOW), SPAN)
        for p in range(HEADS // 2):
            cols = slice(p * PAIR, (p + 1) * PAIR)
            q2, do2 = both_heads(da[at, cols]), both_heads(do[at, cols])
            keys, values = kx[over, cols], vx[over, cols]
            prob = jnp.concatenate(
                [db[at, 2 * p * SPAN : (2 * p + 1) * SPAN], db[at, (2 * p + 1) * SPAN : (2 * p + 2) * SPAN]], axis=0
            )
            wide_prob = prob.astype(F32)
            grad_prob = mm_nt(do2, values)
            inner = jnp.sum(wide_prob * grad_prob, axis=-1, keepdims=True)
            grad_score = (wide_prob * (grad_prob - inner)).astype(LOW)
            da[at, cols] = (merge_heads(mm(grad_score, keys)) * scale).astype(LOW)
            grad_keys = mm_tn(grad_score, q2) * scale
            grad_values = mm_tn(prob, do2)
            kx[at, cols] = (kc[:, cols] + grad_keys[:WINDOW]).astype(LOW)
            vx[at, cols] = (vc[:, cols] + grad_values[:WINDOW]).astype(LOW)
            kc[:, cols] = grad_keys[WINDOW:]
            vc[:, cols] = grad_values[WINDOW:]
        return 0

    lax.fori_loop(0, rows // WINDOW, attend, 0)
    rims = [to_partner(3, kx.at[pl.ds(0, WINDOW), :], rim_k), to_partner(4, vx.at[pl.ds(0, WINDOW), :], rim_v)]
    got_q = to_partner(5, da.at[:, own(columns, 1)], qr)
    events("qkv")
    got_q.wait_recv()
    get_ha.wait()
    weight_grad_to(4, 0, lambda: da[:, own(columns)], qr)
    for copy, ref, carry, rim in ((rims[0], kx, kc, rim_k), (rims[1], vx, vc, rim_v)):
        copy.wait_recv()
        ref[pl.ds(rows, WINDOW), :] = (carry[...] + rim[...].astype(F32)).astype(LOW)
    later = pl.ds(WINDOW, rows)
    got_k = to_partner(6, kx.at[later, own(columns, 1)], kr)
    got_v = to_partner(7, vx.at[later, own(columns, 1)], vr)
    got_k.wait_recv()
    weight_grad_to(5, 0, lambda: kx[later, own(columns)], kr)
    got_v.wait_recv()
    weight_grad_to(6, 0, lambda: vx[later, own(columns)], vr)
    events("dh1")

    def dh1_body(j, slot):
        part = None
        for k, (grad, skip) in enumerate(((da, 0), (kx, WINDOW), (vx, WINDOW))):
            for side in range(2):
                left = grad[pl.ds(skip, rows), side * columns : (side + 1) * columns]
                term = mm_nt(left, small[slot, k, side])
                part = term if part is None else part + term
        dh[:, pl.ds(pl.multiple_of(j * tile, tile), tile)] = part

    qkv_tiles.run(dh1_body)
    get_x.wait()

    def norm1_body(at):
        back, gain_part = norm_grad(da[at, pl.ds(width, width)].astype(F32), dh[at, :], gains[0:1, :])
        gain_sum[0:1, :] += gain_part
        x1[at, :] = x1[at, :] + back

    each_rows(rows, 64, norm1_body)
    give = pltpu.make_async_copy(x1, gtok_o, out_sem)
    give.start()
    got_gain = to_partner(8, gain_sum, gain_other)
    got_gain.wait_recv()
    lanes = plan.tensors[7][1]
    for c in range(NZ * NY * NX):
        at = slice(c // 2 * lanes, (c // 2 + 1) * lanes)
        total[7][c // 4, c // 2 % 2, c % 2] = gain_sum[:, at] + gain_other[:, at]
    begin(7)
    events("end")
    for i in range(len(plan.items)):
        scatter.finish(i)
    for k, copy in enumerate(halves):
        if k >= 2:
            copy.wait_send()
    give.wait()


def backward_all(plan, ws, tokens, cotangent, acts):
    n, k = len(plan.tensors), len(plan.items)
    rows, width = tokens.shape
    columns, wide = ws[0].shape[2], ws[4].shape[2]
    anywhere = pl.BlockSpec(memory_space=pl.ANY)
    inside = pl.BlockSpec(memory_space=pltpu.VMEM)
    over = WINDOW + rows
    scratch = [
        ((rows, 2 * wide), LOW),
        ((rows, 2 * wide), LOW),
        ((over, width), LOW),
        ((over, width), LOW),
        ((rows, wide), LOW),
        ((rows, wide), LOW),
        ((rows, columns), LOW),
        ((rows, columns), LOW),
        ((rows, columns), LOW),
        ((rows, columns), LOW),
        ((2 * rows, columns), LOW),
        ((2, width, 2 * rows), LOW),
        ((2, 3, 2, 256, columns), LOW),
        ((2, 2, 2, 256, wide), LOW),
        ((rows, width), LOW),
        ((rows, width), F32),
        ((rows, width), F32),
        ((rows, width), LOW),
        ((rows, width), LOW),
        ((WINDOW, width), F32),
        ((WINDOW, width), F32),
        ((WINDOW, width), LOW),
        ((WINDOW, width), LOW),
        ((8, width), F32),
        ((8, width), F32),
    ]
    totals = [((NZ, NY, NX) + t[:2], t[4]) for t in plan.tensors]
    got = [shape for shapes in got_shapes(plan) for shape in shapes]
    dma = pltpu.SemaphoreType.DMA
    return pl.pallas_call(
        functools.partial(backward_kernel, plan),
        out_shape=[jax.ShapeDtypeStruct((rows, width), F32)]
        + [jax.ShapeDtypeStruct(t[:2], F32) for t in plan.tensors],
        in_specs=[anywhere] * (7 + 14) + [inside],
        out_specs=[anywhere] + [inside] * n,
        scratch_shapes=[pltpu.VMEM(*s) for s in totals + got + scratch]
        + [dma((k, 3, 3)), dma((k, 3, 3)), dma((16,)), dma((2, 3)), dma((2, 2)), dma((2, 1)), dma((9,)), dma((9,)), dma],
        compiler_params=pltpu.CompilerParams(
            collective_id=1, has_side_effects=True, vmem_limit_bytes=63 * 2**20
        ),
        name="backward_all",
    )(*ws, tokens, cotangent, *acts)


def pad_columns(w, part, tile):
    rows = w.shape[0]
    return jnp.pad(w.reshape(rows, -1, part), ((0, 0), (0, 0), (0, tile - part))).reshape(rows, -1)


def unpad_columns(w, part, tile):
    rows = w.shape[0]
    return w.reshape(rows, -1, tile)[:, :, :part].reshape(rows, -1)


def kinds(w_query, w_gate, w_down):
    rows, columns = w_query.shape
    part = w_down.shape[0]
    tile = -(-part // 16) * 16
    wide = w_gate.shape[1] // part * tile
    first = -(-tile // 32) * 16
    halves = (rows // 2, rows // 2)
    return {
        "square": (rows, columns, "zf", halves, LOW),
        "square_m": (rows, columns, "zm", halves, LOW),
        "broad": (rows, wide, "zf", halves, LOW),
        "tall": (tile, columns, "zm", (first, tile - first), LOW),
        "gain": (16, 2 * rows, "zf", (16,), LOW),
        "gain_grad": (8, 2 * rows, "zf", (8,), F32),
    }


def gather_plan(w_query, w_key, w_value, w_out, w_gate, w_up, w_down, gain_attn, gain_mlp):
    kind = kinds(w_query, w_gate, w_down)
    names = ("gain", "square", "square", "square_m", "square", "broad", "broad", "tall")
    plan = Plan([kind[name] for name in names])
    rows, part, tile = w_query.shape[0], w_down.shape[0], kind["tall"][0]
    both = jnp.stack([gain_attn, gain_mlp])
    left = jnp.pad(both, ((0, 14), (0, rows)))
    right = jnp.pad(both, ((0, 14), (rows, 0)))
    pair = jnp.where(lax.axis_index("dp") % 2 == 0, left, right)
    shards = [
        pair,
        w_query,
        w_key,
        w_value,
        w_out,
        pad_columns(w_gate, part, tile),
        pad_columns(w_up, part, tile),
        jnp.pad(w_down, ((0, tile - part), (0, 0))),
    ]
    return plan, shards


def swift_block(
    tokens,
    seq_lengths,
    w_query,
    w_key,
    w_value,
    w_out,
    w_gate,
    w_up,
    w_down,
    gain_attn,
    gain_mlp,
    cotangent,
):
    plan, shards = gather_plan(w_query, w_key, w_value, w_out, w_gate, w_up, w_down, gain_attn, gain_mlp)
    ws, acts = forward_all(plan, seq_lengths, tokens, cotangent, shards)
    ws = [w.reshape(2, -1, w.shape[-1]) for w in ws]
    kind = kinds(w_query, w_gate, w_down)
    names = ("tall", "broad", "broad", "square", "square", "square", "square_m", "gain_grad")
    back = Plan([kind[name] for name in names])
    grad_tokens, *sums = backward_all(back, ws, tokens, cotangent, acts[1:])
    rows, part, tile = w_query.shape[0], w_down.shape[0], kind["tall"][0]
    own = lax.dynamic_slice_in_dim(sums[7], (lax.axis_index("dp") % 2) * rows, rows, 1)
    return (
        acts[0],
        grad_tokens,
        sums[4],
        sums[5],
        sums[6],
        sums[3],
        unpad_columns(sums[2], part, tile),
        unpad_columns(sums[1], part, tile),
        sums[0][:part],
        own[0],
        own[1],
    )


def solution(mesh):
    fast = (mesh.shape["dp"], mesh.shape["seq"]) == (NZ * NY * NX, 2)
    shards = swift_block if fast else plain_block
    in_specs = (
        P(("dp", "seq"), None),
        P("dp", None),
        P("dp", "seq"),
        P("dp", "seq"),
        P("dp", "seq"),
        P("dp", "seq"),
        P("dp", "seq"),
        P("dp", "seq"),
        P("dp", "seq"),
        P("dp"),
        P("dp"),
        P(("dp", "seq"), None),
    )
    out_specs = (
        P(("dp", "seq"), None),
        P(("dp", "seq"), None),
        P("dp", "seq"),
        P("dp", "seq"),
        P("dp", "seq"),
        P("dp", "seq"),
        P("dp", "seq"),
        P("dp", "seq"),
        P("dp", "seq"),
        P("dp"),
        P("dp"),
    )
    return jax.shard_map(shards, mesh=mesh, in_specs=in_specs, out_specs=out_specs, check_vma=False)
```

```python
import functools

import jax
import jax.numpy as jnp
from jax import lax
from jax.experimental import pallas as pl
from jax.experimental.pallas import tpu as pltpu
from jax.sharding import PartitionSpec as P

HEADS = 16
HEAD_DIM = 64
WINDOW = 64


eps_norm = 1e-05


def from_behind(block, axis, distance):
    devices = range(lax.axis_size(axis))
    route = [(i - distance, i) for i in devices if i - distance in devices]
    return lax.ppermute(block, axis, route)


def inverse_rms(values):
    return lax.rsqrt(jnp.mean(values * values, axis=-1, keepdims=True) + eps_norm)


def doc_numbers(lengths_row, positions):
    first_end = lengths_row[0]
    second_end = lengths_row[0] + lengths_row[1]
    return (positions >= first_end).astype(jnp.int32) + (positions >= second_end).astype(jnp.int32)


def window_mask(query_pos, query_doc, key_pos, key_doc, window):
    after = key_pos[None, :] >= query_pos[:, None] - window
    before = key_pos[None, :] <= query_pos[:, None]
    inside = (key_pos[None, :] >= 0) & (key_doc[None, :] == query_doc[:, None])
    return after & before & inside


def norm_back(values, inverse, gain, grad_norm):
    scaled = grad_norm * gain
    mean_term = jnp.mean(values * scaled, axis=-1, keepdims=True)
    grad_values = inverse * scaled - values * (inverse * inverse * inverse) * mean_term
    grad_gain = jnp.sum(values * inverse * grad_norm, axis=0)
    return (grad_values, grad_gain)


def project(left, right):
    return jnp.dot(left, right, preferred_element_type=jnp.float32)


def project_back(grad_rows, weight):
    return jnp.einsum("tf,df->td", grad_rows, weight, preferred_element_type=jnp.float32)


def weight_grad(inputs, grad_rows):
    return jnp.einsum("td,tf->df", inputs, grad_rows, preferred_element_type=jnp.float32)


def plain_block(
    tokens,
    seq_lengths,
    w_query,
    w_key,
    w_value,
    w_out,
    w_gate,
    w_up,
    w_down,
    gain_attn,
    gain_mlp,
    cotangent,
):
    row_count = tokens.shape[0]
    block_rows = min(512, row_count)
    head_group = HEADS // 2
    score_scale = HEAD_DIM ** (-0.5)
    row_parts = (
        lax.all_gather(w_query, "dp", axis=0, tiled=True),
        lax.all_gather(w_key, "dp", axis=0, tiled=True),
        lax.all_gather(w_value, "dp", axis=0, tiled=True),
        lax.all_gather(w_out, "dp", axis=0, tiled=True),
        lax.all_gather(w_gate, "dp", axis=0, tiled=True),
        lax.all_gather(w_up, "dp", axis=0, tiled=True),
        lax.all_gather(w_down, "dp", axis=0, tiled=True),
        lax.all_gather(gain_attn, "dp", axis=0, tiled=True),
        lax.all_gather(gain_mlp, "dp", axis=0, tiled=True),
    )
    full_mats = (
        lax.all_gather(row_parts[0], "seq", axis=1, tiled=True),
        lax.all_gather(row_parts[1], "seq", axis=1, tiled=True),
        lax.all_gather(row_parts[2], "seq", axis=1, tiled=True),
        lax.all_gather(row_parts[3], "seq", axis=1, tiled=True),
        lax.all_gather(row_parts[4], "seq", axis=1, tiled=True),
        lax.all_gather(row_parts[5], "seq", axis=1, tiled=True),
        lax.all_gather(row_parts[6], "seq", axis=1, tiled=True),
    )
    query_w, key_w, value_w, out_w, gate_w, up_w, down_full = full_mats
    gain_one = row_parts[7].astype(jnp.float32)
    gain_two = row_parts[8].astype(jnp.float32)
    inputs = tokens.astype(jnp.float32)
    inv_one = inverse_rms(inputs)
    normed_one = (inputs * inv_one * gain_one).astype(jnp.bfloat16)
    query_low = project(normed_one, query_w).astype(jnp.bfloat16)
    key_low = project(normed_one, key_w).astype(jnp.bfloat16)
    value_low = project(normed_one, value_w).astype(jnp.bfloat16)
    rim_pairs = from_behind(
        (key_low[row_count - WINDOW :], value_low[row_count - WINDOW :]), "seq", 1
    )
    keys_ext = jnp.concatenate([rim_pairs[0], key_low], axis=0).reshape(
        row_count + WINDOW, HEADS, HEAD_DIM
    )
    values_ext = jnp.concatenate([rim_pairs[1], value_low], axis=0).reshape(
        row_count + WINDOW, HEADS, HEAD_DIM
    )
    query_heads = query_low.reshape(row_count, HEADS, HEAD_DIM)
    span_start = lax.axis_index("seq") * row_count
    query_pos = span_start + jnp.arange(row_count, dtype=jnp.int32)
    key_pos = span_start - WINDOW + jnp.arange(row_count + WINDOW, dtype=jnp.int32)
    query_doc = doc_numbers(seq_lengths[0], query_pos)
    key_doc = doc_numbers(seq_lengths[0], key_pos)

    def tile_scores(row_start, head_start):
        visible = window_mask(query_pos, query_doc, key_pos, key_doc, WINDOW)
        scores_raw = (
            jnp.einsum(
                "qhd,khd->hqk",
                query_heads[
                    row_start : row_start + block_rows, head_start : head_start + head_group
                ],
                keys_ext[
                    row_start : row_start + block_rows + WINDOW,
                    head_start : head_start + head_group,
                ],
                preferred_element_type=jnp.float32,
            )
            * score_scale
        )
        return jnp.where(visible[None], scores_raw, -1e30)

    log_totals = {}
    row_start = 0
    head_parts = []
    for head_start in range(0, HEADS, head_group):
        masked_scores = tile_scores(row_start, head_start)
        top_score = jnp.max(masked_scores, axis=-1, keepdims=True)
        log_total = top_score + jnp.log(
            jnp.sum(jnp.exp(masked_scores - top_score), axis=-1, keepdims=True)
        )
        prob_low = jnp.exp(masked_scores - log_total).astype(jnp.bfloat16)
        value_tile = values_ext[
            row_start : row_start + block_rows + WINDOW, head_start : head_start + head_group
        ]
        head_parts.append(
            jnp.einsum("hqk,khd->qhd", prob_low, value_tile, preferred_element_type=jnp.float32)
        )
        log_totals[row_start, head_start] = log_total
    attn_blocks = jnp.concatenate(head_parts, axis=1)
    attended = attn_blocks.reshape(row_count, HEADS * HEAD_DIM).astype(jnp.bfloat16)
    middle = inputs + project(attended, out_w)
    inv_two = inverse_rms(middle)
    normed_two = (middle * inv_two * gain_two).astype(jnp.bfloat16)
    gate_pre = project(normed_two, gate_w)
    up_pre = project(normed_two, up_w)
    gate_act = jax.nn.silu(gate_pre)
    hidden = (gate_act * up_pre).astype(jnp.bfloat16)
    block_out = (middle + project(hidden, down_full)).astype(jnp.bfloat16)
    rows_again = (
        lax.all_gather(w_query, "dp", axis=0, tiled=True),
        lax.all_gather(w_key, "dp", axis=0, tiled=True),
        lax.all_gather(w_value, "dp", axis=0, tiled=True),
        lax.all_gather(w_out, "dp", axis=0, tiled=True),
        lax.all_gather(w_gate, "dp", axis=0, tiled=True),
        lax.all_gather(w_up, "dp", axis=0, tiled=True),
        lax.all_gather(w_down, "dp", axis=0, tiled=True),
        lax.all_gather(gain_attn, "dp", axis=0, tiled=True),
        lax.all_gather(gain_mlp, "dp", axis=0, tiled=True),
    )
    mats_again = (
        lax.all_gather(rows_again[0], "seq", axis=1, tiled=True),
        lax.all_gather(rows_again[1], "seq", axis=1, tiled=True),
        lax.all_gather(rows_again[2], "seq", axis=1, tiled=True),
        lax.all_gather(rows_again[3], "seq", axis=1, tiled=True),
        lax.all_gather(rows_again[4], "seq", axis=1, tiled=True),
        lax.all_gather(rows_again[5], "seq", axis=1, tiled=True),
        lax.all_gather(rows_again[6], "seq", axis=1, tiled=True),
    )
    back_query, back_key, back_value, back_out, back_gate, back_up, back_down = mats_again
    back_gain_one = rows_again[7].astype(jnp.float32)
    back_gain_two = rows_again[8].astype(jnp.float32)
    grad_final = cotangent.astype(jnp.float32)
    d_down = weight_grad(hidden, cotangent)
    grad_hidden = project_back(cotangent, back_down)
    sigmoid_gate = jax.nn.sigmoid(gate_pre)
    grad_gate_low = (
        grad_hidden * up_pre * sigmoid_gate * (1.0 + gate_pre * (1.0 - sigmoid_gate))
    ).astype(jnp.bfloat16)
    grad_up_low = (grad_hidden * gate_act).astype(jnp.bfloat16)
    d_gate = weight_grad(normed_two, grad_gate_low)
    d_up = weight_grad(normed_two, grad_up_low)
    grad_normed_two = project_back(grad_gate_low, back_gate) + project_back(grad_up_low, back_up)
    grad_mid_norm, d_gain_two = norm_back(middle, inv_two, back_gain_two, grad_normed_two)
    grad_middle = grad_final + grad_mid_norm
    grad_proj = grad_middle.astype(jnp.bfloat16)
    d_out = weight_grad(attended, grad_proj)
    grad_attended = (
        project_back(grad_proj, back_out).astype(jnp.bfloat16).reshape(row_count, HEADS, HEAD_DIM)
    )
    grad_keys_ext = jnp.zeros((row_count + WINDOW, HEADS, HEAD_DIM), jnp.float32)
    grad_values_ext = jnp.zeros((row_count + WINDOW, HEADS, HEAD_DIM), jnp.float32)
    row_start = 0
    head_parts = []
    for head_start in range(0, HEADS, head_group):
        head_end = head_start + head_group
        masked_scores = tile_scores(row_start, head_start)
        prob_full = jnp.exp(masked_scores - log_totals[row_start, head_start])
        grad_tile = grad_attended[row_start : row_start + block_rows, head_start:head_end]
        key_tile = keys_ext[row_start : row_start + block_rows + WINDOW, head_start:head_end]
        value_tile = values_ext[row_start : row_start + block_rows + WINDOW, head_start:head_end]
        query_tile = query_heads[row_start : row_start + block_rows, head_start:head_end]
        grad_prob = jnp.einsum(
            "qhd,khd->hqk", grad_tile, value_tile, preferred_element_type=jnp.float32
        )
        inner = jnp.sum(prob_full * grad_prob, axis=-1, keepdims=True)
        grad_score = (prob_full * (grad_prob - inner)).astype(jnp.bfloat16)
        head_parts.append(
            jnp.einsum("hqk,khd->qhd", grad_score, key_tile, preferred_element_type=jnp.float32)
            * score_scale
        )
        key_term = (
            jnp.einsum("hqk,qhd->khd", grad_score, query_tile, preferred_element_type=jnp.float32)
            * score_scale
        )
        value_term = jnp.einsum(
            "hqk,qhd->khd",
            prob_full.astype(jnp.bfloat16),
            grad_tile,
            preferred_element_type=jnp.float32,
        )
        grad_keys_ext = grad_keys_ext.at[
            row_start : row_start + block_rows + WINDOW, head_start:head_end
        ].add(key_term)
        grad_values_ext = grad_values_ext.at[
            row_start : row_start + block_rows + WINDOW, head_start:head_end
        ].add(value_term)
    grad_query_blocks = jnp.concatenate(head_parts, axis=1)
    rim_back = (
        from_behind(
            grad_keys_ext[:WINDOW].reshape(WINDOW, HEADS * HEAD_DIM).astype(jnp.bfloat16), "seq", -1
        ).astype(jnp.float32),
        from_behind(
            grad_values_ext[:WINDOW].reshape(WINDOW, HEADS * HEAD_DIM).astype(jnp.bfloat16),
            "seq",
            -1,
        ).astype(jnp.float32),
    )
    grad_keys = (
        grad_keys_ext[WINDOW:]
        .reshape(row_count, HEADS * HEAD_DIM)
        .at[row_count - WINDOW :]
        .add(rim_back[0])
    )
    grad_values = (
        grad_values_ext[WINDOW:]
        .reshape(row_count, HEADS * HEAD_DIM)
        .at[row_count - WINDOW :]
        .add(rim_back[1])
    )
    grad_query_low = grad_query_blocks.reshape(row_count, HEADS * HEAD_DIM).astype(jnp.bfloat16)
    grad_key_low = grad_keys.astype(jnp.bfloat16)
    grad_value_low = grad_values.astype(jnp.bfloat16)
    d_query = weight_grad(normed_one, grad_query_low)
    d_key = weight_grad(normed_one, grad_key_low)
    d_value = weight_grad(normed_one, grad_value_low)
    grad_normed_one = (
        project_back(grad_query_low, back_query)
        + project_back(grad_key_low, back_key)
        + project_back(grad_value_low, back_value)
    )
    grad_in_norm, d_gain_one = norm_back(inputs, inv_one, back_gain_one, grad_normed_one)
    grad_inputs = grad_middle + grad_in_norm
    row_sums = (
        lax.psum_scatter(
            d_query.astype(jnp.bfloat16), "dp", scatter_dimension=0, tiled=True
        ).astype(jnp.float32),
        lax.psum_scatter(d_key.astype(jnp.bfloat16), "dp", scatter_dimension=0, tiled=True).astype(
            jnp.float32
        ),
        lax.psum_scatter(
            d_value.astype(jnp.bfloat16), "dp", scatter_dimension=0, tiled=True
        ).astype(jnp.float32),
        lax.psum_scatter(d_out.astype(jnp.bfloat16), "dp", scatter_dimension=0, tiled=True).astype(
            jnp.float32
        ),
        lax.psum_scatter(d_gate.astype(jnp.bfloat16), "dp", scatter_dimension=0, tiled=True).astype(
            jnp.float32
        ),
        lax.psum_scatter(d_up.astype(jnp.bfloat16), "dp", scatter_dimension=0, tiled=True).astype(
            jnp.float32
        ),
        lax.psum_scatter(d_down.astype(jnp.bfloat16), "dp", scatter_dimension=0, tiled=True).astype(
            jnp.float32
        ),
        lax.psum_scatter(
            d_gain_one.astype(jnp.bfloat16), "dp", scatter_dimension=0, tiled=True
        ).astype(jnp.float32),
        lax.psum_scatter(
            d_gain_two.astype(jnp.bfloat16), "dp", scatter_dimension=0, tiled=True
        ).astype(jnp.float32),
    )
    owned_mats = (
        lax.psum_scatter(
            row_sums[0].astype(jnp.bfloat16), "seq", scatter_dimension=1, tiled=True
        ).astype(jnp.float32),
        lax.psum_scatter(
            row_sums[1].astype(jnp.bfloat16), "seq", scatter_dimension=1, tiled=True
        ).astype(jnp.float32),
        lax.psum_scatter(
            row_sums[2].astype(jnp.bfloat16), "seq", scatter_dimension=1, tiled=True
        ).astype(jnp.float32),
        lax.psum_scatter(
            row_sums[3].astype(jnp.bfloat16), "seq", scatter_dimension=1, tiled=True
        ).astype(jnp.float32),
        lax.psum_scatter(
            row_sums[4].astype(jnp.bfloat16), "seq", scatter_dimension=1, tiled=True
        ).astype(jnp.float32),
        lax.psum_scatter(
            row_sums[5].astype(jnp.bfloat16), "seq", scatter_dimension=1, tiled=True
        ).astype(jnp.float32),
        lax.psum_scatter(
            row_sums[6].astype(jnp.bfloat16), "seq", scatter_dimension=1, tiled=True
        ).astype(jnp.float32),
    )
    owned_gains = lax.psum((row_sums[7], row_sums[8]), "seq")
    return (
        block_out,
        grad_inputs,
        owned_mats[0],
        owned_mats[1],
        owned_mats[2],
        owned_mats[3],
        owned_mats[4],
        owned_mats[5],
        owned_mats[6],
        owned_gains[0],
        owned_gains[1],
    )


MESH = pl.DeviceIdType.MESH
NZ, NY, NX = 4, 2, 2
SEQUENCE = {"zfx": "zxy", "zfy": "zyx", "zmx": "xzy", "zmy": "yzx"}
ALL_Z, ALL_Y, ALL_X = pl.ds(0, NZ), pl.ds(0, NY), pl.ds(0, NX)


class Plan:
    def __init__(self, tensors):
        self.tensors = tensors
        self.items, self.of_tensor = [], []
        for t, (_, _, _, cuts) in enumerate(tensors):
            begin, mine = 0, []
            for kind, count in cuts:
                mine.append(len(self.items))
                self.items.append((t, SEQUENCE[kind], begin, count))
                begin += count
            self.of_tensor.append(mine)


class Place:
    def __init__(self):
        self.c, self.s = lax.axis_index("dp"), lax.axis_index("seq")
        self.z, self.y, self.x = self.c // 4, (self.c // 2) % 2, self.c % 2

    def at(self, z, y, x):
        return (z * 4 + y * 2 + x, self.s)

    def to_x(self):
        return self.at(self.z, self.y, 1 - self.x)

    def to_y(self):
        return self.at(self.z, 1 - self.y, self.x)

    def to_z(self, step):
        return self.at((self.z + step) % NZ, self.y, self.x)

    def to_core(self):
        return (self.c, 1 - self.s)

    def greet(self):
        barrier = pltpu.get_barrier_semaphore()
        peers = [self.to_x(), self.to_y(), self.to_core()] + [self.to_z(k) for k in (1, 2, 3)]
        for peer in peers:
            pl.semaphore_signal(barrier, inc=1, device_id=peer, device_id_type=MESH)
        pl.semaphore_wait(barrier, len(peers))


def remote(src, dst, send, recv, device):
    return pltpu.make_async_remote_copy(
        src_ref=src, dst_ref=dst, send_sem=send, recv_sem=recv, device_id=device, device_id_type=MESH
    )


class Gather:
    def __init__(self, plan, place, shards, bufs, send, recv, local):
        self.plan, self.me, self.shards, self.bufs = plan, place, shards, bufs
        self.send, self.recv, self.local = send, recv, local

    def own_copy(self, t):
        me = self.me
        return pltpu.make_async_copy(
            self.shards[t], self.bufs[t].at[me.s, me.z, me.y, me.x], self.local.at[t]
        )

    def moves(self, i, phase):
        t, seq, begin, count = self.plan.items[i]
        me, buf = self.me, self.bufs[t]
        rows = pl.ds(begin, count)

        def view(z, y, x, half=me.s):
            return buf.at[half, z, y, x, rows, :]

        if phase == 3:
            whole = view(ALL_Z, ALL_Y, ALL_X)
            return [(whole, whole, me.to_core(), view(ALL_Z, ALL_Y, ALL_X, 1 - me.s), 0)]
        done, axis = seq[:phase], seq[phase]
        z = ALL_Z if "z" in done else me.z
        y = ALL_Y if "y" in done else me.y
        x = ALL_X if "x" in done else me.x
        there = view(z, y, x)
        here = self.shards[t].at[rows, :] if phase == 0 else there
        if axis == "x":
            return [(here, there, me.to_x(), view(z, y, 1 - me.x), 0)]
        if axis == "y":
            return [(here, there, me.to_y(), view(z, 1 - me.y, x), 0)]
        return [
            (here, there, me.to_z(k), view((me.z + NZ - k) % NZ, y, x), k - 1) for k in (1, 2, 3)
        ]

    def copy(self, i, phase, src, dst, device, k):
        return remote(src, dst, self.send.at[i, phase, k], self.recv.at[i, phase, k], device)

    def start(self, i, phase):
        for here, there, device, _, k in self.moves(i, phase):
            self.copy(i, phase, here, there, device, k).start()

    def wait(self, i, phase):
        for _, _, device, arrived, k in self.moves(i, phase):
            self.copy(i, phase, arrived, arrived, device, k).wait_recv()

    def finish(self, i):
        for phase in range(4):
            for here, there, device, _, k in self.moves(i, phase):
                self.copy(i, phase, here, there, device, k).wait_send()


def got_shapes(plan):
    shapes = []
    for t, seq, _, count in plan.items:
        _, columns, dtype, _ = plan.tensors[t]
        second, third = ((1, NZ), (3,)) if seq[0] == "z" else ((3, 2), (1,))
        shapes.append([(d + (count, columns), dtype) for d in ((NZ, 2), second, third)])
    return shapes


class Scatter:
    def __init__(self, plan, place, total, got, out, send, recv):
        self.plan, self.me, self.total, self.got, self.out = plan, place, total, got, out
        self.send, self.recv = send, recv

    def moves(self, i, phase):
        t, seq, begin, count = self.plan.items[i]
        me, total, got = self.me, self.total[t], self.got[i][phase]
        rows = pl.ds(begin, count)
        axis, done = seq[2 - phase], seq[3 - phase :]
        z = me.z if "z" in done else ALL_Z
        y = me.y if "y" in done else ALL_Y
        x = me.x if "x" in done else ALL_X
        if phase == 0:
            lands = [got]
        else:
            lands = [got.at[k] for k in range(got.shape[0])]
        if axis == "x":
            return [(total.at[z, y, 1 - me.x, rows, :], lands[0], me.to_x(), 0)]
        if axis == "y":
            return [(total.at[z, 1 - me.y, x, rows, :], lands[0], me.to_y(), 0)]
        return [
            (total.at[(me.z + k) % NZ, y, x, rows, :], lands[k - 1], me.to_z(k), k - 1)
            for k in (1, 2, 3)
        ]

    def copy(self, i, phase, src, dst, device, k):
        return remote(src, dst, self.send.at[i, phase, k], self.recv.at[i, phase, k], device)

    def start(self, i, phase):
        for here, there, device, k in self.moves(i, phase):
            self.copy(i, phase, here, there, device, k).start()

    def wait(self, i, phase):
        for here, there, device, k in self.moves(i, phase):
            self.copy(i, phase, there, there, device, k).wait_recv()

    def add(self, i, phase):
        t, seq, begin, count = self.plan.items[i]
        me, total, got = self.me, self.total[t], self.got[i][phase]
        rows = pl.ds(begin, count)
        if phase == 0:
            for z in range(NZ):
                for o in range(2):
                    at = (z, me.y, o) if seq[2] == "y" else (z, o, me.x)
                    total[at + (rows,)] += got[z, o]
        elif phase == 1 and seq[1] != "z":
            for z in range(NZ):
                total[z, me.y, me.x, rows] += got[0, z]
        elif phase == 1:
            for o in range(2):
                at = (me.z, me.y, o) if seq[2] == "y" else (me.z, o, me.x)
                part = total[at + (rows,)].astype(jnp.float32)
                for k in range(3):
                    part += got[k, o].astype(jnp.float32)
                total[at + (rows,)] = part.astype(total.dtype)
        else:
            part = total[me.z, me.y, me.x, rows].astype(jnp.float32)
            for k in range(got.shape[0]):
                part += got[k].astype(jnp.float32)
            self.out[t][rows] = part

    def finish(self, i):
        for phase in range(3):
            for here, there, device, k in self.moves(i, phase):
                self.copy(i, phase, here, there, device, k).wait_send()


FORWARD_SCRIPT = (
    ("start", 12), ("start", 2), ("start", 0), ("start", 11), (0, 0), ("start", 1), (2, 0), ("start", 3),
    ("start", 6), (1, 0), ("start", 5), (1, 1), (2, 1), ("start", 7), (6, 0), (5, 0), (0, 1), (3, 0),
    ("start", 4), ("start", 16), (2, 2), ("start", 10), ("start", 17), (4, 0), (6, 1), (4, 1), (12, 0),
    (1, 2), (3, 1), (5, 1), ("start", 8), (0, 2), (10, 0), ("start", 9), "norm", ("start", 15), "query",
    (7, 0), (9, 0), (7, 1), (4, 2), ("start", 19), (5, 2), (17, 0), ("start", 14), (8, 0), (11, 0), (9, 1),
    (14, 0), ("start", 13), (15, 0), (3, 2), (8, 1), ("start", 18), (6, 2), (12, 1), (14, 1), ("start", 20),
    (7, 2), (11, 1), (10, 1), "key", (9, 2), (16, 0), "value", ("attend", 0), ("attend", 1), (18, 0), (13, 0),
    (15, 1), (19, 0), (8, 2), (13, 1), (11, 2), (16, 1), ("attend", 2), (14, 2), (19, 1), ("attend", 3),
    "out", (10, 2), (20, 0), (18, 1), (16, 2), (15, 2), (12, 2), (20, 1), (13, 2), (17, 1), ("mlp", 0),
    (19, 2), ("mlp", 1), (18, 2), ("mlp", 2), (20, 2), (17, 2), ("mlp", 3), "down",
)
BACKWARD_SCRIPT = (
    "down", ("hidden", 0), ("hidden", 1), "up", (3, 0), (1, 0), "gate", (0, 0), ("dh2", 0), ("dh2", 1),
    (2, 0), "norm2", (0, 1), (1, 1), "heads", (3, 1), "out", (11, 0), (5, 0), (6, 0), (7, 0), ("attend", 0),
    ("attend", 1), (4, 0), (10, 0), ("attend", 2), ("attend", 3), ("qkv", 0), (6, 1), (2, 1), (15, 0), (5, 1),
    ("qkv", 1), (9, 0), (12, 0), (14, 0), (4, 1), (7, 1), (5, 2), (15, 1), ("qkv", 2), (1, 2), (2, 2),
    (13, 0), (9, 1), "dh1", (14, 1), (16, 0), (12, 1), (6, 2), (19, 0), (17, 0), (16, 1), (10, 1), (8, 0),
    (7, 2), "norm1", (13, 1), (9, 2), (19, 1), (16, 2), (12, 2), (18, 0), (8, 1), "gains", (18, 1), (17, 1),
    (4, 2), (11, 1), (10, 2), (14, 2), (20, 0), (11, 2), (13, 2), (8, 2), (3, 2), (20, 1), (15, 2), (19, 2),
    (0, 2), (18, 2), (17, 2), (20, 2),
)


EPS = 1e-05
PAIR = 2 * HEAD_DIM
SPAN = 2 * WINDOW
GROUP = 8
LOW = jnp.bfloat16
F32 = jnp.float32


def mm(left, right):
    return jnp.dot(left, right, preferred_element_type=F32)


def mm_nt(left, right):
    return lax.dot_general(left, right, (((1,), (1,)), ((), ())), preferred_element_type=F32)


def mm_tn(left, right):
    return lax.dot_general(left, right, (((0,), (0,)), ((), ())), preferred_element_type=F32)


def column_tiles(columns, size):
    full = columns // size
    tiles = [(0, size, full)]
    if columns % size:
        tiles.append((full * size, columns % size, 1))
    return tiles


def each_tile(columns, size, body):
    for begin, width, count in column_tiles(columns, size):
        if count == 1:
            body(begin, width)
        else:

            def step(j, _, begin=begin, width=width):
                body(pl.multiple_of(begin + j * width, 128), width)
                return 0

            lax.fori_loop(0, count, step, 0)


def each_rows(rows, size, body):
    def step(j, _):
        body(pl.ds(pl.multiple_of(j * size, size), size))
        return 0

    lax.fori_loop(0, rows // size, step, 0)


def both_heads(block):
    first = lax.broadcasted_iota(jnp.int32, block.shape, 1) < HEAD_DIM
    zero = jnp.zeros_like(block)
    return jnp.concatenate([jnp.where(first, block, zero), jnp.where(first, zero, block)], axis=0)


def merge_heads(stacked):
    rows = stacked.shape[0] // 2
    first = lax.broadcasted_iota(jnp.int32, (rows, PAIR), 1) < HEAD_DIM
    return jnp.where(first, stacked[:rows], stacked[rows:])


class Copies:
    def __init__(self, sems):
        self.sems, self.made = sems, []

    def start(self, src, dst):
        copy = pltpu.make_async_copy(src, dst, self.sems.at[len(self.made)])
        copy.start()
        self.made.append(copy)
        return copy

    def wait_all(self):
        for copy in self.made:
            copy.wait()


def forward_kernel(plan, *refs):
    n = len(plan.tensors)
    lens, x_in, dy_in, refs = refs[0], refs[1], refs[2], refs[3:]
    raw, refs = refs[:n], refs[n:]
    w_out, refs = refs[: n - 1], refs[n - 1 :]
    (mixed_o, q_o, k_o, v_o, p_o, x1_o, ha_o, ho_o, hm_o, hid_o, dact_o, act_o, dyh_o, gain_o), refs = refs[:14], refs[14:]
    bufs, refs = refs[:n], refs[n:]
    gate_pad, up_pad, down_pad, refs = refs[0], refs[1], refs[2], refs[3:]
    shards = list(raw[:5]) + [gate_pad, up_pad, down_pad]
    (gains, h1, q, kx, vx, probs, o, x1, h2, hid, act, dact, ha, ho, hm, hidt, mixed), refs = refs[:17], refs[17:]
    send, recv, own_sem, out_sem, rim_send, rim_recv, half_send, half_recv = refs
    rows, width = x_in.shape
    chips = NZ * NY * NX
    me = Place()
    me.greet()
    gather = Gather(plan, me, shards, bufs, send, recv, own_sem)
    copies = Copies(out_sem)
    sends = []

    def to_partner(k, src, dst):
        copy = remote(src, dst, half_send.at[k], half_recv.at[k], me.to_core())
        copy.start()
        sends.append(copy)

    def lanes(ref):
        return ref.at[:, pl.ds(pl.multiple_of(me.s * rows, 128), rows)]

    def share(k, mine, whole):
        copies.start(mine, lanes(whole))
        to_partner(k, mine, lanes(whole))

    for t in range(5):
        gather.own_copy(t).start()
    part, tile = raw[7].shape[0], down_pad.shape[0]
    zero = jnp.zeros((raw[5].shape[0], tile - part), LOW)
    for src, dst in ((raw[5], gate_pad), (raw[6], up_pad)):
        value, pieces = src[...], []
        for k in range(value.shape[1] // part):
            pieces += [value[:, k * part : (k + 1) * part], zero]
        dst[...] = jnp.concatenate(pieces, axis=1)
    down_pad[...] = jnp.concatenate([raw[7][...], jnp.zeros((tile - part, down_pad.shape[1]), LOW)], axis=0)
    for t in range(5, n):
        gather.own_copy(t).start()
    for t in range(n):
        gather.own_copy(t).wait()
    half = dyh_o.shape[1]
    mine = pl.ds(pl.multiple_of(me.s * rows, 16), rows)
    copies.start(dy_in.at[:, pl.ds(pl.multiple_of(me.s * half, 128), half)], dyh_o.at[mine, :])
    to_partner(0, dy_in.at[:, pl.ds(pl.multiple_of((1 - me.s) * half, 128), half)], dyh_o.at[mine, :])

    def weight(t, side, cols):
        w = bufs[t][side, :, :, :, :, cols]
        return w.reshape(chips * w.shape[3], w.shape[4])

    def norm(values, gain):
        inverse = lax.rsqrt(jnp.mean(values * values, axis=-1, keepdims=True) + EPS)
        return (values * inverse * gain).astype(LOW)

    def first_norm():
        parts = []
        for z in range(NZ):
            for y in range(NY):
                pair = [bufs[0][me.s, z, y, x].astype(F32) for x in range(NX)]
                parts.append(pair[0] + pair[1])
        gains[...] = jnp.concatenate(parts, axis=1)[0:8]
        copies.start(gains, gain_o)

        def body(at):
            h1[at, :] = norm(x_in[at, :].astype(F32), gains[0:1, :])

        each_rows(rows, 64, body)
        turn(h1, ha)
        share(1, ha, ha_o)

    def turn(src, dst):
        def body(j, _):
            at = pl.ds(pl.multiple_of(j * 128, 128), 128)
            dst[at, :] = src[:, at].T
            return 0

        lax.fori_loop(0, src.shape[1] // 128, body, 0)

    def project_to(t, src, dst, skip):
        columns = plan.tensors[t][1]
        for side in range(2):

            def body(begin, size, side=side):
                part = mm(src[...], weight(t, side, pl.ds(begin, size)))
                dst[pl.ds(skip, rows), pl.ds(side * columns + begin, size)] = part.astype(LOW)

            each_tile(columns, 256, body)

    def rim(k, ref):
        return remote(ref.at[pl.ds(rows, WINDOW), :], ref.at[pl.ds(0, WINDOW), :], rim_send.at[k], rim_recv.at[k], me.to_core())

    def do_query():
        project_to(1, h1, q, 0)
        copies.start(q, q_o)

    def do_key():
        project_to(2, h1, kx, WINDOW)
        rim(0, kx).start()

    def do_value():
        project_to(3, h1, vx, WINDOW)
        rim(1, vx).start()

    def rims():
        for k, ref in ((0, kx), (1, vx)):
            rim(k, ref).wait_recv()
        copies.start(kx, k_o)
        copies.start(vx, v_o)

    first_end = lens[0, 0]
    second_end = first_end + lens[0, 1]

    def attend(b):
        base = me.s * rows + b * WINDOW
        at = pl.ds(pl.multiple_of(b * WINDOW, WINDOW), WINDOW)
        over = pl.ds(pl.multiple_of(b * WINDOW, WINDOW), SPAN)
        row = lax.broadcasted_iota(jnp.int32, (WINDOW, SPAN), 0)
        col = lax.broadcasted_iota(jnp.int32, (WINDOW, SPAN), 1)
        q_pos, k_pos = base + row, base - WINDOW + col

        def doc(pos):
            return (pos >= first_end).astype(jnp.int32) + (pos >= second_end).astype(jnp.int32)

        visible = (col >= row) & (col <= row + WINDOW) & (k_pos >= 0) & (doc(q_pos) == doc(k_pos))
        bias = jnp.where(visible, 0.0, -1e30)
        bias = jnp.concatenate([bias, bias], axis=0)
        for group in range(0, HEADS // 2, GROUP):
            pairs = range(group, group + GROUP)
            cols = [slice(p * PAIR, (p + 1) * PAIR) for p in pairs]
            queries = [both_heads(q[at, c]) for c in cols]
            keys, values = [kx[over, c] for c in cols], [vx[over, c] for c in cols]
            scores = [mm_nt(q2, k) * HEAD_DIM ** (-0.5) + bias for q2, k in zip(queries, keys)]
            tops = [jnp.max(s, axis=-1, keepdims=True) for s in scores]
            exps = [jnp.exp(s - top) for s, top in zip(scores, tops)]
            sums = [jnp.sum(e, axis=-1, keepdims=True) for e in exps]
            weights = [(e * (1.0 / total)).astype(LOW) for e, total in zip(exps, sums)]
            parts = [merge_heads(mm(w, v)).astype(LOW) for w, v in zip(weights, values)]
            for p, c, w, part in zip(pairs, cols, weights, parts):
                probs[at, 2 * p * SPAN : (2 * p + 1) * SPAN] = w[:WINDOW]
                probs[at, (2 * p + 1) * SPAN : (2 * p + 2) * SPAN] = w[WINDOW:]
                o[at, c] = part

    def attend_some(begin, count):
        def step(b, _):
            attend(b)
            return 0

        lax.fori_loop(begin, begin + count, step, 0)

    def after_attention():
        copies.start(probs, p_o)
        turn(o, ho)
        share(2, ho, ho_o)

    def add_out():
        columns = plan.tensors[4][1]
        for side in range(2):

            def body(begin, size, side=side):
                cols = pl.ds(side * columns + begin, size)
                x1[:, cols] = x_in[:, cols].astype(F32) + mm(o[...], weight(4, side, pl.ds(begin, size)))

            each_tile(columns, 256, body)
        copies.start(x1, x1_o)

        def body(at):
            h2[at, :] = norm(x1[at, :], gains[1:2, :])

        each_rows(rows, 64, body)
        turn(h2, hm)
        share(3, hm, hm_o)

    wide = plan.tensors[5][1]

    def mlp(side, begin, size):
        cols = pl.ds(begin, size)
        a = mm(h2[...], weight(5, side, cols))
        b = mm(h2[...], weight(6, side, cols))
        sig = 1.0 / (1.0 + jnp.exp(-a))
        silu = a * sig
        to = pl.ds(side * wide + begin, size)
        act[:, to] = silu.astype(LOW)
        dact[:, to] = (b * sig * (1.0 + a * (1.0 - sig))).astype(LOW)
        hidden = (silu * b).astype(LOW)
        hid[:, to] = hidden
        hidt[to, :] = hidden.T

    def mlp_some(side, begin, size, count):
        def step(j, _):
            mlp(side, pl.multiple_of(begin + j * size, 128), size)
            return 0

        lax.fori_loop(0, count, step, 0)

    def after_mlp():
        copies.start(act, act_o)
        copies.start(dact, dact_o)
        share(4, hidt, hid_o)

    def add_down():
        columns = plan.tensors[7][1]
        for side in range(2):

            def body(begin, size, side=side):
                cols = pl.ds(side * columns + begin, size)
                part = mm(hid[...], weight(7, side, pl.ds(begin, size)))
                mixed[:, cols] = (x1[:, cols] + part).astype(LOW)

            each_tile(columns, 256, body)
        copies.start(mixed, mixed_o)

    whole = wide // 256
    rest = wide - whole * 256
    quarter = rows // WINDOW // 4
    passed = set()

    def need(t):
        for k in range(t + 1):
            if k not in passed:
                passed.add(k)
                for i in plan.of_tensor[k]:
                    gather.wait(i, 3)
                if k:
                    copies.start(bufs[k], w_out[k - 1])

    def mlp_part(side, part):
        need(6)
        count = (whole + 1) // 2
        if part == 0:
            mlp_some(side, 0, 256, count)
        else:
            mlp_some(side, count * 256, 256, whole - count)
            if rest:
                mlp(side, whole * 256, rest)
            if side == 1:
                after_mlp()

    def attend_part(k):
        if k == 0:
            rims()
        attend_some(k * quarter, quarter)
        if k == 3:
            after_attention()

    def with_weight(t, piece):
        need(t)
        piece()

    work = {
        "norm": lambda: with_weight(0, first_norm),
        "query": lambda: with_weight(1, do_query),
        "key": lambda: with_weight(2, do_key),
        "value": lambda: with_weight(3, do_value),
        "out": lambda: with_weight(4, add_out),
        "down": lambda: with_weight(7, add_down),
    }
    for k in range(4):
        work["attend", k] = functools.partial(attend_part, k)
        work["mlp", k] = functools.partial(mlp_part, k // 2, k % 2)
    for step in FORWARD_SCRIPT:
        if step in work:
            work[step]()
        elif step[0] == "start":
            gather.start(step[1], 0)
        else:
            i, phase = step
            gather.wait(i, phase)
            gather.start(i, phase + 1)
    for i in range(len(plan.items)):
        gather.finish(i)
    for k, ref in ((0, kx), (1, vx)):
        rim(k, ref).wait_send()
    for copy in sends:
        copy.wait()
    copies.wait_all()


def forward_all(plan, lens, tokens, cotangent, shards):
    n, k = len(plan.tensors), len(plan.items)
    rows, width = tokens.shape
    wide = 2 * plan.tensors[5][1]
    anywhere = pl.BlockSpec(memory_space=pl.ANY)
    inside = pl.BlockSpec(memory_space=pltpu.VMEM)
    shape = jax.ShapeDtypeStruct
    bufs = [(2, NZ, NY, NX) + t[:2] for t in plan.tensors]
    over = WINDOW + rows
    kept = [
        ((rows, width), LOW),
        ((rows, width), LOW),
        ((over, width), LOW),
        ((over, width), LOW),
        ((rows, HEADS * SPAN), LOW),
        ((rows, width), F32),
        ((width, 2 * rows), LOW),
        ((width, 2 * rows), LOW),
        ((width, 2 * rows), LOW),
        ((wide, 2 * rows), LOW),
        ((rows, wide), LOW),
        ((rows, wide), LOW),
        ((2 * rows, width // 2), LOW),
        ((8, width), F32),
    ]
    scratch = [
        ((8, width), F32),
        ((rows, width), LOW),
        ((rows, width), LOW),
        ((over, width), LOW),
        ((over, width), LOW),
        ((rows, HEADS * SPAN), LOW),
        ((rows, width), LOW),
        ((rows, width), F32),
        ((rows, width), LOW),
        ((rows, wide), LOW),
        ((rows, wide), LOW),
        ((rows, wide), LOW),
        ((width, rows), LOW),
        ((width, rows), LOW),
        ((width, rows), LOW),
        ((wide, rows), LOW),
        ((rows, width), LOW),
    ]
    dma = pltpu.SemaphoreType.DMA
    outs = pl.pallas_call(
        functools.partial(forward_kernel, plan),
        out_shape=[shape(b, LOW) for b in bufs[1:]] + [shape(*s) for s in kept],
        in_specs=[pl.BlockSpec(memory_space=pltpu.SMEM), inside, anywhere] + [anywhere] * (n - 3) + [inside] * 3,
        out_specs=[anywhere] * (n - 1 + len(kept)),
        scratch_shapes=[pltpu.VMEM(b, LOW) for b in bufs]
        + [pltpu.VMEM(t[:2], LOW) for t in plan.tensors[5:]]
        + [pltpu.VMEM(*s) for s in scratch]
        + [dma((k, 4, 3)), dma((k, 4, 3)), dma((n,)), dma((24,)), dma((2,)), dma((2,)), dma((5,)), dma((5,))],
        compiler_params=pltpu.CompilerParams(
            collective_id=0, has_side_effects=True, vmem_limit_bytes=62 * 2**20
        ),
        name="forward_all",
    )(lens, tokens, cotangent, *shards)
    return outs[: n - 1], outs[n - 1 :]


class Stream:
    def __init__(self, count, sems, fetch):
        self.count, self.sems, self.fetch = count, sems, fetch

    def copies(self, j, slot):
        return [
            pltpu.make_async_copy(src, dst, self.sems.at[slot, k])
            for k, (src, dst) in enumerate(self.fetch(j, slot))
        ]

    def prime(self):
        for copy in self.copies(0, 0):
            copy.start()

    def run(self, body, first=0, last=None):
        def step(j, _):
            slot = j % 2

            @pl.when(j + 1 < self.count)
            def _():
                for copy in self.copies(j + 1, 1 - slot):
                    copy.start()

            for copy in self.copies(j, slot):
                copy.wait()
            body(j, slot)
            return 0

        lax.fori_loop(first, self.count if last is None else last, step, 0)


def backward_kernel(plan, *refs):
    n = len(plan.tensors)
    ws, refs = refs[:7], refs[7:]
    (x_h, dy_h, q_h, k_h, v_h, p_h, x1_h, ha_h, ho_h, hm_h, hid_h, dact_h, act_h, dyh_h, gains), refs = refs[:15], refs[15:]
    (gtok_o,), outs, refs = refs[:1], refs[1 : 1 + n], refs[1 + n :]
    total, refs = refs[:n], refs[n:]
    k = len(plan.items)
    got, refs = [refs[3 * i : 3 * i + 3] for i in range(k)], refs[3 * k :]
    (da, db, kx, vx, dar, dbr, dxr_r, qr, kr, vr, dyh, turned, small, broad, dy, x1, dh, dxr, do), refs = refs[:19], refs[19:]
    (kc, vc, rim_k, rim_v, gain_sum, gain_other), refs = refs[:6], refs[6:]
    send, recv, load_sem, small_sem, broad_sem, turn_sem, half_send, half_recv, out_sem = refs
    wq, wk, wv, wo, wg, wu, wd = ws
    rows, width = dy.shape
    wide = wg.shape[2]
    columns = wq.shape[2]
    me = Place()
    me.greet()
    scatter = Scatter(plan, me, total, got, outs, send, recv)
    halves = []

    def to_partner(k, src, dst):
        copy = remote(src, dst, half_send.at[k], half_recv.at[k], me.to_core())
        copy.start()
        halves.append(copy)
        return copy

    loads = [0]

    def load(src, dst):
        copy = pltpu.make_async_copy(src, dst, load_sem.at[loads[0]])
        loads[0] += 1
        copy.start()
        return copy

    def own(size, side=0):
        return pl.ds(pl.multiple_of((me.s if side == 0 else 1 - me.s) * size, 128), size)

    tall = plan.tensors[0][0] * NY * NX
    hid_tiles = Stream(
        NZ, turn_sem, lambda j, slot: [(hid_h.at[pl.ds(pl.multiple_of(j * tall, 16), tall), :], turned.at[slot, pl.ds(0, tall), :])]
    )
    tile = 256

    def weight_tiles(w, k=0, slots=small):
        return lambda j, slot: (w.at[:, pl.ds(pl.multiple_of(j * tile, tile), tile), :], slots.at[slot, k])

    def stream_of(fetchers, count, sems):
        return Stream(count, sems, lambda j, slot: [f(j, slot) for f in fetchers])

    down_tiles = stream_of([weight_tiles(wd)], wd.shape[1] // tile, small_sem)
    mlp_tiles = stream_of([weight_tiles(wg, 0, broad), weight_tiles(wu, 1, broad)], width // tile, broad_sem)
    out_tiles = stream_of([weight_tiles(wo)], width // tile, small_sem)
    qkv_tiles = stream_of([weight_tiles(w, k) for k, w in enumerate((wq, wk, wv))], width // tile, small_sem)

    get_dyh = load(dyh_h, dyh)
    hid_tiles.prime()
    get_dy = load(dy_h, dy)
    down_tiles.prime()
    get_dact = load(dact_h, da)
    get_act = load(act_h, db)
    mlp_tiles.prime()
    get_x1 = load(x1_h, x1)
    get_k, get_v = load(k_h, kx), load(v_h, vx)

    def begin(t):
        for i in plan.of_tensor[t]:
            scatter.start(i, 0)

    def put(t, z, part):
        row_count, column_count = plan.tensors[t][:2]
        total[t][z] = part.reshape(NY, NX, row_count, column_count).astype(total[t].dtype)

    later = {}

    def grad_down():
        get_dyh.wait()
        hid_tiles.run(lambda z, slot: put(0, z, mm(turned[slot, :tall], dyh[...])))
        begin(0)
        later["hm"] = load(hm_h, turned.at[0])
        later["ho"] = load(ho_h, turned.at[1])

    def hidden_body(j, slot):
        part = mm_nt(dy[:, :columns], small[slot, 0, 0]) + mm_nt(dy[:, columns:], small[slot, 0, 1])
        at = pl.ds(pl.multiple_of(j * tile, tile), tile)
        da[:, at] = (part * da[:, at].astype(F32)).astype(LOW)
        db[:, at] = (part * db[:, at].astype(F32)).astype(LOW)

    def hidden(k):
        middle = down_tiles.count // 2
        if k == 0:
            for copy in (get_dy, get_dact, get_act):
                copy.wait()
            down_tiles.run(hidden_body, 0, middle)
            return
        down_tiles.run(hidden_body, middle)
        out_tiles.prime()
        later["db"] = to_partner(0, db.at[:, own(wide, 1)], dbr)
        later["da"] = to_partner(1, da.at[:, own(wide, 1)], dar)

    def weight_grad_to(t, slot, mine, theirs):
        row_count = plan.tensors[t][0] * NY * NX

        def step(z, _):
            at = pl.ds(pl.multiple_of(z * row_count, 16), row_count)
            put(t, z, mm(turned[slot, at, own(rows)], mine()) + mm(turned[slot, at, own(rows, 1)], theirs[...]))
            return 0

        lax.fori_loop(0, NZ, step, 0)
        begin(t)

    def grad_up():
        later["hm"].wait()
        later["db"].wait_recv()
        weight_grad_to(1, 0, lambda: db[:, own(wide)], dbr)

    def grad_gate():
        later["da"].wait_recv()
        weight_grad_to(2, 0, lambda: da[:, own(wide)], dar)
        later["ha"] = load(ha_h, turned.at[0])

    def dh2_body(j, slot):
        part = None
        for k, grad in ((0, da), (1, db)):
            for side in range(2):
                term = mm_nt(grad[:, side * wide : (side + 1) * wide], broad[slot, k, side])
                part = term if part is None else part + term
        dh[:, pl.ds(pl.multiple_of(j * tile, tile), tile)] = part

    def grad_norm2(k):
        middle = mlp_tiles.count // 2
        if k == 0:
            mlp_tiles.run(dh2_body, 0, middle)
            return
        mlp_tiles.run(dh2_body, middle)
        later["db"].wait_send()
        later["da"].wait_send()
        later["q"] = load(q_h, da.at[:, pl.ds(0, width)])
        later["p"] = load(p_h, db.at[:, pl.ds(0, HEADS * SPAN)])
        later["x"] = load(x_h, da.at[:, pl.ds(width, width)])

    def norm_grad(values, grad_norm, gain):
        inverse = lax.rsqrt(jnp.mean(values * values, axis=-1, keepdims=True) + EPS)
        scaled = grad_norm * gain
        mean_term = jnp.mean(values * scaled, axis=-1, keepdims=True)
        back = inverse * scaled - values * (inverse * inverse * inverse) * mean_term
        return back, jnp.sum(values * inverse * grad_norm, axis=0, keepdims=True)

    def norm2_body(at):
        back, gain_part = norm_grad(x1[at, :], dh[at, :], gains[1:2, :])
        gain_sum[1:2, :] += gain_part
        grad = dy[at, :].astype(F32) + back
        x1[at, :] = grad
        dxr[at, :] = grad.astype(LOW)

    def norm2():
        gain_sum[...] = jnp.zeros_like(gain_sum)
        get_x1.wait()
        each_rows(rows, 64, norm2_body)
        later["dxr"] = to_partner(2, dxr.at[:, own(columns, 1)], dxr_r)

    def out_body(j, slot):
        part = mm_nt(dxr[:, :columns], small[slot, 0, 0]) + mm_nt(dxr[:, columns:], small[slot, 0, 1])
        do[:, pl.ds(pl.multiple_of(j * tile, tile), tile)] = part.astype(LOW)

    def grad_heads():
        out_tiles.run(out_body)
        qkv_tiles.prime()

    def grad_out():
        later["ho"].wait()
        later["dxr"].wait_recv()
        weight_grad_to(3, 1, lambda: dxr[:, own(columns)], dxr_r)

    scale = HEAD_DIM ** (-0.5)

    def attend(b, _):
        at = pl.ds(pl.multiple_of(b * WINDOW, WINDOW), WINDOW)
        over = pl.ds(pl.multiple_of(b * WINDOW, WINDOW), SPAN)
        for group in range(0, HEADS // 2, GROUP):
            pairs = range(group, group + GROUP)
            cols = [slice(p * PAIR, (p + 1) * PAIR) for p in pairs]
            queries, grads = [both_heads(da[at, c]) for c in cols], [both_heads(do[at, c]) for c in cols]
            keys, values = [kx[over, c] for c in cols], [vx[over, c] for c in cols]
            lows = [
                jnp.concatenate([db[at, (2 * p + h) * SPAN : (2 * p + h + 1) * SPAN] for h in range(2)], axis=0)
                for p in pairs
            ]
            carry_k, carry_v = [kc[:, c] for c in cols], [vc[:, c] for c in cols]
            probs = [low.astype(F32) for low in lows]
            grad_probs = [mm_nt(g, v) for g, v in zip(grads, values)]
            grad_values = [mm_tn(low, g) for low, g in zip(lows, grads)]
            inners = [jnp.sum(p * g, axis=-1, keepdims=True) for p, g in zip(probs, grad_probs)]
            scores = [(p * (g - i)).astype(LOW) for p, g, i in zip(probs, grad_probs, inners)]
            grad_queries = [(merge_heads(mm(s, k)) * scale).astype(LOW) for s, k in zip(scores, keys)]
            grad_keys = [mm_tn(s, q2) * scale for s, q2 in zip(scores, queries)]
            new_k = [(old + g[:WINDOW]).astype(LOW) for old, g in zip(carry_k, grad_keys)]
            new_v = [(old + g[:WINDOW]).astype(LOW) for old, g in zip(carry_v, grad_values)]
            for c, gq, gk, gv, nk, nv in zip(cols, grad_queries, grad_keys, grad_values, new_k, new_v):
                da[at, c] = gq
                kx[at, c] = nk
                vx[at, c] = nv
                kc[:, c] = gk[WINDOW:]
                vc[:, c] = gv[WINDOW:]
        return 0

    def attend_part(k):
        quarter = rows // WINDOW // 4
        if k == 0:
            kc[...] = jnp.zeros_like(kc)
            vc[...] = jnp.zeros_like(vc)
            for copy in (later["q"], later["p"], get_k, get_v):
                copy.wait()
        lax.fori_loop(k * quarter, (k + 1) * quarter, attend, 0)
        if k == 0:
            later["rim"] = [
                to_partner(3, kx.at[pl.ds(0, WINDOW), :], rim_k),
                to_partner(4, vx.at[pl.ds(0, WINDOW), :], rim_v),
            ]
        if k == 3:
            for copy, ref, carry, rim in ((later["rim"][0], kx, kc, rim_k), (later["rim"][1], vx, vc, rim_v)):
                copy.wait_recv()
                ref[pl.ds(rows, WINDOW), :] = (carry[...] + rim[...].astype(F32)).astype(LOW)
            later["dq"] = to_partner(5, da.at[:, own(columns, 1)], qr)
            later["dk"] = to_partner(6, kx.at[own_rows, own(columns, 1)], kr)
            later["dv"] = to_partner(7, vx.at[own_rows, own(columns, 1)], vr)

    own_rows = pl.ds(WINDOW, rows)

    def grad_qkv(k):
        if k == 0:
            later["ha"].wait()
        later[("dq", "dk", "dv")[k]].wait_recv()
        mine = (lambda: da[:, own(columns)], lambda: kx[own_rows, own(columns)], lambda: vx[own_rows, own(columns)])[k]
        weight_grad_to(4 + k, 0, mine, (qr, kr, vr)[k])

    def dh1_body(j, slot):
        part = None
        for k, (grad, skip) in enumerate(((da, 0), (kx, WINDOW), (vx, WINDOW))):
            for side in range(2):
                left = grad[pl.ds(skip, rows), side * columns : (side + 1) * columns]
                term = mm_nt(left, small[slot, k, side])
                part = term if part is None else part + term
        dh[:, pl.ds(pl.multiple_of(j * tile, tile), tile)] = part

    def grad_norm1():
        qkv_tiles.run(dh1_body)

    def norm1_body(at):
        back, gain_part = norm_grad(da[at, pl.ds(width, width)].astype(F32), dh[at, :], gains[0:1, :])
        gain_sum[0:1, :] += gain_part
        x1[at, :] = x1[at, :] + back

    give = pltpu.make_async_copy(x1, gtok_o, out_sem)

    def norm1():
        later["x"].wait()
        each_rows(rows, 64, norm1_body)
        give.start()
        later["gain"] = to_partner(8, gain_sum, gain_other)

    def grad_gains():
        later["gain"].wait_recv()
        lanes = plan.tensors[7][1]
        for c in range(NZ * NY * NX):
            at = slice(c // 2 * lanes, (c // 2 + 1) * lanes)
            total[7][c // 4, c // 2 % 2, c % 2] = gain_sum[:, at] + gain_other[:, at]
        begin(7)

    work = {
        "down": grad_down,
        "up": grad_up,
        "gate": grad_gate,
        "norm2": norm2,
        "heads": grad_heads,
        "out": grad_out,
        "dh1": grad_norm1,
        "norm1": norm1,
        "gains": grad_gains,
    }
    for k in range(4):
        work["attend", k] = functools.partial(attend_part, k)
    for k in range(3):
        work["qkv", k] = functools.partial(grad_qkv, k)
    for k in range(2):
        work["hidden", k] = functools.partial(hidden, k)
        work["dh2", k] = functools.partial(grad_norm2, k)
    for step in BACKWARD_SCRIPT:
        if step in work:
            work[step]()
            continue
        i, phase = step
        scatter.wait(i, phase)
        scatter.add(i, phase)
        if phase < 2:
            scatter.start(i, phase + 1)
    for i in range(len(plan.items)):
        scatter.finish(i)
    for copy in halves[2:]:
        copy.wait_send()
    give.wait()


def backward_all(plan, ws, tokens, cotangent, acts):
    n, k = len(plan.tensors), len(plan.items)
    rows, width = tokens.shape
    columns, wide = ws[0].shape[2], ws[4].shape[2]
    anywhere = pl.BlockSpec(memory_space=pl.ANY)
    inside = pl.BlockSpec(memory_space=pltpu.VMEM)
    over = WINDOW + rows
    scratch = [
        ((rows, 2 * wide), LOW),
        ((rows, 2 * wide), LOW),
        ((over, width), LOW),
        ((over, width), LOW),
        ((rows, wide), LOW),
        ((rows, wide), LOW),
        ((rows, columns), LOW),
        ((rows, columns), LOW),
        ((rows, columns), LOW),
        ((rows, columns), LOW),
        ((2 * rows, columns), LOW),
        ((2, width, 2 * rows), LOW),
        ((2, 3, 2, 256, columns), LOW),
        ((2, 2, 2, 256, wide), LOW),
        ((rows, width), LOW),
        ((rows, width), F32),
        ((rows, width), F32),
        ((rows, width), LOW),
        ((rows, width), LOW),
        ((WINDOW, width), F32),
        ((WINDOW, width), F32),
        ((WINDOW, width), LOW),
        ((WINDOW, width), LOW),
        ((8, width), F32),
        ((8, width), F32),
    ]
    totals = [((NZ, NY, NX) + t[:2], t[2]) for t in plan.tensors]
    got = [shape for shapes in got_shapes(plan) for shape in shapes]
    dma = pltpu.SemaphoreType.DMA
    return pl.pallas_call(
        functools.partial(backward_kernel, plan),
        out_shape=[jax.ShapeDtypeStruct((rows, width), F32)]
        + [jax.ShapeDtypeStruct(t[:2], F32) for t in plan.tensors],
        in_specs=[anywhere] * (7 + 14) + [inside],
        out_specs=[anywhere] + [inside] * n,
        scratch_shapes=[pltpu.VMEM(*s) for s in totals + got + scratch]
        + [dma((k, 3, 3)), dma((k, 3, 3)), dma((16,)), dma((2, 3)), dma((2, 2)), dma((2, 1)), dma((9,)), dma((9,)), dma],
        compiler_params=pltpu.CompilerParams(
            collective_id=1, has_side_effects=True, vmem_limit_bytes=63 * 2**20
        ),
        name="backward_all",
    )(*ws, tokens, cotangent, *acts)


def finish_kernel(*refs):
    n = 10
    ins, outs, held, made = refs[:n], refs[n : 2 * n + 1], refs[2 * n + 1 : 3 * n + 1], refs[3 * n + 1 : 4 * n + 2]
    sem_in, sem_out = refs[4 * n + 2 :]
    gets = [pltpu.make_async_copy(src, dst, sem_in.at[k]) for k, (src, dst) in enumerate(zip(ins, held))]
    for copy in gets:
        copy.start()
    puts = []

    def put(k, src):
        copy = pltpu.make_async_copy(src, outs[k], sem_out.at[k])
        copy.start()
        puts.append(copy)

    down, up, gate, out, query, key, value, gain = held[2:]
    for copy in gets[2:]:
        copy.wait()
    for k, src in ((2, query), (3, key), (4, value), (5, out)):
        put(k, src)
    rows, part, tile = query.shape[0], outs[8].shape[0], down.shape[0]
    made[8][...] = down[...][:part]
    put(8, made[8])
    for k, src in ((6, gate), (7, up)):
        values = src[...]
        made[k][...] = jnp.concatenate(
            [values[:, j * tile : j * tile + part] for j in range(values.shape[1] // tile)], axis=1
        )
        put(k, made[k])
    both = gain[...]
    own = jnp.where(lax.axis_index("dp") % 2 == 0, both[:, :rows], both[:, rows:])
    made[9][...] = own[0:1]
    made[10][...] = own[1:2]
    put(9, made[9])
    put(10, made[10])
    for k in range(2):
        gets[k].wait()
        put(k, held[k])
    for copy in puts:
        copy.wait()


def finish_all(mixed, tokens, sums, w_query, w_gate, w_down):
    anywhere = pl.BlockSpec(memory_space=pl.ANY)
    shape = jax.ShapeDtypeStruct
    outs = [shape(mixed.shape, mixed.dtype), shape(tokens.shape, F32)]
    outs += [shape(w_query.shape, F32)] * 4 + [shape(w_gate.shape, F32)] * 2 + [shape(w_down.shape, F32)]
    outs += [shape((1, w_query.shape[0]), F32)] * 2
    ins = [mixed, tokens, *sums]
    return pl.pallas_call(
        finish_kernel,
        out_shape=outs,
        in_specs=[anywhere] * len(ins),
        out_specs=[anywhere] * len(outs),
        scratch_shapes=[pltpu.VMEM(a.shape, a.dtype) for a in ins + outs]
        + [pltpu.SemaphoreType.DMA((len(ins),)), pltpu.SemaphoreType.DMA((len(outs),))],
        compiler_params=pltpu.CompilerParams(vmem_limit_bytes=62 * 2**20),
        name="finish_all",
    )(*ins)


def kinds(w_query, w_gate, w_down):
    rows, columns = w_query.shape
    part = w_down.shape[0]
    tile = -(-part // 16) * 16
    wide = w_gate.shape[1] // part * tile
    half, part16 = rows // 2, rows // 4
    long, short = -(-tile // 64) * 16, tile - 3 * (-(-tile // 64) * 16)

    def cuts(kinds, counts):
        return tuple(zip(kinds, counts, strict=True))

    return {
        "square": (rows, columns, LOW, cuts(("zfx", "zfy"), (half, half))),
        "broad": (rows, wide, LOW, cuts(("zfx", "zfy", "zmx", "zmy"), (part16,) * 4)),
        "broad_f": (rows, wide, LOW, cuts(("zfx", "zfy", "zfx", "zfy"), (part16,) * 4)),
        "tall": (tile, columns, LOW, cuts(("zfx", "zfy", "zmx", "zmy"), (long, long, long, short))),
        "gain": (16, 2 * rows, LOW, cuts(("zfx",), (16,))),
        "gain_grad": (8, 2 * rows, F32, cuts(("zfx",), (8,))),
    }


def gather_plan(w_query, w_key, w_value, w_out, w_gate, w_up, w_down, gain_attn, gain_mlp):
    kind = kinds(w_query, w_gate, w_down)
    names = ("gain", "square", "square", "square", "square", "broad", "broad", "tall")
    plan = Plan([kind[name] for name in names])
    rows = w_query.shape[0]
    both = jnp.stack([gain_attn, gain_mlp])
    left = jnp.pad(both, ((0, 14), (0, rows)))
    right = jnp.pad(both, ((0, 14), (rows, 0)))
    pair = jnp.where(lax.axis_index("dp") % 2 == 0, left, right)
    shards = [
        pair,
        w_query,
        w_key,
        w_value,
        w_out,
        w_gate,
        w_up,
        w_down,
    ]
    return plan, shards


def swift_block(
    tokens,
    seq_lengths,
    w_query,
    w_key,
    w_value,
    w_out,
    w_gate,
    w_up,
    w_down,
    gain_attn,
    gain_mlp,
    cotangent,
):
    plan, shards = gather_plan(w_query, w_key, w_value, w_out, w_gate, w_up, w_down, gain_attn, gain_mlp)
    ws, acts = forward_all(plan, seq_lengths, tokens, cotangent, shards)
    ws = [w.reshape(2, -1, w.shape[-1]) for w in ws]
    kind = kinds(w_query, w_gate, w_down)
    names = ("tall", "broad_f", "broad", "square", "square", "square", "square", "gain_grad")
    back = Plan([kind[name] for name in names])
    grad_tokens, *sums = backward_all(back, ws, tokens, cotangent, acts[1:])
    outs = finish_all(acts[0], grad_tokens, sums, w_query, w_gate, w_down)
    return (*outs[:9], outs[9].reshape(-1), outs[10].reshape(-1))


def solution(mesh):
    fast = (mesh.shape["dp"], mesh.shape["seq"]) == (NZ * NY * NX, 2)
    shards = swift_block if fast else plain_block
    in_specs = (
        P(("dp", "seq"), None),
        P("dp", None),
        P("dp", "seq"),
        P("dp", "seq"),
        P("dp", "seq"),
        P("dp", "seq"),
        P("dp", "seq"),
        P("dp", "seq"),
        P("dp", "seq"),
        P("dp"),
        P("dp"),
        P(("dp", "seq"), None),
    )
    out_specs = (
        P(("dp", "seq"), None),
        P(("dp", "seq"), None),
        P("dp", "seq"),
        P("dp", "seq"),
        P("dp", "seq"),
        P("dp", "seq"),
        P("dp", "seq"),
        P("dp", "seq"),
        P("dp", "seq"),
        P("dp"),
        P("dp"),
    )
    return jax.shard_map(shards, mesh=mesh, in_specs=in_specs, out_specs=out_specs, check_vma=False)
```

```python
import functools

import jax
import jax.numpy as jnp
from jax import lax
from jax.experimental import pallas as pl
from jax.experimental.pallas import tpu as pltpu
from jax.sharding import PartitionSpec as P

HEADS = 16
HEAD_DIM = 64
WINDOW = 64


eps_norm = 1e-05


def from_behind(block, axis, distance):
    devices = range(lax.axis_size(axis))
    route = [(i - distance, i) for i in devices if i - distance in devices]
    return lax.ppermute(block, axis, route)


def inverse_rms(values):
    return lax.rsqrt(jnp.mean(values * values, axis=-1, keepdims=True) + eps_norm)


def doc_numbers(lengths_row, positions):
    first_end = lengths_row[0]
    second_end = lengths_row[0] + lengths_row[1]
    return (positions >= first_end).astype(jnp.int32) + (positions >= second_end).astype(jnp.int32)


def window_mask(query_pos, query_doc, key_pos, key_doc, window):
    after = key_pos[None, :] >= query_pos[:, None] - window
    before = key_pos[None, :] <= query_pos[:, None]
    inside = (key_pos[None, :] >= 0) & (key_doc[None, :] == query_doc[:, None])
    return after & before & inside


def norm_back(values, inverse, gain, grad_norm):
    scaled = grad_norm * gain
    mean_term = jnp.mean(values * scaled, axis=-1, keepdims=True)
    grad_values = inverse * scaled - values * (inverse * inverse * inverse) * mean_term
    grad_gain = jnp.sum(values * inverse * grad_norm, axis=0)
    return (grad_values, grad_gain)


def project(left, right):
    return jnp.dot(left, right, preferred_element_type=jnp.float32)


def project_back(grad_rows, weight):
    return jnp.einsum("tf,df->td", grad_rows, weight, preferred_element_type=jnp.float32)


def weight_grad(inputs, grad_rows):
    return jnp.einsum("td,tf->df", inputs, grad_rows, preferred_element_type=jnp.float32)


def plain_block(
    tokens,
    seq_lengths,
    w_query,
    w_key,
    w_value,
    w_out,
    w_gate,
    w_up,
    w_down,
    gain_attn,
    gain_mlp,
    cotangent,
):
    row_count = tokens.shape[0]
    block_rows = min(512, row_count)
    head_group = HEADS // 2
    score_scale = HEAD_DIM ** (-0.5)
    row_parts = (
        lax.all_gather(w_query, "dp", axis=0, tiled=True),
        lax.all_gather(w_key, "dp", axis=0, tiled=True),
        lax.all_gather(w_value, "dp", axis=0, tiled=True),
        lax.all_gather(w_out, "dp", axis=0, tiled=True),
        lax.all_gather(w_gate, "dp", axis=0, tiled=True),
        lax.all_gather(w_up, "dp", axis=0, tiled=True),
        lax.all_gather(w_down, "dp", axis=0, tiled=True),
        lax.all_gather(gain_attn, "dp", axis=0, tiled=True),
        lax.all_gather(gain_mlp, "dp", axis=0, tiled=True),
    )
    full_mats = (
        lax.all_gather(row_parts[0], "seq", axis=1, tiled=True),
        lax.all_gather(row_parts[1], "seq", axis=1, tiled=True),
        lax.all_gather(row_parts[2], "seq", axis=1, tiled=True),
        lax.all_gather(row_parts[3], "seq", axis=1, tiled=True),
        lax.all_gather(row_parts[4], "seq", axis=1, tiled=True),
        lax.all_gather(row_parts[5], "seq", axis=1, tiled=True),
        lax.all_gather(row_parts[6], "seq", axis=1, tiled=True),
    )
    query_w, key_w, value_w, out_w, gate_w, up_w, down_full = full_mats
    gain_one = row_parts[7].astype(jnp.float32)
    gain_two = row_parts[8].astype(jnp.float32)
    inputs = tokens.astype(jnp.float32)
    inv_one = inverse_rms(inputs)
    normed_one = (inputs * inv_one * gain_one).astype(jnp.bfloat16)
    query_low = project(normed_one, query_w).astype(jnp.bfloat16)
    key_low = project(normed_one, key_w).astype(jnp.bfloat16)
    value_low = project(normed_one, value_w).astype(jnp.bfloat16)
    rim_pairs = from_behind(
        (key_low[row_count - WINDOW :], value_low[row_count - WINDOW :]), "seq", 1
    )
    keys_ext = jnp.concatenate([rim_pairs[0], key_low], axis=0).reshape(
        row_count + WINDOW, HEADS, HEAD_DIM
    )
    values_ext = jnp.concatenate([rim_pairs[1], value_low], axis=0).reshape(
        row_count + WINDOW, HEADS, HEAD_DIM
    )
    query_heads = query_low.reshape(row_count, HEADS, HEAD_DIM)
    span_start = lax.axis_index("seq") * row_count
    query_pos = span_start + jnp.arange(row_count, dtype=jnp.int32)
    key_pos = span_start - WINDOW + jnp.arange(row_count + WINDOW, dtype=jnp.int32)
    query_doc = doc_numbers(seq_lengths[0], query_pos)
    key_doc = doc_numbers(seq_lengths[0], key_pos)

    def tile_scores(row_start, head_start):
        visible = window_mask(query_pos, query_doc, key_pos, key_doc, WINDOW)
        scores_raw = (
            jnp.einsum(
                "qhd,khd->hqk",
                query_heads[
                    row_start : row_start + block_rows, head_start : head_start + head_group
                ],
                keys_ext[
                    row_start : row_start + block_rows + WINDOW,
                    head_start : head_start + head_group,
                ],
                preferred_element_type=jnp.float32,
            )
            * score_scale
        )
        return jnp.where(visible[None], scores_raw, -1e30)

    log_totals = {}
    row_start = 0
    head_parts = []
    for head_start in range(0, HEADS, head_group):
        masked_scores = tile_scores(row_start, head_start)
        top_score = jnp.max(masked_scores, axis=-1, keepdims=True)
        log_total = top_score + jnp.log(
            jnp.sum(jnp.exp(masked_scores - top_score), axis=-1, keepdims=True)
        )
        prob_low = jnp.exp(masked_scores - log_total).astype(jnp.bfloat16)
        value_tile = values_ext[
            row_start : row_start + block_rows + WINDOW, head_start : head_start + head_group
        ]
        head_parts.append(
            jnp.einsum("hqk,khd->qhd", prob_low, value_tile, preferred_element_type=jnp.float32)
        )
        log_totals[row_start, head_start] = log_total
    attn_blocks = jnp.concatenate(head_parts, axis=1)
    attended = attn_blocks.reshape(row_count, HEADS * HEAD_DIM).astype(jnp.bfloat16)
    middle = inputs + project(attended, out_w)
    inv_two = inverse_rms(middle)
    normed_two = (middle * inv_two * gain_two).astype(jnp.bfloat16)
    gate_pre = project(normed_two, gate_w)
    up_pre = project(normed_two, up_w)
    gate_act = jax.nn.silu(gate_pre)
    hidden = (gate_act * up_pre).astype(jnp.bfloat16)
    block_out = (middle + project(hidden, down_full)).astype(jnp.bfloat16)
    rows_again = (
        lax.all_gather(w_query, "dp", axis=0, tiled=True),
        lax.all_gather(w_key, "dp", axis=0, tiled=True),
        lax.all_gather(w_value, "dp", axis=0, tiled=True),
        lax.all_gather(w_out, "dp", axis=0, tiled=True),
        lax.all_gather(w_gate, "dp", axis=0, tiled=True),
        lax.all_gather(w_up, "dp", axis=0, tiled=True),
        lax.all_gather(w_down, "dp", axis=0, tiled=True),
        lax.all_gather(gain_attn, "dp", axis=0, tiled=True),
        lax.all_gather(gain_mlp, "dp", axis=0, tiled=True),
    )
    mats_again = (
        lax.all_gather(rows_again[0], "seq", axis=1, tiled=True),
        lax.all_gather(rows_again[1], "seq", axis=1, tiled=True),
        lax.all_gather(rows_again[2], "seq", axis=1, tiled=True),
        lax.all_gather(rows_again[3], "seq", axis=1, tiled=True),
        lax.all_gather(rows_again[4], "seq", axis=1, tiled=True),
        lax.all_gather(rows_again[5], "seq", axis=1, tiled=True),
        lax.all_gather(rows_again[6], "seq", axis=1, tiled=True),
    )
    back_query, back_key, back_value, back_out, back_gate, back_up, back_down = mats_again
    back_gain_one = rows_again[7].astype(jnp.float32)
    back_gain_two = rows_again[8].astype(jnp.float32)
    grad_final = cotangent.astype(jnp.float32)
    d_down = weight_grad(hidden, cotangent)
    grad_hidden = project_back(cotangent, back_down)
    sigmoid_gate = jax.nn.sigmoid(gate_pre)
    grad_gate_low = (
        grad_hidden * up_pre * sigmoid_gate * (1.0 + gate_pre * (1.0 - sigmoid_gate))
    ).astype(jnp.bfloat16)
    grad_up_low = (grad_hidden * gate_act).astype(jnp.bfloat16)
    d_gate = weight_grad(normed_two, grad_gate_low)
    d_up = weight_grad(normed_two, grad_up_low)
    grad_normed_two = project_back(grad_gate_low, back_gate) + project_back(grad_up_low, back_up)
    grad_mid_norm, d_gain_two = norm_back(middle, inv_two, back_gain_two, grad_normed_two)
    grad_middle = grad_final + grad_mid_norm
    grad_proj = grad_middle.astype(jnp.bfloat16)
    d_out = weight_grad(attended, grad_proj)
    grad_attended = (
        project_back(grad_proj, back_out).astype(jnp.bfloat16).reshape(row_count, HEADS, HEAD_DIM)
    )
    grad_keys_ext = jnp.zeros((row_count + WINDOW, HEADS, HEAD_DIM), jnp.float32)
    grad_values_ext = jnp.zeros((row_count + WINDOW, HEADS, HEAD_DIM), jnp.float32)
    row_start = 0
    head_parts = []
    for head_start in range(0, HEADS, head_group):
        head_end = head_start + head_group
        masked_scores = tile_scores(row_start, head_start)
        prob_full = jnp.exp(masked_scores - log_totals[row_start, head_start])
        grad_tile = grad_attended[row_start : row_start + block_rows, head_start:head_end]
        key_tile = keys_ext[row_start : row_start + block_rows + WINDOW, head_start:head_end]
        value_tile = values_ext[row_start : row_start + block_rows + WINDOW, head_start:head_end]
        query_tile = query_heads[row_start : row_start + block_rows, head_start:head_end]
        grad_prob = jnp.einsum(
            "qhd,khd->hqk", grad_tile, value_tile, preferred_element_type=jnp.float32
        )
        inner = jnp.sum(prob_full * grad_prob, axis=-1, keepdims=True)
        grad_score = (prob_full * (grad_prob - inner)).astype(jnp.bfloat16)
        head_parts.append(
            jnp.einsum("hqk,khd->qhd", grad_score, key_tile, preferred_element_type=jnp.float32)
            * score_scale
        )
        key_term = (
            jnp.einsum("hqk,qhd->khd", grad_score, query_tile, preferred_element_type=jnp.float32)
            * score_scale
        )
        value_term = jnp.einsum(
            "hqk,qhd->khd",
            prob_full.astype(jnp.bfloat16),
            grad_tile,
            preferred_element_type=jnp.float32,
        )
        grad_keys_ext = grad_keys_ext.at[
            row_start : row_start + block_rows + WINDOW, head_start:head_end
        ].add(key_term)
        grad_values_ext = grad_values_ext.at[
            row_start : row_start + block_rows + WINDOW, head_start:head_end
        ].add(value_term)
    grad_query_blocks = jnp.concatenate(head_parts, axis=1)
    rim_back = (
        from_behind(
            grad_keys_ext[:WINDOW].reshape(WINDOW, HEADS * HEAD_DIM).astype(jnp.bfloat16), "seq", -1
        ).astype(jnp.float32),
        from_behind(
            grad_values_ext[:WINDOW].reshape(WINDOW, HEADS * HEAD_DIM).astype(jnp.bfloat16),
            "seq",
            -1,
        ).astype(jnp.float32),
    )
    grad_keys = (
        grad_keys_ext[WINDOW:]
        .reshape(row_count, HEADS * HEAD_DIM)
        .at[row_count - WINDOW :]
        .add(rim_back[0])
    )
    grad_values = (
        grad_values_ext[WINDOW:]
        .reshape(row_count, HEADS * HEAD_DIM)
        .at[row_count - WINDOW :]
        .add(rim_back[1])
    )
    grad_query_low = grad_query_blocks.reshape(row_count, HEADS * HEAD_DIM).astype(jnp.bfloat16)
    grad_key_low = grad_keys.astype(jnp.bfloat16)
    grad_value_low = grad_values.astype(jnp.bfloat16)
    d_query = weight_grad(normed_one, grad_query_low)
    d_key = weight_grad(normed_one, grad_key_low)
    d_value = weight_grad(normed_one, grad_value_low)
    grad_normed_one = (
        project_back(grad_query_low, back_query)
        + project_back(grad_key_low, back_key)
        + project_back(grad_value_low, back_value)
    )
    grad_in_norm, d_gain_one = norm_back(inputs, inv_one, back_gain_one, grad_normed_one)
    grad_inputs = grad_middle + grad_in_norm
    row_sums = (
        lax.psum_scatter(
            d_query.astype(jnp.bfloat16), "dp", scatter_dimension=0, tiled=True
        ).astype(jnp.float32),
        lax.psum_scatter(d_key.astype(jnp.bfloat16), "dp", scatter_dimension=0, tiled=True).astype(
            jnp.float32
        ),
        lax.psum_scatter(
            d_value.astype(jnp.bfloat16), "dp", scatter_dimension=0, tiled=True
        ).astype(jnp.float32),
        lax.psum_scatter(d_out.astype(jnp.bfloat16), "dp", scatter_dimension=0, tiled=True).astype(
            jnp.float32
        ),
        lax.psum_scatter(d_gate.astype(jnp.bfloat16), "dp", scatter_dimension=0, tiled=True).astype(
            jnp.float32
        ),
        lax.psum_scatter(d_up.astype(jnp.bfloat16), "dp", scatter_dimension=0, tiled=True).astype(
            jnp.float32
        ),
        lax.psum_scatter(d_down.astype(jnp.bfloat16), "dp", scatter_dimension=0, tiled=True).astype(
            jnp.float32
        ),
        lax.psum_scatter(
            d_gain_one.astype(jnp.bfloat16), "dp", scatter_dimension=0, tiled=True
        ).astype(jnp.float32),
        lax.psum_scatter(
            d_gain_two.astype(jnp.bfloat16), "dp", scatter_dimension=0, tiled=True
        ).astype(jnp.float32),
    )
    owned_mats = (
        lax.psum_scatter(
            row_sums[0].astype(jnp.bfloat16), "seq", scatter_dimension=1, tiled=True
        ).astype(jnp.float32),
        lax.psum_scatter(
            row_sums[1].astype(jnp.bfloat16), "seq", scatter_dimension=1, tiled=True
        ).astype(jnp.float32),
        lax.psum_scatter(
            row_sums[2].astype(jnp.bfloat16), "seq", scatter_dimension=1, tiled=True
        ).astype(jnp.float32),
        lax.psum_scatter(
            row_sums[3].astype(jnp.bfloat16), "seq", scatter_dimension=1, tiled=True
        ).astype(jnp.float32),
        lax.psum_scatter(
            row_sums[4].astype(jnp.bfloat16), "seq", scatter_dimension=1, tiled=True
        ).astype(jnp.float32),
        lax.psum_scatter(
            row_sums[5].astype(jnp.bfloat16), "seq", scatter_dimension=1, tiled=True
        ).astype(jnp.float32),
        lax.psum_scatter(
            row_sums[6].astype(jnp.bfloat16), "seq", scatter_dimension=1, tiled=True
        ).astype(jnp.float32),
    )
    owned_gains = lax.psum((row_sums[7], row_sums[8]), "seq")
    return (
        block_out,
        grad_inputs,
        owned_mats[0],
        owned_mats[1],
        owned_mats[2],
        owned_mats[3],
        owned_mats[4],
        owned_mats[5],
        owned_mats[6],
        owned_gains[0],
        owned_gains[1],
    )


SCRIPT = (
    ("start", 16), ("start", 19), ("start", 11), ("start", 0), ("start", 2), ("start", 12), ("start", 15),
    ("start", 3), (0, 0, 0), ("start", 20), ("start", 13), (0, 3, 0), ("start", 4), (0, 2, 0), (0, 13, 0),
    ("start", 1), ("start", 7), (0, 2, 1), (0, 3, 1), (0, 4, 0), ("start", 10), (0, 1, 0), ("start", 14),
    ("start", 5), (0, 13, 1), (0, 0, 1), (0, 4, 1), (0, 7, 0), (0, 2, 2), (0, 10, 0), ("start", 6), (0, 5, 0),
    ("start", 17), (0, 14, 0), (0, 10, 1), ("start", 9), (0, 4, 2), (0, 1, 1), (0, 15, 0), (0, 14, 1),
    (0, 5, 1), (0, 6, 0), (0, 9, 0), (0, 12, 0), (0, 15, 1), (0, 6, 1), ("start", 8), (0, 0, 2), (0, 7, 1),
    (0, 1, 2), (0, 3, 2), "norm", (0, 11, 0), (0, 12, 1), (0, 8, 0), (0, 13, 2), (0, 5, 2), "key", (0, 6, 2),
    "query", (0, 17, 0), (0, 16, 0), (0, 11, 1), "value", (0, 8, 1), ("see", 0), (0, 7, 2), (0, 12, 2),
    (0, 14, 2), (0, 9, 1), ("start", 18), (0, 16, 1), ("see", 1), (0, 8, 2), (0, 11, 2), (0, 20, 0),
    ("see", 2), (0, 15, 2), (0, 18, 0), ("see", 3), (0, 19, 0), (0, 10, 2), (0, 17, 1), (0, 16, 2), (0, 9, 2),
    "project", ("mlp", 0), (0, 18, 1), ("mlp", 1), ("mlp", 2), ("mlp", 3), (0, 19, 1), (0, 20, 1), (0, 17, 2),
    ("mlp", 4), ("mlp", 5), "down", (0, 19, 2), (0, 20, 2), (0, 18, 2), "mix", ("hidden", 0), (1, 1, 0),
    ("hidden", 1), (1, 2, 0), (1, 3, 0), "up", ("dh2", 0), "gate", (1, 2, 1), (1, 2, 2), (1, 1, 1),
    ("dh2", 1), (1, 3, 1), "norm2", "heads", ("attend", 0), (1, 5, 0), ("attend", 1), (1, 4, 0),
    ("attend", 2), ("attend", 3), (1, 8, 0), (1, 7, 0), (1, 4, 1), (1, 9, 0), (1, 11, 0), (1, 5, 1),
    (1, 6, 0), "out", (1, 8, 1), (1, 6, 1), (1, 1, 2), ("qkv", 0), (1, 7, 1), "dh1", (1, 11, 1), (1, 9, 1),
    (1, 10, 0), "norm1", (1, 15, 0), (1, 13, 0), (1, 12, 0), (1, 10, 1), (1, 0, 0), (1, 14, 0), ("qkv", 1),
    "gains", (1, 12, 1), (1, 13, 1), (1, 15, 1), (1, 14, 1), ("qkv", 2), (1, 9, 2), (1, 16, 0), (1, 20, 0),
    (1, 5, 2), (1, 0, 1), (1, 17, 0), (1, 20, 1), (1, 16, 1), (1, 18, 0), (1, 6, 2), (1, 4, 2), (1, 15, 2),
    (1, 19, 0), (1, 17, 1), (1, 13, 2), (1, 8, 2), (1, 18, 1), (1, 16, 2), (1, 19, 1), (1, 7, 2), (1, 0, 2),
    (1, 3, 2), (1, 14, 2), (1, 20, 2), (1, 10, 2), (1, 11, 2), (1, 12, 2), (1, 17, 2), (1, 18, 2), (1, 19, 2),
)


MESH = pl.DeviceIdType.MESH
NZ, NY, NX = 4, 2, 2
SEQUENCE = {"zfx": "zxy", "zfy": "zyx", "zmx": "xzy", "zmy": "yzx"}
ALL_Z, ALL_Y, ALL_X = pl.ds(0, NZ), pl.ds(0, NY), pl.ds(0, NX)


class Plan:
    def __init__(self, tensors):
        self.tensors = tensors
        self.items, self.of_tensor = [], []
        for t, (_, _, _, cuts) in enumerate(tensors):
            begin, mine = 0, []
            for kind, count in cuts:
                mine.append(len(self.items))
                self.items.append((t, SEQUENCE[kind], begin, count))
                begin += count
            self.of_tensor.append(mine)


class Place:
    def __init__(self):
        self.c, self.s = lax.axis_index("dp"), lax.axis_index("seq")
        self.z, self.y, self.x = self.c // 4, (self.c // 2) % 2, self.c % 2

    def at(self, z, y, x):
        return (z * 4 + y * 2 + x, self.s)

    def to_x(self):
        return self.at(self.z, self.y, 1 - self.x)

    def to_y(self):
        return self.at(self.z, 1 - self.y, self.x)

    def to_z(self, step):
        return self.at((self.z + step) % NZ, self.y, self.x)

    def to_core(self):
        return (self.c, 1 - self.s)

    def greet(self):
        barrier = pltpu.get_barrier_semaphore()
        peers = [self.to_x(), self.to_y(), self.to_core()] + [self.to_z(k) for k in (1, 2, 3)]
        for peer in peers:
            pl.semaphore_signal(barrier, inc=1, device_id=peer, device_id_type=MESH)
        pl.semaphore_wait(barrier, len(peers))


def remote(src, dst, send, recv, device):
    return pltpu.make_async_remote_copy(
        src_ref=src, dst_ref=dst, send_sem=send, recv_sem=recv, device_id=device, device_id_type=MESH
    )


def slots(seq, count):
    firsts, used = [], 0
    for phase in range(count):
        firsts.append(used)
        used += 3 if phase < 3 and seq[phase] == "z" else 1
    return firsts


class Gather:
    def __init__(self, plan, place, shards, bufs, send, recv, local):
        self.plan, self.me, self.shards, self.bufs = plan, place, shards, bufs
        self.send, self.recv, self.local = send, recv, local

    def own_copy(self, t):
        me = self.me
        return pltpu.make_async_copy(
            self.shards[t], self.bufs[t].at[me.s, me.z, me.y, me.x], self.local.at[t]
        )

    def moves(self, i, phase):
        t, seq, begin, count = self.plan.items[i]
        me, buf = self.me, self.bufs[t]
        rows = pl.ds(begin, count)

        def view(z, y, x, half=me.s):
            return buf.at[half, z, y, x, rows, :]

        if phase == 3:
            whole = view(ALL_Z, ALL_Y, ALL_X)
            return [(whole, whole, me.to_core(), view(ALL_Z, ALL_Y, ALL_X, 1 - me.s), 0)]
        done, axis = seq[:phase], seq[phase]
        z = ALL_Z if "z" in done else me.z
        y = ALL_Y if "y" in done else me.y
        x = ALL_X if "x" in done else me.x
        there = view(z, y, x)
        here = self.shards[t].at[rows, :] if phase == 0 else there
        if axis == "x":
            return [(here, there, me.to_x(), view(z, y, 1 - me.x), 0)]
        if axis == "y":
            return [(here, there, me.to_y(), view(z, 1 - me.y, x), 0)]
        return [
            (here, there, me.to_z(k), view((me.z + NZ - k) % NZ, y, x), k - 1) for k in (1, 2, 3)
        ]

    def copy(self, i, phase, src, dst, device, k):
        at = 6 * i + slots(self.plan.items[i][1], 4)[phase] + k
        return remote(src, dst, self.send.at[at], self.recv.at[at], device)

    def start(self, i, phase):
        for here, there, device, _, k in self.moves(i, phase):
            self.copy(i, phase, here, there, device, k).start()

    def wait(self, i, phase):
        for _, _, device, arrived, k in self.moves(i, phase):
            self.copy(i, phase, arrived, arrived, device, k).wait_recv()

    def finish(self, i):
        for phase in range(4):
            for here, there, device, _, k in self.moves(i, phase):
                self.copy(i, phase, here, there, device, k).wait_send()


def got_shapes(plan):
    shapes = []
    for t, seq, _, count in plan.items:
        _, columns, dtype, _ = plan.tensors[t]
        second, third = ((1, NZ), (3,)) if seq[0] == "z" else ((3, 2), (1,))
        shapes.append([(d + (count, columns), dtype) for d in ((NZ, 2), second, third)])
    return shapes


class Scatter:
    def __init__(self, plan, place, total, got, out, send, recv):
        self.plan, self.me, self.total, self.got, self.out = plan, place, total, got, out
        self.send, self.recv = send, recv

    def moves(self, i, phase):
        t, seq, begin, count = self.plan.items[i]
        me, total, got = self.me, self.total[t], self.got[i][phase]
        rows = pl.ds(begin, count)
        axis, done = seq[2 - phase], seq[3 - phase :]
        z = me.z if "z" in done else ALL_Z
        y = me.y if "y" in done else ALL_Y
        x = me.x if "x" in done else ALL_X
        if phase == 0:
            lands = [got]
        else:
            lands = [got.at[k] for k in range(got.shape[0])]
        if axis == "x":
            return [(total.at[z, y, 1 - me.x, rows, :], lands[0], me.to_x(), 0)]
        if axis == "y":
            return [(total.at[z, 1 - me.y, x, rows, :], lands[0], me.to_y(), 0)]
        return [
            (total.at[(me.z + k) % NZ, y, x, rows, :], lands[k - 1], me.to_z(k), k - 1)
            for k in (1, 2, 3)
        ]

    def copy(self, i, phase, src, dst, device, k):
        at = 5 * i + slots(self.plan.items[i][1][::-1], 3)[phase] + k
        return remote(src, dst, self.send.at[at], self.recv.at[at], device)

    def start(self, i, phase):
        for here, there, device, k in self.moves(i, phase):
            self.copy(i, phase, here, there, device, k).start()

    def wait(self, i, phase):
        for here, there, device, k in self.moves(i, phase):
            self.copy(i, phase, there, there, device, k).wait_recv()

    def add(self, i, phase):
        t, seq, begin, count = self.plan.items[i]
        me, total, got = self.me, self.total[t], self.got[i][phase]
        rows = pl.ds(begin, count)
        if phase == 0:
            for z in range(NZ):
                for o in range(2):
                    at = (z, me.y, o) if seq[2] == "y" else (z, o, me.x)
                    total[at + (rows,)] += got[z, o]
        elif phase == 1 and seq[1] != "z":
            for z in range(NZ):
                total[z, me.y, me.x, rows] += got[0, z]
        elif phase == 1:
            for o in range(2):
                at = (me.z, me.y, o) if seq[2] == "y" else (me.z, o, me.x)
                part = total[at + (rows,)].astype(jnp.float32)
                for k in range(3):
                    part += got[k, o].astype(jnp.float32)
                total[at + (rows,)] = part.astype(total.dtype)
        else:
            part = total[me.z, me.y, me.x, rows].astype(jnp.float32)
            for k in range(got.shape[0]):
                part += got[k].astype(jnp.float32)
            self.out[t][rows] = part

    def finish(self, i):
        for phase in range(3):
            for here, there, device, k in self.moves(i, phase):
                self.copy(i, phase, here, there, device, k).wait_send()


EPS = 1e-05
PAIR = 2 * HEAD_DIM
SPAN = 2 * WINDOW
LOW = jnp.bfloat16
F32 = jnp.float32


def mm(left, right):
    return jnp.dot(left, right, preferred_element_type=F32)


def mm_nt(left, right):
    return lax.dot_general(left, right, (((1,), (1,)), ((), ())), preferred_element_type=F32)


def mm_tn(left, right):
    return lax.dot_general(left, right, (((0,), (0,)), ((), ())), preferred_element_type=F32)


def column_tiles(columns, size):
    full = columns // size
    tiles = [(0, size, full)]
    if columns % size:
        tiles.append((full * size, columns % size, 1))
    return tiles


def each_tile(columns, size, body):
    for begin, width, count in column_tiles(columns, size):
        if count == 1:
            body(begin, width)
        else:

            def step(j, _, begin=begin, width=width):
                body(pl.multiple_of(begin + j * width, 128), width)
                return 0

            lax.fori_loop(0, count, step, 0)


def each_rows(rows, size, body):
    def step(j, _):
        body(pl.ds(pl.multiple_of(j * size, size), size))
        return 0

    lax.fori_loop(0, rows // size, step, 0)


def both_heads(block):
    first = lax.broadcasted_iota(jnp.int32, block.shape, 1) < HEAD_DIM
    zero = jnp.zeros_like(block)
    return jnp.concatenate([jnp.where(first, block, zero), jnp.where(first, zero, block)], axis=0)


def merge_heads(stacked):
    rows = stacked.shape[0] // 2
    first = lax.broadcasted_iota(jnp.int32, (rows, PAIR), 1) < HEAD_DIM
    return jnp.where(first, stacked[:rows], stacked[rows:])


VMEM_LIMIT = 64 * 2**20


class Stream:
    def __init__(self, count, sems, fetch):
        self.count, self.sems, self.fetch = count, sems, fetch

    def copies(self, j, slot):
        return [
            pltpu.make_async_copy(src, dst, self.sems.at[slot, k])
            for k, (src, dst) in enumerate(self.fetch(j, slot))
        ]

    def prime(self):
        for copy in self.copies(0, 0):
            copy.start()

    def run(self, body, first=0, last=None):
        def step(j, _):
            slot = j % 2

            @pl.when(j + 1 < self.count)
            def _():
                for copy in self.copies(j + 1, 1 - slot):
                    copy.start()

            for copy in self.copies(j, slot):
                copy.wait()
            body(j, slot)
            return 0

        lax.fori_loop(first, self.count if last is None else last, step, 0)


def block_kernel(ahead, back, *refs):
    n = len(ahead.tensors)
    (lens, x_h, dy_h), raw, refs = refs[:3], refs[3 : 3 + n], refs[3 + n :]
    hbm_bufs, refs = refs[: n - 1], refs[n - 1 :]
    (mixed_o, gtok_o, q_h, p_h, ha_h, ho_h, hm_h, hid_h), refs = refs[:8], refs[8:]
    outs, refs = refs[:n], refs[n:]
    total, refs = refs[:n], refs[n:]
    count = len(back.items)
    got, refs = [refs[3 * i : 3 * i + 3] for i in range(count)], refs[3 * count :]
    (gate_pad, up_pad, down_pad, gain_buf, gains, xb, h1, da, db, kx, vx, o, x1, hid), refs = refs[:14], refs[14:]
    (dy, dyr, dh, dxr_r, qr, kr, vr, turned, pool, broad), refs = refs[:10], refs[10:]
    (kc, vc, rim_k, rim_v, gain_sum, gain_other), refs = refs[:6], refs[6:]
    (a_send, a_recv, own_sem, b_send, b_recv, load_sem, pool_sem, broad_sem, turn_sem), refs = refs[:9], refs[9:]
    half_send, half_recv, clear = refs
    rows, width = xb.shape
    wide, columns = ahead.tensors[5][1], ahead.tensors[1][1]
    chips = NZ * NY * NX
    me = Place()
    halves, loads, later = {}, [0], {}

    def load(src, dst):
        copy = pltpu.make_async_copy(src, dst, load_sem.at[loads[0]])
        loads[0] += 1
        copy.start()
        return copy

    def to_partner(k, src, dst):
        copy = remote(src, dst, half_send.at[k], half_recv.at[k], me.to_core())
        copy.start()
        halves[k] = copy
        return copy

    def own(size, side=0):
        return pl.ds(pl.multiple_of((me.s if side == 0 else 1 - me.s) * size, 128), size)

    get_x, get_dy = load(x_h, xb), load(dy_h, dy)
    me.greet()
    shards = list(raw[:5]) + [gate_pad, up_pad, down_pad]
    bufs = [gain_buf] + list(hbm_bufs)
    flat = [b.reshape(2, chips * b.shape[4], b.shape[5]) for b in bufs]
    gather = Gather(ahead, me, shards, bufs, a_send, a_recv, own_sem)
    scatter = Scatter(back, me, total, got, outs, b_send, b_recv)
    ready = set()

    def pad_shards():
        part, tile = raw[7].shape[0], down_pad.shape[0]
        zero = jnp.zeros((raw[5].shape[0], tile - part), LOW)
        for src, dst in ((raw[5], gate_pad), (raw[6], up_pad)):
            value, pieces = src[...], []
            for k in range(value.shape[1] // part):
                pieces += [value[:, k * part : (k + 1) * part], zero]
            dst[...] = jnp.concatenate(pieces, axis=1)
        down_pad[...] = jnp.concatenate([raw[7][...], jnp.zeros((tile - part, down_pad.shape[1]), LOW)], axis=0)

    def prepare(t):
        if t >= 5 and 5 not in ready:
            pad_shards()
            for k in range(5, n):
                gather.own_copy(k).start()
                ready.add(k)
        elif t not in ready:
            gather.own_copy(t).start()
            ready.add(t)

    landed, arrived = set(), set()

    def land(t):
        if t not in landed:
            landed.add(t)
            gather.own_copy(t).wait()

    def need(t):
        for k in range(t + 1):
            if k not in arrived:
                arrived.add(k)
                for i in ahead.of_tensor[k]:
                    gather.wait(i, 3)

    def norm(values, gain):
        inverse = lax.rsqrt(jnp.mean(values * values, axis=-1, keepdims=True) + EPS)
        return (values * inverse * gain).astype(LOW)

    def share(name, k, mine, whole):
        to = whole.at[:, own(rows)]
        later[name] = (load(mine, to), to_partner(k, mine, to))

    def shared(name):
        copy, sent = later[name]
        copy.wait()
        sent.wait()

    def turn(src, dst, lane):
        def body(j, _):
            at = pl.ds(pl.multiple_of(j * 128, 128), 128)
            dst[at, pl.ds(lane, rows)] = src[:, at].T
            return 0

        lax.fori_loop(0, src.shape[1] // 128, body, 0)
        return dst.at[:, pl.ds(lane, rows)]

    def first_norm():
        need(0)
        get_dy.wait()
        later["dy"] = to_partner(0, dy.at[:, own(columns, 1)], dyr)
        parts = []
        for z in range(NZ):
            for y in range(NY):
                pair = [gain_buf[me.s, z, y, x].astype(F32) for x in range(NX)]
                parts.append(pair[0] + pair[1])
        gains[...] = jnp.concatenate(parts, axis=1)[0:8]
        get_x.wait()

        def body(at):
            h1[at, :] = norm(xb[at, :].astype(F32), gains[0:1, :])

        each_rows(rows, 64, body)
        share("ha", 1, turn(h1, turned.at[0], 0), ha_h)

    def project(t, src, store):
        need(t)
        tiles = Stream(2, pool_sem, lambda j, slot: [(flat[t].at[j], pool.at[slot, pl.ds(0, width), :])])
        tiles.prime()

        def body(side, slot):
            for begin in range(0, columns, 256):
                part = mm(src[...], pool[slot, :width, begin : begin + 256])
                store(pl.ds(pl.multiple_of(side * columns + begin, 128), 256), part)

        tiles.run(body)

    def rim(k, ref):
        to = ref.at[pl.ds(0, WINDOW), :]
        return remote(ref.at[pl.ds(rows, WINDOW), :], to, half_send.at[2 + k], half_recv.at[2 + k], me.to_core())

    def put_into(ref, skip):
        def store(cols, part):
            ref[pl.ds(skip, rows), cols] = part.astype(LOW)

        return store

    def do_query():
        project(1, h1, put_into(da, 0))
        later["q_out"] = load(da.at[:, pl.ds(0, width)], q_h)

    def do_key():
        project(2, h1, put_into(kx, WINDOW))
        rim(0, kx).start()

    def do_value():
        project(3, h1, put_into(vx, WINDOW))
        rim(1, vx).start()

    first_end = lens[0, 0]
    second_end = first_end + lens[0, 1]

    def attend(b, _):
        base = me.s * rows + b * WINDOW
        at = pl.ds(pl.multiple_of(b * WINDOW, WINDOW), WINDOW)
        over = pl.ds(pl.multiple_of(b * WINDOW, WINDOW), SPAN)
        row = lax.broadcasted_iota(jnp.int32, (WINDOW, SPAN), 0)
        col = lax.broadcasted_iota(jnp.int32, (WINDOW, SPAN), 1)
        q_pos, k_pos = base + row, base - WINDOW + col

        def doc(pos):
            return (pos >= first_end).astype(jnp.int32) + (pos >= second_end).astype(jnp.int32)

        visible = (col >= row) & (col <= row + WINDOW) & (k_pos >= 0) & (doc(q_pos) == doc(k_pos))
        bias = jnp.where(visible, 0.0, -1e30)
        bias = jnp.concatenate([bias, bias], axis=0)
        pairs = range(HEADS // 2)
        cols = [slice(p * PAIR, (p + 1) * PAIR) for p in pairs]
        queries = [both_heads(da[at, c]) for c in cols]
        keys, values = [kx[over, c] for c in cols], [vx[over, c] for c in cols]
        scores = [mm_nt(q2, k) * HEAD_DIM ** (-0.5) + bias for q2, k in zip(queries, keys)]
        tops = [jnp.max(s, axis=-1, keepdims=True) for s in scores]
        exps = [jnp.exp(s - top) for s, top in zip(scores, tops)]
        sums = [jnp.sum(e, axis=-1, keepdims=True) for e in exps]
        weights = [(e * (1.0 / t)).astype(LOW) for e, t in zip(exps, sums)]
        parts = [merge_heads(mm(w, v)).astype(LOW) for w, v in zip(weights, values)]
        for p, c, w, part in zip(pairs, cols, weights, parts):
            db[at, 2 * p * SPAN : (2 * p + 1) * SPAN] = w[:WINDOW]
            db[at, (2 * p + 1) * SPAN : (2 * p + 2) * SPAN] = w[WINDOW:]
            o[at, c] = part
        return 0

    quarter = rows // WINDOW // 4

    def attend_part(k):
        if k == 0:
            for j, ref in ((0, kx), (1, vx)):
                rim(j, ref).wait_recv()
        lax.fori_loop(k * quarter, (k + 1) * quarter, attend, 0)
        if k == 3:
            later["p_out"] = load(db.at[:, pl.ds(0, HEADS * SPAN)], p_h)
            share("ho", 4, turn(o, turned.at[0], rows), ho_h)

    def add_out():
        def store(cols, part):
            x1[:, cols] = xb[:, cols].astype(F32) + part

        project(4, o, store)

        def body(at):
            xb[at, :] = norm(x1[at, :], gains[1:2, :])

        each_rows(rows, 64, body)
        share("hm", 5, turn(xb, turned.at[1], rows), hm_h)

    tiles = [(side, begin, min(512, wide - begin)) for side in range(2) for begin in range(0, wide, 512)]
    stages = [(1, 0), (1, 1), (0, 0), (0, 1), (0, 2), (0, 3)]

    def mlp_copies(j):
        side, begin, size = tiles[j]
        cols = pl.ds(begin, size)
        return [
            pltpu.make_async_copy(
                flat[5 + k].at[side, :, cols], pool.at[j % 2, pl.ds(k * width, width), pl.ds(0, size)], pool_sem.at[j % 2, k]
            )
            for k in range(2)
        ]

    def mlp(j):
        if j == 0:
            need(6)
            for copy in mlp_copies(0):
                copy.start()
            later["q_out"].wait()
            later["p_out"].wait()
            shared("ha")
            shared("ho")
        if j + 1 < len(tiles):
            for copy in mlp_copies(j + 1):
                copy.start()
        for copy in mlp_copies(j):
            copy.wait()
        side, begin, size = tiles[j]
        which, place = stages[j]
        lane, first = (0, place * 512) if place < 2 else (rows, (place - 2) * 512)
        for skip in range(0, size, 256):
            w = min(256, size - skip)
            cols = slice(skip, skip + w)
            a = mm(xb[...], pool[j % 2, :width, cols])
            b = mm(xb[...], pool[j % 2, width : 2 * width, cols])
            sig = 1.0 / (1.0 + jnp.exp(-a))
            silu = a * sig
            at = side * wide + begin + skip
            db[:, at : at + w] = silu.astype(LOW)
            da[:, at : at + w] = (b * sig * (1.0 + a * (1.0 - sig))).astype(LOW)
            hidden = (silu * b).astype(LOW)
            hid[side, :, begin + skip : begin + skip + w] = hidden
            turned[which, first + skip : first + skip + w, lane : lane + rows] = hidden.T
        at = side * wide + begin
        mine = turned.at[which, pl.ds(first, size), pl.ds(lane, rows)]
        share(("hid", j), 6 + j, mine, hid_h.at[pl.ds(at, size), :])

    tall = back.tensors[0][0] * NY * NX
    hid_tiles = Stream(
        NZ, turn_sem, lambda j, slot: [(hid_h.at[pl.ds(pl.multiple_of(j * tall, 16), tall), :], turned.at[slot, pl.ds(0, tall), :])]
    )
    tile, thin = 256, 128
    small = pool.reshape(2, pool.shape[1] // tile, tile, columns)

    def row_tiles(w, size, dst):
        return lambda j, slot: (w.at[:, pl.ds(pl.multiple_of(j * size, size), size), :], dst(slot))

    def small_at(k):
        return lambda slot: small.at[slot, pl.ds(2 * k, 2)]

    def broad_at(k):
        return lambda slot: broad.at[slot, k]

    def stream_of(fetchers, count, sems):
        return Stream(count, sems, lambda j, slot: [f(j, slot) for f in fetchers])

    def down_rows(j, slot):
        side = jnp.where(j < wide // thin, 1 - me.s, me.s)
        at = pl.ds(pl.multiple_of(side * wide + j % (wide // thin) * thin, thin), thin)
        return [(flat[7].at[:, at, :], small.at[slot, pl.ds(0, 2), pl.ds(0, thin), :])]

    down_tiles = Stream(2 * wide // thin, pool_sem, down_rows)
    mlp_tiles = stream_of([row_tiles(flat[5 + k], thin, broad_at(k)) for k in range(2)], width // thin, broad_sem)
    out_tiles = stream_of([row_tiles(flat[4], tile, small_at(0))], width // tile, pool_sem)
    qkv_tiles = stream_of([row_tiles(flat[1 + k], tile, small_at(k)) for k in range(3)], width // tile, pool_sem)

    def begin_scatter(t):
        for i in back.of_tensor[t]:
            scatter.start(i, 0)

    def put(t, z, part):
        row_count, column_count = back.tensors[t][:2]
        total[t][z] = part.reshape(NY, NX, row_count, column_count).astype(total[t].dtype)

    def grad_down():
        for j in range(len(tiles)):
            shared(("hid", j))
        shared("hm")
        later["dy"].wait_recv()
        hid_tiles.prime()

        def body(z, slot):
            mine = mm(turned[slot, :tall, own(rows)], dy[:, own(columns)])
            put(0, z, mine + mm(turned[slot, :tall, own(rows, 1)], dyr[...]))

        hid_tiles.run(body)
        begin_scatter(0)
        later["hm"] = load(hm_h, turned.at[0])
        later["ho"] = load(ho_h, turned.at[1])

    def add_down():
        need(7)
        tiles2 = Stream(2, pool_sem, lambda j, slot: [(flat[7].at[j], pool.at[slot])])
        tiles2.prime()

        def body(side, slot):
            for begin in range(0, columns, 256):
                part = mm(hid[0], pool[slot, :wide, begin : begin + 256])
                part += mm(hid[1], pool[slot, wide:, begin : begin + 256])
                cols = pl.ds(pl.multiple_of(side * columns + begin, 128), 256)
                xb[:, cols] = (x1[:, cols] + part).astype(LOW)

        tiles2.run(body)
        down_tiles.prime()
        mlp_tiles.prime()
        later["mixed"] = load(xb, mixed_o)
        pl.semaphore_signal(clear, inc=1, device_id=me.to_core(), device_id_type=MESH)

    def hidden_body(j, slot):
        part = mm_nt(dy[:, :columns], small[slot, 0, :thin]) + mm_nt(dy[:, columns:], small[slot, 1, :thin])
        side = jnp.where(j < wide // thin, 1 - me.s, me.s)
        at = pl.ds(pl.multiple_of(side * wide + j % (wide // thin) * thin, thin), thin)
        da[:, at] = (part * da[:, at].astype(F32)).astype(LOW)
        db[:, at] = (part * db[:, at].astype(F32)).astype(LOW)

    def hidden(k):
        middle = down_tiles.count // 2
        if k == 0:
            down_tiles.run(hidden_body, 0, middle)
            pl.semaphore_wait(clear, 1)
            later["db"] = to_partner(12, db.at[:, own(wide, 1)], hid.at[1])
            later["da"] = to_partner(13, da.at[:, own(wide, 1)], hid.at[0])
            return
        down_tiles.run(hidden_body, middle)
        out_tiles.prime()

    def weight_grad_to(t, slot, mine, theirs):
        row_count = back.tensors[t][0] * NY * NX

        def step(z, _):
            at = pl.ds(pl.multiple_of(z * row_count, 16), row_count)
            put(t, z, mm(turned[slot, at, own(rows)], mine()) + mm(turned[slot, at, own(rows, 1)], theirs[...]))
            return 0

        lax.fori_loop(0, NZ, step, 0)
        begin_scatter(t)

    def grad_up():
        later["hm"].wait()
        later["db"].wait_recv()
        weight_grad_to(1, 0, lambda: db[:, own(wide)], hid.at[1])

    def grad_gate():
        later["da"].wait_recv()
        weight_grad_to(2, 0, lambda: da[:, own(wide)], hid.at[0])
        later["ha"] = load(ha_h, turned.at[0])

    def dh2_body(j, slot):
        part = None
        for k, grad in ((0, da), (1, db)):
            for side in range(2):
                term = mm_nt(grad[:, side * wide : (side + 1) * wide], broad[slot, k, side])
                part = term if part is None else part + term
        dh[:, pl.ds(pl.multiple_of(j * thin, thin), thin)] = part

    def grad_norm2(k):
        middle = mlp_tiles.count // 2
        if k == 0:
            mlp_tiles.run(dh2_body, 0, middle)
            return
        mlp_tiles.run(dh2_body, middle)
        later["db"].wait_send()
        later["da"].wait_send()
        later["q"] = load(q_h, da.at[:, pl.ds(0, width)])
        later["p"] = load(p_h, db.at[:, pl.ds(0, HEADS * SPAN)])
        later["mixed"].wait()
        later["x"] = load(x_h, xb)

    def norm_grad(values, grad_norm, gain):
        inverse = lax.rsqrt(jnp.mean(values * values, axis=-1, keepdims=True) + EPS)
        scaled = grad_norm * gain
        mean_term = jnp.mean(values * scaled, axis=-1, keepdims=True)
        back_part = inverse * scaled - values * (inverse * inverse * inverse) * mean_term
        return back_part, jnp.sum(values * inverse * grad_norm, axis=0, keepdims=True)

    def norm2_body(at):
        back_part, gain_part = norm_grad(x1[at, :], dh[at, :], gains[1:2, :])
        gain_sum[1:2, :] += gain_part
        grad = dy[at, :].astype(F32) + back_part
        x1[at, :] = grad
        h1[at, :] = grad.astype(LOW)

    def norm2():
        gain_sum[...] = jnp.zeros_like(gain_sum)
        each_rows(rows, 64, norm2_body)
        later["dxr"] = to_partner(14, h1.at[:, own(columns, 1)], dxr_r)

    def out_body(j, slot):
        part = mm_nt(h1[:, :columns], small[slot, 0]) + mm_nt(h1[:, columns:], small[slot, 1])
        o[:, pl.ds(pl.multiple_of(j * tile, tile), tile)] = part.astype(LOW)

    def grad_heads():
        out_tiles.run(out_body)
        qkv_tiles.prime()

    def grad_out():
        later["ho"].wait()
        later["dxr"].wait_recv()
        weight_grad_to(3, 1, lambda: h1[:, own(columns)], dxr_r)

    scale = HEAD_DIM ** (-0.5)

    def attend_back(b, _):
        at = pl.ds(pl.multiple_of(b * WINDOW, WINDOW), WINDOW)
        over = pl.ds(pl.multiple_of(b * WINDOW, WINDOW), SPAN)
        pairs = range(HEADS // 2)
        cols = [slice(p * PAIR, (p + 1) * PAIR) for p in pairs]
        queries, grads = [both_heads(da[at, c]) for c in cols], [both_heads(o[at, c]) for c in cols]
        keys, values = [kx[over, c] for c in cols], [vx[over, c] for c in cols]
        lows = [
            jnp.concatenate([db[at, (2 * p + h) * SPAN : (2 * p + h + 1) * SPAN] for h in range(2)], axis=0)
            for p in pairs
        ]
        carry_k, carry_v = [kc[:, c] for c in cols], [vc[:, c] for c in cols]
        probs = [low.astype(F32) for low in lows]
        grad_probs = [mm_nt(g, v) for g, v in zip(grads, values)]
        grad_values = [mm_tn(low, g) for low, g in zip(lows, grads)]
        inners = [jnp.sum(p * g, axis=-1, keepdims=True) for p, g in zip(probs, grad_probs)]
        scores = [(p * (g - i)).astype(LOW) for p, g, i in zip(probs, grad_probs, inners)]
        grad_queries = [(merge_heads(mm(s, k)) * scale).astype(LOW) for s, k in zip(scores, keys)]
        grad_keys = [mm_tn(s, q2) * scale for s, q2 in zip(scores, queries)]
        new_k = [(old + g[:WINDOW]).astype(LOW) for old, g in zip(carry_k, grad_keys)]
        new_v = [(old + g[:WINDOW]).astype(LOW) for old, g in zip(carry_v, grad_values)]
        for c, gq, gk, gv, nk, nv in zip(cols, grad_queries, grad_keys, grad_values, new_k, new_v):
            da[at, c] = gq
            kx[at, c] = nk
            vx[at, c] = nv
            kc[:, c] = gk[WINDOW:]
            vc[:, c] = gv[WINDOW:]
        return 0

    own_rows = pl.ds(WINDOW, rows)

    def attend_back_part(k):
        if k == 0:
            kc[...] = jnp.zeros_like(kc)
            vc[...] = jnp.zeros_like(vc)
            for j, ref in ((0, kx), (1, vx)):
                rim(j, ref).wait_send()
            later["q"].wait()
            later["p"].wait()
        lax.fori_loop(k * quarter, (k + 1) * quarter, attend_back, 0)
        if k == 0:
            later["rim"] = [
                to_partner(15, kx.at[pl.ds(0, WINDOW), :], rim_k),
                to_partner(16, vx.at[pl.ds(0, WINDOW), :], rim_v),
            ]
        if k == 3:
            for copy, ref, carry, rim_in in ((later["rim"][0], kx, kc, rim_k), (later["rim"][1], vx, vc, rim_v)):
                copy.wait_recv()
                ref[pl.ds(rows, WINDOW), :] = (carry[...] + rim_in[...].astype(F32)).astype(LOW)
            later["dq"] = to_partner(17, da.at[:, own(columns, 1)], qr)
            later["dk"] = to_partner(18, kx.at[own_rows, own(columns, 1)], kr)
            later["dv"] = to_partner(19, vx.at[own_rows, own(columns, 1)], vr)

    def grad_qkv(k):
        if k == 0:
            later["ha"].wait()
        later[("dq", "dk", "dv")[k]].wait_recv()
        mine = (lambda: da[:, own(columns)], lambda: kx[own_rows, own(columns)], lambda: vx[own_rows, own(columns)])[k]
        weight_grad_to(4 + k, 0, mine, (qr, kr, vr)[k])

    def dh1_body(j, slot):
        part = None
        for k, (grad, skip) in enumerate(((da, 0), (kx, WINDOW), (vx, WINDOW))):
            for side in range(2):
                left = grad[pl.ds(skip, rows), side * columns : (side + 1) * columns]
                term = mm_nt(left, small[slot, 2 * k + side])
                part = term if part is None else part + term
        dh[:, pl.ds(pl.multiple_of(j * tile, tile), tile)] = part

    def grad_norm1():
        qkv_tiles.run(dh1_body)

    def norm1_body(at):
        back_part, gain_part = norm_grad(xb[at, :].astype(F32), dh[at, :], gains[0:1, :])
        gain_sum[0:1, :] += gain_part
        x1[at, :] = x1[at, :] + back_part

    def norm1():
        later["x"].wait()
        each_rows(rows, 64, norm1_body)
        later["gtok"] = load(x1, gtok_o)
        later["gain"] = to_partner(20, gain_sum, gain_other)

    def grad_gains():
        later["gain"].wait_recv()
        lanes = back.tensors[7][1]
        for c in range(chips):
            at = slice(c // 2 * lanes, (c // 2 + 1) * lanes)
            total[7][c // 4, c // 2 % 2, c % 2] = gain_sum[:, at] + gain_other[:, at]
        begin_scatter(7)

    work = {
        "norm": first_norm,
        "query": do_query,
        "key": do_key,
        "value": do_value,
        "project": add_out,
        "mix": add_down,
        "down": grad_down,
        "up": grad_up,
        "gate": grad_gate,
        "norm2": norm2,
        "heads": grad_heads,
        "out": grad_out,
        "dh1": grad_norm1,
        "norm1": norm1,
        "gains": grad_gains,
    }
    for k in range(4):
        work["see", k] = functools.partial(attend_part, k)
        work["attend", k] = functools.partial(attend_back_part, k)
    for k in range(len(tiles)):
        work["mlp", k] = functools.partial(mlp, k)
    for k in range(3):
        work["qkv", k] = functools.partial(grad_qkv, k)
    for k in range(2):
        work["hidden", k] = functools.partial(hidden, k)
        work["dh2", k] = functools.partial(grad_norm2, k)
    for step in SCRIPT:
        if step in work:
            work[step]()
        elif step[0] == "start":
            prepare(ahead.items[step[1]][0])
            gather.start(step[1], 0)
        elif step[0] == 0:
            _, i, phase = step
            land(ahead.items[i][0])
            gather.wait(i, phase)
            gather.start(i, phase + 1)
        else:
            _, i, phase = step
            scatter.wait(i, phase)
            scatter.add(i, phase)
            if phase < 2:
                scatter.start(i, phase + 1)
    for i in range(len(ahead.items)):
        gather.finish(i)
    for i in range(len(back.items)):
        scatter.finish(i)
    for k in (0, 14, 15, 16, 17, 18, 19, 20):
        halves[k].wait_send()
    later["gtok"].wait()


def block_all(ahead, back, lens, tokens, cotangent, shards):
    n, na, nb = len(ahead.tensors), len(ahead.items), len(back.items)
    rows, width = tokens.shape
    columns, wide = ahead.tensors[1][1], ahead.tensors[5][1]
    anywhere = pl.BlockSpec(memory_space=pl.ANY)
    inside = pl.BlockSpec(memory_space=pltpu.VMEM)
    shape = jax.ShapeDtypeStruct
    over = WINDOW + rows
    bufs = [(2, NZ, NY, NX) + t[:2] for t in ahead.tensors]
    kept = [
        ((rows, width), LOW),
        ((rows, width), F32),
        ((rows, width), LOW),
        ((rows, HEADS * SPAN), LOW),
        ((width, 2 * rows), LOW),
        ((width, 2 * rows), LOW),
        ((width, 2 * rows), LOW),
        ((2 * wide, 2 * rows), LOW),
    ]
    scratch = [
        (ahead.tensors[5][:2], LOW),
        (ahead.tensors[6][:2], LOW),
        (ahead.tensors[7][:2], LOW),
        (bufs[0], LOW),
        ((8, width), F32),
        ((rows, width), LOW),
        ((rows, width), LOW),
        ((rows, 2 * wide), LOW),
        ((rows, 2 * wide), LOW),
        ((over, width), LOW),
        ((over, width), LOW),
        ((rows, width), LOW),
        ((rows, width), F32),
        ((2, rows, wide), LOW),
        ((rows, width), LOW),
        ((rows, columns), LOW),
        ((rows, width), F32),
        ((rows, columns), LOW),
        ((rows, columns), LOW),
        ((rows, columns), LOW),
        ((rows, columns), LOW),
        ((2, width, 2 * rows), LOW),
        ((2, 2 * wide, columns), LOW),
        ((2, 2, 2, 128, wide), LOW),
        ((WINDOW, width), F32),
        ((WINDOW, width), F32),
        ((WINDOW, width), LOW),
        ((WINDOW, width), LOW),
        ((8, width), F32),
        ((8, width), F32),
    ]
    totals = [((NZ, NY, NX) + t[:2], t[2]) for t in back.tensors]
    got = [part for parts in got_shapes(back) for part in parts]
    dma = pltpu.SemaphoreType.DMA
    outs = pl.pallas_call(
        functools.partial(block_kernel, ahead, back),
        out_shape=[shape(b, LOW) for b in bufs[1:]]
        + [shape(*s) for s in kept]
        + [shape(t[:2], F32) for t in back.tensors],
        in_specs=[pl.BlockSpec(memory_space=pltpu.SMEM), anywhere, anywhere] + [inside] * n,
        out_specs=[anywhere] * (n - 1 + len(kept)) + [inside] * n,
        scratch_shapes=[pltpu.VMEM(*s) for s in totals + got + scratch]
        + [dma((6 * na,)), dma((6 * na,)), dma((n,)), dma((5 * nb,)), dma((5 * nb,)), dma((24,))]
        + [dma((2, 3)), dma((2, 2)), dma((2, 1)), dma((21,)), dma((21,)), pltpu.SemaphoreType.REGULAR],
        compiler_params=pltpu.CompilerParams(
            collective_id=0, has_side_effects=True, vmem_limit_bytes=VMEM_LIMIT
        ),
        name="block_all",
    )(lens, tokens, cotangent, *shards)
    return outs[n - 1 : n + 1], outs[n - 1 + len(kept) :]


def finish_kernel(*refs):
    n = 10
    ins, outs, held, made = refs[:n], refs[n : 2 * n + 1], refs[2 * n + 1 : 3 * n + 1], refs[3 * n + 1 : 4 * n + 2]
    sem_in, sem_out = refs[4 * n + 2 :]
    gets = [pltpu.make_async_copy(src, dst, sem_in.at[k]) for k, (src, dst) in enumerate(zip(ins, held))]
    for copy in gets:
        copy.start()
    puts = []

    def put(k, src):
        copy = pltpu.make_async_copy(src, outs[k], sem_out.at[k])
        copy.start()
        puts.append(copy)

    down, up, gate, out, query, key, value, gain = held[2:]
    for copy in gets[2:]:
        copy.wait()
    for k, src in ((2, query), (3, key), (4, value), (5, out)):
        put(k, src)
    rows, part, tile = query.shape[0], outs[8].shape[0], down.shape[0]
    made[8][...] = down[...][:part]
    put(8, made[8])
    for k, src in ((6, gate), (7, up)):
        values = src[...]
        made[k][...] = jnp.concatenate(
            [values[:, j * tile : j * tile + part] for j in range(values.shape[1] // tile)], axis=1
        )
        put(k, made[k])
    both = gain[...]
    own = jnp.where(lax.axis_index("dp") % 2 == 0, both[:, :rows], both[:, rows:])
    made[9][...] = own[0:1]
    made[10][...] = own[1:2]
    put(9, made[9])
    put(10, made[10])
    for k in range(2):
        gets[k].wait()
        put(k, held[k])
    for copy in puts:
        copy.wait()


def finish_all(mixed, tokens, sums, w_query, w_gate, w_down):
    anywhere = pl.BlockSpec(memory_space=pl.ANY)
    shape = jax.ShapeDtypeStruct
    outs = [shape(mixed.shape, mixed.dtype), shape(tokens.shape, F32)]
    outs += [shape(w_query.shape, F32)] * 4 + [shape(w_gate.shape, F32)] * 2 + [shape(w_down.shape, F32)]
    outs += [shape((1, w_query.shape[0]), F32)] * 2
    ins = [mixed, tokens, *sums]
    return pl.pallas_call(
        finish_kernel,
        out_shape=outs,
        in_specs=[anywhere] * len(ins),
        out_specs=[anywhere] * len(outs),
        scratch_shapes=[pltpu.VMEM(a.shape, a.dtype) for a in ins + outs]
        + [pltpu.SemaphoreType.DMA((len(ins),)), pltpu.SemaphoreType.DMA((len(outs),))],
        compiler_params=pltpu.CompilerParams(vmem_limit_bytes=62 * 2**20),
        name="finish_all",
    )(*ins)


def kinds(w_query, w_gate, w_down):
    rows, columns = w_query.shape
    part = w_down.shape[0]
    tile = -(-part // 16) * 16
    wide = w_gate.shape[1] // part * tile
    half, part16 = rows // 2, rows // 4
    long, short = -(-tile // 64) * 16, tile - 3 * (-(-tile // 64) * 16)

    def cuts(kinds, counts):
        return tuple(zip(kinds, counts, strict=True))

    return {
        "square": (rows, columns, LOW, cuts(("zfx", "zfy"), (half, half))),
        "broad": (rows, wide, LOW, cuts(("zfx", "zfy", "zmx", "zmy"), (part16,) * 4)),
        "broad_f": (rows, wide, LOW, cuts(("zfx", "zfy", "zfx", "zfy"), (part16,) * 4)),
        "tall": (tile, columns, LOW, cuts(("zfx", "zfy", "zmx", "zmy"), (long, long, long, short))),
        "square_m": (rows, columns, LOW, cuts(("zmx", "zmy"), (half, half))),
        "tall_f": (tile, columns, LOW, cuts(("zfx", "zfy", "zfx", "zfy"), (long, long, long, short))),
        "gain": (16, 2 * rows, LOW, cuts(("zfx",), (16,))),
        "gain_grad": (8, 2 * rows, F32, cuts(("zfx",), (8,))),
    }


def gather_plan(w_query, w_key, w_value, w_out, w_gate, w_up, w_down, gain_attn, gain_mlp):
    kind = kinds(w_query, w_gate, w_down)
    names = ("gain", "square", "square", "square", "square", "broad", "broad", "tall")
    plan = Plan([kind[name] for name in names])
    rows = w_query.shape[0]
    both = jnp.stack([gain_attn, gain_mlp])
    left = jnp.pad(both, ((0, 14), (0, rows)))
    right = jnp.pad(both, ((0, 14), (rows, 0)))
    pair = jnp.where(lax.axis_index("dp") % 2 == 0, left, right)
    shards = [
        pair,
        w_query,
        w_key,
        w_value,
        w_out,
        w_gate,
        w_up,
        w_down,
    ]
    return plan, shards


def swift_block(
    tokens,
    seq_lengths,
    w_query,
    w_key,
    w_value,
    w_out,
    w_gate,
    w_up,
    w_down,
    gain_attn,
    gain_mlp,
    cotangent,
):
    plan, shards = gather_plan(w_query, w_key, w_value, w_out, w_gate, w_up, w_down, gain_attn, gain_mlp)
    kind = kinds(w_query, w_gate, w_down)
    names = ("tall_f", "broad_f", "broad_f", "square", "square", "square", "square", "gain_grad")
    back = Plan([kind[name] for name in names])
    results, sums = block_all(plan, back, seq_lengths, tokens, cotangent, shards)
    outs = finish_all(results[0], results[1], sums, w_query, w_gate, w_down)
    return (*outs[:9], outs[9].reshape(-1), outs[10].reshape(-1))


def solution(mesh):
    fast = (mesh.shape["dp"], mesh.shape["seq"]) == (NZ * NY * NX, 2)
    shards = swift_block if fast else plain_block
    in_specs = (
        P(("dp", "seq"), None),
        P("dp", None),
        P("dp", "seq"),
        P("dp", "seq"),
        P("dp", "seq"),
        P("dp", "seq"),
        P("dp", "seq"),
        P("dp", "seq"),
        P("dp", "seq"),
        P("dp"),
        P("dp"),
        P(("dp", "seq"), None),
    )
    out_specs = (
        P(("dp", "seq"), None),
        P(("dp", "seq"), None),
        P("dp", "seq"),
        P("dp", "seq"),
        P("dp", "seq"),
        P("dp", "seq"),
        P("dp", "seq"),
        P("dp", "seq"),
        P("dp", "seq"),
        P("dp"),
        P("dp"),
    )
    return jax.shard_map(shards, mesh=mesh, in_specs=in_specs, out_specs=out_specs, check_vma=False)
```

```python
import functools

import jax
import jax.numpy as jnp
from jax import lax
from jax.experimental import pallas as pl
from jax.experimental.pallas import tpu as pltpu
from jax.sharding import PartitionSpec as P

HEADS = 16
HEAD_DIM = 64
WINDOW = 64


eps_norm = 1e-05


def from_behind(block, axis, distance):
    devices = range(lax.axis_size(axis))
    route = [(i - distance, i) for i in devices if i - distance in devices]
    return lax.ppermute(block, axis, route)


def inverse_rms(values):
    return lax.rsqrt(jnp.mean(values * values, axis=-1, keepdims=True) + eps_norm)


def doc_numbers(lengths_row, positions):
    first_end = lengths_row[0]
    second_end = lengths_row[0] + lengths_row[1]
    return (positions >= first_end).astype(jnp.int32) + (positions >= second_end).astype(jnp.int32)


def window_mask(query_pos, query_doc, key_pos, key_doc, window):
    after = key_pos[None, :] >= query_pos[:, None] - window
    before = key_pos[None, :] <= query_pos[:, None]
    inside = (key_pos[None, :] >= 0) & (key_doc[None, :] == query_doc[:, None])
    return after & before & inside


def norm_back(values, inverse, gain, grad_norm):
    scaled = grad_norm * gain
    mean_term = jnp.mean(values * scaled, axis=-1, keepdims=True)
    grad_values = inverse * scaled - values * (inverse * inverse * inverse) * mean_term
    grad_gain = jnp.sum(values * inverse * grad_norm, axis=0)
    return (grad_values, grad_gain)


def project(left, right):
    return jnp.dot(left, right, preferred_element_type=jnp.float32)


def project_back(grad_rows, weight):
    return jnp.einsum("tf,df->td", grad_rows, weight, preferred_element_type=jnp.float32)


def weight_grad(inputs, grad_rows):
    return jnp.einsum("td,tf->df", inputs, grad_rows, preferred_element_type=jnp.float32)


def plain_block(
    tokens,
    seq_lengths,
    w_query,
    w_key,
    w_value,
    w_out,
    w_gate,
    w_up,
    w_down,
    gain_attn,
    gain_mlp,
    cotangent,
):
    row_count = tokens.shape[0]
    block_rows = min(512, row_count)
    head_group = HEADS // 2
    score_scale = HEAD_DIM ** (-0.5)
    row_parts = (
        lax.all_gather(w_query, "dp", axis=0, tiled=True),
        lax.all_gather(w_key, "dp", axis=0, tiled=True),
        lax.all_gather(w_value, "dp", axis=0, tiled=True),
        lax.all_gather(w_out, "dp", axis=0, tiled=True),
        lax.all_gather(w_gate, "dp", axis=0, tiled=True),
        lax.all_gather(w_up, "dp", axis=0, tiled=True),
        lax.all_gather(w_down, "dp", axis=0, tiled=True),
        lax.all_gather(gain_attn, "dp", axis=0, tiled=True),
        lax.all_gather(gain_mlp, "dp", axis=0, tiled=True),
    )
    full_mats = (
        lax.all_gather(row_parts[0], "seq", axis=1, tiled=True),
        lax.all_gather(row_parts[1], "seq", axis=1, tiled=True),
        lax.all_gather(row_parts[2], "seq", axis=1, tiled=True),
        lax.all_gather(row_parts[3], "seq", axis=1, tiled=True),
        lax.all_gather(row_parts[4], "seq", axis=1, tiled=True),
        lax.all_gather(row_parts[5], "seq", axis=1, tiled=True),
        lax.all_gather(row_parts[6], "seq", axis=1, tiled=True),
    )
    query_w, key_w, value_w, out_w, gate_w, up_w, down_full = full_mats
    gain_one = row_parts[7].astype(jnp.float32)
    gain_two = row_parts[8].astype(jnp.float32)
    inputs = tokens.astype(jnp.float32)
    inv_one = inverse_rms(inputs)
    normed_one = (inputs * inv_one * gain_one).astype(jnp.bfloat16)
    query_low = project(normed_one, query_w).astype(jnp.bfloat16)
    key_low = project(normed_one, key_w).astype(jnp.bfloat16)
    value_low = project(normed_one, value_w).astype(jnp.bfloat16)
    rim_pairs = from_behind(
        (key_low[row_count - WINDOW :], value_low[row_count - WINDOW :]), "seq", 1
    )
    keys_ext = jnp.concatenate([rim_pairs[0], key_low], axis=0).reshape(
        row_count + WINDOW, HEADS, HEAD_DIM
    )
    values_ext = jnp.concatenate([rim_pairs[1], value_low], axis=0).reshape(
        row_count + WINDOW, HEADS, HEAD_DIM
    )
    query_heads = query_low.reshape(row_count, HEADS, HEAD_DIM)
    span_start = lax.axis_index("seq") * row_count
    query_pos = span_start + jnp.arange(row_count, dtype=jnp.int32)
    key_pos = span_start - WINDOW + jnp.arange(row_count + WINDOW, dtype=jnp.int32)
    query_doc = doc_numbers(seq_lengths[0], query_pos)
    key_doc = doc_numbers(seq_lengths[0], key_pos)

    def tile_scores(row_start, head_start):
        visible = window_mask(query_pos, query_doc, key_pos, key_doc, WINDOW)
        scores_raw = (
            jnp.einsum(
                "qhd,khd->hqk",
                query_heads[
                    row_start : row_start + block_rows, head_start : head_start + head_group
                ],
                keys_ext[
                    row_start : row_start + block_rows + WINDOW,
                    head_start : head_start + head_group,
                ],
                preferred_element_type=jnp.float32,
            )
            * score_scale
        )
        return jnp.where(visible[None], scores_raw, -1e30)

    log_totals = {}
    row_start = 0
    head_parts = []
    for head_start in range(0, HEADS, head_group):
        masked_scores = tile_scores(row_start, head_start)
        top_score = jnp.max(masked_scores, axis=-1, keepdims=True)
        log_total = top_score + jnp.log(
            jnp.sum(jnp.exp(masked_scores - top_score), axis=-1, keepdims=True)
        )
        prob_low = jnp.exp(masked_scores - log_total).astype(jnp.bfloat16)
        value_tile = values_ext[
            row_start : row_start + block_rows + WINDOW, head_start : head_start + head_group
        ]
        head_parts.append(
            jnp.einsum("hqk,khd->qhd", prob_low, value_tile, preferred_element_type=jnp.float32)
        )
        log_totals[row_start, head_start] = log_total
    attn_blocks = jnp.concatenate(head_parts, axis=1)
    attended = attn_blocks.reshape(row_count, HEADS * HEAD_DIM).astype(jnp.bfloat16)
    middle = inputs + project(attended, out_w)
    inv_two = inverse_rms(middle)
    normed_two = (middle * inv_two * gain_two).astype(jnp.bfloat16)
    gate_pre = project(normed_two, gate_w)
    up_pre = project(normed_two, up_w)
    gate_act = jax.nn.silu(gate_pre)
    hidden = (gate_act * up_pre).astype(jnp.bfloat16)
    block_out = (middle + project(hidden, down_full)).astype(jnp.bfloat16)
    rows_again = (
        lax.all_gather(w_query, "dp", axis=0, tiled=True),
        lax.all_gather(w_key, "dp", axis=0, tiled=True),
        lax.all_gather(w_value, "dp", axis=0, tiled=True),
        lax.all_gather(w_out, "dp", axis=0, tiled=True),
        lax.all_gather(w_gate, "dp", axis=0, tiled=True),
        lax.all_gather(w_up, "dp", axis=0, tiled=True),
        lax.all_gather(w_down, "dp", axis=0, tiled=True),
        lax.all_gather(gain_attn, "dp", axis=0, tiled=True),
        lax.all_gather(gain_mlp, "dp", axis=0, tiled=True),
    )
    mats_again = (
        lax.all_gather(rows_again[0], "seq", axis=1, tiled=True),
        lax.all_gather(rows_again[1], "seq", axis=1, tiled=True),
        lax.all_gather(rows_again[2], "seq", axis=1, tiled=True),
        lax.all_gather(rows_again[3], "seq", axis=1, tiled=True),
        lax.all_gather(rows_again[4], "seq", axis=1, tiled=True),
        lax.all_gather(rows_again[5], "seq", axis=1, tiled=True),
        lax.all_gather(rows_again[6], "seq", axis=1, tiled=True),
    )
    back_query, back_key, back_value, back_out, back_gate, back_up, back_down = mats_again
    back_gain_one = rows_again[7].astype(jnp.float32)
    back_gain_two = rows_again[8].astype(jnp.float32)
    grad_final = cotangent.astype(jnp.float32)
    d_down = weight_grad(hidden, cotangent)
    grad_hidden = project_back(cotangent, back_down)
    sigmoid_gate = jax.nn.sigmoid(gate_pre)
    grad_gate_low = (
        grad_hidden * up_pre * sigmoid_gate * (1.0 + gate_pre * (1.0 - sigmoid_gate))
    ).astype(jnp.bfloat16)
    grad_up_low = (grad_hidden * gate_act).astype(jnp.bfloat16)
    d_gate = weight_grad(normed_two, grad_gate_low)
    d_up = weight_grad(normed_two, grad_up_low)
    grad_normed_two = project_back(grad_gate_low, back_gate) + project_back(grad_up_low, back_up)
    grad_mid_norm, d_gain_two = norm_back(middle, inv_two, back_gain_two, grad_normed_two)
    grad_middle = grad_final + grad_mid_norm
    grad_proj = grad_middle.astype(jnp.bfloat16)
    d_out = weight_grad(attended, grad_proj)
    grad_attended = (
        project_back(grad_proj, back_out).astype(jnp.bfloat16).reshape(row_count, HEADS, HEAD_DIM)
    )
    grad_keys_ext = jnp.zeros((row_count + WINDOW, HEADS, HEAD_DIM), jnp.float32)
    grad_values_ext = jnp.zeros((row_count + WINDOW, HEADS, HEAD_DIM), jnp.float32)
    row_start = 0
    head_parts = []
    for head_start in range(0, HEADS, head_group):
        head_end = head_start + head_group
        masked_scores = tile_scores(row_start, head_start)
        prob_full = jnp.exp(masked_scores - log_totals[row_start, head_start])
        grad_tile = grad_attended[row_start : row_start + block_rows, head_start:head_end]
        key_tile = keys_ext[row_start : row_start + block_rows + WINDOW, head_start:head_end]
        value_tile = values_ext[row_start : row_start + block_rows + WINDOW, head_start:head_end]
        query_tile = query_heads[row_start : row_start + block_rows, head_start:head_end]
        grad_prob = jnp.einsum(
            "qhd,khd->hqk", grad_tile, value_tile, preferred_element_type=jnp.float32
        )
        inner = jnp.sum(prob_full * grad_prob, axis=-1, keepdims=True)
        grad_score = (prob_full * (grad_prob - inner)).astype(jnp.bfloat16)
        head_parts.append(
            jnp.einsum("hqk,khd->qhd", grad_score, key_tile, preferred_element_type=jnp.float32)
            * score_scale
        )
        key_term = (
            jnp.einsum("hqk,qhd->khd", grad_score, query_tile, preferred_element_type=jnp.float32)
            * score_scale
        )
        value_term = jnp.einsum(
            "hqk,qhd->khd",
            prob_full.astype(jnp.bfloat16),
            grad_tile,
            preferred_element_type=jnp.float32,
        )
        grad_keys_ext = grad_keys_ext.at[
            row_start : row_start + block_rows + WINDOW, head_start:head_end
        ].add(key_term)
        grad_values_ext = grad_values_ext.at[
            row_start : row_start + block_rows + WINDOW, head_start:head_end
        ].add(value_term)
    grad_query_blocks = jnp.concatenate(head_parts, axis=1)
    rim_back = (
        from_behind(
            grad_keys_ext[:WINDOW].reshape(WINDOW, HEADS * HEAD_DIM).astype(jnp.bfloat16), "seq", -1
        ).astype(jnp.float32),
        from_behind(
            grad_values_ext[:WINDOW].reshape(WINDOW, HEADS * HEAD_DIM).astype(jnp.bfloat16),
            "seq",
            -1,
        ).astype(jnp.float32),
    )
    grad_keys = (
        grad_keys_ext[WINDOW:]
        .reshape(row_count, HEADS * HEAD_DIM)
        .at[row_count - WINDOW :]
        .add(rim_back[0])
    )
    grad_values = (
        grad_values_ext[WINDOW:]
        .reshape(row_count, HEADS * HEAD_DIM)
        .at[row_count - WINDOW :]
        .add(rim_back[1])
    )
    grad_query_low = grad_query_blocks.reshape(row_count, HEADS * HEAD_DIM).astype(jnp.bfloat16)
    grad_key_low = grad_keys.astype(jnp.bfloat16)
    grad_value_low = grad_values.astype(jnp.bfloat16)
    d_query = weight_grad(normed_one, grad_query_low)
    d_key = weight_grad(normed_one, grad_key_low)
    d_value = weight_grad(normed_one, grad_value_low)
    grad_normed_one = (
        project_back(grad_query_low, back_query)
        + project_back(grad_key_low, back_key)
        + project_back(grad_value_low, back_value)
    )
    grad_in_norm, d_gain_one = norm_back(inputs, inv_one, back_gain_one, grad_normed_one)
    grad_inputs = grad_middle + grad_in_norm
    row_sums = (
        lax.psum_scatter(
            d_query.astype(jnp.bfloat16), "dp", scatter_dimension=0, tiled=True
        ).astype(jnp.float32),
        lax.psum_scatter(d_key.astype(jnp.bfloat16), "dp", scatter_dimension=0, tiled=True).astype(
            jnp.float32
        ),
        lax.psum_scatter(
            d_value.astype(jnp.bfloat16), "dp", scatter_dimension=0, tiled=True
        ).astype(jnp.float32),
        lax.psum_scatter(d_out.astype(jnp.bfloat16), "dp", scatter_dimension=0, tiled=True).astype(
            jnp.float32
        ),
        lax.psum_scatter(d_gate.astype(jnp.bfloat16), "dp", scatter_dimension=0, tiled=True).astype(
            jnp.float32
        ),
        lax.psum_scatter(d_up.astype(jnp.bfloat16), "dp", scatter_dimension=0, tiled=True).astype(
            jnp.float32
        ),
        lax.psum_scatter(d_down.astype(jnp.bfloat16), "dp", scatter_dimension=0, tiled=True).astype(
            jnp.float32
        ),
        lax.psum_scatter(
            d_gain_one.astype(jnp.bfloat16), "dp", scatter_dimension=0, tiled=True
        ).astype(jnp.float32),
        lax.psum_scatter(
            d_gain_two.astype(jnp.bfloat16), "dp", scatter_dimension=0, tiled=True
        ).astype(jnp.float32),
    )
    owned_mats = (
        lax.psum_scatter(
            row_sums[0].astype(jnp.bfloat16), "seq", scatter_dimension=1, tiled=True
        ).astype(jnp.float32),
        lax.psum_scatter(
            row_sums[1].astype(jnp.bfloat16), "seq", scatter_dimension=1, tiled=True
        ).astype(jnp.float32),
        lax.psum_scatter(
            row_sums[2].astype(jnp.bfloat16), "seq", scatter_dimension=1, tiled=True
        ).astype(jnp.float32),
        lax.psum_scatter(
            row_sums[3].astype(jnp.bfloat16), "seq", scatter_dimension=1, tiled=True
        ).astype(jnp.float32),
        lax.psum_scatter(
            row_sums[4].astype(jnp.bfloat16), "seq", scatter_dimension=1, tiled=True
        ).astype(jnp.float32),
        lax.psum_scatter(
            row_sums[5].astype(jnp.bfloat16), "seq", scatter_dimension=1, tiled=True
        ).astype(jnp.float32),
        lax.psum_scatter(
            row_sums[6].astype(jnp.bfloat16), "seq", scatter_dimension=1, tiled=True
        ).astype(jnp.float32),
    )
    owned_gains = lax.psum((row_sums[7], row_sums[8]), "seq")
    return (
        block_out,
        grad_inputs,
        owned_mats[0],
        owned_mats[1],
        owned_mats[2],
        owned_mats[3],
        owned_mats[4],
        owned_mats[5],
        owned_mats[6],
        owned_gains[0],
        owned_gains[1],
    )


SCRIPT = (
    ("start", 7), ("start", 14), ("start", 4), ("start", 1), ("start", 20), ("start", 0), ("start", 18),
    ("start", 16), ("start", 6), ("start", 3), ("start", 5), ("start", 9), ("start", 10), (0, 0, 0, 1),
    (0, 5, 0), (0, 4, 0, 1), (0, 3, 0, 1), (0, 9, 0, 1), ("start", 11), (0, 1, 0, 1), (0, 5, 1, 1),
    (0, 3, 0, 2), (0, 0, 0, 2), (0, 4, 0, 2), ("start", 19), (0, 20, 0), (0, 5, 1, 2), ("start", 2),
    (0, 4, 0, 3), (0, 0, 0, 3), ("start", 12), (0, 3, 0, 3), (0, 19, 0), ("start", 17), (0, 0, 1),
    (0, 14, 0, 1), ("start", 15), (0, 2, 0, 1), (0, 6, 0), ("start", 13), (0, 5, 1, 3), (0, 20, 1, 1),
    (0, 9, 0, 2), (0, 4, 1), (0, 9, 0, 3), (0, 2, 0, 2), (0, 3, 1), (0, 18, 0), (0, 19, 1, 1), (0, 20, 1, 2),
    ("start", 8), (0, 2, 0, 3), (0, 0, 2), (0, 1, 0, 2), (0, 18, 1, 1), (0, 9, 1), (0, 6, 1, 1), (0, 1, 0, 3),
    (0, 19, 1, 2), (0, 5, 2), (0, 2, 1), (0, 14, 0, 2), (0, 3, 2), (0, 8, 0), (0, 6, 1, 2), (0, 12, 0),
    (0, 19, 1, 3), (0, 17, 0), (0, 16, 0), (0, 20, 1, 3), (0, 13, 0, 1), "norm", (0, 6, 1, 3), (0, 8, 1, 1),
    (0, 18, 1, 2), (0, 7, 0), (0, 14, 0, 3), (0, 18, 1, 3), (0, 2, 2), (0, 17, 1, 1), (0, 17, 1, 2),
    (0, 7, 1, 1), (0, 1, 1), (0, 4, 2), (0, 17, 1, 3), (0, 6, 2), (0, 14, 1), (0, 19, 2), (0, 11, 0),
    (0, 10, 0, 1), (0, 10, 0, 2), (0, 15, 0), (0, 7, 1, 2), "value", (0, 9, 2), (0, 10, 0, 3), (0, 18, 2),
    (0, 1, 2), (0, 8, 1, 2), (0, 7, 1, 3), (0, 13, 0, 2), (0, 13, 0, 3), (0, 11, 1, 1), "key", (0, 8, 1, 3),
    (0, 14, 2), "query", ("see", 0), (0, 20, 2), (0, 13, 1), ("see", 1), (0, 16, 1, 1), (0, 10, 1),
    (0, 12, 1, 1), (0, 17, 2), (0, 15, 1, 1), ("see", 2), (0, 7, 2), (0, 8, 2), ("see", 3), (0, 11, 1, 2),
    ("hidden", 0), (0, 15, 1, 2), (0, 11, 1, 3), (0, 12, 1, 2), ("hidden", 1), (0, 16, 1, 2), (0, 13, 2),
    "project", (0, 15, 1, 3), (0, 16, 1, 3), (0, 10, 2), ("mlp", 0), (0, 12, 1, 3), (0, 11, 2), ("mlp", 1),
    ("up", 0), ("gate", 0), (0, 15, 2), ("gate", 1), ("up", 1), (0, 12, 2), (0, 16, 2), ("mlp", 2),
    ("mlp", 3), ("gate", 2), (1, 8, 0), ("dh2", 0), ("up", 2), ("up", 3), (1, 5, 0), (1, 4, 0), ("gate", 3),
    (1, 8, 1), (1, 9, 0), (1, 10, 0), "mix", "down", (1, 5, 1), ("dh2", 1), (1, 9, 1), "norm2", (1, 11, 0),
    "heads", "out", ("attend", 0), (1, 3, 0), ("attend", 1), (1, 6, 0), (1, 4, 1), ("attend", 2), (1, 1, 0),
    ("attend", 3), (1, 2, 0), (1, 7, 0), (1, 0, 0), (1, 6, 1), ("qkv", 0), "dh1", (1, 8, 2), (1, 7, 1),
    ("qkv", 1), (1, 3, 1), (1, 9, 2), (1, 13, 0), (1, 15, 0), (1, 1, 1), (1, 14, 0), (1, 0, 1), "norm1",
    (1, 5, 2), (1, 3, 2), ("qkv", 2), (1, 12, 0), (1, 14, 1), "gains", (1, 2, 1), (1, 17, 0), (1, 15, 1),
    (1, 13, 1), (1, 16, 0), (1, 1, 2), (1, 12, 1), (1, 6, 2), (1, 19, 0), (1, 2, 2), (1, 10, 1), (1, 17, 1),
    (1, 18, 0), (1, 0, 2), (1, 15, 2), (1, 16, 1), (1, 20, 0), (1, 12, 2), (1, 19, 1), (1, 13, 2), (1, 11, 1),
    (1, 7, 2), (1, 14, 2), (1, 10, 2), (1, 20, 1), (1, 17, 2), (1, 18, 1), (1, 16, 2), (1, 20, 2), (1, 19, 2),
    (1, 4, 2), (1, 11, 2), (1, 18, 2),
)


MESH = pl.DeviceIdType.MESH
NZ, NY, NX = 4, 2, 2
SEQUENCE = {"zfx": "zxy", "zfy": "zyx", "zmx": "xzy", "zmy": "yzx"}
ALL_Z, ALL_Y, ALL_X = pl.ds(0, NZ), pl.ds(0, NY), pl.ds(0, NX)


class Plan:
    def __init__(self, tensors):
        self.tensors = tensors
        self.items, self.of_tensor = [], []
        for t, (_, _, _, cuts) in enumerate(tensors):
            begin, mine = 0, []
            for kind, along, count in cuts:
                mine.append(len(self.items))
                whole = [(0, tensors[t][0]), (0, tensors[t][1])]
                whole[along] = (begin, count)
                self.items.append((t, SEQUENCE[kind], *whole))
                begin += count
            self.of_tensor.append(mine)


class Place:
    def __init__(self):
        self.c, self.s = lax.axis_index("dp"), lax.axis_index("seq")
        self.z, self.y, self.x = self.c // 4, (self.c // 2) % 2, self.c % 2

    def at(self, z, y, x):
        return (z * 4 + y * 2 + x, self.s)

    def to_x(self):
        return self.at(self.z, self.y, 1 - self.x)

    def to_y(self):
        return self.at(self.z, 1 - self.y, self.x)

    def to_z(self, step):
        return self.at((self.z + step) % NZ, self.y, self.x)

    def to_core(self):
        return (self.c, 1 - self.s)

    def greet(self):
        barrier = pltpu.get_barrier_semaphore()
        peers = [self.to_x(), self.to_y(), self.to_core()] + [self.to_z(k) for k in (1, 2, 3)]
        for peer in peers:
            pl.semaphore_signal(barrier, inc=1, device_id=peer, device_id_type=MESH)
        pl.semaphore_wait(barrier, len(peers))


def remote(src, dst, send, recv, device):
    return pltpu.make_async_remote_copy(
        src_ref=src, dst_ref=dst, send_sem=send, recv_sem=recv, device_id=device, device_id_type=MESH
    )


def slots(seq, count, along_z):
    firsts, used = [], 0
    for phase in range(count):
        firsts.append(used)
        used += along_z if phase < 3 and seq[phase] == "z" else 1
    return firsts


class Gather:
    def __init__(self, plan, place, shards, bufs, send, recv, local):
        self.plan, self.me, self.shards, self.bufs = plan, place, shards, bufs
        self.send, self.recv, self.local = send, recv, local

    def own_copy(self, t):
        me = self.me
        return pltpu.make_async_copy(
            self.shards[t], self.bufs[t].at[me.s, me.z, me.y, me.x], self.local.at[t]
        )

    def moves(self, i, phase):
        t, seq, rows, cols = self.plan.items[i]
        me, buf = self.me, self.bufs[t]
        rows, cols = pl.ds(*rows), pl.ds(*cols)

        def view(z, y, x, half=me.s):
            return buf.at[half, z, y, x, rows, cols]

        if phase == 3:
            whole = view(ALL_Z, ALL_Y, ALL_X)
            return [(whole, whole, me.to_core(), view(ALL_Z, ALL_Y, ALL_X, 1 - me.s), 0)]
        done, axis = seq[:phase], seq[phase]
        z = ALL_Z if "z" in done else me.z
        y = ALL_Y if "y" in done else me.y
        x = ALL_X if "x" in done else me.x
        there = view(z, y, x)
        here = self.shards[t].at[rows, cols] if phase == 0 else there
        if axis == "x":
            return [(here, there, me.to_x(), view(z, y, 1 - me.x), 0)]
        return [(here, there, me.to_y(), view(z, 1 - me.y, x), 0)]

    def hops(self, i, phase, hop):
        t, seq, rows, cols = self.plan.items[i]
        me, buf = self.me, self.bufs[t]
        rows, cols = pl.ds(*rows), pl.ds(*cols)
        done = seq[:phase]
        y = ALL_Y if "y" in done else me.y
        x = ALL_X if "x" in done else me.x
        moves = []
        for k, way in enumerate((1, -1)):
            first, last = (me.z, NZ - 1 - me.z) if way == 1 else (NZ - 1 - me.z, me.z)
            sends = (first >= hop - 1) & (last >= 1)
            takes = first >= hop
            z = me.z - way * (hop - 1)
            there = buf.at[me.s, z, y, x, rows, cols]
            here = self.shards[t].at[rows, cols] if phase == 0 and hop == 1 else there
            arrived = buf.at[me.s, me.z - way * hop, y, x, rows, cols]
            moves.append((sends, takes, here, there, me.at(me.z + way, me.y, me.x), arrived, 3 * k + hop - 1))
        return moves

    def along_z(self, i, phase):
        return phase < 3 and self.plan.items[i][1][phase] == "z"

    def copy(self, i, phase, src, dst, device, k):
        at = 9 * i + slots(self.plan.items[i][1], 4, 6)[phase] + k
        return remote(src, dst, self.send.at[at], self.recv.at[at], device)

    def send_hop(self, i, phase, hop):
        for sends, _, here, there, device, _, k in self.hops(i, phase, hop):

            @pl.when(sends)
            def _(here=here, there=there, device=device, k=k):
                self.copy(i, phase, here, there, device, k).start()

    def take_hop(self, i, phase, hop):
        for _, takes, _, _, device, arrived, k in self.hops(i, phase, hop):

            @pl.when(takes)
            def _(device=device, arrived=arrived, k=k):
                self.copy(i, phase, arrived, arrived, device, k).wait_recv()

        if hop < NZ - 1:
            self.send_hop(i, phase, hop + 1)

    def start(self, i, phase):
        if self.along_z(i, phase):
            self.send_hop(i, phase, 1)
            return
        for here, there, device, _, k in self.moves(i, phase):
            self.copy(i, phase, here, there, device, k).start()

    def wait(self, i, phase):
        for _, _, device, arrived, k in self.moves(i, phase):
            self.copy(i, phase, arrived, arrived, device, k).wait_recv()

    def finish(self, i):
        for phase in range(4):
            if self.along_z(i, phase):
                for hop in range(1, NZ):
                    for sends, _, here, there, device, _, k in self.hops(i, phase, hop):

                        @pl.when(sends)
                        def _(here=here, there=there, device=device, k=k):
                            self.copy(i, phase, here, there, device, k).wait_send()

                continue
            for here, there, device, _, k in self.moves(i, phase):
                self.copy(i, phase, here, there, device, k).wait_send()


def got_shapes(plan):
    shapes = []
    for t, seq, (_, rows), (_, columns) in plan.items:
        dtype = plan.tensors[t][2]
        second, third = ((1, NZ), (3,)) if seq[0] == "z" else ((3, 2), (1,))
        shapes.append([(d + (rows, columns), dtype) for d in ((NZ, 2), second, third)])
    return shapes


class Scatter:
    def __init__(self, plan, place, total, got, out, send, recv):
        self.plan, self.me, self.total, self.got, self.out = plan, place, total, got, out
        self.send, self.recv = send, recv

    def moves(self, i, phase):
        t, seq, rows, cols = self.plan.items[i]
        me, total, got = self.me, self.total[t], self.got[i][phase]
        rows, cols = pl.ds(*rows), pl.ds(*cols)
        axis, done = seq[2 - phase], seq[3 - phase :]
        z = me.z if "z" in done else ALL_Z
        y = me.y if "y" in done else ALL_Y
        x = me.x if "x" in done else ALL_X
        if phase == 0:
            lands = [got]
        else:
            lands = [got.at[k] for k in range(got.shape[0])]
        if axis == "x":
            return [(total.at[z, y, 1 - me.x, rows, cols], lands[0], me.to_x(), 0)]
        if axis == "y":
            return [(total.at[z, 1 - me.y, x, rows, cols], lands[0], me.to_y(), 0)]
        return [
            (total.at[(me.z + k) % NZ, y, x, rows, cols], lands[k - 1], me.to_z(k), k - 1)
            for k in (1, 2, 3)
        ]

    def copy(self, i, phase, src, dst, device, k):
        at = 5 * i + slots(self.plan.items[i][1][::-1], 3, 3)[phase] + k
        return remote(src, dst, self.send.at[at], self.recv.at[at], device)

    def start(self, i, phase):
        for here, there, device, k in self.moves(i, phase):
            self.copy(i, phase, here, there, device, k).start()

    def wait(self, i, phase):
        for here, there, device, k in self.moves(i, phase):
            self.copy(i, phase, there, there, device, k).wait_recv()

    def add(self, i, phase):
        t, seq, rows, cols = self.plan.items[i]
        me, total, got = self.me, self.total[t], self.got[i][phase]
        rows, cols = pl.ds(*rows), pl.ds(*cols)
        if phase == 0:
            for z in range(NZ):
                for o in range(2):
                    at = (z, me.y, o) if seq[2] == "y" else (z, o, me.x)
                    total[at + (rows, cols)] += got[z, o]
        elif phase == 1 and seq[1] != "z":
            for z in range(NZ):
                total[z, me.y, me.x, rows, cols] += got[0, z]
        elif phase == 1:
            for o in range(2):
                at = (me.z, me.y, o) if seq[2] == "y" else (me.z, o, me.x)
                part = total[at + (rows, cols)].astype(jnp.float32)
                for k in range(3):
                    part += got[k, o].astype(jnp.float32)
                total[at + (rows, cols)] = part.astype(total.dtype)
        else:
            part = total[me.z, me.y, me.x, rows, cols].astype(jnp.float32)
            for k in range(got.shape[0]):
                part += got[k].astype(jnp.float32)
            self.out[t][rows, cols] = part

    def finish(self, i):
        for phase in range(3):
            for here, there, device, k in self.moves(i, phase):
                self.copy(i, phase, here, there, device, k).wait_send()


EPS = 1e-05
PAIR = 2 * HEAD_DIM
SPAN = 2 * WINDOW
LOW = jnp.bfloat16
F32 = jnp.float32


def mm(left, right):
    return jnp.dot(left, right, preferred_element_type=F32)


def mm_nt(left, right):
    return lax.dot_general(left, right, (((1,), (1,)), ((), ())), preferred_element_type=F32)


def mm_tn(left, right):
    return lax.dot_general(left, right, (((0,), (0,)), ((), ())), preferred_element_type=F32)


def column_tiles(columns, size):
    full = columns // size
    tiles = [(0, size, full)]
    if columns % size:
        tiles.append((full * size, columns % size, 1))
    return tiles


def each_tile(columns, size, body):
    for begin, width, count in column_tiles(columns, size):
        if count == 1:
            body(begin, width)
        else:

            def step(j, _, begin=begin, width=width):
                body(pl.multiple_of(begin + j * width, 128), width)
                return 0

            lax.fori_loop(0, count, step, 0)


def each_rows(rows, size, body):
    def step(j, _):
        body(pl.ds(pl.multiple_of(j * size, size), size))
        return 0

    lax.fori_loop(0, rows // size, step, 0)


def both_heads(block):
    first = lax.broadcasted_iota(jnp.int32, block.shape, 1) < HEAD_DIM
    zero = jnp.zeros_like(block)
    return jnp.concatenate([jnp.where(first, block, zero), jnp.where(first, zero, block)], axis=0)


def merge_heads(stacked):
    rows = stacked.shape[0] // 2
    first = lax.broadcasted_iota(jnp.int32, (rows, PAIR), 1) < HEAD_DIM
    return jnp.where(first, stacked[:rows], stacked[rows:])


VMEM_LIMIT = 64 * 2**20


class Stream:
    def __init__(self, count, sems, fetch):
        self.count, self.sems, self.fetch = count, sems, fetch

    def copies(self, j, slot):
        return [
            pltpu.make_async_copy(src, dst, self.sems.at[slot, k])
            for k, (src, dst) in enumerate(self.fetch(j, slot))
        ]

    def prime(self):
        for copy in self.copies(0, 0):
            copy.start()

    def run(self, body, first=0, last=None):
        def step(j, _):
            slot = j % 2

            @pl.when(j + 1 < self.count)
            def _():
                for copy in self.copies(j + 1, 1 - slot):
                    copy.start()

            for copy in self.copies(j, slot):
                copy.wait()
            body(j, slot)
            return 0

        lax.fori_loop(first, self.count if last is None else last, step, 0)


def block_kernel(ahead, back, *refs):
    n = len(ahead.tensors)
    (lens, x_h, dy_h), raw, refs = refs[:3], refs[3 : 3 + n], refs[3 + n :]
    hbm_bufs, refs = refs[: n - 1], refs[n - 1 :]
    (mixed_o, gtok_o, q_h, p_h, ha_h, ho_h, hm_h, hid_h), refs = refs[:8], refs[8:]
    outs, refs = refs[:n], refs[n:]
    total, refs = refs[:n], refs[n:]
    count = len(back.items)
    got, refs = [refs[3 * i : 3 * i + 3] for i in range(count)], refs[3 * count :]
    (gate_pad, up_pad, down_pad, gain_buf, gains, xb, h1, da, db, kx, vx, o, x1, hid), refs = refs[:14], refs[14:]
    (dar, dbr), refs = refs[:2], refs[2:]
    (dy, dyr, dh, dxr_r, turned, pool, broad), refs = refs[:7], refs[7:]
    (kc, vc, rim_k, rim_v, gain_sum, gain_other), refs = refs[:6], refs[6:]
    (a_send, a_recv, own_sem, b_send, b_recv, load_sem, pool_sem, broad_sem, turn_sem), refs = refs[:9], refs[9:]
    half_send, half_recv = refs
    rows, width = xb.shape
    wide, columns = ahead.tensors[5][1], ahead.tensors[1][1]
    chips = NZ * NY * NX
    me = Place()
    halves, loads, later = {}, [0], {}

    def load(src, dst):
        copy = pltpu.make_async_copy(src, dst, load_sem.at[loads[0]])
        loads[0] += 1
        copy.start()
        return copy

    def to_partner(k, src, dst):
        copy = remote(src, dst, half_send.at[k], half_recv.at[k], me.to_core())
        copy.start()
        halves[k] = copy
        return copy

    def own(size, side=0):
        return pl.ds(pl.multiple_of((me.s if side == 0 else 1 - me.s) * size, 128), size)

    get_x, get_dy = load(x_h, xb), load(dy_h, dy)
    me.greet()
    shards = list(raw[:5]) + [gate_pad, up_pad, down_pad]
    bufs = [gain_buf] + list(hbm_bufs)
    flat = [b.reshape(2, chips * b.shape[4], b.shape[5]) for b in bufs]
    gather = Gather(ahead, me, shards, bufs, a_send, a_recv, own_sem)
    scatter = Scatter(back, me, total, got, outs, b_send, b_recv)
    ready = set()

    def pad_shards():
        part, tile = raw[7].shape[0], down_pad.shape[0]
        zero = jnp.zeros((raw[5].shape[0], tile - part), LOW)
        for src, dst in ((raw[5], gate_pad), (raw[6], up_pad)):
            value, pieces = src[...], []
            for k in range(value.shape[1] // part):
                pieces += [value[:, k * part : (k + 1) * part], zero]
            dst[...] = jnp.concatenate(pieces, axis=1)
        down_pad[...] = jnp.concatenate([raw[7][...], jnp.zeros((tile - part, down_pad.shape[1]), LOW)], axis=0)

    def prepare(t):
        if t >= 5 and 5 not in ready:
            pad_shards()
            for k in range(5, n):
                gather.own_copy(k).start()
                ready.add(k)
        elif t not in ready:
            gather.own_copy(t).start()
            ready.add(t)

    landed, arrived = set(), set()

    def land(t):
        if t not in landed:
            landed.add(t)
            gather.own_copy(t).wait()

    def need(*tensors, part=None):
        for t in tensors:
            mine = ahead.of_tensor[t]
            for i in mine if part is None else mine[part : part + 1]:
                if i not in arrived:
                    arrived.add(i)
                    gather.wait(i, 3)

    def norm(values, gain):
        inverse = lax.rsqrt(jnp.mean(values * values, axis=-1, keepdims=True) + EPS)
        return (values * inverse * gain).astype(LOW)

    def share(name, k, mine, whole):
        to = whole.at[:, own(rows)]
        later[name] = (load(mine, to), to_partner(k, mine, to))

    def shared(name):
        copy, sent = later[name]
        copy.wait()
        sent.wait()

    def turn(src, dst, lane):
        def body(j, _):
            at = pl.ds(pl.multiple_of(j * 128, 128), 128)
            dst[at, pl.ds(lane, rows)] = src[:, at].T
            return 0

        lax.fori_loop(0, src.shape[1] // 128, body, 0)
        return dst.at[:, pl.ds(lane, rows)]

    def first_norm():
        need(0)
        get_dy.wait()
        later["dy"] = to_partner(0, dy.at[:, own(columns, 1)], dyr)
        parts = []
        for z in range(NZ):
            for y in range(NY):
                pair = [gain_buf[me.s, z, y, x].astype(F32) for x in range(NX)]
                parts.append(pair[0] + pair[1])
        gains[...] = jnp.concatenate(parts, axis=1)[0:8]
        get_x.wait()

        def body(at):
            h1[at, :] = norm(xb[at, :].astype(F32), gains[0:1, :])

        each_rows(rows, 64, body)
        share("ha", 1, turn(h1, turned.at[0], 0), ha_h)

    def project(t, src, store):
        need(t)
        tiles = Stream(2, pool_sem, lambda j, slot: [(flat[t].at[j], pool.at[slot, pl.ds(0, width), :])])
        tiles.prime()

        def body(side, slot):
            for begin in range(0, columns, 256):
                part = mm(src[...], pool[slot, :width, begin : begin + 256])
                store(pl.ds(pl.multiple_of(side * columns + begin, 128), 256), part)

        tiles.run(body)

    def rim(k, ref):
        to = ref.at[pl.ds(0, WINDOW), :]
        return remote(ref.at[pl.ds(rows, WINDOW), :], to, half_send.at[2 + k], half_recv.at[2 + k], me.to_core())

    def put_into(ref, skip):
        def store(cols, part):
            ref[pl.ds(skip, rows), cols] = part.astype(LOW)

        return store

    def do_query():
        project(1, h1, put_into(da, 0))
        later["q_out"] = load(da.at[:, pl.ds(0, width)], q_h)

    def do_key():
        project(2, h1, put_into(kx, WINDOW))
        rim(0, kx).start()

    def do_value():
        project(3, h1, put_into(vx, WINDOW))
        rim(1, vx).start()

    first_end = lens[0, 0]
    second_end = first_end + lens[0, 1]

    def attend(b, _):
        base = me.s * rows + b * WINDOW
        at = pl.ds(pl.multiple_of(b * WINDOW, WINDOW), WINDOW)
        over = pl.ds(pl.multiple_of(b * WINDOW, WINDOW), SPAN)
        row = lax.broadcasted_iota(jnp.int32, (WINDOW, SPAN), 0)
        col = lax.broadcasted_iota(jnp.int32, (WINDOW, SPAN), 1)
        q_pos, k_pos = base + row, base - WINDOW + col

        def doc(pos):
            return (pos >= first_end).astype(jnp.int32) + (pos >= second_end).astype(jnp.int32)

        visible = (col >= row) & (col <= row + WINDOW) & (k_pos >= 0) & (doc(q_pos) == doc(k_pos))
        bias = jnp.where(visible, 0.0, -1e30)
        bias = jnp.concatenate([bias, bias], axis=0)
        pairs = range(HEADS // 2)
        cols = [slice(p * PAIR, (p + 1) * PAIR) for p in pairs]
        queries = [both_heads(da[at, c]) for c in cols]
        keys, values = [kx[over, c] for c in cols], [vx[over, c] for c in cols]
        scores = [mm_nt(q2, k) * HEAD_DIM ** (-0.5) + bias for q2, k in zip(queries, keys)]
        tops = [jnp.max(s, axis=-1, keepdims=True) for s in scores]
        exps = [jnp.exp(s - top) for s, top in zip(scores, tops)]
        sums = [jnp.sum(e, axis=-1, keepdims=True) for e in exps]
        weights = [(e * (1.0 / t)).astype(LOW) for e, t in zip(exps, sums)]
        parts = [merge_heads(mm(w, v)).astype(LOW) for w, v in zip(weights, values)]
        for p, c, w, part in zip(pairs, cols, weights, parts):
            db[at, 2 * p * SPAN : (2 * p + 1) * SPAN] = w[:WINDOW]
            db[at, (2 * p + 1) * SPAN : (2 * p + 2) * SPAN] = w[WINDOW:]
            o[at, c] = part
        return 0

    quarter = rows // WINDOW // 4

    def attend_part(k):
        if k == 0:
            for j, ref in ((0, kx), (1, vx)):
                rim(j, ref).wait_recv()
        lax.fori_loop(k * quarter, (k + 1) * quarter, attend, 0)
        if k == 3:
            later["p_out"] = load(db.at[:, pl.ds(0, HEADS * SPAN)], p_h)
            share("ho", 4, turn(o, turned.at[0], rows), ho_h)

    def add_out():
        def store(cols, part):
            x1[:, cols] = xb[:, cols].astype(F32) + part

        project(4, o, store)

        def body(at):
            xb[at, :] = norm(x1[at, :], gains[1:2, :])

        each_rows(rows, 64, body)
        share("hm", 5, turn(xb, turned.at[1], rows), hm_h)

    strips = [ahead.items[i][3] for i in ahead.of_tensor[5]]

    def strip_copies(p, side):
        begin, size = strips[p]
        return [
            pltpu.make_async_copy(
                flat[5 + k].at[side, :, pl.ds(begin, size)],
                pool.at[side, pl.ds(k * width, width), pl.ds(0, size)],
                pool_sem.at[side, k],
            )
            for k in range(2)
        ]

    def mlp(p):
        need(5, 6, part=p)
        for side in range(2):
            for copy in strip_copies(p, side):
                copy.start()
        if p == 0:
            later["p_out"].wait()
            for name in ("ha", "ho", "hm"):
                shared(name)
            later["hm"] = load(hm_h, turned.at[0])
        if p >= 2:
            for side in range(2):
                shared(("hid", p - 2, side))
        begin, size = strips[p]
        for side in range(2):
            for copy in strip_copies(p, side):
                copy.wait()
            for skip in range(0, size, 256):
                w = min(256, size - skip)
                cols = slice(skip, skip + w)
                a = mm(xb[...], pool[side, :width, cols])
                b = mm(xb[...], pool[side, width : 2 * width, cols])
                sig = 1.0 / (1.0 + jnp.exp(-a))
                silu = a * sig
                at = slice(side * wide + begin + skip, side * wide + begin + skip + w)
                grad = da[:, at].astype(F32)
                db[:, at] = (grad * silu).astype(LOW)
                da[:, at] = (grad * b * sig * (1.0 + a * (1.0 - sig))).astype(LOW)
                hidden_low = (silu * b).astype(LOW)
                hid[side, :, begin + skip : begin + skip + w] = hidden_low
                first = p % 2 * 512 + skip
                turned[1, first : first + w, side * rows : (side + 1) * rows] = hidden_low.T
        across = pl.ds(pl.multiple_of((1 - me.s) * wide + begin, 128), size)
        here = pl.ds(begin, size)
        later["db", p] = to_partner(6 + 4 * p, db.at[:, across], dbr.at[:, here])
        later["da", p] = to_partner(7 + 4 * p, da.at[:, across], dar.at[:, here])
        for side in range(2):
            mine = turned.at[1, pl.ds(p % 2 * 512, size), pl.ds(side * rows, rows)]
            share(("hid", p, side), 8 + 4 * p + side, mine, hid_h.at[pl.ds(side * wide + begin, size), :])
        if p == len(strips) - 1:
            mlp_tiles.prime()

    tall = back.tensors[0][0] * NY * NX
    hid_tiles = Stream(
        NZ, turn_sem, lambda j, slot: [(hid_h.at[pl.ds(pl.multiple_of(j * tall, 16), tall), :], turned.at[slot, pl.ds(0, tall), :])]
    )
    tile, thin = 256, 128
    small = pool.reshape(2, pool.shape[1] // tile, tile, columns)

    def row_tiles(w, size, dst):
        return lambda j, slot: (w.at[:, pl.ds(pl.multiple_of(j * size, size), size), :], dst(slot))

    def small_at(k):
        return lambda slot: small.at[slot, pl.ds(2 * k, 2)]

    def broad_at(k):
        return lambda slot: broad.at[slot, k]

    def stream_of(fetchers, count, sems):
        return Stream(count, sems, lambda j, slot: [f(j, slot) for f in fetchers])

    down_tiles = stream_of([row_tiles(flat[7], tile, small_at(0))], flat[7].shape[1] // tile, pool_sem)
    mlp_tiles = stream_of([row_tiles(flat[5 + k], thin, broad_at(k)) for k in range(2)], width // thin, broad_sem)
    out_tiles = stream_of([row_tiles(flat[4], tile, small_at(0))], width // tile, pool_sem)
    qkv_tiles = stream_of([row_tiles(flat[1 + k], tile, small_at(k)) for k in range(3)], width // tile, pool_sem)

    def begin_scatter(t):
        for i in back.of_tensor[t]:
            scatter.start(i, 0)

    def put(t, z, part, cols=slice(None)):
        low = part.reshape(NY, NX, back.tensors[t][0], part.shape[1]).astype(total[t].dtype)
        total[t][z, :, :, :, cols] = low

    def grad_down():
        for p in range(len(strips)):
            for side in range(2):
                if p + 2 >= len(strips):
                    shared(("hid", p, side))
        later["dy"].wait_recv()
        hid_tiles.prime()

        def body(z, slot):
            mine = mm(turned[slot, :tall, own(rows)], dy[:, own(columns)])
            put(0, z, mine + mm(turned[slot, :tall, own(rows, 1)], dyr[...]))

        hid_tiles.run(body)
        begin_scatter(0)
        later["ha"] = load(ha_h, turned.at[0])
        later["ho"] = load(ho_h, turned.at[1])

    def add_down():
        tiles2 = Stream(2, pool_sem, lambda j, slot: [(flat[7].at[j], pool.at[slot])])
        tiles2.prime()

        def body(side, slot):
            for begin in range(0, columns, 256):
                part = mm(hid[0], pool[slot, :wide, begin : begin + 256])
                part += mm(hid[1], pool[slot, wide:, begin : begin + 256])
                cols = pl.ds(pl.multiple_of(side * columns + begin, 128), 256)
                xb[:, cols] = (x1[:, cols] + part).astype(LOW)

        tiles2.run(body)
        later["mixed"] = load(xb, mixed_o)

    def hidden_body(j, slot):
        part = mm_nt(dy[:, :columns], small[slot, 0]) + mm_nt(dy[:, columns:], small[slot, 1])
        da[:, pl.ds(pl.multiple_of(j * tile, tile), tile)] = part.astype(LOW)

    def hidden(k):
        middle = down_tiles.count // 2
        if k == 0:
            need(7)
            down_tiles.prime()
            later["q_out"].wait()
            down_tiles.run(hidden_body, 0, middle)
            return
        down_tiles.run(hidden_body, middle)

    def weight_grad_to(t, slot, mine, theirs, cols=slice(None)):
        row_count = back.tensors[t][0] * NY * NX

        def step(z, _):
            at = pl.ds(pl.multiple_of(z * row_count, 16), row_count)
            put(t, z, mm(turned[slot, at, own(rows)], mine()) + mm(turned[slot, at, own(rows, 1)], theirs()), cols)
            return 0

        lax.fori_loop(0, NZ, step, 0)

    def grad_strip(t, name, grad, other, p):
        begin, size = strips[p]
        if p == 0 and t == 1:
            later["hm"].wait()
        later[name, p].wait_recv()
        cols = slice(begin, begin + size)
        mine = pl.ds(pl.multiple_of(me.s * wide + begin, 128), size)
        weight_grad_to(t, 0, lambda: grad[:, mine], lambda: other[:, cols], cols)
        scatter.start(back.of_tensor[t][p], 0)

    def dh2_body(j, slot):
        part = None
        for k, grad in ((0, da), (1, db)):
            for side in range(2):
                term = mm_nt(grad[:, side * wide : (side + 1) * wide], broad[slot, k, side])
                part = term if part is None else part + term
        dh[:, pl.ds(pl.multiple_of(j * thin, thin), thin)] = part

    def grad_norm2(k):
        middle = mlp_tiles.count // 2
        if k == 0:
            mlp_tiles.run(dh2_body, 0, middle)
            return
        mlp_tiles.run(dh2_body, middle)
        for p in range(len(strips)):
            later["db", p].wait_send()
            later["da", p].wait_send()
        out_tiles.prime()
        later["q"] = load(q_h, da.at[:, pl.ds(0, width)])
        later["p"] = load(p_h, db.at[:, pl.ds(0, HEADS * SPAN)])
        later["mixed"].wait()
        later["x"] = load(x_h, xb)

    def norm_grad(values, grad_norm, gain):
        inverse = lax.rsqrt(jnp.mean(values * values, axis=-1, keepdims=True) + EPS)
        scaled = grad_norm * gain
        mean_term = jnp.mean(values * scaled, axis=-1, keepdims=True)
        back_part = inverse * scaled - values * (inverse * inverse * inverse) * mean_term
        return back_part, jnp.sum(values * inverse * grad_norm, axis=0, keepdims=True)

    def norm2_body(at):
        back_part, gain_part = norm_grad(x1[at, :], dh[at, :], gains[1:2, :])
        gain_sum[1:2, :] += gain_part
        grad = dy[at, :].astype(F32) + back_part
        x1[at, :] = grad
        h1[at, :] = grad.astype(LOW)

    def norm2():
        gain_sum[...] = jnp.zeros_like(gain_sum)
        each_rows(rows, 64, norm2_body)
        later["dxr"] = to_partner(22, h1.at[:, own(columns, 1)], dxr_r)

    def out_body(j, slot):
        part = mm_nt(h1[:, :columns], small[slot, 0]) + mm_nt(h1[:, columns:], small[slot, 1])
        o[:, pl.ds(pl.multiple_of(j * tile, tile), tile)] = part.astype(LOW)

    def grad_heads():
        out_tiles.run(out_body)
        qkv_tiles.prime()

    def grad_out():
        later["ho"].wait()
        later["dxr"].wait_recv()
        weight_grad_to(3, 1, lambda: h1[:, own(columns)], lambda: dxr_r[...])
        begin_scatter(3)

    scale = HEAD_DIM ** (-0.5)

    def attend_back(b, _):
        at = pl.ds(pl.multiple_of(b * WINDOW, WINDOW), WINDOW)
        over = pl.ds(pl.multiple_of(b * WINDOW, WINDOW), SPAN)
        pairs = range(HEADS // 2)
        cols = [slice(p * PAIR, (p + 1) * PAIR) for p in pairs]
        queries, grads = [both_heads(da[at, c]) for c in cols], [both_heads(o[at, c]) for c in cols]
        keys, values = [kx[over, c] for c in cols], [vx[over, c] for c in cols]
        lows = [
            jnp.concatenate([db[at, (2 * p + h) * SPAN : (2 * p + h + 1) * SPAN] for h in range(2)], axis=0)
            for p in pairs
        ]
        carry_k, carry_v = [kc[:, c] for c in cols], [vc[:, c] for c in cols]
        probs = [low.astype(F32) for low in lows]
        grad_probs = [mm_nt(g, v) for g, v in zip(grads, values)]
        grad_values = [mm_tn(low, g) for low, g in zip(lows, grads)]
        inners = [jnp.sum(p * g, axis=-1, keepdims=True) for p, g in zip(probs, grad_probs)]
        scores = [(p * (g - i)).astype(LOW) for p, g, i in zip(probs, grad_probs, inners)]
        grad_queries = [(merge_heads(mm(s, k)) * scale).astype(LOW) for s, k in zip(scores, keys)]
        grad_keys = [mm_tn(s, q2) * scale for s, q2 in zip(scores, queries)]
        new_k = [(old + g[:WINDOW]).astype(LOW) for old, g in zip(carry_k, grad_keys)]
        new_v = [(old + g[:WINDOW]).astype(LOW) for old, g in zip(carry_v, grad_values)]
        for c, gq, gk, gv, nk, nv in zip(cols, grad_queries, grad_keys, grad_values, new_k, new_v):
            da[at, c] = gq
            kx[at, c] = nk
            vx[at, c] = nv
            kc[:, c] = gk[WINDOW:]
            vc[:, c] = gv[WINDOW:]
        return 0

    own_rows = pl.ds(WINDOW, rows)
    qr, kr, vr = dar.at[:, pl.ds(0, columns)], dar.at[:, pl.ds(columns, columns)], dbr.at[:, pl.ds(0, columns)]

    def attend_back_part(k):
        if k == 0:
            kc[...] = jnp.zeros_like(kc)
            vc[...] = jnp.zeros_like(vc)
            for j, ref in ((0, kx), (1, vx)):
                rim(j, ref).wait_send()
            later["q"].wait()
            later["p"].wait()
        lax.fori_loop(k * quarter, (k + 1) * quarter, attend_back, 0)
        if k == 0:
            later["rim"] = [
                to_partner(23, kx.at[pl.ds(0, WINDOW), :], rim_k),
                to_partner(24, vx.at[pl.ds(0, WINDOW), :], rim_v),
            ]
        if k == 3:
            for copy, ref, carry, rim_in in ((later["rim"][0], kx, kc, rim_k), (later["rim"][1], vx, vc, rim_v)):
                copy.wait_recv()
                ref[pl.ds(rows, WINDOW), :] = (carry[...] + rim_in[...].astype(F32)).astype(LOW)
            later["dq"] = to_partner(25, da.at[:, own(columns, 1)], qr)
            later["dk"] = to_partner(26, kx.at[own_rows, own(columns, 1)], kr)
            later["dv"] = to_partner(27, vx.at[own_rows, own(columns, 1)], vr)

    def grad_qkv(k):
        if k == 0:
            later["ha"].wait()
        later[("dq", "dk", "dv")[k]].wait_recv()
        mine = (lambda: da[:, own(columns)], lambda: kx[own_rows, own(columns)], lambda: vx[own_rows, own(columns)])[k]
        theirs = (qr, kr, vr)[k]
        weight_grad_to(4 + k, 0, mine, lambda: theirs[...])
        begin_scatter(4 + k)

    def dh1_body(j, slot):
        part = None
        for k, (grad, skip) in enumerate(((da, 0), (kx, WINDOW), (vx, WINDOW))):
            for side in range(2):
                left = grad[pl.ds(skip, rows), side * columns : (side + 1) * columns]
                term = mm_nt(left, small[slot, 2 * k + side])
                part = term if part is None else part + term
        dh[:, pl.ds(pl.multiple_of(j * tile, tile), tile)] = part

    def grad_norm1():
        qkv_tiles.run(dh1_body)

    def norm1_body(at):
        back_part, gain_part = norm_grad(xb[at, :].astype(F32), dh[at, :], gains[0:1, :])
        gain_sum[0:1, :] += gain_part
        x1[at, :] = x1[at, :] + back_part

    def norm1():
        later["x"].wait()
        each_rows(rows, 64, norm1_body)
        later["gtok"] = load(x1, gtok_o)
        later["gain"] = to_partner(28, gain_sum, gain_other)

    def grad_gains():
        later["gain"].wait_recv()
        lanes = back.tensors[7][1]
        for c in range(chips):
            at = slice(c // 2 * lanes, (c // 2 + 1) * lanes)
            total[7][c // 4, c // 2 % 2, c % 2] = gain_sum[:, at] + gain_other[:, at]
        begin_scatter(7)

    work = {
        "norm": first_norm,
        "query": do_query,
        "key": do_key,
        "value": do_value,
        "project": add_out,
        "mix": add_down,
        "down": grad_down,
        "norm2": norm2,
        "heads": grad_heads,
        "out": grad_out,
        "dh1": grad_norm1,
        "norm1": norm1,
        "gains": grad_gains,
    }
    for k in range(4):
        work["see", k] = functools.partial(attend_part, k)
        work["attend", k] = functools.partial(attend_back_part, k)
    for k in range(len(strips)):
        work["mlp", k] = functools.partial(mlp, k)
        work["up", k] = functools.partial(grad_strip, 1, "db", db, dbr, k)
        work["gate", k] = functools.partial(grad_strip, 2, "da", da, dar, k)
    for k in range(3):
        work["qkv", k] = functools.partial(grad_qkv, k)
    for k in range(2):
        work["hidden", k] = functools.partial(hidden, k)
        work["dh2", k] = functools.partial(grad_norm2, k)
    for step in SCRIPT:
        if step in work:
            work[step]()
        elif step[0] == "start":
            prepare(ahead.items[step[1]][0])
            gather.start(step[1], 0)
        elif step[0] == 0:
            _, i, phase, *hop = step
            land(ahead.items[i][0])
            if hop:
                gather.take_hop(i, phase, hop[0])
            else:
                gather.wait(i, phase)
            if hop in ([], [NZ - 1]):
                gather.start(i, phase + 1)
        else:
            _, i, phase = step
            scatter.wait(i, phase)
            scatter.add(i, phase)
            if phase < 2:
                scatter.start(i, phase + 1)
    for i in range(len(ahead.items)):
        gather.finish(i)
    for i in range(len(back.items)):
        scatter.finish(i)
    for k in (0, 22, 23, 24, 25, 26, 27, 28):
        halves[k].wait_send()
    later["gtok"].wait()


def block_all(ahead, back, lens, tokens, cotangent, shards):
    n, na, nb = len(ahead.tensors), len(ahead.items), len(back.items)
    rows, width = tokens.shape
    columns, wide = ahead.tensors[1][1], ahead.tensors[5][1]
    anywhere = pl.BlockSpec(memory_space=pl.ANY)
    inside = pl.BlockSpec(memory_space=pltpu.VMEM)
    shape = jax.ShapeDtypeStruct
    over = WINDOW + rows
    bufs = [(2, NZ, NY, NX) + t[:2] for t in ahead.tensors]
    kept = [
        ((rows, width), LOW),
        ((rows, width), F32),
        ((rows, width), LOW),
        ((rows, HEADS * SPAN), LOW),
        ((width, 2 * rows), LOW),
        ((width, 2 * rows), LOW),
        ((width, 2 * rows), LOW),
        ((2 * wide, 2 * rows), LOW),
    ]
    scratch = [
        (ahead.tensors[5][:2], LOW),
        (ahead.tensors[6][:2], LOW),
        (ahead.tensors[7][:2], LOW),
        (bufs[0], LOW),
        ((8, width), F32),
        ((rows, width), LOW),
        ((rows, width), LOW),
        ((rows, 2 * wide), LOW),
        ((rows, 2 * wide), LOW),
        ((over, width), LOW),
        ((over, width), LOW),
        ((rows, width), LOW),
        ((rows, width), F32),
        ((2, rows, wide), LOW),
        ((rows, wide), LOW),
        ((rows, wide), LOW),
        ((rows, width), LOW),
        ((rows, columns), LOW),
        ((rows, width), F32),
        ((rows, columns), LOW),
        ((2, width, 2 * rows), LOW),
        ((2, 2 * wide, columns), LOW),
        ((2, 2, 2, 128, wide), LOW),
        ((WINDOW, width), F32),
        ((WINDOW, width), F32),
        ((WINDOW, width), LOW),
        ((WINDOW, width), LOW),
        ((8, width), F32),
        ((8, width), F32),
    ]
    totals = [((NZ, NY, NX) + t[:2], t[2]) for t in back.tensors]
    got = [part for parts in got_shapes(back) for part in parts]
    dma = pltpu.SemaphoreType.DMA
    outs = pl.pallas_call(
        functools.partial(block_kernel, ahead, back),
        out_shape=[shape(b, LOW) for b in bufs[1:]]
        + [shape(*s) for s in kept]
        + [shape(t[:2], F32) for t in back.tensors],
        in_specs=[pl.BlockSpec(memory_space=pltpu.SMEM), anywhere, anywhere] + [inside] * n,
        out_specs=[anywhere] * (n - 1 + len(kept)) + [inside] * n,
        scratch_shapes=[pltpu.VMEM(*s) for s in totals + got + scratch]
        + [dma((9 * na,)), dma((9 * na,)), dma((n,)), dma((5 * nb,)), dma((5 * nb,)), dma((28,))]
        + [dma((2, 3)), dma((2, 2)), dma((2, 1)), dma((29,)), dma((29,))],
        compiler_params=pltpu.CompilerParams(
            collective_id=0, has_side_effects=True, vmem_limit_bytes=VMEM_LIMIT
        ),
        name="block_all",
    )(lens, tokens, cotangent, *shards)
    return outs[n - 1 : n + 1], outs[n - 1 + len(kept) :]


def finish_kernel(*refs):
    n = 10
    ins, outs, held, made = refs[:n], refs[n : 2 * n + 1], refs[2 * n + 1 : 3 * n + 1], refs[3 * n + 1 : 4 * n + 2]
    sem_in, sem_out = refs[4 * n + 2 :]
    gets = [pltpu.make_async_copy(src, dst, sem_in.at[k]) for k, (src, dst) in enumerate(zip(ins, held))]
    for copy in gets:
        copy.start()
    puts = []

    def put(k, src):
        copy = pltpu.make_async_copy(src, outs[k], sem_out.at[k])
        copy.start()
        puts.append(copy)

    down, up, gate, out, query, key, value, gain = held[2:]
    for copy in gets[2:]:
        copy.wait()
    for k, src in ((2, query), (3, key), (4, value), (5, out)):
        put(k, src)
    rows, part, tile = query.shape[0], outs[8].shape[0], down.shape[0]
    made[8][...] = down[...][:part]
    put(8, made[8])
    for k, src in ((6, gate), (7, up)):
        values = src[...]
        made[k][...] = jnp.concatenate(
            [values[:, j * tile : j * tile + part] for j in range(values.shape[1] // tile)], axis=1
        )
        put(k, made[k])
    both = gain[...]
    own = jnp.where(lax.axis_index("dp") % 2 == 0, both[:, :rows], both[:, rows:])
    made[9][...] = own[0:1]
    made[10][...] = own[1:2]
    put(9, made[9])
    put(10, made[10])
    for k in range(2):
        gets[k].wait()
        put(k, held[k])
    for copy in puts:
        copy.wait()


def finish_all(mixed, tokens, sums, w_query, w_gate, w_down):
    anywhere = pl.BlockSpec(memory_space=pl.ANY)
    shape = jax.ShapeDtypeStruct
    outs = [shape(mixed.shape, mixed.dtype), shape(tokens.shape, F32)]
    outs += [shape(w_query.shape, F32)] * 4 + [shape(w_gate.shape, F32)] * 2 + [shape(w_down.shape, F32)]
    outs += [shape((1, w_query.shape[0]), F32)] * 2
    ins = [mixed, tokens, *sums]
    return pl.pallas_call(
        finish_kernel,
        out_shape=outs,
        in_specs=[anywhere] * len(ins),
        out_specs=[anywhere] * len(outs),
        scratch_shapes=[pltpu.VMEM(a.shape, a.dtype) for a in ins + outs]
        + [pltpu.SemaphoreType.DMA((len(ins),)), pltpu.SemaphoreType.DMA((len(outs),))],
        compiler_params=pltpu.CompilerParams(vmem_limit_bytes=62 * 2**20),
        name="finish_all",
    )(*ins)


def kinds(w_query, w_gate, w_down):
    rows, columns = w_query.shape
    part = w_down.shape[0]
    tile = -(-part // 16) * 16
    wide = w_gate.shape[1] // part * tile
    half, strip = rows // 2, -(-wide // 512) * 128
    long, short = -(-tile // 64) * 16, tile - 3 * (-(-tile // 64) * 16)

    def cuts(kinds, counts):
        return tuple((kind, 0, count) for kind, count in zip(kinds, counts, strict=True))

    def strips(kinds):
        return tuple((kind, 1, min(strip, wide - k * strip)) for k, kind in enumerate(kinds))

    return {
        "square": (rows, columns, LOW, cuts(("zfx", "zfy"), (half, half))),
        "broad": (rows, wide, LOW, strips(("zfx", "zfy", "zmx", "zmy"))),
        "broad_f": (rows, wide, LOW, strips(("zfx", "zfy", "zfx", "zfy"))),
        "broad_m": (rows, wide, LOW, strips(("zmx", "zmy", "zmx", "zmy"))),
        "tall": (tile, columns, LOW, cuts(("zfx", "zfy", "zmx", "zmy"), (long, long, long, short))),
        "square_m": (rows, columns, LOW, cuts(("zmx", "zmy"), (half, half))),
        "tall_f": (tile, columns, LOW, cuts(("zfx", "zfy", "zfx", "zfy"), (long, long, long, short))),
        "tall_m": (tile, columns, LOW, cuts(("zmx", "zmy", "zmx", "zmy"), (long, long, long, short))),
        "gain": (16, 2 * rows, LOW, cuts(("zfx",), (16,))),
        "gain_grad": (8, 2 * rows, F32, cuts(("zfx",), (8,))),
    }


def gather_plan(w_query, w_key, w_value, w_out, w_gate, w_up, w_down, gain_attn, gain_mlp):
    kind = kinds(w_query, w_gate, w_down)
    names = ("gain", "square", "square", "square_m", "square_m", "broad", "broad", "tall_m")
    plan = Plan([kind[name] for name in names])
    rows = w_query.shape[0]
    both = jnp.stack([gain_attn, gain_mlp])
    left = jnp.pad(both, ((0, 14), (0, rows)))
    right = jnp.pad(both, ((0, 14), (rows, 0)))
    pair = jnp.where(lax.axis_index("dp") % 2 == 0, left, right)
    shards = [
        pair,
        w_query,
        w_key,
        w_value,
        w_out,
        w_gate,
        w_up,
        w_down,
    ]
    return plan, shards


def swift_block(
    tokens,
    seq_lengths,
    w_query,
    w_key,
    w_value,
    w_out,
    w_gate,
    w_up,
    w_down,
    gain_attn,
    gain_mlp,
    cotangent,
):
    plan, shards = gather_plan(w_query, w_key, w_value, w_out, w_gate, w_up, w_down, gain_attn, gain_mlp)
    kind = kinds(w_query, w_gate, w_down)
    names = ("tall", "broad_f", "broad", "square", "square", "square", "square", "gain_grad")
    back = Plan([kind[name] for name in names])
    results, sums = block_all(plan, back, seq_lengths, tokens, cotangent, shards)
    outs = finish_all(results[0], results[1], sums, w_query, w_gate, w_down)
    return (*outs[:9], outs[9].reshape(-1), outs[10].reshape(-1))


def solution(mesh):
    fast = (mesh.shape["dp"], mesh.shape["seq"]) == (NZ * NY * NX, 2)
    shards = swift_block if fast else plain_block
    in_specs = (
        P(("dp", "seq"), None),
        P("dp", None),
        P("dp", "seq"),
        P("dp", "seq"),
        P("dp", "seq"),
        P("dp", "seq"),
        P("dp", "seq"),
        P("dp", "seq"),
        P("dp", "seq"),
        P("dp"),
        P("dp"),
        P(("dp", "seq"), None),
    )
    out_specs = (
        P(("dp", "seq"), None),
        P(("dp", "seq"), None),
        P("dp", "seq"),
        P("dp", "seq"),
        P("dp", "seq"),
        P("dp", "seq"),
        P("dp", "seq"),
        P("dp", "seq"),
        P("dp", "seq"),
        P("dp"),
        P("dp"),
    )
    return jax.shard_map(shards, mesh=mesh, in_specs=in_specs, out_specs=out_specs, check_vma=False)
```

```python
import functools

import jax
import jax.numpy as jnp
from jax import lax
from jax.experimental import pallas as pl
from jax.experimental.pallas import tpu as pltpu
from jax.sharding import PartitionSpec as P

HEADS = 16
HEAD_DIM = 64
WINDOW = 64


eps_norm = 1e-05


def from_behind(block, axis, distance):
    devices = range(lax.axis_size(axis))
    route = [(i - distance, i) for i in devices if i - distance in devices]
    return lax.ppermute(block, axis, route)


def inverse_rms(values):
    return lax.rsqrt(jnp.mean(values * values, axis=-1, keepdims=True) + eps_norm)


def doc_numbers(lengths_row, positions):
    first_end = lengths_row[0]
    second_end = lengths_row[0] + lengths_row[1]
    return (positions >= first_end).astype(jnp.int32) + (positions >= second_end).astype(jnp.int32)


def window_mask(query_pos, query_doc, key_pos, key_doc, window):
    after = key_pos[None, :] >= query_pos[:, None] - window
    before = key_pos[None, :] <= query_pos[:, None]
    inside = (key_pos[None, :] >= 0) & (key_doc[None, :] == query_doc[:, None])
    return after & before & inside


def norm_back(values, inverse, gain, grad_norm):
    scaled = grad_norm * gain
    mean_term = jnp.mean(values * scaled, axis=-1, keepdims=True)
    grad_values = inverse * scaled - values * (inverse * inverse * inverse) * mean_term
    grad_gain = jnp.sum(values * inverse * grad_norm, axis=0)
    return (grad_values, grad_gain)


def project(left, right):
    return jnp.dot(left, right, preferred_element_type=jnp.float32)


def project_back(grad_rows, weight):
    return jnp.einsum("tf,df->td", grad_rows, weight, preferred_element_type=jnp.float32)


def weight_grad(inputs, grad_rows):
    return jnp.einsum("td,tf->df", inputs, grad_rows, preferred_element_type=jnp.float32)


def plain_block(
    tokens,
    seq_lengths,
    w_query,
    w_key,
    w_value,
    w_out,
    w_gate,
    w_up,
    w_down,
    gain_attn,
    gain_mlp,
    cotangent,
):
    row_count = tokens.shape[0]
    block_rows = min(512, row_count)
    head_group = HEADS // 2
    score_scale = HEAD_DIM ** (-0.5)
    row_parts = (
        lax.all_gather(w_query, "dp", axis=0, tiled=True),
        lax.all_gather(w_key, "dp", axis=0, tiled=True),
        lax.all_gather(w_value, "dp", axis=0, tiled=True),
        lax.all_gather(w_out, "dp", axis=0, tiled=True),
        lax.all_gather(w_gate, "dp", axis=0, tiled=True),
        lax.all_gather(w_up, "dp", axis=0, tiled=True),
        lax.all_gather(w_down, "dp", axis=0, tiled=True),
        lax.all_gather(gain_attn, "dp", axis=0, tiled=True),
        lax.all_gather(gain_mlp, "dp", axis=0, tiled=True),
    )
    full_mats = (
        lax.all_gather(row_parts[0], "seq", axis=1, tiled=True),
        lax.all_gather(row_parts[1], "seq", axis=1, tiled=True),
        lax.all_gather(row_parts[2], "seq", axis=1, tiled=True),
        lax.all_gather(row_parts[3], "seq", axis=1, tiled=True),
        lax.all_gather(row_parts[4], "seq", axis=1, tiled=True),
        lax.all_gather(row_parts[5], "seq", axis=1, tiled=True),
        lax.all_gather(row_parts[6], "seq", axis=1, tiled=True),
    )
    query_w, key_w, value_w, out_w, gate_w, up_w, down_full = full_mats
    gain_one = row_parts[7].astype(jnp.float32)
    gain_two = row_parts[8].astype(jnp.float32)
    inputs = tokens.astype(jnp.float32)
    inv_one = inverse_rms(inputs)
    normed_one = (inputs * inv_one * gain_one).astype(jnp.bfloat16)
    query_low = project(normed_one, query_w).astype(jnp.bfloat16)
    key_low = project(normed_one, key_w).astype(jnp.bfloat16)
    value_low = project(normed_one, value_w).astype(jnp.bfloat16)
    rim_pairs = from_behind(
        (key_low[row_count - WINDOW :], value_low[row_count - WINDOW :]), "seq", 1
    )
    keys_ext = jnp.concatenate([rim_pairs[0], key_low], axis=0).reshape(
        row_count + WINDOW, HEADS, HEAD_DIM
    )
    values_ext = jnp.concatenate([rim_pairs[1], value_low], axis=0).reshape(
        row_count + WINDOW, HEADS, HEAD_DIM
    )
    query_heads = query_low.reshape(row_count, HEADS, HEAD_DIM)
    span_start = lax.axis_index("seq") * row_count
    query_pos = span_start + jnp.arange(row_count, dtype=jnp.int32)
    key_pos = span_start - WINDOW + jnp.arange(row_count + WINDOW, dtype=jnp.int32)
    query_doc = doc_numbers(seq_lengths[0], query_pos)
    key_doc = doc_numbers(seq_lengths[0], key_pos)

    def tile_scores(row_start, head_start):
        visible = window_mask(query_pos, query_doc, key_pos, key_doc, WINDOW)
        scores_raw = (
            jnp.einsum(
                "qhd,khd->hqk",
                query_heads[
                    row_start : row_start + block_rows, head_start : head_start + head_group
                ],
                keys_ext[
                    row_start : row_start + block_rows + WINDOW,
                    head_start : head_start + head_group,
                ],
                preferred_element_type=jnp.float32,
            )
            * score_scale
        )
        return jnp.where(visible[None], scores_raw, -1e30)

    log_totals = {}
    row_start = 0
    head_parts = []
    for head_start in range(0, HEADS, head_group):
        masked_scores = tile_scores(row_start, head_start)
        top_score = jnp.max(masked_scores, axis=-1, keepdims=True)
        log_total = top_score + jnp.log(
            jnp.sum(jnp.exp(masked_scores - top_score), axis=-1, keepdims=True)
        )
        prob_low = jnp.exp(masked_scores - log_total).astype(jnp.bfloat16)
        value_tile = values_ext[
            row_start : row_start + block_rows + WINDOW, head_start : head_start + head_group
        ]
        head_parts.append(
            jnp.einsum("hqk,khd->qhd", prob_low, value_tile, preferred_element_type=jnp.float32)
        )
        log_totals[row_start, head_start] = log_total
    attn_blocks = jnp.concatenate(head_parts, axis=1)
    attended = attn_blocks.reshape(row_count, HEADS * HEAD_DIM).astype(jnp.bfloat16)
    middle = inputs + project(attended, out_w)
    inv_two = inverse_rms(middle)
    normed_two = (middle * inv_two * gain_two).astype(jnp.bfloat16)
    gate_pre = project(normed_two, gate_w)
    up_pre = project(normed_two, up_w)
    gate_act = jax.nn.silu(gate_pre)
    hidden = (gate_act * up_pre).astype(jnp.bfloat16)
    block_out = (middle + project(hidden, down_full)).astype(jnp.bfloat16)
    rows_again = (
        lax.all_gather(w_query, "dp", axis=0, tiled=True),
        lax.all_gather(w_key, "dp", axis=0, tiled=True),
        lax.all_gather(w_value, "dp", axis=0, tiled=True),
        lax.all_gather(w_out, "dp", axis=0, tiled=True),
        lax.all_gather(w_gate, "dp", axis=0, tiled=True),
        lax.all_gather(w_up, "dp", axis=0, tiled=True),
        lax.all_gather(w_down, "dp", axis=0, tiled=True),
        lax.all_gather(gain_attn, "dp", axis=0, tiled=True),
        lax.all_gather(gain_mlp, "dp", axis=0, tiled=True),
    )
    mats_again = (
        lax.all_gather(rows_again[0], "seq", axis=1, tiled=True),
        lax.all_gather(rows_again[1], "seq", axis=1, tiled=True),
        lax.all_gather(rows_again[2], "seq", axis=1, tiled=True),
        lax.all_gather(rows_again[3], "seq", axis=1, tiled=True),
        lax.all_gather(rows_again[4], "seq", axis=1, tiled=True),
        lax.all_gather(rows_again[5], "seq", axis=1, tiled=True),
        lax.all_gather(rows_again[6], "seq", axis=1, tiled=True),
    )
    back_query, back_key, back_value, back_out, back_gate, back_up, back_down = mats_again
    back_gain_one = rows_again[7].astype(jnp.float32)
    back_gain_two = rows_again[8].astype(jnp.float32)
    grad_final = cotangent.astype(jnp.float32)
    d_down = weight_grad(hidden, cotangent)
    grad_hidden = project_back(cotangent, back_down)
    sigmoid_gate = jax.nn.sigmoid(gate_pre)
    grad_gate_low = (
        grad_hidden * up_pre * sigmoid_gate * (1.0 + gate_pre * (1.0 - sigmoid_gate))
    ).astype(jnp.bfloat16)
    grad_up_low = (grad_hidden * gate_act).astype(jnp.bfloat16)
    d_gate = weight_grad(normed_two, grad_gate_low)
    d_up = weight_grad(normed_two, grad_up_low)
    grad_normed_two = project_back(grad_gate_low, back_gate) + project_back(grad_up_low, back_up)
    grad_mid_norm, d_gain_two = norm_back(middle, inv_two, back_gain_two, grad_normed_two)
    grad_middle = grad_final + grad_mid_norm
    grad_proj = grad_middle.astype(jnp.bfloat16)
    d_out = weight_grad(attended, grad_proj)
    grad_attended = (
        project_back(grad_proj, back_out).astype(jnp.bfloat16).reshape(row_count, HEADS, HEAD_DIM)
    )
    grad_keys_ext = jnp.zeros((row_count + WINDOW, HEADS, HEAD_DIM), jnp.float32)
    grad_values_ext = jnp.zeros((row_count + WINDOW, HEADS, HEAD_DIM), jnp.float32)
    row_start = 0
    head_parts = []
    for head_start in range(0, HEADS, head_group):
        head_end = head_start + head_group
        masked_scores = tile_scores(row_start, head_start)
        prob_full = jnp.exp(masked_scores - log_totals[row_start, head_start])
        grad_tile = grad_attended[row_start : row_start + block_rows, head_start:head_end]
        key_tile = keys_ext[row_start : row_start + block_rows + WINDOW, head_start:head_end]
        value_tile = values_ext[row_start : row_start + block_rows + WINDOW, head_start:head_end]
        query_tile = query_heads[row_start : row_start + block_rows, head_start:head_end]
        grad_prob = jnp.einsum(
            "qhd,khd->hqk", grad_tile, value_tile, preferred_element_type=jnp.float32
        )
        inner = jnp.sum(prob_full * grad_prob, axis=-1, keepdims=True)
        grad_score = (prob_full * (grad_prob - inner)).astype(jnp.bfloat16)
        head_parts.append(
            jnp.einsum("hqk,khd->qhd", grad_score, key_tile, preferred_element_type=jnp.float32)
            * score_scale
        )
        key_term = (
            jnp.einsum("hqk,qhd->khd", grad_score, query_tile, preferred_element_type=jnp.float32)
            * score_scale
        )
        value_term = jnp.einsum(
            "hqk,qhd->khd",
            prob_full.astype(jnp.bfloat16),
            grad_tile,
            preferred_element_type=jnp.float32,
        )
        grad_keys_ext = grad_keys_ext.at[
            row_start : row_start + block_rows + WINDOW, head_start:head_end
        ].add(key_term)
        grad_values_ext = grad_values_ext.at[
            row_start : row_start + block_rows + WINDOW, head_start:head_end
        ].add(value_term)
    grad_query_blocks = jnp.concatenate(head_parts, axis=1)
    rim_back = (
        from_behind(
            grad_keys_ext[:WINDOW].reshape(WINDOW, HEADS * HEAD_DIM).astype(jnp.bfloat16), "seq", -1
        ).astype(jnp.float32),
        from_behind(
            grad_values_ext[:WINDOW].reshape(WINDOW, HEADS * HEAD_DIM).astype(jnp.bfloat16),
            "seq",
            -1,
        ).astype(jnp.float32),
    )
    grad_keys = (
        grad_keys_ext[WINDOW:]
        .reshape(row_count, HEADS * HEAD_DIM)
        .at[row_count - WINDOW :]
        .add(rim_back[0])
    )
    grad_values = (
        grad_values_ext[WINDOW:]
        .reshape(row_count, HEADS * HEAD_DIM)
        .at[row_count - WINDOW :]
        .add(rim_back[1])
    )
    grad_query_low = grad_query_blocks.reshape(row_count, HEADS * HEAD_DIM).astype(jnp.bfloat16)
    grad_key_low = grad_keys.astype(jnp.bfloat16)
    grad_value_low = grad_values.astype(jnp.bfloat16)
    d_query = weight_grad(normed_one, grad_query_low)
    d_key = weight_grad(normed_one, grad_key_low)
    d_value = weight_grad(normed_one, grad_value_low)
    grad_normed_one = (
        project_back(grad_query_low, back_query)
        + project_back(grad_key_low, back_key)
        + project_back(grad_value_low, back_value)
    )
    grad_in_norm, d_gain_one = norm_back(inputs, inv_one, back_gain_one, grad_normed_one)
    grad_inputs = grad_middle + grad_in_norm
    row_sums = (
        lax.psum_scatter(
            d_query.astype(jnp.bfloat16), "dp", scatter_dimension=0, tiled=True
        ).astype(jnp.float32),
        lax.psum_scatter(d_key.astype(jnp.bfloat16), "dp", scatter_dimension=0, tiled=True).astype(
            jnp.float32
        ),
        lax.psum_scatter(
            d_value.astype(jnp.bfloat16), "dp", scatter_dimension=0, tiled=True
        ).astype(jnp.float32),
        lax.psum_scatter(d_out.astype(jnp.bfloat16), "dp", scatter_dimension=0, tiled=True).astype(
            jnp.float32
        ),
        lax.psum_scatter(d_gate.astype(jnp.bfloat16), "dp", scatter_dimension=0, tiled=True).astype(
            jnp.float32
        ),
        lax.psum_scatter(d_up.astype(jnp.bfloat16), "dp", scatter_dimension=0, tiled=True).astype(
            jnp.float32
        ),
        lax.psum_scatter(d_down.astype(jnp.bfloat16), "dp", scatter_dimension=0, tiled=True).astype(
            jnp.float32
        ),
        lax.psum_scatter(
            d_gain_one.astype(jnp.bfloat16), "dp", scatter_dimension=0, tiled=True
        ).astype(jnp.float32),
        lax.psum_scatter(
            d_gain_two.astype(jnp.bfloat16), "dp", scatter_dimension=0, tiled=True
        ).astype(jnp.float32),
    )
    owned_mats = (
        lax.psum_scatter(
            row_sums[0].astype(jnp.bfloat16), "seq", scatter_dimension=1, tiled=True
        ).astype(jnp.float32),
        lax.psum_scatter(
            row_sums[1].astype(jnp.bfloat16), "seq", scatter_dimension=1, tiled=True
        ).astype(jnp.float32),
        lax.psum_scatter(
            row_sums[2].astype(jnp.bfloat16), "seq", scatter_dimension=1, tiled=True
        ).astype(jnp.float32),
        lax.psum_scatter(
            row_sums[3].astype(jnp.bfloat16), "seq", scatter_dimension=1, tiled=True
        ).astype(jnp.float32),
        lax.psum_scatter(
            row_sums[4].astype(jnp.bfloat16), "seq", scatter_dimension=1, tiled=True
        ).astype(jnp.float32),
        lax.psum_scatter(
            row_sums[5].astype(jnp.bfloat16), "seq", scatter_dimension=1, tiled=True
        ).astype(jnp.float32),
        lax.psum_scatter(
            row_sums[6].astype(jnp.bfloat16), "seq", scatter_dimension=1, tiled=True
        ).astype(jnp.float32),
    )
    owned_gains = lax.psum((row_sums[7], row_sums[8]), "seq")
    return (
        block_out,
        grad_inputs,
        owned_mats[0],
        owned_mats[1],
        owned_mats[2],
        owned_mats[3],
        owned_mats[4],
        owned_mats[5],
        owned_mats[6],
        owned_gains[0],
        owned_gains[1],
    )


SCRIPT = (
    ("start", 7), ("start", 6), ("start", 8), ("start", 2), ("start", 5), ("start", 9), ("start", 3),
    ("start", 0), ("start", 10), ("start", 17), ("start", 4), (0, 4, 0), ("start", 13), ("start", 1),
    ("start", 19), (0, 7, 0, 1), ("start", 18), ("start", 12), (0, 9, 0, 1), ("start", 15), ("start", 16),
    (0, 8, 0, 1), ("start", 14), (0, 1, 0, 1), (0, 17, 0), (0, 8, 0, 2), (0, 0, 0, 1), (0, 2, 0, 1),
    (0, 14, 0), (0, 1, 0, 2), (0, 7, 0, 2), (0, 0, 0, 2), (0, 4, 1, 1), (0, 0, 0, 3), ("start", 20),
    (0, 5, 0), (0, 2, 0, 2), (0, 9, 0, 2), (0, 8, 0, 3), (0, 1, 0, 3), (0, 6, 0), (0, 1, 1), (0, 0, 1),
    (0, 3, 0), (0, 4, 1, 2), (0, 18, 0), (0, 2, 0, 3), (0, 9, 0, 3), (0, 0, 2), (0, 4, 1, 3), (0, 7, 0, 3),
    (0, 19, 0), (0, 9, 1), (0, 17, 1, 1), (0, 5, 1, 1), (0, 2, 1), (0, 6, 1, 1), (0, 15, 0), (0, 19, 1, 1),
    (0, 7, 1), (0, 5, 1, 2), (0, 8, 1), (0, 3, 1, 1), (0, 20, 0), (0, 6, 1, 2), (0, 3, 1, 2), (0, 5, 1, 3),
    (0, 17, 1, 2), (0, 20, 1, 1), (0, 6, 1, 3), "norm", (0, 16, 0), (0, 1, 2), (0, 3, 1, 3), (0, 20, 1, 2),
    (0, 18, 1, 1), (0, 20, 1, 3), (0, 2, 2), (0, 5, 2), (0, 13, 0), (0, 19, 1, 2), (0, 17, 1, 3), (0, 6, 2),
    (0, 18, 1, 2), (0, 10, 0, 1), ("start", 11), (0, 7, 2), (0, 3, 2), (0, 10, 0, 2), (0, 15, 1, 1), "query",
    (0, 10, 0, 3), (0, 18, 1, 3), (0, 4, 2), (0, 13, 1, 1), "value", (0, 11, 0), (0, 17, 2), (0, 12, 0),
    (0, 19, 1, 3), (0, 14, 1, 1), "key", (0, 13, 1, 2), (0, 10, 1), (0, 8, 2), ("see", 0), ("see", 1),
    (0, 16, 1, 1), (0, 9, 2), (0, 13, 1, 3), ("see", 2), (0, 14, 1, 2), ("see", 3), (0, 15, 1, 2), (0, 19, 2),
    (0, 20, 2), (0, 14, 1, 3), (0, 16, 1, 2), (0, 12, 1, 1), (0, 18, 2), (0, 11, 1, 1), "project",
    (0, 15, 1, 3), (0, 12, 1, 2), (0, 10, 2), (0, 13, 2), ("hidden", 0), (0, 16, 1, 3), (0, 11, 1, 2),
    ("hidden", 1), (0, 11, 1, 3), (0, 12, 1, 3), (0, 14, 2), ("mlp", 0), ("mlp", 1), ("up", 0), ("gate", 0),
    (0, 15, 2), (0, 11, 2), ("up", 1), ("gate", 1), (0, 12, 2), (0, 16, 2), ("mlp", 2), ("mlp", 3),
    ("gate", 2), (1, 4, 0), "mix", ("gate", 3), (1, 5, 0), ("up", 2), (1, 4, 1), ("up", 3), (1, 8, 0),
    (1, 10, 0), "down", (1, 5, 1), ("dh2", 0), (1, 11, 0), ("dh2", 1), (1, 8, 1), "norm2", "heads",
    ("attend", 0), (1, 10, 1), "out", (1, 3, 0), ("attend", 1), ("attend", 2), (1, 2, 0), (1, 7, 0),
    (1, 9, 0), ("attend", 3), (1, 6, 0), (1, 8, 2), (1, 13, 0), (1, 1, 0), (1, 0, 0), "dh1", ("qkv", 0),
    (1, 6, 1), (1, 7, 1), (1, 12, 0), (1, 0, 1), (1, 13, 1), ("qkv", 1), "norm1", (1, 2, 1), (1, 10, 2),
    (1, 9, 1), (1, 1, 1), (1, 5, 2), (1, 14, 0), (1, 12, 1), (1, 15, 0), "gains", ("qkv", 2), (1, 17, 0),
    (1, 2, 2), (1, 20, 0), (1, 13, 2), (1, 14, 1), (1, 20, 1), (1, 16, 0), (1, 0, 2), (1, 15, 1), (1, 17, 1),
    (1, 19, 0), (1, 18, 0), (1, 16, 1), (1, 14, 2), (1, 4, 2), (1, 19, 1), (1, 15, 2), (1, 1, 2), (1, 20, 2),
    (1, 12, 2), (1, 11, 1), (1, 3, 1), (1, 18, 1), (1, 16, 2), (1, 6, 2), (1, 7, 2), (1, 9, 2), (1, 17, 2),
    (1, 19, 2), (1, 3, 2), (1, 11, 2), (1, 18, 2),
)


MESH = pl.DeviceIdType.MESH
NZ, NY, NX = 4, 2, 2
SEQUENCE = {"zfx": "zxy", "zfy": "zyx", "zmx": "xzy", "zmy": "yzx"}
ALL_Z, ALL_Y, ALL_X = pl.ds(0, NZ), pl.ds(0, NY), pl.ds(0, NX)


class Plan:
    def __init__(self, tensors):
        self.tensors = tensors
        self.items, self.of_tensor = [], []
        for t, (_, _, _, cuts) in enumerate(tensors):
            begin, mine = 0, []
            for kind, along, count in cuts:
                mine.append(len(self.items))
                whole = [(0, tensors[t][0]), (0, tensors[t][1])]
                whole[along] = (begin, count)
                self.items.append((t, SEQUENCE[kind], *whole))
                begin += count
            self.of_tensor.append(mine)


class Place:
    def __init__(self):
        self.c, self.s = lax.axis_index("dp"), lax.axis_index("seq")
        self.z, self.y, self.x = self.c // 4, (self.c // 2) % 2, self.c % 2

    def at(self, z, y, x):
        return (z * 4 + y * 2 + x, self.s)

    def to_x(self):
        return self.at(self.z, self.y, 1 - self.x)

    def to_y(self):
        return self.at(self.z, 1 - self.y, self.x)

    def to_z(self, step):
        return self.at((self.z + step) % NZ, self.y, self.x)

    def to_core(self):
        return (self.c, 1 - self.s)

    def greet(self):
        barrier = pltpu.get_barrier_semaphore()
        peers = [self.to_x(), self.to_y(), self.to_core()] + [self.to_z(k) for k in (1, 2, 3)]
        for peer in peers:
            pl.semaphore_signal(barrier, inc=1, device_id=peer, device_id_type=MESH)
        pl.semaphore_wait(barrier, len(peers))


def remote(src, dst, send, recv, device):
    return pltpu.make_async_remote_copy(
        src_ref=src, dst_ref=dst, send_sem=send, recv_sem=recv, device_id=device, device_id_type=MESH
    )


def slots(seq, count, along_z):
    firsts, used = [], 0
    for phase in range(count):
        firsts.append(used)
        used += along_z if phase < 3 and seq[phase] == "z" else 1
    return firsts


class Gather:
    def __init__(self, plan, place, shards, bufs, send, recv, local):
        self.plan, self.me, self.shards, self.bufs = plan, place, shards, bufs
        self.send, self.recv, self.local = send, recv, local

    def own_copy(self, t):
        me = self.me
        return pltpu.make_async_copy(
            self.shards[t], self.bufs[t].at[me.s, me.z, me.y, me.x], self.local.at[t]
        )

    def moves(self, i, phase):
        t, seq, rows, cols = self.plan.items[i]
        me, buf = self.me, self.bufs[t]
        rows, cols = pl.ds(*rows), pl.ds(*cols)

        def view(z, y, x, half=me.s):
            return buf.at[half, z, y, x, rows, cols]

        if phase == 3:
            whole = view(ALL_Z, ALL_Y, ALL_X)
            return [(whole, whole, me.to_core(), view(ALL_Z, ALL_Y, ALL_X, 1 - me.s), 0)]
        done, axis = seq[:phase], seq[phase]
        z = ALL_Z if "z" in done else me.z
        y = ALL_Y if "y" in done else me.y
        x = ALL_X if "x" in done else me.x
        there = view(z, y, x)
        here = self.shards[t].at[rows, cols] if phase == 0 else there
        if axis == "x":
            return [(here, there, me.to_x(), view(z, y, 1 - me.x), 0)]
        return [(here, there, me.to_y(), view(z, 1 - me.y, x), 0)]

    def hops(self, i, phase, hop):
        t, seq, rows, cols = self.plan.items[i]
        me, buf = self.me, self.bufs[t]
        rows, cols = pl.ds(*rows), pl.ds(*cols)
        done = seq[:phase]
        y = ALL_Y if "y" in done else me.y
        x = ALL_X if "x" in done else me.x
        moves = []
        for k, way in enumerate((1, -1)):
            first, last = (me.z, NZ - 1 - me.z) if way == 1 else (NZ - 1 - me.z, me.z)
            sends = (first >= hop - 1) & (last >= 1)
            takes = first >= hop
            z = me.z - way * (hop - 1)
            there = buf.at[me.s, z, y, x, rows, cols]
            here = self.shards[t].at[rows, cols] if phase == 0 and hop == 1 else there
            arrived = buf.at[me.s, me.z - way * hop, y, x, rows, cols]
            moves.append((sends, takes, here, there, me.at(me.z + way, me.y, me.x), arrived, 3 * k + hop - 1))
        return moves

    def along_z(self, i, phase):
        return phase < 3 and self.plan.items[i][1][phase] == "z"

    def copy(self, i, phase, src, dst, device, k):
        at = 9 * i + slots(self.plan.items[i][1], 4, 6)[phase] + k
        return remote(src, dst, self.send.at[at], self.recv.at[at], device)

    def send_hop(self, i, phase, hop):
        for sends, _, here, there, device, _, k in self.hops(i, phase, hop):

            @pl.when(sends)
            def _(here=here, there=there, device=device, k=k):
                self.copy(i, phase, here, there, device, k).start()

    def take_hop(self, i, phase, hop):
        for _, takes, _, _, device, arrived, k in self.hops(i, phase, hop):

            @pl.when(takes)
            def _(device=device, arrived=arrived, k=k):
                self.copy(i, phase, arrived, arrived, device, k).wait_recv()

        if hop < NZ - 1:
            self.send_hop(i, phase, hop + 1)

    def start(self, i, phase):
        if self.along_z(i, phase):
            self.send_hop(i, phase, 1)
            return
        for here, there, device, _, k in self.moves(i, phase):
            self.copy(i, phase, here, there, device, k).start()

    def wait(self, i, phase):
        for _, _, device, arrived, k in self.moves(i, phase):
            self.copy(i, phase, arrived, arrived, device, k).wait_recv()

    def finish(self, i):
        for phase in range(4):
            if self.along_z(i, phase):
                for hop in range(1, NZ):
                    for sends, _, here, there, device, _, k in self.hops(i, phase, hop):

                        @pl.when(sends)
                        def _(here=here, there=there, device=device, k=k):
                            self.copy(i, phase, here, there, device, k).wait_send()

                continue
            for here, there, device, _, k in self.moves(i, phase):
                self.copy(i, phase, here, there, device, k).wait_send()


def got_shapes(plan):
    shapes = []
    for t, seq, (_, rows), (_, columns) in plan.items:
        dtype = plan.tensors[t][2]
        second, third = ((1, NZ), (3,)) if seq[0] == "z" else ((3, 2), (1,))
        shapes.append([(d + (rows, columns), dtype) for d in ((NZ, 2), second, third)])
    return shapes


class Scatter:
    def __init__(self, plan, place, total, got, out, send, recv):
        self.plan, self.me, self.total, self.got, self.out = plan, place, total, got, out
        self.send, self.recv = send, recv

    def moves(self, i, phase):
        t, seq, rows, cols = self.plan.items[i]
        me, total, got = self.me, self.total[t], self.got[i][phase]
        rows, cols = pl.ds(*rows), pl.ds(*cols)
        axis, done = seq[2 - phase], seq[3 - phase :]
        z = me.z if "z" in done else ALL_Z
        y = me.y if "y" in done else ALL_Y
        x = me.x if "x" in done else ALL_X
        if phase == 0:
            lands = [got]
        else:
            lands = [got.at[k] for k in range(got.shape[0])]
        if axis == "x":
            return [(total.at[z, y, 1 - me.x, rows, cols], lands[0], me.to_x(), 0)]
        if axis == "y":
            return [(total.at[z, 1 - me.y, x, rows, cols], lands[0], me.to_y(), 0)]
        return [
            (total.at[(me.z + k) % NZ, y, x, rows, cols], lands[k - 1], me.to_z(k), k - 1)
            for k in (1, 2, 3)
        ]

    def copy(self, i, phase, src, dst, device, k):
        at = 5 * i + slots(self.plan.items[i][1][::-1], 3, 3)[phase] + k
        return remote(src, dst, self.send.at[at], self.recv.at[at], device)

    def start(self, i, phase):
        for here, there, device, k in self.moves(i, phase):
            self.copy(i, phase, here, there, device, k).start()

    def wait(self, i, phase):
        for here, there, device, k in self.moves(i, phase):
            self.copy(i, phase, there, there, device, k).wait_recv()

    def add(self, i, phase):
        t, seq, rows, cols = self.plan.items[i]
        me, total, got = self.me, self.total[t], self.got[i][phase]
        rows, cols = pl.ds(*rows), pl.ds(*cols)
        if phase == 0:
            for z in range(NZ):
                for o in range(2):
                    at = (z, me.y, o) if seq[2] == "y" else (z, o, me.x)
                    total[at + (rows, cols)] += got[z, o]
        elif phase == 1 and seq[1] != "z":
            for z in range(NZ):
                total[z, me.y, me.x, rows, cols] += got[0, z]
        elif phase == 1:
            for o in range(2):
                at = (me.z, me.y, o) if seq[2] == "y" else (me.z, o, me.x)
                part = total[at + (rows, cols)].astype(jnp.float32)
                for k in range(3):
                    part += got[k, o].astype(jnp.float32)
                total[at + (rows, cols)] = part.astype(total.dtype)
        else:
            part = total[me.z, me.y, me.x, rows, cols].astype(jnp.float32)
            for k in range(got.shape[0]):
                part += got[k].astype(jnp.float32)
            self.out[t][rows, cols] = part

    def finish(self, i):
        for phase in range(3):
            for here, there, device, k in self.moves(i, phase):
                self.copy(i, phase, here, there, device, k).wait_send()


EPS = 1e-05
PAIR = 2 * HEAD_DIM
SPAN = 2 * WINDOW
LOW = jnp.bfloat16
F32 = jnp.float32


def mm(left, right):
    return jnp.dot(left, right, preferred_element_type=F32)


def mm_nt(left, right):
    return lax.dot_general(left, right, (((1,), (1,)), ((), ())), preferred_element_type=F32)


def mm_tn(left, right):
    return lax.dot_general(left, right, (((0,), (0,)), ((), ())), preferred_element_type=F32)


def column_tiles(columns, size):
    full = columns // size
    tiles = [(0, size, full)]
    if columns % size:
        tiles.append((full * size, columns % size, 1))
    return tiles


def each_tile(columns, size, body):
    for begin, width, count in column_tiles(columns, size):
        if count == 1:
            body(begin, width)
        else:

            def step(j, _, begin=begin, width=width):
                body(pl.multiple_of(begin + j * width, 128), width)
                return 0

            lax.fori_loop(0, count, step, 0)


def each_rows(rows, size, body):
    def step(j, _):
        body(pl.ds(pl.multiple_of(j * size, size), size))
        return 0

    lax.fori_loop(0, rows // size, step, 0)


def both_heads(block):
    first = lax.broadcasted_iota(jnp.int32, block.shape, 1) < HEAD_DIM
    zero = jnp.zeros_like(block)
    return jnp.concatenate([jnp.where(first, block, zero), jnp.where(first, zero, block)], axis=0)


def merge_heads(stacked):
    rows = stacked.shape[0] // 2
    first = lax.broadcasted_iota(jnp.int32, (rows, PAIR), 1) < HEAD_DIM
    return jnp.where(first, stacked[:rows], stacked[rows:])


VMEM_LIMIT = 64 * 2**20


class Stream:
    def __init__(self, count, sems, fetch):
        self.count, self.sems, self.fetch = count, sems, fetch

    def copies(self, j, slot):
        return [
            pltpu.make_async_copy(src, dst, self.sems.at[slot, k])
            for k, (src, dst) in enumerate(self.fetch(j, slot))
        ]

    def prime(self):
        for copy in self.copies(0, 0):
            copy.start()

    def run(self, body, first=0, last=None):
        def step(j, _):
            slot = j % 2

            @pl.when(j + 1 < self.count)
            def _():
                for copy in self.copies(j + 1, 1 - slot):
                    copy.start()

            for copy in self.copies(j, slot):
                copy.wait()
            body(j, slot)
            return 0

        lax.fori_loop(first, self.count if last is None else last, step, 0)


def block_kernel(ahead, back, *refs):
    n = len(ahead.tensors)
    (lens, x_h, dy_h), raw, refs = refs[:3], refs[3 : 3 + n], refs[3 + n :]
    hbm_bufs, refs = refs[: n - 1], refs[n - 1 :]
    (mixed_o, gtok_o, q_h, p_h, ha_h, ho_h, hm_h, hid_h), refs = refs[:8], refs[8:]
    outs_h, refs = refs[:n], refs[n:]
    outs, refs = refs[:n], refs[n:]
    total, refs = refs[:n], refs[n:]
    count = len(back.items)
    got, refs = [refs[3 * i : 3 * i + 3] for i in range(count)], refs[3 * count :]
    (gate_pad, up_pad, down_pad, gain_buf, gains, xb, h1, da, db, kx, vx, o, x1, hid), refs = refs[:14], refs[14:]
    (dar, dbr, pair_of, pair_low), refs = refs[:4], refs[4:]
    (dy, dyr, dh, dxr_r, turned, pool, broad), refs = refs[:7], refs[7:]
    (kc, vc, rim_k, rim_v, gain_sum, gain_other), refs = refs[:6], refs[6:]
    (a_send, a_recv, own_sem, b_send, b_recv, load_sem, pool_sem, broad_sem, turn_sem), refs = refs[:9], refs[9:]
    half_send, half_recv = refs
    rows, width = xb.shape
    wide, columns = ahead.tensors[5][1], ahead.tensors[1][1]
    chips = NZ * NY * NX
    me = Place()
    halves, loads, later = {}, [0], {}

    def load(src, dst):
        copy = pltpu.make_async_copy(src, dst, load_sem.at[loads[0]])
        loads[0] += 1
        copy.start()
        return copy

    def to_partner(k, src, dst):
        copy = remote(src, dst, half_send.at[k], half_recv.at[k], me.to_core())
        copy.start()
        halves[k] = copy
        return copy

    def own(size, side=0):
        return pl.ds(pl.multiple_of((me.s if side == 0 else 1 - me.s) * size, 128), size)

    get_x, get_dy = load(x_h, xb), load(dy_h, dy)
    me.greet()
    pair_of[...] = jnp.zeros_like(pair_of)
    blank = jnp.zeros((1, raw[0].shape[1]), F32)
    for k in range(2):
        gain = raw[0][k : k + 1, :].astype(F32)
        left, right = jnp.concatenate([gain, blank], axis=1), jnp.concatenate([blank, gain], axis=1)
        pair_of[k : k + 1, :] = jnp.where(me.x == 0, left, right)
    pair_low[...] = pair_of[...].astype(LOW)
    shards = [pair_low] + list(raw[1:5]) + [gate_pad, up_pad, down_pad]
    bufs = [gain_buf] + list(hbm_bufs)
    flat = [b.reshape(2, chips * b.shape[4], b.shape[5]) for b in bufs]
    gather = Gather(ahead, me, shards, bufs, a_send, a_recv, own_sem)
    scatter = Scatter(back, me, total, got, outs, b_send, b_recv)
    ready = set()

    def pad_shards():
        part, tile = raw[7].shape[0], down_pad.shape[0]
        zero = jnp.zeros((raw[5].shape[0], tile - part), LOW)
        for src, dst in ((raw[5], gate_pad), (raw[6], up_pad)):
            value, pieces = src[...], []
            for k in range(value.shape[1] // part):
                pieces += [value[:, k * part : (k + 1) * part], zero]
            dst[...] = jnp.concatenate(pieces, axis=1)
        down_pad[...] = jnp.concatenate([raw[7][...], jnp.zeros((tile - part, down_pad.shape[1]), LOW)], axis=0)

    def prepare(t):
        if t >= 5 and 5 not in ready:
            pad_shards()
            for k in range(5, n):
                gather.own_copy(k).start()
                ready.add(k)
        elif t not in ready:
            gather.own_copy(t).start()
            ready.add(t)

    landed, arrived = set(), set()

    def land(t):
        if t not in landed:
            landed.add(t)
            gather.own_copy(t).wait()

    def need(*tensors, part=None):
        for t in tensors:
            mine = ahead.of_tensor[t]
            for i in mine if part is None else mine[part : part + 1]:
                if i not in arrived:
                    arrived.add(i)
                    gather.wait(i, 3)

    def norm(values, gain):
        inverse = lax.rsqrt(jnp.mean(values * values, axis=-1, keepdims=True) + EPS)
        return (values * inverse * gain).astype(LOW)

    def share(name, k, mine, whole):
        to = whole.at[:, own(rows)]
        later[name] = (load(mine, to), to_partner(k, mine, to))

    def shared(name):
        copy, sent = later[name]
        copy.wait()
        sent.wait()

    def turn(src, dst, lane):
        def body(j, _):
            at = pl.ds(pl.multiple_of(j * 128, 128), 128)
            dst[at, pl.ds(lane, rows)] = src[:, at].T
            return 0

        lax.fori_loop(0, src.shape[1] // 128, body, 0)
        return dst.at[:, pl.ds(lane, rows)]

    def first_norm():
        need(0)
        get_dy.wait()
        later["dy"] = to_partner(0, dy.at[:, own(columns, 1)], dyr)
        parts = []
        for z in range(NZ):
            for y in range(NY):
                pair = [gain_buf[me.s, z, y, x].astype(F32) for x in range(NX)]
                parts.append(pair[0] + pair[1])
        gains[...] = jnp.concatenate(parts, axis=1)[0:8]
        get_x.wait()

        def body(at):
            h1[at, :] = norm(xb[at, :].astype(F32), gains[0:1, :])

        each_rows(rows, 64, body)
        share("ha", 1, turn(h1, turned.at[0], 0), ha_h)

    def project(t, src, store):
        need(t)
        tiles = Stream(2, pool_sem, lambda j, slot: [(flat[t].at[j], pool.at[slot, pl.ds(0, width), :])])
        tiles.prime()

        def body(side, slot):
            for begin in range(0, columns, 256):
                part = mm(src[...], pool[slot, :width, begin : begin + 256])
                store(pl.ds(pl.multiple_of(side * columns + begin, 128), 256), part)

        tiles.run(body)

    def rim(k, ref):
        to = ref.at[pl.ds(0, WINDOW), :]
        return remote(ref.at[pl.ds(rows, WINDOW), :], to, half_send.at[2 + k], half_recv.at[2 + k], me.to_core())

    def put_into(ref, skip):
        def store(cols, part):
            ref[pl.ds(skip, rows), cols] = part.astype(LOW)

        return store

    def do_query():
        project(1, h1, put_into(da, 0))
        later["q_out"] = load(da.at[:, pl.ds(0, width)], q_h)

    def do_key():
        project(2, h1, put_into(kx, WINDOW))
        rim(0, kx).start()

    def do_value():
        project(3, h1, put_into(vx, WINDOW))
        rim(1, vx).start()

    first_end = lens[0, 0]
    second_end = first_end + lens[0, 1]

    def attend(b, _):
        base = me.s * rows + b * WINDOW
        at = pl.ds(pl.multiple_of(b * WINDOW, WINDOW), WINDOW)
        over = pl.ds(pl.multiple_of(b * WINDOW, WINDOW), SPAN)
        row = lax.broadcasted_iota(jnp.int32, (WINDOW, SPAN), 0)
        col = lax.broadcasted_iota(jnp.int32, (WINDOW, SPAN), 1)
        q_pos, k_pos = base + row, base - WINDOW + col

        def doc(pos):
            return (pos >= first_end).astype(jnp.int32) + (pos >= second_end).astype(jnp.int32)

        visible = (col >= row) & (col <= row + WINDOW) & (k_pos >= 0) & (doc(q_pos) == doc(k_pos))
        bias = jnp.where(visible, 0.0, -1e30)
        bias = jnp.concatenate([bias, bias], axis=0)
        pairs = range(HEADS // 2)
        cols = [slice(p * PAIR, (p + 1) * PAIR) for p in pairs]
        queries = [both_heads(da[at, c]) for c in cols]
        keys, values = [kx[over, c] for c in cols], [vx[over, c] for c in cols]
        scores = [mm_nt(q2, k) * HEAD_DIM ** (-0.5) + bias for q2, k in zip(queries, keys)]
        tops = [jnp.max(s, axis=-1, keepdims=True) for s in scores]
        exps = [jnp.exp(s - top) for s, top in zip(scores, tops)]
        sums = [jnp.sum(e, axis=-1, keepdims=True) for e in exps]
        weights = [(e * (1.0 / t)).astype(LOW) for e, t in zip(exps, sums)]
        parts = [merge_heads(mm(w, v)).astype(LOW) for w, v in zip(weights, values)]
        for p, c, w, part in zip(pairs, cols, weights, parts):
            db[at, 2 * p * SPAN : (2 * p + 1) * SPAN] = w[:WINDOW]
            db[at, (2 * p + 1) * SPAN : (2 * p + 2) * SPAN] = w[WINDOW:]
            o[at, c] = part
        return 0

    quarter = rows // WINDOW // 4

    def attend_part(k):
        if k == 0:
            for j, ref in ((0, kx), (1, vx)):
                rim(j, ref).wait_recv()
        lax.fori_loop(k * quarter, (k + 1) * quarter, attend, 0)
        if k == 3:
            later["p_out"] = load(db.at[:, pl.ds(0, HEADS * SPAN)], p_h)
            share("ho", 4, turn(o, turned.at[0], rows), ho_h)

    def add_out():
        def store(cols, part):
            x1[:, cols] = xb[:, cols].astype(F32) + part

        project(4, o, store)

        def body(at):
            xb[at, :] = norm(x1[at, :], gains[1:2, :])

        each_rows(rows, 64, body)
        share("hm", 5, turn(xb, turned.at[1], rows), hm_h)

    strips = [ahead.items[i][3] for i in ahead.of_tensor[5]]

    def strip_copies(p, side):
        begin, size = strips[p]
        return [
            pltpu.make_async_copy(
                flat[5 + k].at[side, :, pl.ds(begin, size)],
                pool.at[side, pl.ds(k * width, width), pl.ds(0, size)],
                pool_sem.at[side, k],
            )
            for k in range(2)
        ]

    def mlp(p):
        need(5, 6, part=p)
        for side in range(2):
            for copy in strip_copies(p, side):
                copy.start()
        if p == 0:
            later["p_out"].wait()
            for name in ("ha", "ho", "hm"):
                shared(name)
            later["hm"] = load(hm_h, turned.at[0])
        if p >= 2:
            for side in range(2):
                shared(("hid", p - 2, side))
        begin, size = strips[p]
        for side in range(2):
            for copy in strip_copies(p, side):
                copy.wait()
            for skip in range(0, size, 256):
                w = min(256, size - skip)
                cols = slice(skip, skip + w)
                a = mm(xb[...], pool[side, :width, cols])
                b = mm(xb[...], pool[side, width : 2 * width, cols])
                sig = 1.0 / (1.0 + jnp.exp(-a))
                silu = a * sig
                at = slice(side * wide + begin + skip, side * wide + begin + skip + w)
                grad = da[:, at].astype(F32)
                db[:, at] = (grad * silu).astype(LOW)
                da[:, at] = (grad * b * sig * (1.0 + a * (1.0 - sig))).astype(LOW)
                hidden_low = (silu * b).astype(LOW)
                hid[side, :, begin + skip : begin + skip + w] = hidden_low
                first = p % 2 * 512 + skip
                turned[1, first : first + w, side * rows : (side + 1) * rows] = hidden_low.T
        across = pl.ds(pl.multiple_of((1 - me.s) * wide + begin, 128), size)
        here = pl.ds(begin, size)
        later["db", p] = to_partner(6 + 4 * p, db.at[:, across], dbr.at[:, here])
        later["da", p] = to_partner(7 + 4 * p, da.at[:, across], dar.at[:, here])
        for side in range(2):
            mine = turned.at[1, pl.ds(p % 2 * 512, size), pl.ds(side * rows, rows)]
            share(("hid", p, side), 8 + 4 * p + side, mine, hid_h.at[pl.ds(side * wide + begin, size), :])
        if p == len(strips) - 1:
            mlp_tiles.prime()

    tall = back.tensors[0][0] * NY * NX
    hid_tiles = Stream(
        NZ, turn_sem, lambda j, slot: [(hid_h.at[pl.ds(pl.multiple_of(j * tall, 16), tall), :], turned.at[slot, pl.ds(0, tall), :])]
    )
    tile, thin = 256, 128
    small = pool.reshape(2, pool.shape[1] // tile, tile, columns)

    def row_tiles(w, size, dst):
        return lambda j, slot: (w.at[:, pl.ds(pl.multiple_of(j * size, size), size), :], dst(slot))

    def small_at(k):
        return lambda slot: small.at[slot, pl.ds(2 * k, 2)]

    def broad_at(k):
        return lambda slot: broad.at[slot, k]

    def stream_of(fetchers, count, sems):
        return Stream(count, sems, lambda j, slot: [f(j, slot) for f in fetchers])

    down_tiles = stream_of([row_tiles(flat[7], tile, small_at(0))], flat[7].shape[1] // tile, pool_sem)
    mlp_tiles = stream_of([row_tiles(flat[5 + k], thin, broad_at(k)) for k in range(2)], width // thin, broad_sem)
    out_tiles = stream_of([row_tiles(flat[4], tile, small_at(0))], width // tile, pool_sem)
    qkv_tiles = stream_of([row_tiles(flat[1 + k], tile, small_at(k)) for k in range(3)], width // tile, pool_sem)

    def begin_scatter(t):
        for i in back.of_tensor[t]:
            scatter.start(i, 0)

    def put(t, z, part, cols=slice(None)):
        low = part.reshape(NY, NX, back.tensors[t][0], part.shape[1]).astype(total[t].dtype)
        total[t][z, :, :, :, cols] = low

    def grad_down():
        for p in range(len(strips)):
            for side in range(2):
                if p + 2 >= len(strips):
                    shared(("hid", p, side))
        later["dy"].wait_recv()
        hid_tiles.prime()

        def body(z, slot):
            mine = mm(turned[slot, :tall, own(rows)], dy[:, own(columns)])
            put(0, z, mine + mm(turned[slot, :tall, own(rows, 1)], dyr[...]))

        hid_tiles.run(body)
        begin_scatter(0)
        later["ha"] = load(ha_h, turned.at[0])
        later["ho"] = load(ho_h, turned.at[1])

    def add_down():
        tiles2 = Stream(2, pool_sem, lambda j, slot: [(flat[7].at[j], pool.at[slot])])
        tiles2.prime()

        def body(side, slot):
            for begin in range(0, columns, 256):
                part = mm(hid[0], pool[slot, :wide, begin : begin + 256])
                part += mm(hid[1], pool[slot, wide:, begin : begin + 256])
                cols = pl.ds(pl.multiple_of(side * columns + begin, 128), 256)
                xb[:, cols] = (x1[:, cols] + part).astype(LOW)

        tiles2.run(body)
        later["mixed"] = load(xb, mixed_o)

    def hidden_body(j, slot):
        part = mm_nt(dy[:, :columns], small[slot, 0]) + mm_nt(dy[:, columns:], small[slot, 1])
        da[:, pl.ds(pl.multiple_of(j * tile, tile), tile)] = part.astype(LOW)

    def hidden(k):
        middle = down_tiles.count // 2
        if k == 0:
            need(7)
            down_tiles.prime()
            later["q_out"].wait()
            down_tiles.run(hidden_body, 0, middle)
            return
        down_tiles.run(hidden_body, middle)

    def weight_grad_to(t, slot, mine, theirs, cols=slice(None)):
        row_count = back.tensors[t][0] * NY * NX

        def step(z, _):
            at = pl.ds(pl.multiple_of(z * row_count, 16), row_count)
            put(t, z, mm(turned[slot, at, own(rows)], mine()) + mm(turned[slot, at, own(rows, 1)], theirs()), cols)
            return 0

        lax.fori_loop(0, NZ, step, 0)

    def grad_strip(t, name, grad, other, p):
        begin, size = strips[p]
        if p == 0 and t == 1:
            later["hm"].wait()
        later[name, p].wait_recv()
        cols = slice(begin, begin + size)
        mine = pl.ds(pl.multiple_of(me.s * wide + begin, 128), size)
        weight_grad_to(t, 0, lambda: grad[:, mine], lambda: other[:, cols], cols)
        scatter.start(back.of_tensor[t][p], 0)

    def dh2_body(j, slot):
        part = None
        for k, grad in ((0, da), (1, db)):
            for side in range(2):
                term = mm_nt(grad[:, side * wide : (side + 1) * wide], broad[slot, k, side])
                part = term if part is None else part + term
        dh[:, pl.ds(pl.multiple_of(j * thin, thin), thin)] = part

    def grad_norm2(k):
        middle = mlp_tiles.count // 2
        if k == 0:
            mlp_tiles.run(dh2_body, 0, middle)
            return
        mlp_tiles.run(dh2_body, middle)
        for p in range(len(strips)):
            later["db", p].wait_send()
            later["da", p].wait_send()
        out_tiles.prime()
        later["q"] = load(q_h, da.at[:, pl.ds(0, width)])
        later["p"] = load(p_h, db.at[:, pl.ds(0, HEADS * SPAN)])
        later["mixed"].wait()
        later["x"] = load(x_h, xb)

    def norm_grad(values, grad_norm, gain):
        inverse = lax.rsqrt(jnp.mean(values * values, axis=-1, keepdims=True) + EPS)
        scaled = grad_norm * gain
        mean_term = jnp.mean(values * scaled, axis=-1, keepdims=True)
        back_part = inverse * scaled - values * (inverse * inverse * inverse) * mean_term
        return back_part, jnp.sum(values * inverse * grad_norm, axis=0, keepdims=True)

    def norm2_body(at):
        back_part, gain_part = norm_grad(x1[at, :], dh[at, :], gains[1:2, :])
        gain_sum[1:2, :] += gain_part
        grad = dy[at, :].astype(F32) + back_part
        x1[at, :] = grad
        h1[at, :] = grad.astype(LOW)

    def norm2():
        gain_sum[...] = jnp.zeros_like(gain_sum)
        each_rows(rows, 64, norm2_body)
        later["dxr"] = to_partner(22, h1.at[:, own(columns, 1)], dxr_r)

    def out_body(j, slot):
        part = mm_nt(h1[:, :columns], small[slot, 0]) + mm_nt(h1[:, columns:], small[slot, 1])
        o[:, pl.ds(pl.multiple_of(j * tile, tile), tile)] = part.astype(LOW)

    def grad_heads():
        out_tiles.run(out_body)
        qkv_tiles.prime()

    def grad_out():
        later["ho"].wait()
        later["dxr"].wait_recv()
        weight_grad_to(3, 1, lambda: h1[:, own(columns)], lambda: dxr_r[...])
        begin_scatter(3)

    scale = HEAD_DIM ** (-0.5)

    def attend_back(b, _):
        at = pl.ds(pl.multiple_of(b * WINDOW, WINDOW), WINDOW)
        over = pl.ds(pl.multiple_of(b * WINDOW, WINDOW), SPAN)
        pairs = range(HEADS // 2)
        cols = [slice(p * PAIR, (p + 1) * PAIR) for p in pairs]
        queries, grads = [both_heads(da[at, c]) for c in cols], [both_heads(o[at, c]) for c in cols]
        keys, values = [kx[over, c] for c in cols], [vx[over, c] for c in cols]
        lows = [
            jnp.concatenate([db[at, (2 * p + h) * SPAN : (2 * p + h + 1) * SPAN] for h in range(2)], axis=0)
            for p in pairs
        ]
        carry_k, carry_v = [kc[:, c] for c in cols], [vc[:, c] for c in cols]
        probs = [low.astype(F32) for low in lows]
        grad_probs = [mm_nt(g, v) for g, v in zip(grads, values)]
        grad_values = [mm_tn(low, g) for low, g in zip(lows, grads)]
        inners = [jnp.sum(p * g, axis=-1, keepdims=True) for p, g in zip(probs, grad_probs)]
        scores = [(p * (g - i)).astype(LOW) for p, g, i in zip(probs, grad_probs, inners)]
        grad_queries = [(merge_heads(mm(s, k)) * scale).astype(LOW) for s, k in zip(scores, keys)]
        grad_keys = [mm_tn(s, q2) * scale for s, q2 in zip(scores, queries)]
        new_k = [(old + g[:WINDOW]).astype(LOW) for old, g in zip(carry_k, grad_keys)]
        new_v = [(old + g[:WINDOW]).astype(LOW) for old, g in zip(carry_v, grad_values)]
        for c, gq, gk, gv, nk, nv in zip(cols, grad_queries, grad_keys, grad_values, new_k, new_v):
            da[at, c] = gq
            kx[at, c] = nk
            vx[at, c] = nv
            kc[:, c] = gk[WINDOW:]
            vc[:, c] = gv[WINDOW:]
        return 0

    own_rows = pl.ds(WINDOW, rows)
    qr, kr, vr = dar.at[:, pl.ds(0, columns)], dar.at[:, pl.ds(columns, columns)], dbr.at[:, pl.ds(0, columns)]

    def attend_back_part(k):
        if k == 0:
            kc[...] = jnp.zeros_like(kc)
            vc[...] = jnp.zeros_like(vc)
            for j, ref in ((0, kx), (1, vx)):
                rim(j, ref).wait_send()
            later["q"].wait()
            later["p"].wait()
        lax.fori_loop(k * quarter, (k + 1) * quarter, attend_back, 0)
        if k == 0:
            later["rim"] = [
                to_partner(23, kx.at[pl.ds(0, WINDOW), :], rim_k),
                to_partner(24, vx.at[pl.ds(0, WINDOW), :], rim_v),
            ]
        if k == 3:
            for copy, ref, carry, rim_in in ((later["rim"][0], kx, kc, rim_k), (later["rim"][1], vx, vc, rim_v)):
                copy.wait_recv()
                ref[pl.ds(rows, WINDOW), :] = (carry[...] + rim_in[...].astype(F32)).astype(LOW)
            later["dq"] = to_partner(25, da.at[:, own(columns, 1)], qr)
            later["dk"] = to_partner(26, kx.at[own_rows, own(columns, 1)], kr)
            later["dv"] = to_partner(27, vx.at[own_rows, own(columns, 1)], vr)

    def grad_qkv(k):
        if k == 0:
            later["ha"].wait()
        later[("dq", "dk", "dv")[k]].wait_recv()
        mine = (lambda: da[:, own(columns)], lambda: kx[own_rows, own(columns)], lambda: vx[own_rows, own(columns)])[k]
        theirs = (qr, kr, vr)[k]
        weight_grad_to(4 + k, 0, mine, lambda: theirs[...])
        begin_scatter(4 + k)

    def dh1_body(j, slot):
        part = None
        for k, (grad, skip) in enumerate(((da, 0), (kx, WINDOW), (vx, WINDOW))):
            for side in range(2):
                left = grad[pl.ds(skip, rows), side * columns : (side + 1) * columns]
                term = mm_nt(left, small[slot, 2 * k + side])
                part = term if part is None else part + term
        dh[:, pl.ds(pl.multiple_of(j * tile, tile), tile)] = part

    def grad_norm1():
        qkv_tiles.run(dh1_body)

    def norm1_body(at):
        back_part, gain_part = norm_grad(xb[at, :].astype(F32), dh[at, :], gains[0:1, :])
        gain_sum[0:1, :] += gain_part
        x1[at, :] = x1[at, :] + back_part

    def norm1():
        later["x"].wait()
        each_rows(rows, 64, norm1_body)
        later["gtok"] = load(x1, gtok_o)
        later["gain"] = to_partner(28, gain_sum, gain_other)

    def grad_gains():
        later["gain"].wait_recv()
        lanes = back.tensors[7][1]
        for c in range(chips):
            at = slice(c // 2 * lanes, (c // 2 + 1) * lanes)
            total[7][c // 4, c // 2 % 2, c % 2] = gain_sum[:, at] + gain_other[:, at]
        begin_scatter(7)

    work = {
        "norm": first_norm,
        "query": do_query,
        "key": do_key,
        "value": do_value,
        "project": add_out,
        "mix": add_down,
        "down": grad_down,
        "norm2": norm2,
        "heads": grad_heads,
        "out": grad_out,
        "dh1": grad_norm1,
        "norm1": norm1,
        "gains": grad_gains,
    }
    for k in range(4):
        work["see", k] = functools.partial(attend_part, k)
        work["attend", k] = functools.partial(attend_back_part, k)
    for k in range(len(strips)):
        work["mlp", k] = functools.partial(mlp, k)
        work["up", k] = functools.partial(grad_strip, 1, "db", db, dbr, k)
        work["gate", k] = functools.partial(grad_strip, 2, "da", da, dar, k)
    for k in range(3):
        work["qkv", k] = functools.partial(grad_qkv, k)
    for k in range(2):
        work["hidden", k] = functools.partial(hidden, k)
        work["dh2", k] = functools.partial(grad_norm2, k)
    summed = []
    for step in SCRIPT:
        if step in work:
            work[step]()
        elif step[0] == "start":
            prepare(ahead.items[step[1]][0])
            gather.start(step[1], 0)
        elif step[0] == 0:
            _, i, phase, *hop = step
            land(ahead.items[i][0])
            if hop:
                gather.take_hop(i, phase, hop[0])
            else:
                gather.wait(i, phase)
            if hop in ([], [NZ - 1]):
                gather.start(i, phase + 1)
        else:
            _, i, phase = step
            scatter.wait(i, phase)
            scatter.add(i, phase)
            if phase < 2:
                scatter.start(i, phase + 1)
                continue
            t = back.items[i][0]
            summed.append(i)
            if all(k in summed for k in back.of_tensor[t]):
                later["sum", t] = load(outs[t], outs_h[t])
    for i in range(len(ahead.items)):
        gather.finish(i)
    for i in range(len(back.items)):
        scatter.finish(i)
    for k in (0, 22, 23, 24, 25, 26, 27, 28):
        halves[k].wait_send()
    later["gtok"].wait()
    for t in range(n):
        later["sum", t].wait()


def block_all(ahead, back, lens, tokens, cotangent, shards):
    n, na, nb = len(ahead.tensors), len(ahead.items), len(back.items)
    rows, width = tokens.shape
    columns, wide = ahead.tensors[1][1], ahead.tensors[5][1]
    anywhere = pl.BlockSpec(memory_space=pl.ANY)
    inside = pl.BlockSpec(memory_space=pltpu.VMEM)
    shape = jax.ShapeDtypeStruct
    over = WINDOW + rows
    bufs = [(2, NZ, NY, NX) + t[:2] for t in ahead.tensors]
    kept = [
        ((rows, width), LOW),
        ((rows, width), F32),
        ((rows, width), LOW),
        ((rows, HEADS * SPAN), LOW),
        ((width, 2 * rows), LOW),
        ((width, 2 * rows), LOW),
        ((width, 2 * rows), LOW),
        ((2 * wide, 2 * rows), LOW),
    ]
    scratch = [
        (ahead.tensors[5][:2], LOW),
        (ahead.tensors[6][:2], LOW),
        (ahead.tensors[7][:2], LOW),
        (bufs[0], LOW),
        ((8, width), F32),
        ((rows, width), LOW),
        ((rows, width), LOW),
        ((rows, 2 * wide), LOW),
        ((rows, 2 * wide), LOW),
        ((over, width), LOW),
        ((over, width), LOW),
        ((rows, width), LOW),
        ((rows, width), F32),
        ((2, rows, wide), LOW),
        ((rows, wide), LOW),
        ((rows, wide), LOW),
        (ahead.tensors[0][:2], F32),
        (ahead.tensors[0][:2], LOW),
        ((rows, width), LOW),
        ((rows, columns), LOW),
        ((rows, width), F32),
        ((rows, columns), LOW),
        ((2, width, 2 * rows), LOW),
        ((2, 2 * wide, columns), LOW),
        ((2, 2, 2, 128, wide), LOW),
        ((WINDOW, width), F32),
        ((WINDOW, width), F32),
        ((WINDOW, width), LOW),
        ((WINDOW, width), LOW),
        ((8, width), F32),
        ((8, width), F32),
    ]
    results = [(t[:2], F32) for t in back.tensors]
    totals = [((NZ, NY, NX) + t[:2], t[2]) for t in back.tensors]
    got = [part for parts in got_shapes(back) for part in parts]
    dma = pltpu.SemaphoreType.DMA
    outs = pl.pallas_call(
        functools.partial(block_kernel, ahead, back),
        out_shape=[shape(b, LOW) for b in bufs[1:]]
        + [shape(*s) for s in kept]
        + [shape(t[:2], F32) for t in back.tensors],
        in_specs=[pl.BlockSpec(memory_space=pltpu.SMEM), anywhere, anywhere] + [inside] * n,
        out_specs=[anywhere] * (n - 1 + len(kept) + n),
        scratch_shapes=[pltpu.VMEM(*s) for s in results + totals + got + scratch]
        + [dma((9 * na,)), dma((9 * na,)), dma((n,)), dma((5 * nb,)), dma((5 * nb,)), dma((36,))]
        + [dma((2, 3)), dma((2, 2)), dma((2, 1)), dma((29,)), dma((29,))],
        compiler_params=pltpu.CompilerParams(
            collective_id=0, has_side_effects=True, vmem_limit_bytes=VMEM_LIMIT
        ),
        name="block_all",
    )(lens, tokens, cotangent, *shards)
    return outs[n - 1 : n + 1], outs[n - 1 + len(kept) :]


def finish_kernel(*refs):
    n = 10
    ins, outs, held, made = refs[:n], refs[n : 2 * n + 1], refs[2 * n + 1 : 3 * n + 1], refs[3 * n + 1 : 4 * n + 2]
    sem_in, sem_out = refs[4 * n + 2 :]
    gets = [pltpu.make_async_copy(src, dst, sem_in.at[k]) for k, (src, dst) in enumerate(zip(ins, held))]
    for copy in gets:
        copy.start()
    puts = []

    def put(k, src):
        copy = pltpu.make_async_copy(src, outs[k], sem_out.at[k])
        copy.start()
        puts.append(copy)

    down, up, gate, out, query, key, value, gain = held[2:]
    for copy in gets[2:]:
        copy.wait()
    for k, src in ((2, query), (3, key), (4, value), (5, out)):
        put(k, src)
    rows, part, tile = query.shape[0], outs[8].shape[0], down.shape[0]
    made[8][...] = down[...][:part]
    put(8, made[8])
    for k, src in ((6, gate), (7, up)):
        values = src[...]
        made[k][...] = jnp.concatenate(
            [values[:, j * tile : j * tile + part] for j in range(values.shape[1] // tile)], axis=1
        )
        put(k, made[k])
    both = gain[...]
    own = jnp.where(lax.axis_index("dp") % 2 == 0, both[:, :rows], both[:, rows:])
    made[9][...] = own[0:1]
    made[10][...] = own[1:2]
    put(9, made[9])
    put(10, made[10])
    for k in range(2):
        gets[k].wait()
        put(k, held[k])
    for copy in puts:
        copy.wait()


def finish_all(mixed, tokens, sums, w_query, w_gate, w_down):
    anywhere = pl.BlockSpec(memory_space=pl.ANY)
    shape = jax.ShapeDtypeStruct
    outs = [shape(mixed.shape, mixed.dtype), shape(tokens.shape, F32)]
    outs += [shape(w_query.shape, F32)] * 4 + [shape(w_gate.shape, F32)] * 2 + [shape(w_down.shape, F32)]
    outs += [shape((1, w_query.shape[0]), F32)] * 2
    ins = [mixed, tokens, *sums]
    return pl.pallas_call(
        finish_kernel,
        out_shape=outs,
        in_specs=[anywhere] * len(ins),
        out_specs=[anywhere] * len(outs),
        scratch_shapes=[pltpu.VMEM(a.shape, a.dtype) for a in ins + outs]
        + [pltpu.SemaphoreType.DMA((len(ins),)), pltpu.SemaphoreType.DMA((len(outs),))],
        compiler_params=pltpu.CompilerParams(vmem_limit_bytes=62 * 2**20),
        name="finish_all",
    )(*ins)


def kinds(w_query, w_gate, w_down):
    rows, columns = w_query.shape
    part = w_down.shape[0]
    tile = -(-part // 16) * 16
    wide = w_gate.shape[1] // part * tile
    half, strip = rows // 2, -(-wide // 512) * 128
    long, short = -(-tile // 64) * 16, tile - 3 * (-(-tile // 64) * 16)

    def cuts(kinds, counts):
        return tuple((kind, 0, count) for kind, count in zip(kinds, counts, strict=True))

    def strips(kinds):
        return tuple((kind, 1, min(strip, wide - k * strip)) for k, kind in enumerate(kinds))

    return {
        "square": (rows, columns, LOW, cuts(("zfx", "zfy"), (half, half))),
        "broad": (rows, wide, LOW, strips(("zfx", "zfy", "zmx", "zmy"))),
        "broad_f": (rows, wide, LOW, strips(("zfx", "zfy", "zfx", "zfy"))),
        "broad_m": (rows, wide, LOW, strips(("zmx", "zmy", "zmx", "zmy"))),
        "tall": (tile, columns, LOW, cuts(("zfx", "zfy", "zmx", "zmy"), (long, long, long, short))),
        "square_m": (rows, columns, LOW, cuts(("zmx", "zmy"), (half, half))),
        "tall_f": (tile, columns, LOW, cuts(("zfx", "zfy", "zfx", "zfy"), (long, long, long, short))),
        "tall_m": (tile, columns, LOW, cuts(("zmx", "zmy", "zmx", "zmy"), (long, long, long, short))),
        "gain": (16, 2 * rows, LOW, cuts(("zfx",), (16,))),
        "gain_grad": (8, 2 * rows, F32, cuts(("zfx",), (8,))),
    }


def gather_plan(w_query, w_key, w_value, w_out, w_gate, w_up, w_down, gain_attn, gain_mlp):
    kind = kinds(w_query, w_gate, w_down)
    names = ("gain", "square", "square_m", "square_m", "square", "broad", "broad_m", "tall_m")
    plan = Plan([kind[name] for name in names])
    both = jnp.concatenate([gain_attn[None], gain_mlp[None]], axis=0)
    shards = [
        both,
        w_query,
        w_key,
        w_value,
        w_out,
        w_gate,
        w_up,
        w_down,
    ]
    return plan, shards


def swift_block(
    tokens,
    seq_lengths,
    w_query,
    w_key,
    w_value,
    w_out,
    w_gate,
    w_up,
    w_down,
    gain_attn,
    gain_mlp,
    cotangent,
):
    plan, shards = gather_plan(w_query, w_key, w_value, w_out, w_gate, w_up, w_down, gain_attn, gain_mlp)
    kind = kinds(w_query, w_gate, w_down)
    names = ("tall", "broad_f", "broad", "square", "square", "square", "square", "gain_grad")
    back = Plan([kind[name] for name in names])
    results, sums = block_all(plan, back, seq_lengths, tokens, cotangent, shards)
    outs = finish_all(results[0], results[1], sums, w_query, w_gate, w_down)
    return (*outs[:9], outs[9].reshape(-1), outs[10].reshape(-1))


def solution(mesh):
    fast = (mesh.shape["dp"], mesh.shape["seq"]) == (NZ * NY * NX, 2)
    shards = swift_block if fast else plain_block
    in_specs = (
        P(("dp", "seq"), None),
        P("dp", None),
        P("dp", "seq"),
        P("dp", "seq"),
        P("dp", "seq"),
        P("dp", "seq"),
        P("dp", "seq"),
        P("dp", "seq"),
        P("dp", "seq"),
        P("dp"),
        P("dp"),
        P(("dp", "seq"), None),
    )
    out_specs = (
        P(("dp", "seq"), None),
        P(("dp", "seq"), None),
        P("dp", "seq"),
        P("dp", "seq"),
        P("dp", "seq"),
        P("dp", "seq"),
        P("dp", "seq"),
        P("dp", "seq"),
        P("dp", "seq"),
        P("dp"),
        P("dp"),
    )
    return jax.shard_map(shards, mesh=mesh, in_specs=in_specs, out_specs=out_specs, check_vma=False)
```

```python
import functools

import jax
import jax.numpy as jnp
from jax import lax
from jax.experimental import pallas as pl
from jax.experimental.pallas import tpu as pltpu
from jax.sharding import PartitionSpec as P

HEADS = 16
HEAD_DIM = 64
WINDOW = 64


eps_norm = 1e-05


def from_behind(block, axis, distance):
    devices = range(lax.axis_size(axis))
    route = [(i - distance, i) for i in devices if i - distance in devices]
    return lax.ppermute(block, axis, route)


def inverse_rms(values):
    return lax.rsqrt(jnp.mean(values * values, axis=-1, keepdims=True) + eps_norm)


def doc_numbers(lengths_row, positions):
    first_end = lengths_row[0]
    second_end = lengths_row[0] + lengths_row[1]
    return (positions >= first_end).astype(jnp.int32) + (positions >= second_end).astype(jnp.int32)


def window_mask(query_pos, query_doc, key_pos, key_doc, window):
    after = key_pos[None, :] >= query_pos[:, None] - window
    before = key_pos[None, :] <= query_pos[:, None]
    inside = (key_pos[None, :] >= 0) & (key_doc[None, :] == query_doc[:, None])
    return after & before & inside


def norm_back(values, inverse, gain, grad_norm):
    scaled = grad_norm * gain
    mean_term = jnp.mean(values * scaled, axis=-1, keepdims=True)
    grad_values = inverse * scaled - values * (inverse * inverse * inverse) * mean_term
    grad_gain = jnp.sum(values * inverse * grad_norm, axis=0)
    return (grad_values, grad_gain)


def project(left, right):
    return jnp.dot(left, right, preferred_element_type=jnp.float32)


def project_back(grad_rows, weight):
    return jnp.einsum("tf,df->td", grad_rows, weight, preferred_element_type=jnp.float32)


def weight_grad(inputs, grad_rows):
    return jnp.einsum("td,tf->df", inputs, grad_rows, preferred_element_type=jnp.float32)


def plain_block(
    tokens,
    seq_lengths,
    w_query,
    w_key,
    w_value,
    w_out,
    w_gate,
    w_up,
    w_down,
    gain_attn,
    gain_mlp,
    cotangent,
):
    row_count = tokens.shape[0]
    block_rows = min(512, row_count)
    head_group = HEADS // 2
    score_scale = HEAD_DIM ** (-0.5)
    row_parts = (
        lax.all_gather(w_query, "dp", axis=0, tiled=True),
        lax.all_gather(w_key, "dp", axis=0, tiled=True),
        lax.all_gather(w_value, "dp", axis=0, tiled=True),
        lax.all_gather(w_out, "dp", axis=0, tiled=True),
        lax.all_gather(w_gate, "dp", axis=0, tiled=True),
        lax.all_gather(w_up, "dp", axis=0, tiled=True),
        lax.all_gather(w_down, "dp", axis=0, tiled=True),
        lax.all_gather(gain_attn, "dp", axis=0, tiled=True),
        lax.all_gather(gain_mlp, "dp", axis=0, tiled=True),
    )
    full_mats = (
        lax.all_gather(row_parts[0], "seq", axis=1, tiled=True),
        lax.all_gather(row_parts[1], "seq", axis=1, tiled=True),
        lax.all_gather(row_parts[2], "seq", axis=1, tiled=True),
        lax.all_gather(row_parts[3], "seq", axis=1, tiled=True),
        lax.all_gather(row_parts[4], "seq", axis=1, tiled=True),
        lax.all_gather(row_parts[5], "seq", axis=1, tiled=True),
        lax.all_gather(row_parts[6], "seq", axis=1, tiled=True),
    )
    query_w, key_w, value_w, out_w, gate_w, up_w, down_full = full_mats
    gain_one = row_parts[7].astype(jnp.float32)
    gain_two = row_parts[8].astype(jnp.float32)
    inputs = tokens.astype(jnp.float32)
    inv_one = inverse_rms(inputs)
    normed_one = (inputs * inv_one * gain_one).astype(jnp.bfloat16)
    query_low = project(normed_one, query_w).astype(jnp.bfloat16)
    key_low = project(normed_one, key_w).astype(jnp.bfloat16)
    value_low = project(normed_one, value_w).astype(jnp.bfloat16)
    rim_pairs = from_behind(
        (key_low[row_count - WINDOW :], value_low[row_count - WINDOW :]), "seq", 1
    )
    keys_ext = jnp.concatenate([rim_pairs[0], key_low], axis=0).reshape(
        row_count + WINDOW, HEADS, HEAD_DIM
    )
    values_ext = jnp.concatenate([rim_pairs[1], value_low], axis=0).reshape(
        row_count + WINDOW, HEADS, HEAD_DIM
    )
    query_heads = query_low.reshape(row_count, HEADS, HEAD_DIM)
    span_start = lax.axis_index("seq") * row_count
    query_pos = span_start + jnp.arange(row_count, dtype=jnp.int32)
    key_pos = span_start - WINDOW + jnp.arange(row_count + WINDOW, dtype=jnp.int32)
    query_doc = doc_numbers(seq_lengths[0], query_pos)
    key_doc = doc_numbers(seq_lengths[0], key_pos)

    def tile_scores(row_start, head_start):
        visible = window_mask(query_pos, query_doc, key_pos, key_doc, WINDOW)
        scores_raw = (
            jnp.einsum(
                "qhd,khd->hqk",
                query_heads[
                    row_start : row_start + block_rows, head_start : head_start + head_group
                ],
                keys_ext[
                    row_start : row_start + block_rows + WINDOW,
                    head_start : head_start + head_group,
                ],
                preferred_element_type=jnp.float32,
            )
            * score_scale
        )
        return jnp.where(visible[None], scores_raw, -1e30)

    log_totals = {}
    row_start = 0
    head_parts = []
    for head_start in range(0, HEADS, head_group):
        masked_scores = tile_scores(row_start, head_start)
        top_score = jnp.max(masked_scores, axis=-1, keepdims=True)
        log_total = top_score + jnp.log(
            jnp.sum(jnp.exp(masked_scores - top_score), axis=-1, keepdims=True)
        )
        prob_low = jnp.exp(masked_scores - log_total).astype(jnp.bfloat16)
        value_tile = values_ext[
            row_start : row_start + block_rows + WINDOW, head_start : head_start + head_group
        ]
        head_parts.append(
            jnp.einsum("hqk,khd->qhd", prob_low, value_tile, preferred_element_type=jnp.float32)
        )
        log_totals[row_start, head_start] = log_total
    attn_blocks = jnp.concatenate(head_parts, axis=1)
    attended = attn_blocks.reshape(row_count, HEADS * HEAD_DIM).astype(jnp.bfloat16)
    middle = inputs + project(attended, out_w)
    inv_two = inverse_rms(middle)
    normed_two = (middle * inv_two * gain_two).astype(jnp.bfloat16)
    gate_pre = project(normed_two, gate_w)
    up_pre = project(normed_two, up_w)
    gate_act = jax.nn.silu(gate_pre)
    hidden = (gate_act * up_pre).astype(jnp.bfloat16)
    block_out = (middle + project(hidden, down_full)).astype(jnp.bfloat16)
    rows_again = (
        lax.all_gather(w_query, "dp", axis=0, tiled=True),
        lax.all_gather(w_key, "dp", axis=0, tiled=True),
        lax.all_gather(w_value, "dp", axis=0, tiled=True),
        lax.all_gather(w_out, "dp", axis=0, tiled=True),
        lax.all_gather(w_gate, "dp", axis=0, tiled=True),
        lax.all_gather(w_up, "dp", axis=0, tiled=True),
        lax.all_gather(w_down, "dp", axis=0, tiled=True),
        lax.all_gather(gain_attn, "dp", axis=0, tiled=True),
        lax.all_gather(gain_mlp, "dp", axis=0, tiled=True),
    )
    mats_again = (
        lax.all_gather(rows_again[0], "seq", axis=1, tiled=True),
        lax.all_gather(rows_again[1], "seq", axis=1, tiled=True),
        lax.all_gather(rows_again[2], "seq", axis=1, tiled=True),
        lax.all_gather(rows_again[3], "seq", axis=1, tiled=True),
        lax.all_gather(rows_again[4], "seq", axis=1, tiled=True),
        lax.all_gather(rows_again[5], "seq", axis=1, tiled=True),
        lax.all_gather(rows_again[6], "seq", axis=1, tiled=True),
    )
    back_query, back_key, back_value, back_out, back_gate, back_up, back_down = mats_again
    back_gain_one = rows_again[7].astype(jnp.float32)
    back_gain_two = rows_again[8].astype(jnp.float32)
    grad_final = cotangent.astype(jnp.float32)
    d_down = weight_grad(hidden, cotangent)
    grad_hidden = project_back(cotangent, back_down)
    sigmoid_gate = jax.nn.sigmoid(gate_pre)
    grad_gate_low = (
        grad_hidden * up_pre * sigmoid_gate * (1.0 + gate_pre * (1.0 - sigmoid_gate))
    ).astype(jnp.bfloat16)
    grad_up_low = (grad_hidden * gate_act).astype(jnp.bfloat16)
    d_gate = weight_grad(normed_two, grad_gate_low)
    d_up = weight_grad(normed_two, grad_up_low)
    grad_normed_two = project_back(grad_gate_low, back_gate) + project_back(grad_up_low, back_up)
    grad_mid_norm, d_gain_two = norm_back(middle, inv_two, back_gain_two, grad_normed_two)
    grad_middle = grad_final + grad_mid_norm
    grad_proj = grad_middle.astype(jnp.bfloat16)
    d_out = weight_grad(attended, grad_proj)
    grad_attended = (
        project_back(grad_proj, back_out).astype(jnp.bfloat16).reshape(row_count, HEADS, HEAD_DIM)
    )
    grad_keys_ext = jnp.zeros((row_count + WINDOW, HEADS, HEAD_DIM), jnp.float32)
    grad_values_ext = jnp.zeros((row_count + WINDOW, HEADS, HEAD_DIM), jnp.float32)
    row_start = 0
    head_parts = []
    for head_start in range(0, HEADS, head_group):
        head_end = head_start + head_group
        masked_scores = tile_scores(row_start, head_start)
        prob_full = jnp.exp(masked_scores - log_totals[row_start, head_start])
        grad_tile = grad_attended[row_start : row_start + block_rows, head_start:head_end]
        key_tile = keys_ext[row_start : row_start + block_rows + WINDOW, head_start:head_end]
        value_tile = values_ext[row_start : row_start + block_rows + WINDOW, head_start:head_end]
        query_tile = query_heads[row_start : row_start + block_rows, head_start:head_end]
        grad_prob = jnp.einsum(
            "qhd,khd->hqk", grad_tile, value_tile, preferred_element_type=jnp.float32
        )
        inner = jnp.sum(prob_full * grad_prob, axis=-1, keepdims=True)
        grad_score = (prob_full * (grad_prob - inner)).astype(jnp.bfloat16)
        head_parts.append(
            jnp.einsum("hqk,khd->qhd", grad_score, key_tile, preferred_element_type=jnp.float32)
            * score_scale
        )
        key_term = (
            jnp.einsum("hqk,qhd->khd", grad_score, query_tile, preferred_element_type=jnp.float32)
            * score_scale
        )
        value_term = jnp.einsum(
            "hqk,qhd->khd",
            prob_full.astype(jnp.bfloat16),
            grad_tile,
            preferred_element_type=jnp.float32,
        )
        grad_keys_ext = grad_keys_ext.at[
            row_start : row_start + block_rows + WINDOW, head_start:head_end
        ].add(key_term)
        grad_values_ext = grad_values_ext.at[
            row_start : row_start + block_rows + WINDOW, head_start:head_end
        ].add(value_term)
    grad_query_blocks = jnp.concatenate(head_parts, axis=1)
    rim_back = (
        from_behind(
            grad_keys_ext[:WINDOW].reshape(WINDOW, HEADS * HEAD_DIM).astype(jnp.bfloat16), "seq", -1
        ).astype(jnp.float32),
        from_behind(
            grad_values_ext[:WINDOW].reshape(WINDOW, HEADS * HEAD_DIM).astype(jnp.bfloat16),
            "seq",
            -1,
        ).astype(jnp.float32),
    )
    grad_keys = (
        grad_keys_ext[WINDOW:]
        .reshape(row_count, HEADS * HEAD_DIM)
        .at[row_count - WINDOW :]
        .add(rim_back[0])
    )
    grad_values = (
        grad_values_ext[WINDOW:]
        .reshape(row_count, HEADS * HEAD_DIM)
        .at[row_count - WINDOW :]
        .add(rim_back[1])
    )
    grad_query_low = grad_query_blocks.reshape(row_count, HEADS * HEAD_DIM).astype(jnp.bfloat16)
    grad_key_low = grad_keys.astype(jnp.bfloat16)
    grad_value_low = grad_values.astype(jnp.bfloat16)
    d_query = weight_grad(normed_one, grad_query_low)
    d_key = weight_grad(normed_one, grad_key_low)
    d_value = weight_grad(normed_one, grad_value_low)
    grad_normed_one = (
        project_back(grad_query_low, back_query)
        + project_back(grad_key_low, back_key)
        + project_back(grad_value_low, back_value)
    )
    grad_in_norm, d_gain_one = norm_back(inputs, inv_one, back_gain_one, grad_normed_one)
    grad_inputs = grad_middle + grad_in_norm
    row_sums = (
        lax.psum_scatter(
            d_query.astype(jnp.bfloat16), "dp", scatter_dimension=0, tiled=True
        ).astype(jnp.float32),
        lax.psum_scatter(d_key.astype(jnp.bfloat16), "dp", scatter_dimension=0, tiled=True).astype(
            jnp.float32
        ),
        lax.psum_scatter(
            d_value.astype(jnp.bfloat16), "dp", scatter_dimension=0, tiled=True
        ).astype(jnp.float32),
        lax.psum_scatter(d_out.astype(jnp.bfloat16), "dp", scatter_dimension=0, tiled=True).astype(
            jnp.float32
        ),
        lax.psum_scatter(d_gate.astype(jnp.bfloat16), "dp", scatter_dimension=0, tiled=True).astype(
            jnp.float32
        ),
        lax.psum_scatter(d_up.astype(jnp.bfloat16), "dp", scatter_dimension=0, tiled=True).astype(
            jnp.float32
        ),
        lax.psum_scatter(d_down.astype(jnp.bfloat16), "dp", scatter_dimension=0, tiled=True).astype(
            jnp.float32
        ),
        lax.psum_scatter(
            d_gain_one.astype(jnp.bfloat16), "dp", scatter_dimension=0, tiled=True
        ).astype(jnp.float32),
        lax.psum_scatter(
            d_gain_two.astype(jnp.bfloat16), "dp", scatter_dimension=0, tiled=True
        ).astype(jnp.float32),
    )
    owned_mats = (
        lax.psum_scatter(
            row_sums[0].astype(jnp.bfloat16), "seq", scatter_dimension=1, tiled=True
        ).astype(jnp.float32),
        lax.psum_scatter(
            row_sums[1].astype(jnp.bfloat16), "seq", scatter_dimension=1, tiled=True
        ).astype(jnp.float32),
        lax.psum_scatter(
            row_sums[2].astype(jnp.bfloat16), "seq", scatter_dimension=1, tiled=True
        ).astype(jnp.float32),
        lax.psum_scatter(
            row_sums[3].astype(jnp.bfloat16), "seq", scatter_dimension=1, tiled=True
        ).astype(jnp.float32),
        lax.psum_scatter(
            row_sums[4].astype(jnp.bfloat16), "seq", scatter_dimension=1, tiled=True
        ).astype(jnp.float32),
        lax.psum_scatter(
            row_sums[5].astype(jnp.bfloat16), "seq", scatter_dimension=1, tiled=True
        ).astype(jnp.float32),
        lax.psum_scatter(
            row_sums[6].astype(jnp.bfloat16), "seq", scatter_dimension=1, tiled=True
        ).astype(jnp.float32),
    )
    owned_gains = lax.psum((row_sums[7], row_sums[8]), "seq")
    return (
        block_out,
        grad_inputs,
        owned_mats[0],
        owned_mats[1],
        owned_mats[2],
        owned_mats[3],
        owned_mats[4],
        owned_mats[5],
        owned_mats[6],
        owned_gains[0],
        owned_gains[1],
    )


SCRIPT = (
    ("start", 4), ("start", 7), ("start", 9), ("start", 0), ("start", 13), ("start", 2), ("start", 11),
    ("start", 5), ("start", 10), (0, 4, 0), ("start", 18), ("start", 15), ("start", 19), ("start", 20),
    (0, 0, 0, 1), ("start", 6), ("start", 3), (0, 5, 0), (0, 10, 0, 1), ("start", 1), (0, 9, 0, 1), (0, 6, 0),
    (0, 5, 1, 1), (0, 2, 0, 1), ("start", 16), (0, 9, 0, 2), (0, 0, 0, 2), (0, 1, 0, 1), (0, 10, 0, 2),
    ("start", 17), ("start", 12), (0, 18, 0), (0, 0, 0, 3), ("start", 14), (0, 3, 0), (0, 1, 0, 2),
    (0, 2, 0, 2), (0, 0, 1), (0, 9, 0, 3), (0, 10, 0, 3), (0, 2, 0, 3), (0, 20, 0), (0, 18, 1, 1), (0, 0, 2),
    (0, 3, 1, 1), (0, 4, 1, 1), (0, 9, 1), (0, 7, 0, 1), (0, 1, 0, 3), (0, 12, 0), (0, 17, 0), (0, 19, 0),
    (0, 2, 1), (0, 5, 1, 2), (0, 6, 1, 1), (0, 4, 1, 2), ("start", 8), (0, 1, 1), (0, 10, 1), (0, 3, 1, 2),
    "norm", (0, 8, 0, 1), (0, 2, 2), (0, 5, 1, 3), (0, 7, 0, 2), (0, 8, 0, 2), (0, 7, 0, 3), (0, 20, 1, 1),
    (0, 19, 1, 1), (0, 9, 2), (0, 1, 2), (0, 13, 0), (0, 17, 1, 1), (0, 6, 1, 2), (0, 4, 1, 3), (0, 3, 1, 3),
    (0, 5, 2), (0, 8, 0, 3), (0, 6, 1, 3), (0, 20, 1, 2), (0, 17, 1, 2), (0, 18, 1, 2), (0, 7, 1), (0, 10, 2),
    (0, 3, 2), (0, 4, 2), (0, 11, 0), "query", (0, 8, 1), (0, 18, 1, 3), (0, 14, 0), (0, 17, 1, 3),
    (0, 13, 1, 1), (0, 16, 0), (0, 6, 2), "key", (0, 19, 1, 2), "value", (0, 19, 1, 3), (0, 16, 1, 1),
    (0, 14, 1, 1), (0, 13, 1, 2), (0, 20, 1, 3), (0, 15, 0), ("see", 0), (0, 7, 2), (0, 8, 2), (0, 11, 1, 1),
    ("see", 1), (0, 17, 2), (0, 13, 1, 3), ("see", 2), (0, 14, 1, 2), ("see", 3), (0, 12, 1, 1), (0, 18, 2),
    (0, 14, 1, 3), (0, 19, 2), (0, 11, 1, 2), (0, 20, 2), (0, 15, 1, 1), "project", (0, 16, 1, 2), (0, 13, 2),
    (0, 11, 1, 3), (0, 15, 1, 2), (0, 12, 1, 2), ("hidden", 0), ("hidden", 1), (0, 15, 1, 3), (0, 16, 1, 3),
    (0, 14, 2), (0, 12, 1, 3), ("mlp", 0), ("mlp", 1), ("up", 0), (0, 11, 2), ("gate", 0), (0, 15, 2),
    ("gate", 1), ("up", 1), (0, 12, 2), (0, 16, 2), ("mlp", 2), ("mlp", 3), (1, 9, 0), ("up", 2), (1, 8, 0),
    ("dh2", 0), ("gate", 2), ("gate", 3), ("up", 3), "mix", (1, 9, 1), (1, 8, 1), "down", (1, 11, 0),
    ("dh2", 1), "norm2", (1, 10, 0), "heads", (1, 6, 0), (1, 7, 0), ("attend", 0), ("attend", 1),
    ("attend", 2), ("attend", 3), (1, 3, 0), "out", (1, 6, 1), (1, 0, 0), ("qkv", 0), (1, 2, 0), "dh1",
    (1, 1, 0), (1, 7, 1), ("qkv", 1), (1, 14, 0), (1, 9, 2), (1, 0, 1), (1, 13, 0), "norm1", (1, 1, 1),
    (1, 15, 0), (1, 12, 0), ("qkv", 2), (1, 14, 1), (1, 7, 2), "gains", (1, 13, 1), (1, 6, 2), (1, 12, 1),
    (1, 16, 0), (1, 15, 1), (1, 17, 0), (1, 20, 0), (1, 5, 0), (1, 19, 0), (1, 18, 0), (1, 20, 1), (1, 0, 2),
    (1, 10, 1), (1, 17, 1), (1, 4, 0), (1, 16, 1), (1, 2, 1), (1, 19, 1), (1, 11, 1), (1, 13, 2), (1, 20, 2),
    (1, 14, 2), (1, 3, 1), (1, 8, 2), (1, 5, 1), (1, 18, 1), (1, 1, 2), (1, 4, 1), (1, 11, 2), (1, 15, 2),
    (1, 12, 2), (1, 10, 2), (1, 2, 2), (1, 17, 2), (1, 16, 2), (1, 5, 2), (1, 3, 2), (1, 4, 2), (1, 19, 2),
    (1, 18, 2),
)
GATHER_KINDS = (("gain", "f"), ("square", "f"), ("square", "m"), ("square", "m"), ("square", "f"), ("broad", "fm"), ("broad", "mm"), ("tall", "mm"))
SCATTER_KINDS = (("tall", "fm"), ("broad", "lf"), ("broad", "fm"), ("square", "f"), ("square", "f"), ("square", "f"), ("square", "f"), ("gain_grad", "f"))


MESH = pl.DeviceIdType.MESH
NZ, NY, NX = 4, 2, 2
SEQUENCE = {"zfx": "zxy", "zfy": "zyx", "zmx": "xzy", "zmy": "yzx", "zlx": "xyz", "zly": "yxz"}
ALL_Z, ALL_Y, ALL_X = pl.ds(0, NZ), pl.ds(0, NY), pl.ds(0, NX)


class Plan:
    def __init__(self, tensors):
        self.tensors = tensors
        self.items, self.of_tensor = [], []
        for t, (_, _, _, cuts) in enumerate(tensors):
            begin, mine = 0, []
            for kind, along, count in cuts:
                mine.append(len(self.items))
                whole = [(0, tensors[t][0]), (0, tensors[t][1])]
                whole[along] = (begin, count)
                self.items.append((t, SEQUENCE[kind], *whole))
                begin += count
            self.of_tensor.append(mine)


class Place:
    def __init__(self):
        self.c, self.s = lax.axis_index("dp"), lax.axis_index("seq")
        self.z, self.y, self.x = self.c // 4, (self.c // 2) % 2, self.c % 2

    def at(self, z, y, x):
        return (z * 4 + y * 2 + x, self.s)

    def to_x(self):
        return self.at(self.z, self.y, 1 - self.x)

    def to_y(self):
        return self.at(self.z, 1 - self.y, self.x)

    def to_z(self, step):
        return self.at((self.z + step) % NZ, self.y, self.x)

    def to_core(self):
        return (self.c, 1 - self.s)

    def greet(self):
        barrier = pltpu.get_barrier_semaphore()
        peers = [self.to_x(), self.to_y(), self.to_core()] + [self.to_z(k) for k in (1, 2, 3)]
        for peer in peers:
            pl.semaphore_signal(barrier, inc=1, device_id=peer, device_id_type=MESH)
        pl.semaphore_wait(barrier, len(peers))


def remote(src, dst, send, recv, device):
    return pltpu.make_async_remote_copy(
        src_ref=src, dst_ref=dst, send_sem=send, recv_sem=recv, device_id=device, device_id_type=MESH
    )


def slots(seq, count, along_z):
    firsts, used = [], 0
    for phase in range(count):
        firsts.append(used)
        used += along_z if phase < 3 and seq[phase] == "z" else 1
    return firsts


class Gather:
    def __init__(self, plan, place, shards, bufs, send, recv, local):
        self.plan, self.me, self.shards, self.bufs = plan, place, shards, bufs
        self.send, self.recv, self.local = send, recv, local

    def own_copy(self, t):
        me = self.me
        return pltpu.make_async_copy(
            self.shards[t], self.bufs[t].at[me.s, me.z, me.y, me.x], self.local.at[t]
        )

    def moves(self, i, phase):
        t, seq, rows, cols = self.plan.items[i]
        me, buf = self.me, self.bufs[t]
        rows, cols = pl.ds(*rows), pl.ds(*cols)

        def view(z, y, x, half=me.s):
            return buf.at[half, z, y, x, rows, cols]

        if phase == 3:
            whole = view(ALL_Z, ALL_Y, ALL_X)
            return [(whole, whole, me.to_core(), view(ALL_Z, ALL_Y, ALL_X, 1 - me.s), 0)]
        done, axis = seq[:phase], seq[phase]
        z = ALL_Z if "z" in done else me.z
        y = ALL_Y if "y" in done else me.y
        x = ALL_X if "x" in done else me.x
        there = view(z, y, x)
        here = self.shards[t].at[rows, cols] if phase == 0 else there
        if axis == "x":
            return [(here, there, me.to_x(), view(z, y, 1 - me.x), 0)]
        return [(here, there, me.to_y(), view(z, 1 - me.y, x), 0)]

    def hops(self, i, phase, hop):
        t, seq, rows, cols = self.plan.items[i]
        me, buf = self.me, self.bufs[t]
        rows, cols = pl.ds(*rows), pl.ds(*cols)
        done = seq[:phase]
        y = ALL_Y if "y" in done else me.y
        x = ALL_X if "x" in done else me.x
        moves = []
        for k, way in enumerate((1, -1)):
            first, last = (me.z, NZ - 1 - me.z) if way == 1 else (NZ - 1 - me.z, me.z)
            sends = (first >= hop - 1) & (last >= 1)
            takes = first >= hop
            z = me.z - way * (hop - 1)
            there = buf.at[me.s, z, y, x, rows, cols]
            here = self.shards[t].at[rows, cols] if phase == 0 and hop == 1 else there
            arrived = buf.at[me.s, me.z - way * hop, y, x, rows, cols]
            moves.append((sends, takes, here, there, me.at(me.z + way, me.y, me.x), arrived, 3 * k + hop - 1))
        return moves

    def along_z(self, i, phase):
        return phase < 3 and self.plan.items[i][1][phase] == "z"

    def copy(self, i, phase, src, dst, device, k):
        at = 9 * i + slots(self.plan.items[i][1], 4, 6)[phase] + k
        return remote(src, dst, self.send.at[at], self.recv.at[at], device)

    def send_hop(self, i, phase, hop):
        for sends, _, here, there, device, _, k in self.hops(i, phase, hop):

            @pl.when(sends)
            def _(here=here, there=there, device=device, k=k):
                self.copy(i, phase, here, there, device, k).start()

    def take_hop(self, i, phase, hop):
        for _, takes, _, _, device, arrived, k in self.hops(i, phase, hop):

            @pl.when(takes)
            def _(device=device, arrived=arrived, k=k):
                self.copy(i, phase, arrived, arrived, device, k).wait_recv()

        if hop < NZ - 1:
            self.send_hop(i, phase, hop + 1)

    def start(self, i, phase):
        if self.along_z(i, phase):
            self.send_hop(i, phase, 1)
            return
        for here, there, device, _, k in self.moves(i, phase):
            self.copy(i, phase, here, there, device, k).start()

    def wait(self, i, phase):
        for _, _, device, arrived, k in self.moves(i, phase):
            self.copy(i, phase, arrived, arrived, device, k).wait_recv()

    def finish(self, i):
        for phase in range(4):
            if self.along_z(i, phase):
                for hop in range(1, NZ):
                    for sends, _, here, there, device, _, k in self.hops(i, phase, hop):

                        @pl.when(sends)
                        def _(here=here, there=there, device=device, k=k):
                            self.copy(i, phase, here, there, device, k).wait_send()

                continue
            for here, there, device, _, k in self.moves(i, phase):
                self.copy(i, phase, here, there, device, k).wait_send()


def got_shapes(plan):
    shapes = []
    for t, seq, (_, rows), (_, columns) in plan.items:
        dtype = plan.tensors[t][2]
        leads = {"z": ((NZ, 2), (1, NZ), (3,)), "m": ((NZ, 2), (3, 2), (1,)), "l": ((3, 2, 2), (1, 2), (1,))}
        lead = leads["zml"[seq.index("z")]]
        shapes.append([(d + (rows, columns), dtype) for d in lead])
    return shapes


class Scatter:
    def __init__(self, plan, place, total, got, out, send, recv):
        self.plan, self.me, self.total, self.got, self.out = plan, place, total, got, out
        self.send, self.recv = send, recv

    def moves(self, i, phase):
        t, seq, rows, cols = self.plan.items[i]
        me, total, got = self.me, self.total[t], self.got[i][phase]
        rows, cols = pl.ds(*rows), pl.ds(*cols)
        axis, done = seq[2 - phase], seq[3 - phase :]
        z = me.z if "z" in done else ALL_Z
        y = me.y if "y" in done else ALL_Y
        x = me.x if "x" in done else ALL_X
        if phase == 0 and axis != "z":
            lands = [got]
        else:
            lands = [got.at[k] for k in range(got.shape[0])]
        if axis == "x":
            return [(total.at[z, y, 1 - me.x, rows, cols], lands[0], me.to_x(), 0)]
        if axis == "y":
            return [(total.at[z, 1 - me.y, x, rows, cols], lands[0], me.to_y(), 0)]
        return [
            (total.at[(me.z + k) % NZ, y, x, rows, cols], lands[k - 1], me.to_z(k), k - 1)
            for k in (1, 2, 3)
        ]

    def copy(self, i, phase, src, dst, device, k):
        at = 5 * i + slots(self.plan.items[i][1][::-1], 3, 3)[phase] + k
        return remote(src, dst, self.send.at[at], self.recv.at[at], device)

    def start(self, i, phase):
        for here, there, device, k in self.moves(i, phase):
            self.copy(i, phase, here, there, device, k).start()

    def wait(self, i, phase):
        for here, there, device, k in self.moves(i, phase):
            self.copy(i, phase, there, there, device, k).wait_recv()

    def add(self, i, phase):
        t, seq, rows, cols = self.plan.items[i]
        me, total, got = self.me, self.total[t], self.got[i][phase]
        rows, cols = pl.ds(*rows), pl.ds(*cols)
        if phase == 0 and seq[2] == "z":
            for y in range(NY):
                for x in range(NX):
                    part = total[me.z, y, x, rows, cols].astype(jnp.float32)
                    for k in range(3):
                        part += got[k, y, x].astype(jnp.float32)
                    total[me.z, y, x, rows, cols] = part.astype(total.dtype)
        elif phase == 1 and seq[2] == "z":
            for o in range(2):
                at = (me.z, me.y, o) if seq[1] == "y" else (me.z, o, me.x)
                total[at + (rows, cols)] += got[0, o]
        elif phase == 0:
            for z in range(NZ):
                for o in range(2):
                    at = (z, me.y, o) if seq[2] == "y" else (z, o, me.x)
                    total[at + (rows, cols)] += got[z, o]
        elif phase == 1 and seq[1] != "z":
            for z in range(NZ):
                total[z, me.y, me.x, rows, cols] += got[0, z]
        elif phase == 1:
            for o in range(2):
                at = (me.z, me.y, o) if seq[2] == "y" else (me.z, o, me.x)
                part = total[at + (rows, cols)].astype(jnp.float32)
                for k in range(3):
                    part += got[k, o].astype(jnp.float32)
                total[at + (rows, cols)] = part.astype(total.dtype)
        else:
            part = total[me.z, me.y, me.x, rows, cols].astype(jnp.float32)
            for k in range(got.shape[0]):
                part += got[k].astype(jnp.float32)
            self.out[t][rows, cols] = part

    def finish(self, i):
        for phase in range(3):
            for here, there, device, k in self.moves(i, phase):
                self.copy(i, phase, here, there, device, k).wait_send()


EPS = 1e-05
PAIR = 2 * HEAD_DIM
SPAN = 2 * WINDOW
LOW = jnp.bfloat16
F32 = jnp.float32


def mm(left, right):
    return jnp.dot(left, right, preferred_element_type=F32)


def mm_nt(left, right):
    return lax.dot_general(left, right, (((1,), (1,)), ((), ())), preferred_element_type=F32)


def mm_tn(left, right):
    return lax.dot_general(left, right, (((0,), (0,)), ((), ())), preferred_element_type=F32)


def column_tiles(columns, size):
    full = columns // size
    tiles = [(0, size, full)]
    if columns % size:
        tiles.append((full * size, columns % size, 1))
    return tiles


def each_tile(columns, size, body):
    for begin, width, count in column_tiles(columns, size):
        if count == 1:
            body(begin, width)
        else:

            def step(j, _, begin=begin, width=width):
                body(pl.multiple_of(begin + j * width, 128), width)
                return 0

            lax.fori_loop(0, count, step, 0)


def each_rows(rows, size, body):
    def step(j, _):
        body(pl.ds(pl.multiple_of(j * size, size), size))
        return 0

    lax.fori_loop(0, rows // size, step, 0)


def both_heads(block):
    first = lax.broadcasted_iota(jnp.int32, block.shape, 1) < HEAD_DIM
    zero = jnp.zeros_like(block)
    return jnp.concatenate([jnp.where(first, block, zero), jnp.where(first, zero, block)], axis=0)


def merge_heads(stacked):
    rows = stacked.shape[0] // 2
    first = lax.broadcasted_iota(jnp.int32, (rows, PAIR), 1) < HEAD_DIM
    return jnp.where(first, stacked[:rows], stacked[rows:])


VMEM_LIMIT = 64 * 2**20


class Stream:
    def __init__(self, count, sems, fetch):
        self.count, self.sems, self.fetch = count, sems, fetch

    def copies(self, j, slot):
        return [
            pltpu.make_async_copy(src, dst, self.sems.at[slot, k])
            for k, (src, dst) in enumerate(self.fetch(j, slot))
        ]

    def prime(self):
        for copy in self.copies(0, 0):
            copy.start()

    def run(self, body, first=0, last=None):
        def step(j, _):
            slot = j % 2

            @pl.when(j + 1 < self.count)
            def _():
                for copy in self.copies(j + 1, 1 - slot):
                    copy.start()

            for copy in self.copies(j, slot):
                copy.wait()
            body(j, slot)
            return 0

        lax.fori_loop(first, self.count if last is None else last, step, 0)


def block_kernel(ahead, back, *refs):
    n = len(ahead.tensors)
    (lens, x_h, dy_h), raw, refs = refs[:3], refs[3 : 3 + n], refs[3 + n :]
    hbm_bufs, refs = refs[: n - 1], refs[n - 1 :]
    (mixed_o, gtok_o, q_h, p_h, ha_h, ho_h, hm_h, hid_h), refs = refs[:8], refs[8:]
    outs_h, refs = refs[:n], refs[n:]
    outs, refs = refs[:n], refs[n:]
    total, refs = refs[:n], refs[n:]
    count = len(back.items)
    got, refs = [refs[3 * i : 3 * i + 3] for i in range(count)], refs[3 * count :]
    (gate_pad, up_pad, down_pad, gain_buf, gains, xb, h1, da, db, kx, vx, o, x1, hid), refs = refs[:14], refs[14:]
    (dar, dbr, pair_of, pair_low), refs = refs[:4], refs[4:]
    (dy, dyr, dh, dxr_r, turned, pool, broad), refs = refs[:7], refs[7:]
    (kc, vc, rim_k, rim_v, gain_sum, gain_other), refs = refs[:6], refs[6:]
    (a_send, a_recv, own_sem, b_send, b_recv, load_sem, pool_sem, broad_sem, turn_sem), refs = refs[:9], refs[9:]
    half_send, half_recv = refs
    rows, width = xb.shape
    wide, columns = ahead.tensors[5][1], ahead.tensors[1][1]
    chips = NZ * NY * NX
    me = Place()
    halves, loads, later = {}, [0], {}

    def load(src, dst):
        copy = pltpu.make_async_copy(src, dst, load_sem.at[loads[0]])
        loads[0] += 1
        copy.start()
        return copy

    def to_partner(k, src, dst):
        copy = remote(src, dst, half_send.at[k], half_recv.at[k], me.to_core())
        copy.start()
        halves[k] = copy
        return copy

    def own(size, side=0):
        return pl.ds(pl.multiple_of((me.s if side == 0 else 1 - me.s) * size, 128), size)

    get_x, get_dy = load(x_h, xb), load(dy_h, dy)
    me.greet()
    pair_of[...] = jnp.zeros_like(pair_of)
    blank = jnp.zeros((1, raw[0].shape[1]), F32)
    for k in range(2):
        gain = raw[0][k : k + 1, :].astype(F32)
        left, right = jnp.concatenate([gain, blank], axis=1), jnp.concatenate([blank, gain], axis=1)
        pair_of[k : k + 1, :] = jnp.where(me.x == 0, left, right)
    pair_low[...] = pair_of[...].astype(LOW)
    shards = [pair_low] + list(raw[1:5]) + [gate_pad, up_pad, down_pad]
    bufs = [gain_buf] + list(hbm_bufs)
    flat = [b.reshape(2, chips * b.shape[4], b.shape[5]) for b in bufs]
    gather = Gather(ahead, me, shards, bufs, a_send, a_recv, own_sem)
    scatter = Scatter(back, me, total, got, outs, b_send, b_recv)
    ready = set()

    def pad_shards():
        part, tile = raw[7].shape[0], down_pad.shape[0]
        zero = jnp.zeros((raw[5].shape[0], tile - part), LOW)
        for src, dst in ((raw[5], gate_pad), (raw[6], up_pad)):
            value, pieces = src[...], []
            for k in range(value.shape[1] // part):
                pieces += [value[:, k * part : (k + 1) * part], zero]
            dst[...] = jnp.concatenate(pieces, axis=1)
        down_pad[...] = jnp.concatenate([raw[7][...], jnp.zeros((tile - part, down_pad.shape[1]), LOW)], axis=0)

    def prepare(t):
        if t >= 5 and 5 not in ready:
            pad_shards()
            for k in range(5, n):
                gather.own_copy(k).start()
                ready.add(k)
        elif t not in ready:
            gather.own_copy(t).start()
            ready.add(t)

    landed, arrived = set(), set()

    def land(t):
        if t not in landed:
            landed.add(t)
            gather.own_copy(t).wait()

    def need(*tensors, part=None):
        for t in tensors:
            mine = ahead.of_tensor[t]
            for i in mine if part is None else mine[part : part + 1]:
                if i not in arrived:
                    arrived.add(i)
                    gather.wait(i, 3)

    def norm(values, gain):
        inverse = lax.rsqrt(jnp.mean(values * values, axis=-1, keepdims=True) + EPS)
        return (values * inverse * gain).astype(LOW)

    def share(name, k, mine, whole):
        to = whole.at[:, own(rows)]
        later[name] = (load(mine, to), to_partner(k, mine, to))

    def shared(name):
        copy, sent = later[name]
        copy.wait()
        sent.wait()

    def turn(src, dst, lane):
        def body(j, _):
            at = pl.ds(pl.multiple_of(j * 128, 128), 128)
            dst[at, pl.ds(lane, rows)] = src[:, at].T
            return 0

        lax.fori_loop(0, src.shape[1] // 128, body, 0)
        return dst.at[:, pl.ds(lane, rows)]

    def first_norm():
        need(0)
        get_dy.wait()
        later["dy"] = to_partner(0, dy.at[:, own(columns, 1)], dyr)
        parts = []
        for z in range(NZ):
            for y in range(NY):
                pair = [gain_buf[me.s, z, y, x].astype(F32) for x in range(NX)]
                parts.append(pair[0] + pair[1])
        gains[...] = jnp.concatenate(parts, axis=1)[0:8]
        get_x.wait()

        def body(at):
            h1[at, :] = norm(xb[at, :].astype(F32), gains[0:1, :])

        each_rows(rows, 64, body)
        share("ha", 1, turn(h1, turned.at[0], 0), ha_h)

    def project(t, src, store):
        need(t)
        tiles = Stream(2, pool_sem, lambda j, slot: [(flat[t].at[j], pool.at[slot, pl.ds(0, width), :])])
        tiles.prime()

        def body(side, slot):
            for begin in range(0, columns, 256):
                part = mm(src[...], pool[slot, :width, begin : begin + 256])
                store(pl.ds(pl.multiple_of(side * columns + begin, 128), 256), part)

        tiles.run(body)

    def rim(k, ref):
        to = ref.at[pl.ds(0, WINDOW), :]
        return remote(ref.at[pl.ds(rows, WINDOW), :], to, half_send.at[2 + k], half_recv.at[2 + k], me.to_core())

    def put_into(ref, skip):
        def store(cols, part):
            ref[pl.ds(skip, rows), cols] = part.astype(LOW)

        return store

    def do_query():
        project(1, h1, put_into(da, 0))
        later["q_out"] = load(da.at[:, pl.ds(0, width)], q_h)

    def do_key():
        project(2, h1, put_into(kx, WINDOW))
        rim(0, kx).start()

    def do_value():
        project(3, h1, put_into(vx, WINDOW))
        rim(1, vx).start()

    first_end = lens[0, 0]
    second_end = first_end + lens[0, 1]

    def attend(b, _):
        base = me.s * rows + b * WINDOW
        at = pl.ds(pl.multiple_of(b * WINDOW, WINDOW), WINDOW)
        over = pl.ds(pl.multiple_of(b * WINDOW, WINDOW), SPAN)
        row = lax.broadcasted_iota(jnp.int32, (WINDOW, SPAN), 0)
        col = lax.broadcasted_iota(jnp.int32, (WINDOW, SPAN), 1)
        q_pos, k_pos = base + row, base - WINDOW + col

        def doc(pos):
            return (pos >= first_end).astype(jnp.int32) + (pos >= second_end).astype(jnp.int32)

        visible = (col >= row) & (col <= row + WINDOW) & (k_pos >= 0) & (doc(q_pos) == doc(k_pos))
        bias = jnp.where(visible, 0.0, -1e30)
        bias = jnp.concatenate([bias, bias], axis=0)
        pairs = range(HEADS // 2)
        cols = [slice(p * PAIR, (p + 1) * PAIR) for p in pairs]
        queries = [both_heads(da[at, c]) for c in cols]
        keys, values = [kx[over, c] for c in cols], [vx[over, c] for c in cols]
        scores = [mm_nt(q2, k) * HEAD_DIM ** (-0.5) + bias for q2, k in zip(queries, keys)]
        tops = [jnp.max(s, axis=-1, keepdims=True) for s in scores]
        exps = [jnp.exp(s - top) for s, top in zip(scores, tops)]
        sums = [jnp.sum(e, axis=-1, keepdims=True) for e in exps]
        weights = [(e * (1.0 / t)).astype(LOW) for e, t in zip(exps, sums)]
        parts = [merge_heads(mm(w, v)).astype(LOW) for w, v in zip(weights, values)]
        for p, c, w, part in zip(pairs, cols, weights, parts):
            db[at, 2 * p * SPAN : (2 * p + 1) * SPAN] = w[:WINDOW]
            db[at, (2 * p + 1) * SPAN : (2 * p + 2) * SPAN] = w[WINDOW:]
            o[at, c] = part
        return 0

    quarter = rows // WINDOW // 4

    def attend_part(k):
        if k == 0:
            for j, ref in ((0, kx), (1, vx)):
                rim(j, ref).wait_recv()
        lax.fori_loop(k * quarter, (k + 1) * quarter, attend, 0)
        if k == 3:
            later["p_out"] = load(db.at[:, pl.ds(0, HEADS * SPAN)], p_h)
            share("ho", 4, turn(o, turned.at[0], rows), ho_h)

    def add_out():
        def store(cols, part):
            x1[:, cols] = xb[:, cols].astype(F32) + part

        project(4, o, store)

        def body(at):
            xb[at, :] = norm(x1[at, :], gains[1:2, :])

        each_rows(rows, 64, body)
        share("hm", 5, turn(xb, turned.at[1], rows), hm_h)

    strips = [ahead.items[i][3] for i in ahead.of_tensor[5]]

    def strip_copies(p, side):
        begin, size = strips[p]
        return [
            pltpu.make_async_copy(
                flat[5 + k].at[side, :, pl.ds(begin, size)],
                pool.at[side, pl.ds(k * width, width), pl.ds(0, size)],
                pool_sem.at[side, k],
            )
            for k in range(2)
        ]

    def mlp(p):
        need(5, 6, part=p)
        for side in range(2):
            for copy in strip_copies(p, side):
                copy.start()
        if p == 0:
            later["p_out"].wait()
            for name in ("ha", "ho", "hm"):
                shared(name)
            later["hm"] = load(hm_h, turned.at[0])
        if p >= 2:
            for side in range(2):
                shared(("hid", p - 2, side))
        begin, size = strips[p]
        for side in range(2):
            for copy in strip_copies(p, side):
                copy.wait()
            for skip in range(0, size, 256):
                w = min(256, size - skip)
                cols = slice(skip, skip + w)
                a = mm(xb[...], pool[side, :width, cols])
                b = mm(xb[...], pool[side, width : 2 * width, cols])
                sig = 1.0 / (1.0 + jnp.exp(-a))
                silu = a * sig
                at = slice(side * wide + begin + skip, side * wide + begin + skip + w)
                grad = da[:, at].astype(F32)
                db[:, at] = (grad * silu).astype(LOW)
                da[:, at] = (grad * b * sig * (1.0 + a * (1.0 - sig))).astype(LOW)
                hidden_low = (silu * b).astype(LOW)
                hid[side, :, begin + skip : begin + skip + w] = hidden_low
                first = p % 2 * 512 + skip
                turned[1, first : first + w, side * rows : (side + 1) * rows] = hidden_low.T
        across = pl.ds(pl.multiple_of((1 - me.s) * wide + begin, 128), size)
        here = pl.ds(begin, size)
        later["db", p] = to_partner(6 + 4 * p, db.at[:, across], dbr.at[:, here])
        later["da", p] = to_partner(7 + 4 * p, da.at[:, across], dar.at[:, here])
        for side in range(2):
            mine = turned.at[1, pl.ds(p % 2 * 512, size), pl.ds(side * rows, rows)]
            share(("hid", p, side), 8 + 4 * p + side, mine, hid_h.at[pl.ds(side * wide + begin, size), :])
        if p == len(strips) - 1:
            mlp_tiles.prime()

    tall = back.tensors[0][0] * NY * NX
    hid_tiles = Stream(
        NZ, turn_sem, lambda j, slot: [(hid_h.at[pl.ds(pl.multiple_of(j * tall, 16), tall), :], turned.at[slot, pl.ds(0, tall), :])]
    )
    tile, thin = 256, 128
    small = pool.reshape(2, pool.shape[1] // tile, tile, columns)

    def row_tiles(w, size, dst):
        return lambda j, slot: (w.at[:, pl.ds(pl.multiple_of(j * size, size), size), :], dst(slot))

    def small_at(k):
        return lambda slot: small.at[slot, pl.ds(2 * k, 2)]

    def broad_at(k):
        return lambda slot: broad.at[slot, k]

    def stream_of(fetchers, count, sems):
        return Stream(count, sems, lambda j, slot: [f(j, slot) for f in fetchers])

    down_tiles = stream_of([row_tiles(flat[7], tile, small_at(0))], flat[7].shape[1] // tile, pool_sem)
    mlp_tiles = stream_of([row_tiles(flat[5 + k], thin, broad_at(k)) for k in range(2)], width // thin, broad_sem)
    out_tiles = stream_of([row_tiles(flat[4], tile, small_at(0))], width // tile, pool_sem)
    qkv_tiles = stream_of([row_tiles(flat[1 + k], tile, small_at(k)) for k in range(3)], width // tile, pool_sem)

    def begin_scatter(t):
        for i in back.of_tensor[t]:
            scatter.start(i, 0)

    def put(t, z, part, cols=slice(None)):
        low = part.reshape(NY, NX, back.tensors[t][0], part.shape[1]).astype(total[t].dtype)
        total[t][z, :, :, :, cols] = low

    def grad_down():
        for p in range(len(strips)):
            for side in range(2):
                if p + 2 >= len(strips):
                    shared(("hid", p, side))
        later["dy"].wait_recv()
        hid_tiles.prime()

        def body(z, slot):
            mine = mm(turned[slot, :tall, own(rows)], dy[:, own(columns)])
            put(0, z, mine + mm(turned[slot, :tall, own(rows, 1)], dyr[...]))

        hid_tiles.run(body)
        begin_scatter(0)
        later["ha"] = load(ha_h, turned.at[0])
        later["ho"] = load(ho_h, turned.at[1])

    def add_down():
        tiles2 = Stream(2, pool_sem, lambda j, slot: [(flat[7].at[j], pool.at[slot])])
        tiles2.prime()

        def body(side, slot):
            for begin in range(0, columns, 256):
                part = mm(hid[0], pool[slot, :wide, begin : begin + 256])
                part += mm(hid[1], pool[slot, wide:, begin : begin + 256])
                cols = pl.ds(pl.multiple_of(side * columns + begin, 128), 256)
                xb[:, cols] = (x1[:, cols] + part).astype(LOW)

        tiles2.run(body)
        later["mixed"] = load(xb, mixed_o)

    def hidden_body(j, slot):
        part = mm_nt(dy[:, :columns], small[slot, 0]) + mm_nt(dy[:, columns:], small[slot, 1])
        da[:, pl.ds(pl.multiple_of(j * tile, tile), tile)] = part.astype(LOW)

    def hidden(k):
        middle = down_tiles.count // 2
        if k == 0:
            need(7)
            down_tiles.prime()
            later["q_out"].wait()
            down_tiles.run(hidden_body, 0, middle)
            return
        down_tiles.run(hidden_body, middle)

    def weight_grad_to(t, slot, mine, theirs, cols=slice(None)):
        row_count = back.tensors[t][0] * NY * NX

        def step(z, _):
            at = pl.ds(pl.multiple_of(z * row_count, 16), row_count)
            put(t, z, mm(turned[slot, at, own(rows)], mine()) + mm(turned[slot, at, own(rows, 1)], theirs()), cols)
            return 0

        lax.fori_loop(0, NZ, step, 0)

    def grad_strip(t, name, grad, other, p):
        begin, size = strips[p]
        if p == 0 and t == 1:
            later["hm"].wait()
        later[name, p].wait_recv()
        cols = slice(begin, begin + size)
        mine = pl.ds(pl.multiple_of(me.s * wide + begin, 128), size)
        weight_grad_to(t, 0, lambda: grad[:, mine], lambda: other[:, cols], cols)
        scatter.start(back.of_tensor[t][p], 0)

    def dh2_body(j, slot):
        part = None
        for k, grad in ((0, da), (1, db)):
            for side in range(2):
                term = mm_nt(grad[:, side * wide : (side + 1) * wide], broad[slot, k, side])
                part = term if part is None else part + term
        dh[:, pl.ds(pl.multiple_of(j * thin, thin), thin)] = part

    def grad_norm2(k):
        middle = mlp_tiles.count // 2
        if k == 0:
            mlp_tiles.run(dh2_body, 0, middle)
            return
        mlp_tiles.run(dh2_body, middle)
        for p in range(len(strips)):
            later["db", p].wait_send()
            later["da", p].wait_send()
        out_tiles.prime()
        later["q"] = load(q_h, da.at[:, pl.ds(0, width)])
        later["p"] = load(p_h, db.at[:, pl.ds(0, HEADS * SPAN)])
        later["mixed"].wait()
        later["x"] = load(x_h, xb)

    def norm_grad(values, grad_norm, gain):
        inverse = lax.rsqrt(jnp.mean(values * values, axis=-1, keepdims=True) + EPS)
        scaled = grad_norm * gain
        mean_term = jnp.mean(values * scaled, axis=-1, keepdims=True)
        back_part = inverse * scaled - values * (inverse * inverse * inverse) * mean_term
        return back_part, jnp.sum(values * inverse * grad_norm, axis=0, keepdims=True)

    def norm2_body(at):
        back_part, gain_part = norm_grad(x1[at, :], dh[at, :], gains[1:2, :])
        gain_sum[1:2, :] += gain_part
        grad = dy[at, :].astype(F32) + back_part
        x1[at, :] = grad
        h1[at, :] = grad.astype(LOW)

    def norm2():
        gain_sum[...] = jnp.zeros_like(gain_sum)
        each_rows(rows, 64, norm2_body)
        later["dxr"] = to_partner(22, h1.at[:, own(columns, 1)], dxr_r)

    def out_body(j, slot):
        part = mm_nt(h1[:, :columns], small[slot, 0]) + mm_nt(h1[:, columns:], small[slot, 1])
        o[:, pl.ds(pl.multiple_of(j * tile, tile), tile)] = part.astype(LOW)

    def grad_heads():
        out_tiles.run(out_body)
        qkv_tiles.prime()

    def grad_out():
        later["ho"].wait()
        later["dxr"].wait_recv()
        weight_grad_to(3, 1, lambda: h1[:, own(columns)], lambda: dxr_r[...])
        begin_scatter(3)

    scale = HEAD_DIM ** (-0.5)

    def attend_back(b, _):
        at = pl.ds(pl.multiple_of(b * WINDOW, WINDOW), WINDOW)
        over = pl.ds(pl.multiple_of(b * WINDOW, WINDOW), SPAN)
        pairs = range(HEADS // 2)
        cols = [slice(p * PAIR, (p + 1) * PAIR) for p in pairs]
        queries, grads = [both_heads(da[at, c]) for c in cols], [both_heads(o[at, c]) for c in cols]
        keys, values = [kx[over, c] for c in cols], [vx[over, c] for c in cols]
        lows = [
            jnp.concatenate([db[at, (2 * p + h) * SPAN : (2 * p + h + 1) * SPAN] for h in range(2)], axis=0)
            for p in pairs
        ]
        carry_k, carry_v = [kc[:, c] for c in cols], [vc[:, c] for c in cols]
        probs = [low.astype(F32) for low in lows]
        grad_probs = [mm_nt(g, v) for g, v in zip(grads, values)]
        grad_values = [mm_tn(low, g) for low, g in zip(lows, grads)]
        inners = [jnp.sum(p * g, axis=-1, keepdims=True) for p, g in zip(probs, grad_probs)]
        scores = [(p * (g - i)).astype(LOW) for p, g, i in zip(probs, grad_probs, inners)]
        grad_queries = [(merge_heads(mm(s, k)) * scale).astype(LOW) for s, k in zip(scores, keys)]
        grad_keys = [mm_tn(s, q2) * scale for s, q2 in zip(scores, queries)]
        new_k = [(old + g[:WINDOW]).astype(LOW) for old, g in zip(carry_k, grad_keys)]
        new_v = [(old + g[:WINDOW]).astype(LOW) for old, g in zip(carry_v, grad_values)]
        for c, gq, gk, gv, nk, nv in zip(cols, grad_queries, grad_keys, grad_values, new_k, new_v):
            da[at, c] = gq
            kx[at, c] = nk
            vx[at, c] = nv
            kc[:, c] = gk[WINDOW:]
            vc[:, c] = gv[WINDOW:]
        return 0

    own_rows = pl.ds(WINDOW, rows)
    qr, kr, vr = dar.at[:, pl.ds(0, columns)], dar.at[:, pl.ds(columns, columns)], dbr.at[:, pl.ds(0, columns)]

    def attend_back_part(k):
        if k == 0:
            kc[...] = jnp.zeros_like(kc)
            vc[...] = jnp.zeros_like(vc)
            for j, ref in ((0, kx), (1, vx)):
                rim(j, ref).wait_send()
            later["q"].wait()
            later["p"].wait()
        lax.fori_loop(k * quarter, (k + 1) * quarter, attend_back, 0)
        if k == 0:
            later["rim"] = [
                to_partner(23, kx.at[pl.ds(0, WINDOW), :], rim_k),
                to_partner(24, vx.at[pl.ds(0, WINDOW), :], rim_v),
            ]
        if k == 3:
            for copy, ref, carry, rim_in in ((later["rim"][0], kx, kc, rim_k), (later["rim"][1], vx, vc, rim_v)):
                copy.wait_recv()
                ref[pl.ds(rows, WINDOW), :] = (carry[...] + rim_in[...].astype(F32)).astype(LOW)
            later["dq"] = to_partner(25, da.at[:, own(columns, 1)], qr)
            later["dk"] = to_partner(26, kx.at[own_rows, own(columns, 1)], kr)
            later["dv"] = to_partner(27, vx.at[own_rows, own(columns, 1)], vr)

    def grad_qkv(k):
        if k == 0:
            later["ha"].wait()
        later[("dq", "dk", "dv")[k]].wait_recv()
        mine = (lambda: da[:, own(columns)], lambda: kx[own_rows, own(columns)], lambda: vx[own_rows, own(columns)])[k]
        theirs = (qr, kr, vr)[k]
        weight_grad_to(4 + k, 0, mine, lambda: theirs[...])
        begin_scatter(4 + k)

    def dh1_body(j, slot):
        part = None
        for k, (grad, skip) in enumerate(((da, 0), (kx, WINDOW), (vx, WINDOW))):
            for side in range(2):
                left = grad[pl.ds(skip, rows), side * columns : (side + 1) * columns]
                term = mm_nt(left, small[slot, 2 * k + side])
                part = term if part is None else part + term
        dh[:, pl.ds(pl.multiple_of(j * tile, tile), tile)] = part

    def grad_norm1():
        qkv_tiles.run(dh1_body)

    def norm1_body(at):
        back_part, gain_part = norm_grad(xb[at, :].astype(F32), dh[at, :], gains[0:1, :])
        gain_sum[0:1, :] += gain_part
        x1[at, :] = x1[at, :] + back_part

    def norm1():
        later["x"].wait()
        each_rows(rows, 64, norm1_body)
        later["gtok"] = load(x1, gtok_o)
        later["gain"] = to_partner(28, gain_sum, gain_other)

    def grad_gains():
        later["gain"].wait_recv()
        lanes = back.tensors[7][1]
        for c in range(chips):
            at = slice(c // 2 * lanes, (c // 2 + 1) * lanes)
            total[7][c // 4, c // 2 % 2, c % 2] = gain_sum[:, at] + gain_other[:, at]
        begin_scatter(7)

    work = {
        "norm": first_norm,
        "query": do_query,
        "key": do_key,
        "value": do_value,
        "project": add_out,
        "mix": add_down,
        "down": grad_down,
        "norm2": norm2,
        "heads": grad_heads,
        "out": grad_out,
        "dh1": grad_norm1,
        "norm1": norm1,
        "gains": grad_gains,
    }
    for k in range(4):
        work["see", k] = functools.partial(attend_part, k)
        work["attend", k] = functools.partial(attend_back_part, k)
    for k in range(len(strips)):
        work["mlp", k] = functools.partial(mlp, k)
        work["up", k] = functools.partial(grad_strip, 1, "db", db, dbr, k)
        work["gate", k] = functools.partial(grad_strip, 2, "da", da, dar, k)
    for k in range(3):
        work["qkv", k] = functools.partial(grad_qkv, k)
    for k in range(2):
        work["hidden", k] = functools.partial(hidden, k)
        work["dh2", k] = functools.partial(grad_norm2, k)
    summed = []
    for step in SCRIPT:
        if step in work:
            work[step]()
        elif step[0] == "start":
            prepare(ahead.items[step[1]][0])
            gather.start(step[1], 0)
        elif step[0] == 0:
            _, i, phase, *hop = step
            land(ahead.items[i][0])
            if hop:
                gather.take_hop(i, phase, hop[0])
            else:
                gather.wait(i, phase)
            if hop in ([], [NZ - 1]):
                gather.start(i, phase + 1)
        else:
            _, i, phase = step
            scatter.wait(i, phase)
            scatter.add(i, phase)
            if phase < 2:
                scatter.start(i, phase + 1)
                continue
            t = back.items[i][0]
            summed.append(i)
            if all(k in summed for k in back.of_tensor[t]):
                later["sum", t] = load(outs[t], outs_h[t])
    for i in range(len(ahead.items)):
        gather.finish(i)
    for i in range(len(back.items)):
        scatter.finish(i)
    for k in (0, 22, 23, 24, 25, 26, 27, 28):
        halves[k].wait_send()
    later["gtok"].wait()
    for t in range(n):
        later["sum", t].wait()


def block_all(ahead, back, lens, tokens, cotangent, shards):
    n, na, nb = len(ahead.tensors), len(ahead.items), len(back.items)
    rows, width = tokens.shape
    columns, wide = ahead.tensors[1][1], ahead.tensors[5][1]
    anywhere = pl.BlockSpec(memory_space=pl.ANY)
    inside = pl.BlockSpec(memory_space=pltpu.VMEM)
    shape = jax.ShapeDtypeStruct
    over = WINDOW + rows
    bufs = [(2, NZ, NY, NX) + t[:2] for t in ahead.tensors]
    kept = [
        ((rows, width), LOW),
        ((rows, width), F32),
        ((rows, width), LOW),
        ((rows, HEADS * SPAN), LOW),
        ((width, 2 * rows), LOW),
        ((width, 2 * rows), LOW),
        ((width, 2 * rows), LOW),
        ((2 * wide, 2 * rows), LOW),
    ]
    scratch = [
        (ahead.tensors[5][:2], LOW),
        (ahead.tensors[6][:2], LOW),
        (ahead.tensors[7][:2], LOW),
        (bufs[0], LOW),
        ((8, width), F32),
        ((rows, width), LOW),
        ((rows, width), LOW),
        ((rows, 2 * wide), LOW),
        ((rows, 2 * wide), LOW),
        ((over, width), LOW),
        ((over, width), LOW),
        ((rows, width), LOW),
        ((rows, width), F32),
        ((2, rows, wide), LOW),
        ((rows, wide), LOW),
        ((rows, wide), LOW),
        (ahead.tensors[0][:2], F32),
        (ahead.tensors[0][:2], LOW),
        ((rows, width), LOW),
        ((rows, columns), LOW),
        ((rows, width), F32),
        ((rows, columns), LOW),
        ((2, width, 2 * rows), LOW),
        ((2, 2 * wide, columns), LOW),
        ((2, 2, 2, 128, wide), LOW),
        ((WINDOW, width), F32),
        ((WINDOW, width), F32),
        ((WINDOW, width), LOW),
        ((WINDOW, width), LOW),
        ((8, width), F32),
        ((8, width), F32),
    ]
    results = [(t[:2], F32) for t in back.tensors]
    totals = [((NZ, NY, NX) + t[:2], t[2]) for t in back.tensors]
    got = [part for parts in got_shapes(back) for part in parts]
    dma = pltpu.SemaphoreType.DMA
    outs = pl.pallas_call(
        functools.partial(block_kernel, ahead, back),
        out_shape=[shape(b, LOW) for b in bufs[1:]]
        + [shape(*s) for s in kept]
        + [shape(t[:2], F32) for t in back.tensors],
        in_specs=[pl.BlockSpec(memory_space=pltpu.SMEM), anywhere, anywhere] + [inside] * n,
        out_specs=[anywhere] * (n - 1 + len(kept) + n),
        scratch_shapes=[pltpu.VMEM(*s) for s in results + totals + got + scratch]
        + [dma((9 * na,)), dma((9 * na,)), dma((n,)), dma((5 * nb,)), dma((5 * nb,)), dma((36,))]
        + [dma((2, 3)), dma((2, 2)), dma((2, 1)), dma((29,)), dma((29,))],
        compiler_params=pltpu.CompilerParams(
            collective_id=0, has_side_effects=True, vmem_limit_bytes=VMEM_LIMIT
        ),
        name="block_all",
    )(lens, tokens, cotangent, *shards)
    return outs[n - 1 : n + 1], outs[n - 1 + len(kept) :]


def finish_kernel(*refs):
    n = 10
    ins, outs, held, made = refs[:n], refs[n : 2 * n + 1], refs[2 * n + 1 : 3 * n + 1], refs[3 * n + 1 : 4 * n + 2]
    sem_in, sem_out = refs[4 * n + 2 :]
    gets = [pltpu.make_async_copy(src, dst, sem_in.at[k]) for k, (src, dst) in enumerate(zip(ins, held))]
    for copy in gets:
        copy.start()
    puts = []

    def put(k, src):
        copy = pltpu.make_async_copy(src, outs[k], sem_out.at[k])
        copy.start()
        puts.append(copy)

    down, up, gate, out, query, key, value, gain = held[2:]
    for copy in gets[2:]:
        copy.wait()
    for k, src in ((2, query), (3, key), (4, value), (5, out)):
        put(k, src)
    rows, part, tile = query.shape[0], outs[8].shape[0], down.shape[0]
    made[8][...] = down[...][:part]
    put(8, made[8])
    for k, src in ((6, gate), (7, up)):
        values = src[...]
        made[k][...] = jnp.concatenate(
            [values[:, j * tile : j * tile + part] for j in range(values.shape[1] // tile)], axis=1
        )
        put(k, made[k])
    both = gain[...]
    own = jnp.where(lax.axis_index("dp") % 2 == 0, both[:, :rows], both[:, rows:])
    made[9][...] = own[0:1]
    made[10][...] = own[1:2]
    put(9, made[9])
    put(10, made[10])
    for k in range(2):
        gets[k].wait()
        put(k, held[k])
    for copy in puts:
        copy.wait()


def finish_all(mixed, tokens, sums, w_query, w_gate, w_down):
    anywhere = pl.BlockSpec(memory_space=pl.ANY)
    shape = jax.ShapeDtypeStruct
    outs = [shape(mixed.shape, mixed.dtype), shape(tokens.shape, F32)]
    outs += [shape(w_query.shape, F32)] * 4 + [shape(w_gate.shape, F32)] * 2 + [shape(w_down.shape, F32)]
    outs += [shape((1, w_query.shape[0]), F32)] * 2
    ins = [mixed, tokens, *sums]
    return pl.pallas_call(
        finish_kernel,
        out_shape=outs,
        in_specs=[anywhere] * len(ins),
        out_specs=[anywhere] * len(outs),
        scratch_shapes=[pltpu.VMEM(a.shape, a.dtype) for a in ins + outs]
        + [pltpu.SemaphoreType.DMA((len(ins),)), pltpu.SemaphoreType.DMA((len(outs),))],
        compiler_params=pltpu.CompilerParams(vmem_limit_bytes=62 * 2**20),
        name="finish_all",
    )(*ins)


def kinds(w_query, w_gate, w_down):
    rows, columns = w_query.shape
    part = w_down.shape[0]
    tile = -(-part // 16) * 16
    wide = w_gate.shape[1] // part * tile
    half, strip = rows // 2, -(-wide // 512) * 128
    long, short = -(-tile // 64) * 16, tile - 3 * (-(-tile // 64) * 16)

    def cuts(kinds, counts):
        return tuple((kind, 0, count) for kind, count in zip(kinds, counts, strict=True))

    def strips(kinds):
        return tuple((kind, 1, min(strip, wide - k * strip)) for k, kind in enumerate(kinds))

    def pairs(letters):
        return tuple("z" + letter + axis for letter in letters for axis in "xy")

    def of(kind, letters):
        if kind == "square":
            return (rows, columns, LOW, cuts(pairs(letters), (half, half)))
        if kind == "broad":
            return (rows, wide, LOW, strips(pairs(letters)))
        if kind == "tall":
            return (tile, columns, LOW, cuts(pairs(letters), (long, long, long, short)))
        if kind == "gain":
            return (16, 2 * rows, LOW, cuts(("zfx",), (16,)))
        return (8, 2 * rows, F32, cuts(("zfx",), (8,)))

    return of


def gather_plan(w_query, w_key, w_value, w_out, w_gate, w_up, w_down, gain_attn, gain_mlp):
    kind = kinds(w_query, w_gate, w_down)
    names = GATHER_KINDS
    plan = Plan([kind(*name) for name in names])
    both = jnp.concatenate([gain_attn[None], gain_mlp[None]], axis=0)
    shards = [
        both,
        w_query,
        w_key,
        w_value,
        w_out,
        w_gate,
        w_up,
        w_down,
    ]
    return plan, shards


def swift_block(
    tokens,
    seq_lengths,
    w_query,
    w_key,
    w_value,
    w_out,
    w_gate,
    w_up,
    w_down,
    gain_attn,
    gain_mlp,
    cotangent,
):
    plan, shards = gather_plan(w_query, w_key, w_value, w_out, w_gate, w_up, w_down, gain_attn, gain_mlp)
    kind = kinds(w_query, w_gate, w_down)
    names = SCATTER_KINDS
    back = Plan([kind(*name) for name in names])
    results, sums = block_all(plan, back, seq_lengths, tokens, cotangent, shards)
    outs = finish_all(results[0], results[1], sums, w_query, w_gate, w_down)
    return (*outs[:9], outs[9].reshape(-1), outs[10].reshape(-1))


def solution(mesh):
    fast = (mesh.shape["dp"], mesh.shape["seq"]) == (NZ * NY * NX, 2)
    shards = swift_block if fast else plain_block
    in_specs = (
        P(("dp", "seq"), None),
        P("dp", None),
        P("dp", "seq"),
        P("dp", "seq"),
        P("dp", "seq"),
        P("dp", "seq"),
        P("dp", "seq"),
        P("dp", "seq"),
        P("dp", "seq"),
        P("dp"),
        P("dp"),
        P(("dp", "seq"), None),
    )
    out_specs = (
        P(("dp", "seq"), None),
        P(("dp", "seq"), None),
        P("dp", "seq"),
        P("dp", "seq"),
        P("dp", "seq"),
        P("dp", "seq"),
        P("dp", "seq"),
        P("dp", "seq"),
        P("dp", "seq"),
        P("dp"),
        P("dp"),
    )
    return jax.shard_map(shards, mesh=mesh, in_specs=in_specs, out_specs=out_specs, check_vma=False)
```

```python
import functools

import jax
import jax.numpy as jnp
from jax import lax
from jax.experimental import pallas as pl
from jax.experimental.pallas import tpu as pltpu
from jax.sharding import PartitionSpec as P

HEADS = 16
HEAD_DIM = 64
WINDOW = 64


eps_norm = 1e-05


def from_behind(block, axis, distance):
    devices = range(lax.axis_size(axis))
    route = [(i - distance, i) for i in devices if i - distance in devices]
    return lax.ppermute(block, axis, route)


def inverse_rms(values):
    return lax.rsqrt(jnp.mean(values * values, axis=-1, keepdims=True) + eps_norm)


def doc_numbers(lengths_row, positions):
    first_end = lengths_row[0]
    second_end = lengths_row[0] + lengths_row[1]
    return (positions >= first_end).astype(jnp.int32) + (positions >= second_end).astype(jnp.int32)


def window_mask(query_pos, query_doc, key_pos, key_doc, window):
    after = key_pos[None, :] >= query_pos[:, None] - window
    before = key_pos[None, :] <= query_pos[:, None]
    inside = (key_pos[None, :] >= 0) & (key_doc[None, :] == query_doc[:, None])
    return after & before & inside


def norm_back(values, inverse, gain, grad_norm):
    scaled = grad_norm * gain
    mean_term = jnp.mean(values * scaled, axis=-1, keepdims=True)
    grad_values = inverse * scaled - values * (inverse * inverse * inverse) * mean_term
    grad_gain = jnp.sum(values * inverse * grad_norm, axis=0)
    return (grad_values, grad_gain)


def project(left, right):
    return jnp.dot(left, right, preferred_element_type=jnp.float32)


def project_back(grad_rows, weight):
    return jnp.einsum("tf,df->td", grad_rows, weight, preferred_element_type=jnp.float32)


def weight_grad(inputs, grad_rows):
    return jnp.einsum("td,tf->df", inputs, grad_rows, preferred_element_type=jnp.float32)


def plain_block(
    tokens,
    seq_lengths,
    w_query,
    w_key,
    w_value,
    w_out,
    w_gate,
    w_up,
    w_down,
    gain_attn,
    gain_mlp,
    cotangent,
):
    row_count = tokens.shape[0]
    block_rows = min(512, row_count)
    head_group = HEADS // 2
    score_scale = HEAD_DIM ** (-0.5)
    row_parts = (
        lax.all_gather(w_query, "dp", axis=0, tiled=True),
        lax.all_gather(w_key, "dp", axis=0, tiled=True),
        lax.all_gather(w_value, "dp", axis=0, tiled=True),
        lax.all_gather(w_out, "dp", axis=0, tiled=True),
        lax.all_gather(w_gate, "dp", axis=0, tiled=True),
        lax.all_gather(w_up, "dp", axis=0, tiled=True),
        lax.all_gather(w_down, "dp", axis=0, tiled=True),
        lax.all_gather(gain_attn, "dp", axis=0, tiled=True),
        lax.all_gather(gain_mlp, "dp", axis=0, tiled=True),
    )
    full_mats = (
        lax.all_gather(row_parts[0], "seq", axis=1, tiled=True),
        lax.all_gather(row_parts[1], "seq", axis=1, tiled=True),
        lax.all_gather(row_parts[2], "seq", axis=1, tiled=True),
        lax.all_gather(row_parts[3], "seq", axis=1, tiled=True),
        lax.all_gather(row_parts[4], "seq", axis=1, tiled=True),
        lax.all_gather(row_parts[5], "seq", axis=1, tiled=True),
        lax.all_gather(row_parts[6], "seq", axis=1, tiled=True),
    )
    query_w, key_w, value_w, out_w, gate_w, up_w, down_full = full_mats
    gain_one = row_parts[7].astype(jnp.float32)
    gain_two = row_parts[8].astype(jnp.float32)
    inputs = tokens.astype(jnp.float32)
    inv_one = inverse_rms(inputs)
    normed_one = (inputs * inv_one * gain_one).astype(jnp.bfloat16)
    query_low = project(normed_one, query_w).astype(jnp.bfloat16)
    key_low = project(normed_one, key_w).astype(jnp.bfloat16)
    value_low = project(normed_one, value_w).astype(jnp.bfloat16)
    rim_pairs = from_behind(
        (key_low[row_count - WINDOW :], value_low[row_count - WINDOW :]), "seq", 1
    )
    keys_ext = jnp.concatenate([rim_pairs[0], key_low], axis=0).reshape(
        row_count + WINDOW, HEADS, HEAD_DIM
    )
    values_ext = jnp.concatenate([rim_pairs[1], value_low], axis=0).reshape(
        row_count + WINDOW, HEADS, HEAD_DIM
    )
    query_heads = query_low.reshape(row_count, HEADS, HEAD_DIM)
    span_start = lax.axis_index("seq") * row_count
    query_pos = span_start + jnp.arange(row_count, dtype=jnp.int32)
    key_pos = span_start - WINDOW + jnp.arange(row_count + WINDOW, dtype=jnp.int32)
    query_doc = doc_numbers(seq_lengths[0], query_pos)
    key_doc = doc_numbers(seq_lengths[0], key_pos)

    def tile_scores(row_start, head_start):
        visible = window_mask(query_pos, query_doc, key_pos, key_doc, WINDOW)
        scores_raw = (
            jnp.einsum(
                "qhd,khd->hqk",
                query_heads[
                    row_start : row_start + block_rows, head_start : head_start + head_group
                ],
                keys_ext[
                    row_start : row_start + block_rows + WINDOW,
                    head_start : head_start + head_group,
                ],
                preferred_element_type=jnp.float32,
            )
            * score_scale
        )
        return jnp.where(visible[None], scores_raw, -1e30)

    log_totals = {}
    row_start = 0
    head_parts = []
    for head_start in range(0, HEADS, head_group):
        masked_scores = tile_scores(row_start, head_start)
        top_score = jnp.max(masked_scores, axis=-1, keepdims=True)
        log_total = top_score + jnp.log(
            jnp.sum(jnp.exp(masked_scores - top_score), axis=-1, keepdims=True)
        )
        prob_low = jnp.exp(masked_scores - log_total).astype(jnp.bfloat16)
        value_tile = values_ext[
            row_start : row_start + block_rows + WINDOW, head_start : head_start + head_group
        ]
        head_parts.append(
            jnp.einsum("hqk,khd->qhd", prob_low, value_tile, preferred_element_type=jnp.float32)
        )
        log_totals[row_start, head_start] = log_total
    attn_blocks = jnp.concatenate(head_parts, axis=1)
    attended = attn_blocks.reshape(row_count, HEADS * HEAD_DIM).astype(jnp.bfloat16)
    middle = inputs + project(attended, out_w)
    inv_two = inverse_rms(middle)
    normed_two = (middle * inv_two * gain_two).astype(jnp.bfloat16)
    gate_pre = project(normed_two, gate_w)
    up_pre = project(normed_two, up_w)
    gate_act = jax.nn.silu(gate_pre)
    hidden = (gate_act * up_pre).astype(jnp.bfloat16)
    block_out = (middle + project(hidden, down_full)).astype(jnp.bfloat16)
    rows_again = (
        lax.all_gather(w_query, "dp", axis=0, tiled=True),
        lax.all_gather(w_key, "dp", axis=0, tiled=True),
        lax.all_gather(w_value, "dp", axis=0, tiled=True),
        lax.all_gather(w_out, "dp", axis=0, tiled=True),
        lax.all_gather(w_gate, "dp", axis=0, tiled=True),
        lax.all_gather(w_up, "dp", axis=0, tiled=True),
        lax.all_gather(w_down, "dp", axis=0, tiled=True),
        lax.all_gather(gain_attn, "dp", axis=0, tiled=True),
        lax.all_gather(gain_mlp, "dp", axis=0, tiled=True),
    )
    mats_again = (
        lax.all_gather(rows_again[0], "seq", axis=1, tiled=True),
        lax.all_gather(rows_again[1], "seq", axis=1, tiled=True),
        lax.all_gather(rows_again[2], "seq", axis=1, tiled=True),
        lax.all_gather(rows_again[3], "seq", axis=1, tiled=True),
        lax.all_gather(rows_again[4], "seq", axis=1, tiled=True),
        lax.all_gather(rows_again[5], "seq", axis=1, tiled=True),
        lax.all_gather(rows_again[6], "seq", axis=1, tiled=True),
    )
    back_query, back_key, back_value, back_out, back_gate, back_up, back_down = mats_again
    back_gain_one = rows_again[7].astype(jnp.float32)
    back_gain_two = rows_again[8].astype(jnp.float32)
    grad_final = cotangent.astype(jnp.float32)
    d_down = weight_grad(hidden, cotangent)
    grad_hidden = project_back(cotangent, back_down)
    sigmoid_gate = jax.nn.sigmoid(gate_pre)
    grad_gate_low = (
        grad_hidden * up_pre * sigmoid_gate * (1.0 + gate_pre * (1.0 - sigmoid_gate))
    ).astype(jnp.bfloat16)
    grad_up_low = (grad_hidden * gate_act).astype(jnp.bfloat16)
    d_gate = weight_grad(normed_two, grad_gate_low)
    d_up = weight_grad(normed_two, grad_up_low)
    grad_normed_two = project_back(grad_gate_low, back_gate) + project_back(grad_up_low, back_up)
    grad_mid_norm, d_gain_two = norm_back(middle, inv_two, back_gain_two, grad_normed_two)
    grad_middle = grad_final + grad_mid_norm
    grad_proj = grad_middle.astype(jnp.bfloat16)
    d_out = weight_grad(attended, grad_proj)
    grad_attended = (
        project_back(grad_proj, back_out).astype(jnp.bfloat16).reshape(row_count, HEADS, HEAD_DIM)
    )
    grad_keys_ext = jnp.zeros((row_count + WINDOW, HEADS, HEAD_DIM), jnp.float32)
    grad_values_ext = jnp.zeros((row_count + WINDOW, HEADS, HEAD_DIM), jnp.float32)
    row_start = 0
    head_parts = []
    for head_start in range(0, HEADS, head_group):
        head_end = head_start + head_group
        masked_scores = tile_scores(row_start, head_start)
        prob_full = jnp.exp(masked_scores - log_totals[row_start, head_start])
        grad_tile = grad_attended[row_start : row_start + block_rows, head_start:head_end]
        key_tile = keys_ext[row_start : row_start + block_rows + WINDOW, head_start:head_end]
        value_tile = values_ext[row_start : row_start + block_rows + WINDOW, head_start:head_end]
        query_tile = query_heads[row_start : row_start + block_rows, head_start:head_end]
        grad_prob = jnp.einsum(
            "qhd,khd->hqk", grad_tile, value_tile, preferred_element_type=jnp.float32
        )
        inner = jnp.sum(prob_full * grad_prob, axis=-1, keepdims=True)
        grad_score = (prob_full * (grad_prob - inner)).astype(jnp.bfloat16)
        head_parts.append(
            jnp.einsum("hqk,khd->qhd", grad_score, key_tile, preferred_element_type=jnp.float32)
            * score_scale
        )
        key_term = (
            jnp.einsum("hqk,qhd->khd", grad_score, query_tile, preferred_element_type=jnp.float32)
            * score_scale
        )
        value_term = jnp.einsum(
            "hqk,qhd->khd",
            prob_full.astype(jnp.bfloat16),
            grad_tile,
            preferred_element_type=jnp.float32,
        )
        grad_keys_ext = grad_keys_ext.at[
            row_start : row_start + block_rows + WINDOW, head_start:head_end
        ].add(key_term)
        grad_values_ext = grad_values_ext.at[
            row_start : row_start + block_rows + WINDOW, head_start:head_end
        ].add(value_term)
    grad_query_blocks = jnp.concatenate(head_parts, axis=1)
    rim_back = (
        from_behind(
            grad_keys_ext[:WINDOW].reshape(WINDOW, HEADS * HEAD_DIM).astype(jnp.bfloat16), "seq", -1
        ).astype(jnp.float32),
        from_behind(
            grad_values_ext[:WINDOW].reshape(WINDOW, HEADS * HEAD_DIM).astype(jnp.bfloat16),
            "seq",
            -1,
        ).astype(jnp.float32),
    )
    grad_keys = (
        grad_keys_ext[WINDOW:]
        .reshape(row_count, HEADS * HEAD_DIM)
        .at[row_count - WINDOW :]
        .add(rim_back[0])
    )
    grad_values = (
        grad_values_ext[WINDOW:]
        .reshape(row_count, HEADS * HEAD_DIM)
        .at[row_count - WINDOW :]
        .add(rim_back[1])
    )
    grad_query_low = grad_query_blocks.reshape(row_count, HEADS * HEAD_DIM).astype(jnp.bfloat16)
    grad_key_low = grad_keys.astype(jnp.bfloat16)
    grad_value_low = grad_values.astype(jnp.bfloat16)
    d_query = weight_grad(normed_one, grad_query_low)
    d_key = weight_grad(normed_one, grad_key_low)
    d_value = weight_grad(normed_one, grad_value_low)
    grad_normed_one = (
        project_back(grad_query_low, back_query)
        + project_back(grad_key_low, back_key)
        + project_back(grad_value_low, back_value)
    )
    grad_in_norm, d_gain_one = norm_back(inputs, inv_one, back_gain_one, grad_normed_one)
    grad_inputs = grad_middle + grad_in_norm
    row_sums = (
        lax.psum_scatter(
            d_query.astype(jnp.bfloat16), "dp", scatter_dimension=0, tiled=True
        ).astype(jnp.float32),
        lax.psum_scatter(d_key.astype(jnp.bfloat16), "dp", scatter_dimension=0, tiled=True).astype(
            jnp.float32
        ),
        lax.psum_scatter(
            d_value.astype(jnp.bfloat16), "dp", scatter_dimension=0, tiled=True
        ).astype(jnp.float32),
        lax.psum_scatter(d_out.astype(jnp.bfloat16), "dp", scatter_dimension=0, tiled=True).astype(
            jnp.float32
        ),
        lax.psum_scatter(d_gate.astype(jnp.bfloat16), "dp", scatter_dimension=0, tiled=True).astype(
            jnp.float32
        ),
        lax.psum_scatter(d_up.astype(jnp.bfloat16), "dp", scatter_dimension=0, tiled=True).astype(
            jnp.float32
        ),
        lax.psum_scatter(d_down.astype(jnp.bfloat16), "dp", scatter_dimension=0, tiled=True).astype(
            jnp.float32
        ),
        lax.psum_scatter(
            d_gain_one.astype(jnp.bfloat16), "dp", scatter_dimension=0, tiled=True
        ).astype(jnp.float32),
        lax.psum_scatter(
            d_gain_two.astype(jnp.bfloat16), "dp", scatter_dimension=0, tiled=True
        ).astype(jnp.float32),
    )
    owned_mats = (
        lax.psum_scatter(
            row_sums[0].astype(jnp.bfloat16), "seq", scatter_dimension=1, tiled=True
        ).astype(jnp.float32),
        lax.psum_scatter(
            row_sums[1].astype(jnp.bfloat16), "seq", scatter_dimension=1, tiled=True
        ).astype(jnp.float32),
        lax.psum_scatter(
            row_sums[2].astype(jnp.bfloat16), "seq", scatter_dimension=1, tiled=True
        ).astype(jnp.float32),
        lax.psum_scatter(
            row_sums[3].astype(jnp.bfloat16), "seq", scatter_dimension=1, tiled=True
        ).astype(jnp.float32),
        lax.psum_scatter(
            row_sums[4].astype(jnp.bfloat16), "seq", scatter_dimension=1, tiled=True
        ).astype(jnp.float32),
        lax.psum_scatter(
            row_sums[5].astype(jnp.bfloat16), "seq", scatter_dimension=1, tiled=True
        ).astype(jnp.float32),
        lax.psum_scatter(
            row_sums[6].astype(jnp.bfloat16), "seq", scatter_dimension=1, tiled=True
        ).astype(jnp.float32),
    )
    owned_gains = lax.psum((row_sums[7], row_sums[8]), "seq")
    return (
        block_out,
        grad_inputs,
        owned_mats[0],
        owned_mats[1],
        owned_mats[2],
        owned_mats[3],
        owned_mats[4],
        owned_mats[5],
        owned_mats[6],
        owned_gains[0],
        owned_gains[1],
    )


SCRIPT = (
    ("start", 7), ("start", 6), ("start", 3), ("start", 10), ("start", 2), ("start", 19), ("start", 0),
    ("start", 9), (0, 3, 0), (0, 0, 0, 1), (0, 2, 0, 1), ("start", 17), ("start", 5), ("start", 18),
    ("start", 14), ("start", 1), ("start", 20), (0, 0, 0, 2), (0, 9, 0, 1), ("start", 15), (0, 3, 1, 1),
    (0, 10, 0, 1), (0, 2, 0, 2), (0, 9, 0, 2), (0, 5, 0), (0, 2, 0, 3), ("start", 16), ("start", 13),
    (0, 0, 0, 3), (0, 10, 0, 2), (0, 1, 0, 1), (0, 9, 0, 3), ("start", 4), (0, 0, 1), (0, 10, 0, 3),
    (0, 5, 1, 1), (0, 1, 0, 2), (0, 1, 0, 3), (0, 6, 0), ("start", 8), (0, 0, 2), (0, 20, 0), (0, 5, 1, 2),
    (0, 3, 1, 2), (0, 9, 1), (0, 18, 0), (0, 2, 1), (0, 17, 0), (0, 7, 0, 1), (0, 1, 1), (0, 8, 0, 1),
    ("start", 12), (0, 10, 1), (0, 6, 1, 1), (0, 4, 0), (0, 3, 1, 3), (0, 7, 0, 2), (0, 7, 0, 3), (0, 19, 0),
    (0, 4, 1, 1), (0, 6, 1, 2), (0, 6, 1, 3), (0, 4, 1, 2), (0, 19, 1, 1), (0, 5, 1, 3), (0, 4, 1, 3),
    (0, 8, 0, 2), (0, 2, 2), (0, 17, 1, 1), (0, 1, 2), (0, 18, 1, 1), (0, 16, 0), (0, 8, 0, 3), "norm",
    (0, 20, 1, 1), (0, 14, 0), (0, 3, 2), (0, 17, 1, 2), ("start", 11), (0, 20, 1, 2), (0, 7, 1), (0, 8, 1),
    (0, 4, 2), "query", (0, 5, 2), (0, 17, 1, 3), (0, 20, 1, 3), (0, 6, 2), (0, 13, 0), (0, 19, 1, 2),
    (0, 18, 1, 2), "key", (0, 14, 1, 1), "value", (0, 19, 1, 3), (0, 18, 1, 3), (0, 14, 1, 2), (0, 13, 1, 1),
    (0, 11, 0), (0, 20, 2), ("see", 0), (0, 7, 2), (0, 8, 2), (0, 15, 0), ("see", 1), (0, 13, 1, 2),
    (0, 9, 2), (0, 14, 1, 3), (0, 17, 2), ("see", 2), (0, 16, 1, 1), ("see", 3), (0, 13, 1, 3), (0, 18, 2),
    (0, 10, 2), (0, 15, 1, 1), (0, 19, 2), (0, 12, 0), (0, 11, 1, 1), "project", (0, 15, 1, 2), ("hidden", 0),
    (0, 11, 1, 2), (0, 15, 1, 3), (0, 16, 1, 2), (0, 13, 2), ("hidden", 1), (0, 14, 2), (0, 16, 1, 3),
    (0, 11, 1, 3), (0, 12, 1, 1), ("mlp", 0), (0, 12, 1, 2), ("mlp", 1), (0, 12, 1, 3), ("up", 0), (0, 15, 2),
    (0, 11, 2), ("gate", 0), ("gate", 1), ("up", 1), (0, 12, 2), (0, 16, 2), ("mlp", 2), ("mlp", 3),
    (1, 9, 0), (1, 8, 0), ("up", 2), ("gate", 2), ("gate", 3), "mix", (1, 8, 1), ("up", 3), ("dh2", 0),
    (1, 11, 0), "down", (1, 7, 0), (1, 9, 1), (1, 10, 0), ("dh2", 1), "norm2", (1, 6, 0), "heads", (1, 7, 1),
    ("attend", 0), (1, 3, 0), "out", ("attend", 1), ("attend", 2), ("attend", 3), (1, 0, 0), (1, 1, 0),
    (1, 6, 1), (1, 2, 0), (1, 12, 0), (1, 10, 1), (1, 13, 0), ("qkv", 0), "dh1", (1, 0, 1), ("qkv", 1),
    (1, 7, 2), (1, 12, 1), (1, 1, 1), (1, 14, 0), (1, 15, 0), ("qkv", 2), "norm1", (1, 8, 2), (1, 13, 1),
    (1, 11, 1), "gains", (1, 14, 1), (1, 16, 0), (1, 15, 1), (1, 9, 2), (1, 17, 0), (1, 11, 2), (1, 10, 2),
    (1, 6, 2), (1, 20, 0), (1, 5, 0), (1, 19, 0), (1, 16, 1), (1, 20, 1), (1, 18, 0), (1, 17, 1), (1, 4, 0),
    (1, 14, 2), (1, 2, 1), (1, 19, 1), (1, 3, 1), (1, 20, 2), (1, 5, 1), (1, 18, 1), (1, 12, 2), (1, 0, 2),
    (1, 4, 1), (1, 15, 2), (1, 16, 2), (1, 17, 2), (1, 3, 2), (1, 5, 2), (1, 2, 2), (1, 1, 2), (1, 13, 2),
    (1, 4, 2), (1, 19, 2), (1, 18, 2),
)
GATHER_KINDS = (("gain", "f"), ("square", "f"), ("square", "m"), ("square", "m"), ("square", "f"), ("broad", "fm"), ("broad", "mm"), ("tall", "mm"))
SCATTER_KINDS = (("tall", "fm"), ("broad", "lf"), ("broad", "fm"), ("square", "f"), ("square", "f"), ("square", "f"), ("square", "f"), ("gain_grad", "f"))


MESH = pl.DeviceIdType.MESH
NZ, NY, NX = 4, 2, 2
SEQUENCE = {"zfx": "zxy", "zfy": "zyx", "zmx": "xzy", "zmy": "yzx", "zlx": "xyz", "zly": "yxz"}
ALL_Z, ALL_Y, ALL_X = pl.ds(0, NZ), pl.ds(0, NY), pl.ds(0, NX)


class Plan:
    def __init__(self, tensors):
        self.tensors = tensors
        self.items, self.of_tensor = [], []
        for t, (_, _, _, cuts) in enumerate(tensors):
            begin, mine = 0, []
            for kind, along, count in cuts:
                mine.append(len(self.items))
                whole = [(0, tensors[t][0]), (0, tensors[t][1])]
                whole[along] = (begin, count)
                self.items.append((t, SEQUENCE[kind], *whole))
                begin += count
            self.of_tensor.append(mine)


class Place:
    def __init__(self):
        self.c, self.s = lax.axis_index("dp"), lax.axis_index("seq")
        self.z, self.y, self.x = self.c // 4, (self.c // 2) % 2, self.c % 2

    def at(self, z, y, x):
        return (z * 4 + y * 2 + x, self.s)

    def to_x(self):
        return self.at(self.z, self.y, 1 - self.x)

    def to_y(self):
        return self.at(self.z, 1 - self.y, self.x)

    def to_z(self, step):
        return self.at((self.z + step) % NZ, self.y, self.x)

    def to_core(self):
        return (self.c, 1 - self.s)

    def greet(self):
        barrier = pltpu.get_barrier_semaphore()
        peers = [self.to_x(), self.to_y(), self.to_core()] + [self.to_z(k) for k in (1, 2, 3)]
        for peer in peers:
            pl.semaphore_signal(barrier, inc=1, device_id=peer, device_id_type=MESH)
        pl.semaphore_wait(barrier, len(peers))


def remote(src, dst, send, recv, device):
    return pltpu.make_async_remote_copy(
        src_ref=src, dst_ref=dst, send_sem=send, recv_sem=recv, device_id=device, device_id_type=MESH
    )


def slots(seq, count, along_z):
    firsts, used = [], 0
    for phase in range(count):
        firsts.append(used)
        used += along_z if phase < 3 and seq[phase] == "z" else 1
    return firsts


class Gather:
    def __init__(self, plan, place, shards, bufs, send, recv, local):
        self.plan, self.me, self.shards, self.bufs = plan, place, shards, bufs
        self.send, self.recv, self.local = send, recv, local

    def own_copy(self, t):
        me = self.me
        return pltpu.make_async_copy(
            self.shards[t], self.bufs[t].at[me.s, me.z, me.y, me.x], self.local.at[t]
        )

    def moves(self, i, phase):
        t, seq, rows, cols = self.plan.items[i]
        me, buf = self.me, self.bufs[t]
        rows, cols = pl.ds(*rows), pl.ds(*cols)

        def view(z, y, x, half=me.s):
            return buf.at[half, z, y, x, rows, cols]

        if phase == 3:
            whole = view(ALL_Z, ALL_Y, ALL_X)
            return [(whole, whole, me.to_core(), view(ALL_Z, ALL_Y, ALL_X, 1 - me.s), 0)]
        done, axis = seq[:phase], seq[phase]
        z = ALL_Z if "z" in done else me.z
        y = ALL_Y if "y" in done else me.y
        x = ALL_X if "x" in done else me.x
        there = view(z, y, x)
        here = self.shards[t].at[rows, cols] if phase == 0 else there
        if axis == "x":
            return [(here, there, me.to_x(), view(z, y, 1 - me.x), 0)]
        return [(here, there, me.to_y(), view(z, 1 - me.y, x), 0)]

    def hops(self, i, phase, hop):
        t, seq, rows, cols = self.plan.items[i]
        me, buf = self.me, self.bufs[t]
        rows, cols = pl.ds(*rows), pl.ds(*cols)
        done = seq[:phase]
        y = ALL_Y if "y" in done else me.y
        x = ALL_X if "x" in done else me.x
        moves = []
        for k, way in enumerate((1, -1)):
            first, last = (me.z, NZ - 1 - me.z) if way == 1 else (NZ - 1 - me.z, me.z)
            sends = (first >= hop - 1) & (last >= 1)
            takes = first >= hop
            z = me.z - way * (hop - 1)
            there = buf.at[me.s, z, y, x, rows, cols]
            here = self.shards[t].at[rows, cols] if phase == 0 and hop == 1 else there
            arrived = buf.at[me.s, me.z - way * hop, y, x, rows, cols]
            moves.append((sends, takes, here, there, me.at(me.z + way, me.y, me.x), arrived, 3 * k + hop - 1))
        return moves

    def along_z(self, i, phase):
        return phase < 3 and self.plan.items[i][1][phase] == "z"

    def copy(self, i, phase, src, dst, device, k):
        at = 9 * i + slots(self.plan.items[i][1], 4, 6)[phase] + k
        return remote(src, dst, self.send.at[at], self.recv.at[at], device)

    def send_hop(self, i, phase, hop):
        for sends, _, here, there, device, _, k in self.hops(i, phase, hop):

            @pl.when(sends)
            def _(here=here, there=there, device=device, k=k):
                self.copy(i, phase, here, there, device, k).start()

    def take_hop(self, i, phase, hop):
        for _, takes, _, _, device, arrived, k in self.hops(i, phase, hop):

            @pl.when(takes)
            def _(device=device, arrived=arrived, k=k):
                self.copy(i, phase, arrived, arrived, device, k).wait_recv()

        if hop < NZ - 1:
            self.send_hop(i, phase, hop + 1)

    def start(self, i, phase):
        if self.along_z(i, phase):
            self.send_hop(i, phase, 1)
            return
        for here, there, device, _, k in self.moves(i, phase):
            self.copy(i, phase, here, there, device, k).start()

    def wait(self, i, phase):
        for _, _, device, arrived, k in self.moves(i, phase):
            self.copy(i, phase, arrived, arrived, device, k).wait_recv()

    def finish(self, i):
        for phase in range(4):
            if self.along_z(i, phase):
                for hop in range(1, NZ):
                    for sends, _, here, there, device, _, k in self.hops(i, phase, hop):

                        @pl.when(sends)
                        def _(here=here, there=there, device=device, k=k):
                            self.copy(i, phase, here, there, device, k).wait_send()

                continue
            for here, there, device, _, k in self.moves(i, phase):
                self.copy(i, phase, here, there, device, k).wait_send()


def got_shapes(plan):
    shapes = []
    for t, seq, (_, rows), (_, columns) in plan.items:
        dtype = plan.tensors[t][2]
        leads = {"z": ((NZ, 2), (1, NZ), (3,)), "m": ((NZ, 2), (3, 2), (1,)), "l": ((3, 2, 2), (1, 2), (1,))}
        lead = leads["zml"[seq.index("z")]]
        shapes.append([(d + (rows, columns), dtype) for d in lead])
    return shapes


class Scatter:
    def __init__(self, plan, place, total, got, out, send, recv):
        self.plan, self.me, self.total, self.got, self.out = plan, place, total, got, out
        self.send, self.recv = send, recv

    def moves(self, i, phase):
        t, seq, rows, cols = self.plan.items[i]
        me, total, got = self.me, self.total[t], self.got[i][phase]
        rows, cols = pl.ds(*rows), pl.ds(*cols)
        axis, done = seq[2 - phase], seq[3 - phase :]
        z = me.z if "z" in done else ALL_Z
        y = me.y if "y" in done else ALL_Y
        x = me.x if "x" in done else ALL_X
        if phase == 0 and axis != "z":
            lands = [got]
        else:
            lands = [got.at[k] for k in range(got.shape[0])]
        if axis == "x":
            return [(total.at[z, y, 1 - me.x, rows, cols], lands[0], me.to_x(), 0)]
        if axis == "y":
            return [(total.at[z, 1 - me.y, x, rows, cols], lands[0], me.to_y(), 0)]
        return [
            (total.at[(me.z + k) % NZ, y, x, rows, cols], lands[k - 1], me.to_z(k), k - 1)
            for k in (1, 2, 3)
        ]

    def copy(self, i, phase, src, dst, device, k):
        at = 5 * i + slots(self.plan.items[i][1][::-1], 3, 3)[phase] + k
        return remote(src, dst, self.send.at[at], self.recv.at[at], device)

    def start(self, i, phase):
        for here, there, device, k in self.moves(i, phase):
            self.copy(i, phase, here, there, device, k).start()

    def wait(self, i, phase):
        for here, there, device, k in self.moves(i, phase):
            self.copy(i, phase, there, there, device, k).wait_recv()

    def add(self, i, phase):
        t, seq, rows, cols = self.plan.items[i]
        me, total, got = self.me, self.total[t], self.got[i][phase]
        rows, cols = pl.ds(*rows), pl.ds(*cols)
        if phase == 0 and seq[2] == "z":
            for y in range(NY):
                for x in range(NX):
                    part = total[me.z, y, x, rows, cols].astype(jnp.float32)
                    for k in range(3):
                        part += got[k, y, x].astype(jnp.float32)
                    total[me.z, y, x, rows, cols] = part.astype(total.dtype)
        elif phase == 1 and seq[2] == "z":
            for o in range(2):
                at = (me.z, me.y, o) if seq[1] == "y" else (me.z, o, me.x)
                total[at + (rows, cols)] += got[0, o]
        elif phase == 0:
            for z in range(NZ):
                for o in range(2):
                    at = (z, me.y, o) if seq[2] == "y" else (z, o, me.x)
                    total[at + (rows, cols)] += got[z, o]
        elif phase == 1 and seq[1] != "z":
            for z in range(NZ):
                total[z, me.y, me.x, rows, cols] += got[0, z]
        elif phase == 1:
            for o in range(2):
                at = (me.z, me.y, o) if seq[2] == "y" else (me.z, o, me.x)
                part = total[at + (rows, cols)].astype(jnp.float32)
                for k in range(3):
                    part += got[k, o].astype(jnp.float32)
                total[at + (rows, cols)] = part.astype(total.dtype)
        else:
            part = total[me.z, me.y, me.x, rows, cols].astype(jnp.float32)
            for k in range(got.shape[0]):
                part += got[k].astype(jnp.float32)
            self.out[t][rows, cols] = part

    def finish(self, i):
        for phase in range(3):
            for here, there, device, k in self.moves(i, phase):
                self.copy(i, phase, here, there, device, k).wait_send()


EPS = 1e-05
PAIR = 2 * HEAD_DIM
SPAN = 2 * WINDOW
LOW = jnp.bfloat16
F32 = jnp.float32


def mm(left, right):
    return jnp.dot(left, right, preferred_element_type=F32)


def mm_nt(left, right):
    return lax.dot_general(left, right, (((1,), (1,)), ((), ())), preferred_element_type=F32)


def mm_tn(left, right):
    return lax.dot_general(left, right, (((0,), (0,)), ((), ())), preferred_element_type=F32)


def column_tiles(columns, size):
    full = columns // size
    tiles = [(0, size, full)]
    if columns % size:
        tiles.append((full * size, columns % size, 1))
    return tiles


def each_tile(columns, size, body):
    for begin, width, count in column_tiles(columns, size):
        if count == 1:
            body(begin, width)
        else:

            def step(j, _, begin=begin, width=width):
                body(pl.multiple_of(begin + j * width, 128), width)
                return 0

            lax.fori_loop(0, count, step, 0)


def each_rows(rows, size, body):
    def step(j, _):
        body(pl.ds(pl.multiple_of(j * size, size), size))
        return 0

    lax.fori_loop(0, rows // size, step, 0)


def both_heads(block):
    first = lax.broadcasted_iota(jnp.int32, block.shape, 1) < HEAD_DIM
    zero = jnp.zeros_like(block)
    return jnp.concatenate([jnp.where(first, block, zero), jnp.where(first, zero, block)], axis=0)


def merge_heads(stacked):
    rows = stacked.shape[0] // 2
    first = lax.broadcasted_iota(jnp.int32, (rows, PAIR), 1) < HEAD_DIM
    return jnp.where(first, stacked[:rows], stacked[rows:])


VMEM_LIMIT = 64 * 2**20


class Stream:
    def __init__(self, count, sems, fetch):
        self.count, self.sems, self.fetch = count, sems, fetch

    def copies(self, j, slot):
        return [
            pltpu.make_async_copy(src, dst, self.sems.at[slot, k])
            for k, (src, dst) in enumerate(self.fetch(j, slot))
        ]

    def prime(self):
        for copy in self.copies(0, 0):
            copy.start()

    def run(self, body, first=0, last=None):
        def step(j, _):
            slot = j % 2

            @pl.when(j + 1 < self.count)
            def _():
                for copy in self.copies(j + 1, 1 - slot):
                    copy.start()

            for copy in self.copies(j, slot):
                copy.wait()
            body(j, slot)
            return 0

        lax.fori_loop(first, self.count if last is None else last, step, 0)


def block_kernel(ahead, back, *refs):
    n = len(ahead.tensors)
    (lens, x_h, dy_h), raw_h, refs = refs[:3], refs[3 : 3 + n], refs[3 + n :]
    hbm_bufs, refs = refs[: n - 1], refs[n - 1 :]
    (mixed_o, gtok_o, q_h, p_h, ha_h, ho_h, hm_h, hid_h), refs = refs[:8], refs[8:]
    outs_h, refs = refs[:n], refs[n:]
    outs, refs = refs[:n], refs[n:]
    total, refs = refs[:n], refs[n:]
    count = len(back.items)
    got, refs = [refs[3 * i : 3 * i + 3] for i in range(count)], refs[3 * count :]
    (gate_pad, up_pad, down_pad, gain_buf, gains, xb, h1, da, db, kx, vx, o, x1, hid), refs = refs[:14], refs[14:]
    (dar, dbr, pair_of, pair_low), refs = refs[:4], refs[4:]
    raw, refs = list(refs[:7]) + [raw_h[7]], refs[7:]
    (dy, dyr, dh, dxr_r, turned, pool, broad), refs = refs[:7], refs[7:]
    (kc, vc, rim_k, rim_v, gain_sum, gain_other), refs = refs[:6], refs[6:]
    (a_send, a_recv, own_sem, b_send, b_recv, load_sem, pool_sem, broad_sem, turn_sem), refs = refs[:9], refs[9:]
    half_send, half_recv = refs
    rows, width = xb.shape
    wide, columns = ahead.tensors[5][1], ahead.tensors[1][1]
    chips = NZ * NY * NX
    me = Place()
    halves, loads, later = {}, [0], {}

    def load(src, dst):
        copy = pltpu.make_async_copy(src, dst, load_sem.at[loads[0]])
        loads[0] += 1
        copy.start()
        return copy

    def to_partner(k, src, dst):
        copy = remote(src, dst, half_send.at[k], half_recv.at[k], me.to_core())
        copy.start()
        halves[k] = copy
        return copy

    def own(size, side=0):
        return pl.ds(pl.multiple_of((me.s if side == 0 else 1 - me.s) * size, 128), size)

    get_raw = [load(raw_h[t], raw[t]) for t in range(7)]
    get_x, get_dy = load(x_h, xb), load(dy_h, dy)
    me.greet()
    pair_of[...] = jnp.zeros_like(pair_of)
    get_raw[0].wait()
    blank = jnp.zeros((1, raw[0].shape[1]), F32)
    for k in range(2):
        gain = raw[0][k : k + 1, :].astype(F32)
        left, right = jnp.concatenate([gain, blank], axis=1), jnp.concatenate([blank, gain], axis=1)
        pair_of[k : k + 1, :] = jnp.where(me.x == 0, left, right)
    pair_low[...] = pair_of[...].astype(LOW)
    shards = [pair_low] + list(raw[1:5]) + [gate_pad, up_pad, down_pad]
    bufs = [gain_buf] + list(hbm_bufs)
    flat = [b.reshape(2, chips * b.shape[4], b.shape[5]) for b in bufs]
    gather = Gather(ahead, me, shards, bufs, a_send, a_recv, own_sem)
    scatter = Scatter(back, me, total, got, outs, b_send, b_recv)
    ready = set()

    def pad_shards():
        part, tile = raw[7].shape[0], down_pad.shape[0]
        zero = jnp.zeros((raw[5].shape[0], tile - part), LOW)
        for src, dst in ((raw[5], gate_pad), (raw[6], up_pad)):
            value, pieces = src[...], []
            for k in range(value.shape[1] // part):
                pieces += [value[:, k * part : (k + 1) * part], zero]
            dst[...] = jnp.concatenate(pieces, axis=1)
        down_pad[...] = jnp.concatenate([raw[7][...], jnp.zeros((tile - part, down_pad.shape[1]), LOW)], axis=0)

    def prepare(t):
        if t not in ready and 0 < t < 5:
            get_raw[t].wait()
        if t >= 5 and 5 not in ready:
            get_raw[5].wait()
            get_raw[6].wait()
            pad_shards()
            for k in range(5, n):
                gather.own_copy(k).start()
                ready.add(k)
        elif t not in ready:
            gather.own_copy(t).start()
            ready.add(t)

    landed, arrived = set(), set()

    def land(t):
        if t not in landed:
            landed.add(t)
            gather.own_copy(t).wait()

    def need(*tensors, part=None):
        for t in tensors:
            mine = ahead.of_tensor[t]
            for i in mine if part is None else mine[part : part + 1]:
                if i not in arrived:
                    arrived.add(i)
                    gather.wait(i, 3)

    def norm(values, gain):
        inverse = lax.rsqrt(jnp.mean(values * values, axis=-1, keepdims=True) + EPS)
        return (values * inverse * gain).astype(LOW)

    def share(name, k, mine, whole):
        to = whole.at[:, own(rows)]
        later[name] = (load(mine, to), to_partner(k, mine, to))

    def shared(name):
        copy, sent = later[name]
        copy.wait()
        sent.wait()

    def turn(src, dst, lane):
        def body(j, _):
            at = pl.ds(pl.multiple_of(j * 128, 128), 128)
            dst[at, pl.ds(lane, rows)] = src[:, at].T
            return 0

        lax.fori_loop(0, src.shape[1] // 128, body, 0)
        return dst.at[:, pl.ds(lane, rows)]

    def first_norm():
        need(0)
        get_dy.wait()
        later["dy"] = to_partner(0, dy.at[:, own(columns, 1)], dyr)
        parts = []
        for z in range(NZ):
            for y in range(NY):
                pair = [gain_buf[me.s, z, y, x].astype(F32) for x in range(NX)]
                parts.append(pair[0] + pair[1])
        gains[...] = jnp.concatenate(parts, axis=1)[0:8]
        get_x.wait()

        def body(at):
            h1[at, :] = norm(xb[at, :].astype(F32), gains[0:1, :])

        each_rows(rows, 64, body)
        share("ha", 1, turn(h1, turned.at[0], 0), ha_h)

    def project(t, src, store):
        need(t)
        tiles = Stream(2, pool_sem, lambda j, slot: [(flat[t].at[j], pool.at[slot, pl.ds(0, width), :])])
        tiles.prime()

        def body(side, slot):
            for begin in range(0, columns, 256):
                part = mm(src[...], pool[slot, :width, begin : begin + 256])
                store(pl.ds(pl.multiple_of(side * columns + begin, 128), 256), part)

        tiles.run(body)

    def rim(k, ref):
        to = ref.at[pl.ds(0, WINDOW), :]
        return remote(ref.at[pl.ds(rows, WINDOW), :], to, half_send.at[2 + k], half_recv.at[2 + k], me.to_core())

    def put_into(ref, skip):
        def store(cols, part):
            ref[pl.ds(skip, rows), cols] = part.astype(LOW)

        return store

    def do_query():
        project(1, h1, put_into(da, 0))
        later["q_out"] = load(da.at[:, pl.ds(0, width)], q_h)

    def do_key():
        project(2, h1, put_into(kx, WINDOW))
        rim(0, kx).start()

    def do_value():
        project(3, h1, put_into(vx, WINDOW))
        rim(1, vx).start()

    first_end = lens[0:1, 0:1]
    second_end = first_end + lens[0:1, 1:2]

    def attend(b, _):
        base = me.s * rows + b * WINDOW
        at = pl.ds(pl.multiple_of(b * WINDOW, WINDOW), WINDOW)
        over = pl.ds(pl.multiple_of(b * WINDOW, WINDOW), SPAN)
        row = lax.broadcasted_iota(jnp.int32, (WINDOW, SPAN), 0)
        col = lax.broadcasted_iota(jnp.int32, (WINDOW, SPAN), 1)
        q_pos, k_pos = base + row, base - WINDOW + col

        def doc(pos):
            return (pos >= first_end).astype(jnp.int32) + (pos >= second_end).astype(jnp.int32)

        visible = (col >= row) & (col <= row + WINDOW) & (k_pos >= 0) & (doc(q_pos) == doc(k_pos))
        bias = jnp.where(visible, 0.0, -1e30)
        bias = jnp.concatenate([bias, bias], axis=0)
        pairs = range(HEADS // 2)
        cols = [slice(p * PAIR, (p + 1) * PAIR) for p in pairs]
        queries = [both_heads(da[at, c]) for c in cols]
        keys, values = [kx[over, c] for c in cols], [vx[over, c] for c in cols]
        scores = [mm_nt(q2, k) * HEAD_DIM ** (-0.5) + bias for q2, k in zip(queries, keys)]
        tops = [jnp.max(s, axis=-1, keepdims=True) for s in scores]
        exps = [jnp.exp(s - top) for s, top in zip(scores, tops)]
        sums = [jnp.sum(e, axis=-1, keepdims=True) for e in exps]
        weights = [(e * (1.0 / t)).astype(LOW) for e, t in zip(exps, sums)]
        parts = [merge_heads(mm(w, v)).astype(LOW) for w, v in zip(weights, values)]
        for p, c, w, part in zip(pairs, cols, weights, parts):
            db[at, 2 * p * SPAN : (2 * p + 1) * SPAN] = w[:WINDOW]
            db[at, (2 * p + 1) * SPAN : (2 * p + 2) * SPAN] = w[WINDOW:]
            o[at, c] = part
        return 0

    quarter = rows // WINDOW // 4

    def attend_part(k):
        if k == 0:
            for j, ref in ((0, kx), (1, vx)):
                rim(j, ref).wait_recv()
        lax.fori_loop(k * quarter, (k + 1) * quarter, attend, 0)
        if k == 3:
            later["p_out"] = load(db.at[:, pl.ds(0, HEADS * SPAN)], p_h)
            share("ho", 4, turn(o, turned.at[0], rows), ho_h)

    def add_out():
        def store(cols, part):
            x1[:, cols] = xb[:, cols].astype(F32) + part

        project(4, o, store)

        def body(at):
            xb[at, :] = norm(x1[at, :], gains[1:2, :])

        each_rows(rows, 64, body)
        share("hm", 5, turn(xb, turned.at[1], rows), hm_h)

    strips = [ahead.items[i][3] for i in ahead.of_tensor[5]]

    def strip_copies(p, side):
        begin, size = strips[p]
        return [
            pltpu.make_async_copy(
                flat[5 + k].at[side, :, pl.ds(begin, size)],
                pool.at[side, pl.ds(k * width, width), pl.ds(0, size)],
                pool_sem.at[side, k],
            )
            for k in range(2)
        ]

    def mlp(p):
        need(5, 6, part=p)
        for side in range(2):
            for copy in strip_copies(p, side):
                copy.start()
        if p == 0:
            later["p_out"].wait()
            for name in ("ha", "ho", "hm"):
                shared(name)
            later["hm"] = load(hm_h, turned.at[0])
        if p >= 2:
            for side in range(2):
                shared(("hid", p - 2, side))
        begin, size = strips[p]
        for side in range(2):
            for copy in strip_copies(p, side):
                copy.wait()
            for skip in range(0, size, 256):
                w = min(256, size - skip)
                cols = slice(skip, skip + w)
                a = mm(xb[...], pool[side, :width, cols])
                b = mm(xb[...], pool[side, width : 2 * width, cols])
                sig = 1.0 / (1.0 + jnp.exp(-a))
                silu = a * sig
                at = slice(side * wide + begin + skip, side * wide + begin + skip + w)
                grad = da[:, at].astype(F32)
                db[:, at] = (grad * silu).astype(LOW)
                da[:, at] = (grad * b * sig * (1.0 + a * (1.0 - sig))).astype(LOW)
                hidden_low = (silu * b).astype(LOW)
                hid[side, :, begin + skip : begin + skip + w] = hidden_low
                first = p % 2 * 512 + skip
                turned[1, first : first + w, side * rows : (side + 1) * rows] = hidden_low.T
        across = pl.ds(pl.multiple_of((1 - me.s) * wide + begin, 128), size)
        here = pl.ds(begin, size)
        later["db", p] = to_partner(6 + 4 * p, db.at[:, across], dbr.at[:, here])
        later["da", p] = to_partner(7 + 4 * p, da.at[:, across], dar.at[:, here])
        for side in range(2):
            mine = turned.at[1, pl.ds(p % 2 * 512, size), pl.ds(side * rows, rows)]
            share(("hid", p, side), 8 + 4 * p + side, mine, hid_h.at[pl.ds(side * wide + begin, size), :])
        if p == len(strips) - 1:
            mlp_tiles.prime()

    tall = back.tensors[0][0] * NY * NX
    hid_tiles = Stream(
        NZ, turn_sem, lambda j, slot: [(hid_h.at[pl.ds(pl.multiple_of(j * tall, 16), tall), :], turned.at[slot, pl.ds(0, tall), :])]
    )
    tile, thin = 256, 128
    small = pool.reshape(2, pool.shape[1] // tile, tile, columns)

    def row_tiles(w, size, dst):
        return lambda j, slot: (w.at[:, pl.ds(pl.multiple_of(j * size, size), size), :], dst(slot))

    def small_at(k):
        return lambda slot: small.at[slot, pl.ds(2 * k, 2)]

    def broad_at(k):
        return lambda slot: broad.at[slot, k]

    def stream_of(fetchers, count, sems):
        return Stream(count, sems, lambda j, slot: [f(j, slot) for f in fetchers])

    down_tiles = stream_of([row_tiles(flat[7], tile, small_at(0))], flat[7].shape[1] // tile, pool_sem)
    mlp_tiles = stream_of([row_tiles(flat[5 + k], thin, broad_at(k)) for k in range(2)], width // thin, broad_sem)
    out_tiles = stream_of([row_tiles(flat[4], tile, small_at(0))], width // tile, pool_sem)
    qkv_tiles = stream_of([row_tiles(flat[1 + k], tile, small_at(k)) for k in range(3)], width // tile, pool_sem)

    def begin_scatter(t):
        for i in back.of_tensor[t]:
            scatter.start(i, 0)

    def put(t, z, part, cols=slice(None)):
        low = part.reshape(NY, NX, back.tensors[t][0], part.shape[1]).astype(total[t].dtype)
        total[t][z, :, :, :, cols] = low

    def grad_down():
        for p in range(len(strips)):
            for side in range(2):
                if p + 2 >= len(strips):
                    shared(("hid", p, side))
        later["dy"].wait_recv()
        hid_tiles.prime()

        def body(z, slot):
            mine = mm(turned[slot, :tall, own(rows)], dy[:, own(columns)])
            put(0, z, mine + mm(turned[slot, :tall, own(rows, 1)], dyr[...]))

        hid_tiles.run(body)
        begin_scatter(0)
        later["ha"] = load(ha_h, turned.at[0])
        later["ho"] = load(ho_h, turned.at[1])

    def add_down():
        tiles2 = Stream(2, pool_sem, lambda j, slot: [(flat[7].at[j], pool.at[slot])])
        tiles2.prime()

        def body(side, slot):
            for begin in range(0, columns, 256):
                part = mm(hid[0], pool[slot, :wide, begin : begin + 256])
                part += mm(hid[1], pool[slot, wide:, begin : begin + 256])
                cols = pl.ds(pl.multiple_of(side * columns + begin, 128), 256)
                xb[:, cols] = (x1[:, cols] + part).astype(LOW)

        tiles2.run(body)
        later["mixed"] = load(xb, mixed_o)

    def hidden_body(j, slot):
        part = mm_nt(dy[:, :columns], small[slot, 0]) + mm_nt(dy[:, columns:], small[slot, 1])
        da[:, pl.ds(pl.multiple_of(j * tile, tile), tile)] = part.astype(LOW)

    def hidden(k):
        middle = down_tiles.count // 2
        if k == 0:
            need(7)
            down_tiles.prime()
            later["q_out"].wait()
            down_tiles.run(hidden_body, 0, middle)
            return
        down_tiles.run(hidden_body, middle)

    def weight_grad_to(t, slot, mine, theirs, cols=slice(None)):
        row_count = back.tensors[t][0] * NY * NX

        def step(z, _):
            at = pl.ds(pl.multiple_of(z * row_count, 16), row_count)
            put(t, z, mm(turned[slot, at, own(rows)], mine()) + mm(turned[slot, at, own(rows, 1)], theirs()), cols)
            return 0

        lax.fori_loop(0, NZ, step, 0)

    def grad_strip(t, name, grad, other, p):
        begin, size = strips[p]
        if p == 0 and t == 1:
            later["hm"].wait()
        later[name, p].wait_recv()
        cols = slice(begin, begin + size)
        mine = pl.ds(pl.multiple_of(me.s * wide + begin, 128), size)
        weight_grad_to(t, 0, lambda: grad[:, mine], lambda: other[:, cols], cols)
        scatter.start(back.of_tensor[t][p], 0)

    def dh2_body(j, slot):
        part = None
        for k, grad in ((0, da), (1, db)):
            for side in range(2):
                term = mm_nt(grad[:, side * wide : (side + 1) * wide], broad[slot, k, side])
                part = term if part is None else part + term
        dh[:, pl.ds(pl.multiple_of(j * thin, thin), thin)] = part

    def grad_norm2(k):
        middle = mlp_tiles.count // 2
        if k == 0:
            mlp_tiles.run(dh2_body, 0, middle)
            return
        mlp_tiles.run(dh2_body, middle)
        for p in range(len(strips)):
            later["db", p].wait_send()
            later["da", p].wait_send()
        out_tiles.prime()
        later["q"] = load(q_h, da.at[:, pl.ds(0, width)])
        later["p"] = load(p_h, db.at[:, pl.ds(0, HEADS * SPAN)])
        later["mixed"].wait()
        later["x"] = load(x_h, xb)

    def norm_grad(values, grad_norm, gain):
        inverse = lax.rsqrt(jnp.mean(values * values, axis=-1, keepdims=True) + EPS)
        scaled = grad_norm * gain
        mean_term = jnp.mean(values * scaled, axis=-1, keepdims=True)
        back_part = inverse * scaled - values * (inverse * inverse * inverse) * mean_term
        return back_part, jnp.sum(values * inverse * grad_norm, axis=0, keepdims=True)

    def norm2_body(at):
        back_part, gain_part = norm_grad(x1[at, :], dh[at, :], gains[1:2, :])
        gain_sum[1:2, :] += gain_part
        grad = dy[at, :].astype(F32) + back_part
        x1[at, :] = grad
        h1[at, :] = grad.astype(LOW)

    def norm2():
        gain_sum[...] = jnp.zeros_like(gain_sum)
        each_rows(rows, 64, norm2_body)
        later["dxr"] = to_partner(22, h1.at[:, own(columns, 1)], dxr_r)

    def out_body(j, slot):
        part = mm_nt(h1[:, :columns], small[slot, 0]) + mm_nt(h1[:, columns:], small[slot, 1])
        o[:, pl.ds(pl.multiple_of(j * tile, tile), tile)] = part.astype(LOW)

    def grad_heads():
        out_tiles.run(out_body)
        qkv_tiles.prime()

    def grad_out():
        later["ho"].wait()
        later["dxr"].wait_recv()
        weight_grad_to(3, 1, lambda: h1[:, own(columns)], lambda: dxr_r[...])
        begin_scatter(3)

    scale = HEAD_DIM ** (-0.5)

    def attend_back(b, _):
        at = pl.ds(pl.multiple_of(b * WINDOW, WINDOW), WINDOW)
        over = pl.ds(pl.multiple_of(b * WINDOW, WINDOW), SPAN)
        pairs = range(HEADS // 2)
        cols = [slice(p * PAIR, (p + 1) * PAIR) for p in pairs]
        queries, grads = [both_heads(da[at, c]) for c in cols], [both_heads(o[at, c]) for c in cols]
        keys, values = [kx[over, c] for c in cols], [vx[over, c] for c in cols]
        lows = [
            jnp.concatenate([db[at, (2 * p + h) * SPAN : (2 * p + h + 1) * SPAN] for h in range(2)], axis=0)
            for p in pairs
        ]
        carry_k, carry_v = [kc[:, c] for c in cols], [vc[:, c] for c in cols]
        probs = [low.astype(F32) for low in lows]
        grad_probs = [mm_nt(g, v) for g, v in zip(grads, values)]
        grad_values = [mm_tn(low, g) for low, g in zip(lows, grads)]
        inners = [jnp.sum(p * g, axis=-1, keepdims=True) for p, g in zip(probs, grad_probs)]
        scores = [(p * (g - i)).astype(LOW) for p, g, i in zip(probs, grad_probs, inners)]
        grad_queries = [(merge_heads(mm(s, k)) * scale).astype(LOW) for s, k in zip(scores, keys)]
        grad_keys = [mm_tn(s, q2) * scale for s, q2 in zip(scores, queries)]
        new_k = [(old + g[:WINDOW]).astype(LOW) for old, g in zip(carry_k, grad_keys)]
        new_v = [(old + g[:WINDOW]).astype(LOW) for old, g in zip(carry_v, grad_values)]
        for c, gq, gk, gv, nk, nv in zip(cols, grad_queries, grad_keys, grad_values, new_k, new_v):
            da[at, c] = gq
            kx[at, c] = nk
            vx[at, c] = nv
            kc[:, c] = gk[WINDOW:]
            vc[:, c] = gv[WINDOW:]
        return 0

    own_rows = pl.ds(WINDOW, rows)
    qr, kr, vr = dar.at[:, pl.ds(0, columns)], dar.at[:, pl.ds(columns, columns)], dbr.at[:, pl.ds(0, columns)]

    def attend_back_part(k):
        if k == 0:
            kc[...] = jnp.zeros_like(kc)
            vc[...] = jnp.zeros_like(vc)
            for j, ref in ((0, kx), (1, vx)):
                rim(j, ref).wait_send()
            later["q"].wait()
            later["p"].wait()
        lax.fori_loop(k * quarter, (k + 1) * quarter, attend_back, 0)
        if k == 0:
            later["rim"] = [
                to_partner(23, kx.at[pl.ds(0, WINDOW), :], rim_k),
                to_partner(24, vx.at[pl.ds(0, WINDOW), :], rim_v),
            ]
        if k == 3:
            for copy, ref, carry, rim_in in ((later["rim"][0], kx, kc, rim_k), (later["rim"][1], vx, vc, rim_v)):
                copy.wait_recv()
                ref[pl.ds(rows, WINDOW), :] = (carry[...] + rim_in[...].astype(F32)).astype(LOW)
            later["dq"] = to_partner(25, da.at[:, own(columns, 1)], qr)
            later["dk"] = to_partner(26, kx.at[own_rows, own(columns, 1)], kr)
            later["dv"] = to_partner(27, vx.at[own_rows, own(columns, 1)], vr)

    def grad_qkv(k):
        if k == 0:
            later["ha"].wait()
        later[("dq", "dk", "dv")[k]].wait_recv()
        mine = (lambda: da[:, own(columns)], lambda: kx[own_rows, own(columns)], lambda: vx[own_rows, own(columns)])[k]
        theirs = (qr, kr, vr)[k]
        weight_grad_to(4 + k, 0, mine, lambda: theirs[...])
        begin_scatter(4 + k)

    def dh1_body(j, slot):
        part = None
        for k, (grad, skip) in enumerate(((da, 0), (kx, WINDOW), (vx, WINDOW))):
            for side in range(2):
                left = grad[pl.ds(skip, rows), side * columns : (side + 1) * columns]
                term = mm_nt(left, small[slot, 2 * k + side])
                part = term if part is None else part + term
        dh[:, pl.ds(pl.multiple_of(j * tile, tile), tile)] = part

    def grad_norm1():
        qkv_tiles.run(dh1_body)

    def norm1_body(at):
        back_part, gain_part = norm_grad(xb[at, :].astype(F32), dh[at, :], gains[0:1, :])
        gain_sum[0:1, :] += gain_part
        x1[at, :] = x1[at, :] + back_part

    def norm1():
        later["x"].wait()
        each_rows(rows, 64, norm1_body)
        later["gtok"] = load(x1, gtok_o)
        later["gain"] = to_partner(28, gain_sum, gain_other)

    def grad_gains():
        later["gain"].wait_recv()
        lanes = back.tensors[7][1]
        for c in range(chips):
            at = slice(c // 2 * lanes, (c // 2 + 1) * lanes)
            total[7][c // 4, c // 2 % 2, c % 2] = gain_sum[:, at] + gain_other[:, at]
        begin_scatter(7)

    work = {
        "norm": first_norm,
        "query": do_query,
        "key": do_key,
        "value": do_value,
        "project": add_out,
        "mix": add_down,
        "down": grad_down,
        "norm2": norm2,
        "heads": grad_heads,
        "out": grad_out,
        "dh1": grad_norm1,
        "norm1": norm1,
        "gains": grad_gains,
    }
    for k in range(4):
        work["see", k] = functools.partial(attend_part, k)
        work["attend", k] = functools.partial(attend_back_part, k)
    for k in range(len(strips)):
        work["mlp", k] = functools.partial(mlp, k)
        work["up", k] = functools.partial(grad_strip, 1, "db", db, dbr, k)
        work["gate", k] = functools.partial(grad_strip, 2, "da", da, dar, k)
    for k in range(3):
        work["qkv", k] = functools.partial(grad_qkv, k)
    for k in range(2):
        work["hidden", k] = functools.partial(hidden, k)
        work["dh2", k] = functools.partial(grad_norm2, k)
    summed = []
    for step in SCRIPT:
        if step in work:
            work[step]()
        elif step[0] == "start":
            prepare(ahead.items[step[1]][0])
            gather.start(step[1], 0)
        elif step[0] == 0:
            _, i, phase, *hop = step
            land(ahead.items[i][0])
            if hop:
                gather.take_hop(i, phase, hop[0])
            else:
                gather.wait(i, phase)
            if hop in ([], [NZ - 1]):
                gather.start(i, phase + 1)
        else:
            _, i, phase = step
            scatter.wait(i, phase)
            scatter.add(i, phase)
            if phase < 2:
                scatter.start(i, phase + 1)
                continue
            t = back.items[i][0]
            summed.append(i)
            if all(k in summed for k in back.of_tensor[t]):
                later["sum", t] = load(outs[t], outs_h[t])
    for i in range(len(ahead.items)):
        gather.finish(i)
    for i in range(len(back.items)):
        scatter.finish(i)
    for k in (0, 22, 23, 24, 25, 26, 27, 28):
        halves[k].wait_send()
    later["gtok"].wait()
    for t in range(n):
        later["sum", t].wait()


def block_all(ahead, back, lens, tokens, cotangent, shards):
    n, na, nb = len(ahead.tensors), len(ahead.items), len(back.items)
    rows, width = tokens.shape
    columns, wide = ahead.tensors[1][1], ahead.tensors[5][1]
    anywhere = pl.BlockSpec(memory_space=pl.ANY)
    inside = pl.BlockSpec(memory_space=pltpu.VMEM)
    shape = jax.ShapeDtypeStruct
    over = WINDOW + rows
    bufs = [(2, NZ, NY, NX) + t[:2] for t in ahead.tensors]
    kept = [
        ((rows, width), LOW),
        ((rows, width), F32),
        ((rows, width), LOW),
        ((rows, HEADS * SPAN), LOW),
        ((width, 2 * rows), LOW),
        ((width, 2 * rows), LOW),
        ((width, 2 * rows), LOW),
        ((2 * wide, 2 * rows), LOW),
    ]
    scratch = [
        (ahead.tensors[5][:2], LOW),
        (ahead.tensors[6][:2], LOW),
        (ahead.tensors[7][:2], LOW),
        (bufs[0], LOW),
        ((8, width), F32),
        ((rows, width), LOW),
        ((rows, width), LOW),
        ((rows, 2 * wide), LOW),
        ((rows, 2 * wide), LOW),
        ((over, width), LOW),
        ((over, width), LOW),
        ((rows, width), LOW),
        ((rows, width), F32),
        ((2, rows, wide), LOW),
        ((rows, wide), LOW),
        ((rows, wide), LOW),
        (ahead.tensors[0][:2], F32),
        (ahead.tensors[0][:2], LOW),
        *((shard.shape, LOW) for shard in shards[:7]),
        ((rows, width), LOW),
        ((rows, columns), LOW),
        ((rows, width), F32),
        ((rows, columns), LOW),
        ((2, width, 2 * rows), LOW),
        ((2, 2 * wide, columns), LOW),
        ((2, 2, 2, 128, wide), LOW),
        ((WINDOW, width), F32),
        ((WINDOW, width), F32),
        ((WINDOW, width), LOW),
        ((WINDOW, width), LOW),
        ((8, width), F32),
        ((8, width), F32),
    ]
    results = [(t[:2], F32) for t in back.tensors]
    totals = [((NZ, NY, NX) + t[:2], t[2]) for t in back.tensors]
    got = [part for parts in got_shapes(back) for part in parts]
    dma = pltpu.SemaphoreType.DMA
    outs = pl.pallas_call(
        functools.partial(block_kernel, ahead, back),
        out_shape=[shape(b, LOW) for b in bufs[1:]]
        + [shape(*s) for s in kept]
        + [shape(t[:2], F32) for t in back.tensors],
        in_specs=[inside, anywhere, anywhere] + [anywhere] * (n - 1) + [inside],
        out_specs=[anywhere] * (n - 1 + len(kept) + n),
        scratch_shapes=[pltpu.VMEM(*s) for s in results + totals + got + scratch]
        + [dma((9 * na,)), dma((9 * na,)), dma((n,)), dma((5 * nb,)), dma((5 * nb,)), dma((44,))]
        + [dma((2, 3)), dma((2, 2)), dma((2, 1)), dma((29,)), dma((29,))],
        compiler_params=pltpu.CompilerParams(
            collective_id=0, has_side_effects=True, vmem_limit_bytes=VMEM_LIMIT
        ),
        name="block_all",
    )(lens, tokens, cotangent, *shards)
    return outs[n - 1 : n + 1], outs[n - 1 + len(kept) :]


def finish_kernel(*refs):
    n = 10
    ins, outs, held, made = refs[:n], refs[n : 2 * n + 1], refs[2 * n + 1 : 3 * n + 1], refs[3 * n + 1 : 4 * n + 2]
    sem_in, sem_out = refs[4 * n + 2 :]
    chunks = [(k, pl.ds(j * (held[k].shape[0] // 4), held[k].shape[0] // 4)) for k in (1, 0) for j in range(4)]
    large = [
        pltpu.make_async_copy(ins[k].at[at, :], held[k].at[at, :], sem_in.at[n + j]) for j, (k, at) in enumerate(chunks)
    ]
    gets = [pltpu.make_async_copy(ins[k], held[k], sem_in.at[k]) for k in range(2, n)]
    for copy in large[:2] + gets + large[2:]:
        copy.start()
    puts = []

    def pass_on(some):
        for j in some:
            k, at = chunks[j]
            large[j].wait()
            copy = pltpu.make_async_copy(held[k].at[at, :], outs[k].at[at, :], sem_out.at[n + 1 + j])
            copy.start()
            puts.append(copy)

    def put(k, src):
        copy = pltpu.make_async_copy(src, outs[k], sem_out.at[k])
        copy.start()
        puts.append(copy)

    down, up, gate, out, query, key, value, gain = held[2:]
    pass_on(range(2))
    for copy in gets:
        copy.wait()
    for k, src in ((2, query), (3, key), (4, value), (5, out)):
        put(k, src)
    pass_on(range(2, 5))
    rows, part, tile = query.shape[0], outs[8].shape[0], down.shape[0]
    made[8][...] = down[...][:part]
    put(8, made[8])
    for k, src in ((6, gate), (7, up)):
        values = src[...]
        made[k][...] = jnp.concatenate(
            [values[:, j * tile : j * tile + part] for j in range(values.shape[1] // tile)], axis=1
        )
        put(k, made[k])
    both = gain[...]
    own = jnp.where(lax.axis_index("dp") % 2 == 0, both[:, :rows], both[:, rows:])
    made[9][...] = own[0:1]
    made[10][...] = own[1:2]
    put(9, made[9])
    put(10, made[10])
    pass_on(range(5, 8))
    for copy in puts:
        copy.wait()


def finish_all(mixed, tokens, sums, w_query, w_gate, w_down):
    anywhere = pl.BlockSpec(memory_space=pl.ANY)
    shape = jax.ShapeDtypeStruct
    outs = [shape(mixed.shape, mixed.dtype), shape(tokens.shape, F32)]
    outs += [shape(w_query.shape, F32)] * 4 + [shape(w_gate.shape, F32)] * 2 + [shape(w_down.shape, F32)]
    outs += [shape((1, w_query.shape[0]), F32)] * 2
    ins = [mixed, tokens, *sums]
    return pl.pallas_call(
        finish_kernel,
        out_shape=outs,
        in_specs=[anywhere] * len(ins),
        out_specs=[anywhere] * len(outs),
        scratch_shapes=[pltpu.VMEM(a.shape, a.dtype) for a in ins + outs]
        + [pltpu.SemaphoreType.DMA((len(ins) + 8,)), pltpu.SemaphoreType.DMA((len(outs) + 8,))],
        compiler_params=pltpu.CompilerParams(vmem_limit_bytes=62 * 2**20),
        name="finish_all",
    )(*ins)


def kinds(w_query, w_gate, w_down):
    rows, columns = w_query.shape
    part = w_down.shape[0]
    tile = -(-part // 16) * 16
    wide = w_gate.shape[1] // part * tile
    half, strip = rows // 2, -(-wide // 512) * 128
    long, short = -(-tile // 64) * 16, tile - 3 * (-(-tile // 64) * 16)

    def cuts(kinds, counts):
        return tuple((kind, 0, count) for kind, count in zip(kinds, counts, strict=True))

    def strips(kinds):
        return tuple((kind, 1, min(strip, wide - k * strip)) for k, kind in enumerate(kinds))

    def pairs(letters):
        return tuple("z" + letter + axis for letter in letters for axis in "xy")

    def of(kind, letters):
        if kind == "square":
            return (rows, columns, LOW, cuts(pairs(letters), (half, half)))
        if kind == "broad":
            return (rows, wide, LOW, strips(pairs(letters)))
        if kind == "tall":
            return (tile, columns, LOW, cuts(pairs(letters), (long, long, long, short)))
        if kind == "gain":
            return (16, 2 * rows, LOW, cuts(("zfx",), (16,)))
        return (8, 2 * rows, F32, cuts(("zfx",), (8,)))

    return of


def gather_plan(w_query, w_key, w_value, w_out, w_gate, w_up, w_down, gain_attn, gain_mlp):
    kind = kinds(w_query, w_gate, w_down)
    names = GATHER_KINDS
    plan = Plan([kind(*name) for name in names])
    both = jnp.concatenate([gain_attn[None], gain_mlp[None]], axis=0)
    shards = [
        both,
        w_query,
        w_key,
        w_value,
        w_out,
        w_gate,
        w_up,
        w_down,
    ]
    return plan, shards


def swift_block(
    tokens,
    seq_lengths,
    w_query,
    w_key,
    w_value,
    w_out,
    w_gate,
    w_up,
    w_down,
    gain_attn,
    gain_mlp,
    cotangent,
):
    plan, shards = gather_plan(w_query, w_key, w_value, w_out, w_gate, w_up, w_down, gain_attn, gain_mlp)
    kind = kinds(w_query, w_gate, w_down)
    names = SCATTER_KINDS
    back = Plan([kind(*name) for name in names])
    results, sums = block_all(plan, back, seq_lengths, tokens, cotangent, shards)
    outs = finish_all(results[0], results[1], sums, w_query, w_gate, w_down)
    return (*outs[:9], outs[9].reshape(-1), outs[10].reshape(-1))


def solution(mesh):
    fast = (mesh.shape["dp"], mesh.shape["seq"]) == (NZ * NY * NX, 2)
    shards = swift_block if fast else plain_block
    in_specs = (
        P(("dp", "seq"), None),
        P("dp", None),
        P("dp", "seq"),
        P("dp", "seq"),
        P("dp", "seq"),
        P("dp", "seq"),
        P("dp", "seq"),
        P("dp", "seq"),
        P("dp", "seq"),
        P("dp"),
        P("dp"),
        P(("dp", "seq"), None),
    )
    out_specs = (
        P(("dp", "seq"), None),
        P(("dp", "seq"), None),
        P("dp", "seq"),
        P("dp", "seq"),
        P("dp", "seq"),
        P("dp", "seq"),
        P("dp", "seq"),
        P("dp", "seq"),
        P("dp", "seq"),
        P("dp"),
        P("dp"),
    )
    return jax.shard_map(shards, mesh=mesh, in_specs=in_specs, out_specs=out_specs, check_vma=False)
```
